32 devices in a mesh: lat: 8 (over z, x), lon: 4 (over y, core).
Axes of the slice: x: 2, y: 2, z: 4, core: 2. Of those that a mesh axis runs over, the one named last changes fastest.
Arguments:
- displacement: float32 [32, 192, 512], P(None, 'lat', 'lon'), may hold values from -6 to 6
- materials: int32 [32, 192, 512], P(None, 'lat', 'lon'), may hold values from 0 to 3
- ice_mask: int32 [192, 512], P('lat', 'lon'), may hold values 0 or 1
- ice_height: float32 [192, 512], P('lat', 'lon'), may hold values from 0.5 to 3
- shear: float32 [4], replicated, may hold values from 0.5 to 4
- restoring: float32 [4], replicated, may hold values from 0.5 to 2
- contrast: float32 [4], replicated, may hold values from 0.3 to 3
- green: float32 [256, 32, 32], P('lat'), may hold values from -1 to 1
Outputs:
- final_displacement: float32 [32, 192, 512], P(None, 'lat', 'lon')
- potential: float32 [32, 192, 512], P(None, 'lat', 'lon')
The draws below stay inside these ranges and needn't reach their ends.
All inputs are finite; a program needn't handle non-finite values. No bound on the sum of `ice_mask` on one device may be relied on, other than what follows from the above.
Results may differ from the reference program's by a relative error of at most 0.0003.
Values sent between devices are 32-bit elements; how exact they have to be, the bound alone decides.
No kernel may reach another device: no remote copies, remote signals or barrier semaphores. Data moves between devices by JAX's collectives and lax.ppermute only.
A program may use at most 128 MiB of HBM per device.

```python
import math
import jax
import jax.numpy as jnp
from jax import lax

L = 32
LMAX = 256
NMAT = 4
ITERS = 2
SWEEPS = 4
NLAT = 192
NLON = 512


def with_ends(values, key, low, high):
    longest = values.shape.index(max(values.shape))
    spots = []
    for shift in (0, 1):
        where = [jax.random.randint(jax.random.fold_in(key, axis), (), 0, length) for axis, length in enumerate(values.shape)]
        where[longest] = (where[longest] + shift) % values.shape[longest]
        spots.append(tuple(where))
    return values.at[spots[0]].set(low).at[spots[1]].set(high)


def levels(own_key, dims, cuts, low, top_value):
    def one(dim, blocks):
        steps = jax.random.uniform(jax.random.fold_in(jax.random.fold_in(own_key, 6), dim), (blocks,), jnp.float32, low / len(cuts), top_value / len(cuts))
        return jnp.repeat(jnp.exp(steps), dims[dim] // blocks).reshape((-1,) + (1,) * (len(dims) - dim - 1))

    factor_of = one(*cuts[0])
    for cut in cuts[1:]:
        factor_of = factor_of * one(*cut)
    return factor_of


def noise(stream_key, shape, deviation, bound, cuts=(), held_as=jnp.bfloat16):
    entries = jax.random.normal(stream_key, shape, jnp.float32) * deviation
    if len(cuts) > 0:
        entries = levels(stream_key, shape, cuts, -0.22, 0.18) * entries
    return jnp.clip(entries, min=-bound, max=bound).astype(held_as)


def setup_inputs(seed: int = 0) -> dict:
    streams_of = jax.random.split(jax.random.key(seed), 9)
    displacement = noise(streams_of[0], (L, NLAT, NLON), 1.0, 6.0, ((1, 8), (2, 4)), jnp.float32)
    materials = with_ends(jax.random.randint(streams_of[1], (L, NLAT, NLON), 0, NMAT), jax.random.fold_in(streams_of[1], 1), 0, NMAT - 1).astype(jnp.int32)
    ice_mask = with_ends((jax.random.randint(streams_of[2], (NLAT, NLON), 0, 3) < 1).astype(jnp.int32), jax.random.fold_in(streams_of[2], 1), 0, 1)
    ice_height = jnp.clip(jnp.exp(math.log(3.0) - 1.7917595 * jax.random.uniform(streams_of[3], (NLAT, NLON), jnp.float32) ** levels(streams_of[3], (NLAT, NLON), ((0, 8), (1, 4)), -0.2, 0.2)), 0.5, 3.0)
    shear = jnp.clip(jnp.exp(jax.random.uniform(streams_of[4], (NMAT,), jnp.float32, math.log(0.5), math.log(4.0))), 0.5, 4.0)
    restoring = jnp.clip(jnp.exp(jax.random.uniform(streams_of[5], (NMAT,), jnp.float32, math.log(0.5), math.log(2.0))), 0.5, 2.0)
    contrast = jnp.clip(jnp.exp(jax.random.uniform(streams_of[6], (NMAT,), jnp.float32, math.log(0.3), math.log(3.0))), 0.3, 3.0)
    green = noise(streams_of[7], (LMAX, L, L), L ** -0.5, 1.0, ((0, 8),), jnp.float32)
    return dict(displacement=displacement, materials=materials, ice_mask=ice_mask, ice_height=ice_height, shear=shear, restoring=restoring, contrast=contrast, green=green)


def legendre(theta):
    orders = jnp.arange(LMAX).astype(jnp.int32)
    order_f = orders.astype(jnp.float32)
    cosine = jnp.cos(theta)[:, None]
    sine = jnp.sin(theta)[:, None]
    safe = jnp.maximum(order_f, 1.0)
    growth = jnp.where(orders >= 2, 0.5 * jnp.log((2.0 * safe + 1.0) / (2.0 * safe)), 0.0)
    log_diag = jnp.where(orders >= 1, 0.5 * jnp.log(3.0) + jnp.cumsum(growth), 0.0)
    diagonal = jnp.exp(log_diag[None, :] + order_f[None, :] * jnp.log(sine))

    def advance(carry, degree):
        prev_one, prev_two = carry
        deg_f = degree.astype(jnp.float32)
        first = jnp.sqrt((4.0 * deg_f * deg_f - 1.0) / jnp.maximum(deg_f * deg_f - order_f * order_f, 1.0))
        second = jnp.sqrt(jnp.maximum((deg_f - 1.0) ** 2 - order_f * order_f, 0.0) / jnp.maximum(4.0 * (deg_f - 1.0) ** 2 - 1.0, 1.0))
        general = first * (cosine * prev_one - second * prev_two)
        start_next = jnp.sqrt(2.0 * order_f + 3.0) * cosine * diagonal
        value = jnp.where(orders == degree, diagonal, jnp.where(orders == degree - 1, start_next, jnp.where(orders < degree - 1, general, 0.0)))
        return ((value, prev_one), value)
    zeros = jnp.zeros((theta.shape[0], LMAX), jnp.float32)
    _, table = lax.scan(advance, (zeros, zeros), jnp.arange(LMAX).astype(jnp.int32))
    return table

def fourier_tables(columns, total):
    orders = jnp.arange(LMAX).astype(jnp.int32)
    phase = columns[:, None] * orders[None, :] % total
    angle = 2.0 * jnp.pi / total * phase.astype(jnp.float32)
    forward = jnp.concatenate([jnp.cos(angle), jnp.sin(angle)], axis=1) * (2.0 * jnp.pi / total)
    inverse = jnp.concatenate([jnp.cos(angle), jnp.sin(angle)], axis=1).T
    return (forward, inverse)

def lookup(materials, table):
    result = jnp.zeros(materials.shape, jnp.float32)
    for material in range(NMAT):
        result = result + jnp.where(materials == material, table[material], 0.0)
    return result

def sweep(field, force, stiff, restore):
    lat_pad = jnp.pad(field, ((0, 0), (1, 1), (0, 0)))
    layer_pad = jnp.pad(field, ((1, 1), (0, 0), (0, 0)))
    beside_all = lat_pad[:, 2:] + lat_pad[:, :-2] + jnp.roll(field, 1, 2) + jnp.roll(field, -1, 2)
    beside_all = beside_all + layer_pad[2:] + layer_pad[:-2]
    return (force + stiff * beside_all) / (6.0 * stiff + restore)

def reference(displacement, materials, ice_mask, ice_height, shear, restoring, contrast, green):
    highest = lax.Precision.HIGHEST
    stiff = lookup(materials, shear)
    restore = lookup(materials, restoring)
    rho_scale = lookup(materials, contrast)
    surface = (ice_mask.astype(jnp.float32) * ice_height)[None]
    load = jnp.concatenate([surface, jnp.zeros((L - 1, NLAT, NLON), jnp.float32)], axis=0)
    theta = (jnp.arange(NLAT).astype(jnp.float32) + 0.5) * (jnp.pi / NLAT)
    table = legendre(theta)
    weights = jnp.sin(theta) / (4.0 * NLAT)
    forward, inverse = fourier_tables(jnp.arange(NLON).astype(jnp.int32), NLON)
    field = displacement
    potential = jnp.zeros((L, NLAT, NLON), jnp.float32)
    for iteration in range(ITERS):
        force = load + potential
        for sweep_index in range(SWEEPS):
            field = sweep(field, force, stiff, restore)
        density = rho_scale * field
        spectrum = jnp.dot(density.reshape(L * NLAT, NLON), forward, precision=highest, preferred_element_type=jnp.float32).reshape(L, NLAT, 2, LMAX)
        spectrum = spectrum * weights[None, :, None, None]
        coeffs = jnp.einsum('lam,kacm->lkcm', table, spectrum, precision=highest)
        pot_coeffs = jnp.einsum('lkj,ljcm->lkcm', green, coeffs, precision=highest)
        synth = jnp.einsum('lam,lkcm->kacm', table, pot_coeffs, precision=highest)
        potential = jnp.dot(synth.reshape(L * NLAT, 2 * LMAX), inverse, precision=highest, preferred_element_type=jnp.float32).reshape(L, NLAT, NLON)
    return (field, potential)
```

```python
import functools
import math

import jax
import jax.numpy as jnp
from jax import lax
from jax.experimental import pallas as pl
from jax.experimental.pallas import tpu as pltpu
from jax.sharding import PartitionSpec as P

LMAX = 256
NMAT = 4
ITERS = 2
SWEEPS = 4
LANES = 128
DEEP = 8
SHALLOW = 4
HALF = jnp.bfloat16
VMEM_LIMIT = 48 * 1024 * 1024
BOTH = ("lat", "lon")


def extended(cells, sides, width, closed):
    for axis, dim in sides:
        count = lax.axis_size(axis)
        ends = count if closed else count - 1
        head = lax.slice_in_dim(cells, 0, width, axis=dim)
        tail = lax.slice_in_dim(cells, cells.shape[dim] - width, cells.shape[dim], axis=dim)
        cells = jnp.concatenate(
            [
                lax.ppermute(tail, axis, [(i, (i + 1) % count) for i in range(ends)]),
                cells,
                lax.ppermute(head, axis, [((i + 1) % count, i) for i in range(ends)]),
            ],
            axis=dim,
        )
    return cells


def legendre(theta):
    orders = jnp.arange(LMAX)
    order_f = orders.astype(jnp.float32)
    cosine = jnp.cos(theta)[:, None]
    sine = jnp.sin(theta)[:, None]
    safe = jnp.maximum(order_f, 1.0)
    growth = jnp.where(orders >= 2, 0.5 * jnp.log((2.0 * safe + 1.0) / (2.0 * safe)), 0.0)
    log_diag = jnp.where(orders >= 1, 0.5 * jnp.log(3.0) + jnp.cumsum(growth), 0.0)
    diagonal = jnp.exp(log_diag[None, :] + order_f[None, :] * jnp.log(sine))

    def advance(carry, degree):
        prev_one, prev_two = carry
        deg_f = degree.astype(jnp.float32)
        first = jnp.sqrt(
            (4.0 * deg_f * deg_f - 1.0) / jnp.maximum(deg_f * deg_f - order_f * order_f, 1.0)
        )
        second = jnp.sqrt(
            jnp.maximum((deg_f - 1.0) ** 2 - order_f * order_f, 0.0)
            / jnp.maximum(4.0 * (deg_f - 1.0) ** 2 - 1.0, 1.0)
        )
        general = first * (cosine * prev_one - second * prev_two)
        start_next = jnp.sqrt(2.0 * order_f + 3.0) * cosine * diagonal
        value = jnp.where(
            orders == degree,
            diagonal,
            jnp.where(
                orders == degree - 1, start_next, jnp.where(orders < degree - 1, general, 0.0)
            ),
        )
        return ((value, prev_one), value)

    zeros = jnp.zeros((theta.shape[0], LMAX), jnp.float32)
    _, table = lax.scan(advance, (zeros, zeros), jnp.arange(LMAX), unroll=8)
    return table


def fourier_tables(columns, total):
    orders = jnp.arange(LMAX)
    phase = columns[:, None] * orders[None, :] % total
    angle = 2.0 * jnp.pi / total * phase.astype(jnp.float32)
    forward = jnp.concatenate([jnp.cos(angle), jnp.sin(angle)], axis=1) * (2.0 * jnp.pi / total)
    inverse = jnp.concatenate([jnp.cos(angle), jnp.sin(angle)], axis=1).T
    return (forward, inverse)


def lookup(materials, table):
    result = jnp.zeros(materials.shape, jnp.float32)
    for material in range(NMAT):
        result = result + jnp.where(materials == material, table[material], 0.0)
    return result


def crop_block(block, margin):
    return block[:, margin : block.shape[1] - margin, margin : block.shape[2] - margin]


def margin_sweeps(field, force, stiff, restore, depth, lat_first, total_lat):
    stacked = jnp.stack([field, force, stiff, restore], axis=0)
    lat_wide = extended(stacked, (("lat", 2),), depth, False)
    wide = extended(lat_wide, (("lon", 3),), depth, True)
    current = wide[0]
    rows_wide = wide.shape[2]
    global_rows = lat_first - depth + jnp.arange(rows_wide)
    inside = ((global_rows >= 0) & (global_rows < total_lat))[None, :, None]
    for step in range(depth):
        margin = step + 1
        inner = current[:, 1:-1, 1:-1]
        beside_all = (
            current[:, 2:, 1:-1]
            + current[:, :-2, 1:-1]
            + current[:, 1:-1, 2:]
            + current[:, 1:-1, :-2]
        )
        layer_pad = jnp.pad(inner, ((1, 1), (0, 0), (0, 0)))
        beside_all = beside_all + layer_pad[2:] + layer_pad[:-2]
        force_part = crop_block(wide[1], margin)
        stiff_part = crop_block(wide[2], margin)
        restore_part = crop_block(wide[3], margin)
        valid = inside[:, margin : rows_wide - margin, :]
        denominator = jnp.where(valid, 6.0 * stiff_part + restore_part, 1.0)
        current = jnp.where(valid, (force_part + stiff_part * beside_all) / denominator, 0.0)
    return current


def general_device(displacement, materials, ice_mask, ice_height, shear, restoring, contrast, green):
    highest = lax.Precision.HIGHEST
    layers, lat_rows, lon_cols = displacement.shape
    lon_count = lax.axis_size("lon")
    lat_count = lax.axis_size("lat")
    total_lat = lat_rows * lat_count
    total_lon = lon_cols * lon_count
    layer_share = layers // lon_count
    stiff = lookup(materials, shear)
    restore = lookup(materials, restoring)
    rho_scale = lookup(materials, contrast)
    surface = (ice_mask.astype(jnp.float32) * ice_height)[None]
    load = jnp.concatenate(
        [surface, jnp.zeros((layers - 1, lat_rows, lon_cols), jnp.float32)], axis=0
    )
    lat_first = lax.axis_index("lat") * lat_rows
    theta = ((lat_first + jnp.arange(lat_rows)).astype(jnp.float32) + 0.5) * (jnp.pi / total_lat)
    table = legendre(theta)
    weights = jnp.sin(theta) / (4.0 * total_lat)
    own_columns = lax.axis_index("lon") * lon_cols + jnp.arange(lon_cols)
    layer_first = lax.axis_index("lon") * layer_share
    depth = 1
    for candidate in range(1, SWEEPS + 1):
        if SWEEPS % candidate == 0 and candidate <= min(lat_rows, lon_cols):
            depth = candidate
    forward, inverse = fourier_tables(own_columns, total_lon)
    field = displacement
    potential = jnp.zeros((layers, lat_rows, lon_cols), jnp.float32)
    for iteration in range(ITERS):
        force = load + potential
        field = margin_sweeps(field, force, stiff, restore, depth, lat_first, total_lat)
        density = rho_scale * field
        product = jnp.dot(
            density.reshape(layer_share * lax.axis_size("lon") * lat_rows, lon_cols),
            forward,
            precision=highest,
            preferred_element_type=jnp.float32,
        )
        spectrum = lax.psum_scatter(
            product.reshape(layer_share * lax.axis_size("lon"), lat_rows, 2 * LMAX),
            "lon",
            scatter_dimension=0,
            tiled=True,
        )
        weighted = spectrum.reshape(layer_share, lat_rows, 2, LMAX) * weights[None, :, None, None]
        coeffs = lax.psum_scatter(
            jnp.einsum("lam,kacm->lkcm", table, weighted, precision=highest),
            "lat",
            scatter_dimension=0,
            tiled=True,
        )
        green_part = lax.dynamic_slice_in_dim(green, layer_first, layer_share, 2)
        partial_pot = jnp.einsum("lkj,ljcm->lkcm", green_part, coeffs, precision=highest)
        pot_coeffs = lax.psum_scatter(partial_pot, "lon", scatter_dimension=1, tiled=True)
        synth = jnp.einsum(
            "lam,lkcm->kacm",
            table,
            lax.all_gather(pot_coeffs, "lat", axis=0, tiled=True),
            precision=highest,
        )
        synth = synth.reshape(layer_share, lat_rows, 2 * LMAX)
        piece = lax.all_gather(synth, "lon", axis=0, tiled=True)
        synth_product = jnp.dot(
            piece.reshape(piece.shape[0] * lat_rows, 2 * LMAX),
            inverse,
            precision=highest,
            preferred_element_type=jnp.float32,
        )
        potential = synth_product.reshape(piece.shape[0], lat_rows, lon_cols)
    return (field, potential)


def call(kernel, outs, scratch=(), cost=0, smem=()):
    def run(*args):
        specs = [
            pl.BlockSpec(memory_space=pltpu.SMEM if i in smem else pltpu.VMEM)
            for i in range(len(args))
        ]
        out_specs = jax.tree.map(lambda _: pl.BlockSpec(memory_space=pltpu.VMEM), outs)
        return pl.pallas_call(
            kernel,
            out_shape=outs,
            in_specs=specs,
            out_specs=out_specs,
            scratch_shapes=list(scratch),
            compiler_params=pltpu.CompilerParams(vmem_limit_bytes=VMEM_LIMIT),
            cost_estimate=pl.CostEstimate(flops=cost, bytes_accessed=1 << 20, transcendentals=0),
        )(*args)

    return run


def f32(*shape):
    return jax.ShapeDtypeStruct(shape, jnp.float32)


def halves(x):
    high = x.astype(HALF)
    return high, (x - high.astype(jnp.float32)).astype(HALF)


def dot(a, b, dims):
    return lax.dot_general(a, b, (dims, ((), ())), preferred_element_type=jnp.float32)


def dot3(a, b, dims):
    return dot(a[0], b[0], dims) + (dot(a[0], b[1], dims) + dot(a[1], b[0], dims))


def every(ref, start, stride, count):
    at = pl.ds(start, count, stride=stride)
    return jnp.concatenate([ref[c, at, :] for c in range(ref.shape[0])], axis=1)


def put_every(ref, start, stride, value):
    at = pl.ds(start, value.shape[0], stride=stride)
    for c in range(ref.shape[0]):
        ref[c, at, :] = value[:, c * LANES : (c + 1) * LANES]


NN = ((1,), (0,))
NT = ((1,), (1,))


def iota(shape, dim):
    return lax.broadcasted_iota(jnp.int32, shape, dim)


def fourier_kernel(total, share, high_ref, low_ref):
    rows = 32

    def block(i, carry):
        column = iota((rows, 2 * LMAX), 1)
        owner = column // (2 * share)
        part = (column // share) % 2
        order = owner * share + column % share
        j = iota((rows, 2 * LMAX), 0) + i * rows
        phase = lax.rem(j * order + part * (total - total // 4), total)
        value = jnp.cos((2.0 * math.pi / total) * phase.astype(jnp.float32))
        at = pl.ds(pl.multiple_of(i * rows, rows), rows)
        high, low = halves(value)
        high_ref[at, :] = high
        low_ref[at, :] = low
        return carry

    lax.fori_loop(0, total // rows, block, 0)


def legendre_kernel(total_lat, share, index_ref, high_ref, low_ref, table):
    width = table.shape[0] * LANES
    base = index_ref[0] * share
    shape = (share, width)
    order = iota(shape, 0) + base
    order_f = order.astype(jnp.float32)
    row = iota(shape, 1)
    theta = (row.astype(jnp.float32) + 0.5) * (math.pi / total_lat)
    cosine = jnp.cos(theta)
    sine = jnp.where(row < total_lat, jnp.sin(theta), 1.0)
    terms = (share, LMAX)
    term = iota(terms, 1)
    term_f = jnp.maximum(term.astype(jnp.float32), 1.0)
    growth = 0.5 * jnp.log((2.0 * term_f + 1.0) / (2.0 * term_f))
    used = (term >= 2) & (term <= iota(terms, 0) + base)
    total = jnp.sum(jnp.where(used, growth, 0.0), axis=1, keepdims=True)
    log_diag = jnp.where(order >= 1, 0.5 * math.log(3.0) + total, 0.0)
    diagonal = jnp.exp(log_diag + order_f * jnp.log(sine))
    diagonal = jnp.where(row < total_lat, diagonal, 0.0)
    start_next = jnp.sqrt(2.0 * order_f + 3.0) * cosine * diagonal
    narrow = (share, LANES)
    square = ((iota(narrow, 0) + base).astype(jnp.float32)) ** 2

    def wide(x):
        return jnp.concatenate([x] * (width // LANES), axis=1)

    def advance(degree, carry):
        prev_one, prev_two = carry
        deg = jnp.full(narrow, degree, jnp.int32).astype(jnp.float32)
        first = jnp.sqrt((4.0 * deg * deg - 1.0) / jnp.maximum(deg * deg - square, 1.0))
        below = (deg - 1.0) * (deg - 1.0)
        second = jnp.sqrt(jnp.maximum(below - square, 0.0) / jnp.maximum(4.0 * below - 1.0, 1.0))
        general = wide(first) * (cosine * prev_one - wide(second) * prev_two)
        value = jnp.where(
            order == degree,
            diagonal,
            jnp.where(
                order == degree - 1, start_next, jnp.where(order < degree - 1, general, 0.0)
            ),
        )
        for c in range(width // LANES):
            at = pl.ds(pl.multiple_of(degree * share, share), share)
            table[c, at, :] = value[:, c * LANES : (c + 1) * LANES]
        return (value, prev_one)

    table[:, 0:share, :] = jnp.zeros((width // LANES, share, LANES), jnp.float32)
    zeros = jnp.concatenate([table[c, 0:share, :] for c in range(width // LANES)], axis=1)
    lax.fori_loop(0, LMAX, advance, (zeros, zeros), unroll=8)
    for m in range(share):
        high, low = halves(every(table, m, share, LMAX))
        high_ref[m] = high
        low_ref[m] = low


def turn_kernel(x_ref, o_ref):
    o_ref[...] = x_ref[...].T


def pack_kernel(u_ref, mat_ref, mask_ref, height_ref, above_ref, below_ref, first_ref, last_ref):
    layers, rows, cols = u_ref.shape
    group = LANES // DEEP
    lane = iota((rows + 2 * DEEP, cols), 1)

    def pack(cells, count):
        for block in range(-(-count // group)):
            first = jnp.zeros(lane.shape, jnp.float32)
            last = first
            for t in range(min(group, count - block * group)):
                x = cells(block * group + t)
                chosen = lane // DEEP == t
                first = jnp.where(chosen, roll(x, t * DEEP, 1), first)
                last = jnp.where(chosen, roll(x, (t + 1) * DEEP, 1), last)
            yield first, last

    def tall(own, at):
        return jnp.concatenate([above_ref[at], own, below_ref[at]], axis=0)

    surface = mask_ref[...].astype(jnp.float32) * height_ref[...]
    blocks = [
        *pack(lambda k: tall(u_ref[k], k), layers),
        *pack(lambda k: tall(mat_ref[k].astype(jnp.float32), layers + k), layers),
        *pack(lambda k: tall(surface, 2 * layers), 1),
    ]
    for i, (first, last) in enumerate(blocks):
        first_ref[i] = first
        last_ref[i] = last


def roll(x, shift, axis):
    shift = shift % x.shape[axis]
    return x if shift == 0 else pltpu.roll(x, shift, axis)


def pick(material, table):
    value = jnp.full(material.shape, table[NMAT - 1], jnp.float32)
    for i in range(NMAT - 1):
        value = jnp.where(material == i, table[i], value)
    return value


def run_sweeps(a_ref, f_ref, now, other):
    layers, rows, width = a_ref.shape
    for sweep in range(SWEEPS):
        src, dst = (now, other) if sweep % 2 == 0 else (other, now)

        def layer(k, carry, src=src, dst=dst):
            x = src[k + 1]
            total = roll(x, 1, 1) + roll(x, width - 1, 1) + roll(x, 1, 0) + roll(x, rows - 1, 0)
            total = total + src[k] + src[k + 2]
            dst[k + 1] = a_ref[k] * total + f_ref[k]
            return carry

        lax.fori_loop(0, layers, layer, 0, unroll=2)


def clear_ends(ref):
    zero = jnp.zeros(ref.shape[1:], jnp.float32)
    ref[0] = zero
    ref[ref.shape[0] - 1] = zero


def put_density(material, field, contrast, index_ref, lon_count, layers, scratch, pieces):
    share = layers // lon_count
    for k in range(layers):
        scratch[k // share, k % share] = pick(material(k), contrast) * field(k)
    for s in range(lon_count):
        pieces[s][...] = scratch[lax.rem(index_ref[1] + s, lon_count)]


def first_sweeps_kernel(
    lon_count, total_lat, index_ref, shear_ref, restoring_ref, contrast_ref, u_ref, mat_ref, mask_ref,
    height_ref, above_ref, below_ref, left_ref, right_ref, *rest,
):
    pieces, rest = rest[:lon_count], rest[lon_count:]
    u_out, a_out, b_out, load_out, now, other, a_scr, b_scr, f_scr, d_scr = rest
    layers, rows, cols = u_ref.shape
    tall_rows = rows + 2 * DEEP
    group = LANES // DEEP
    cell = (8, LANES)
    a_of, b_of = [], []
    for i in range(NMAT):
        stiff = jnp.full(cell, shear_ref[i], jnp.float32)
        restore = jnp.full(cell, restoring_ref[i], jnp.float32)
        b_of.append(1.0 / (6.0 * stiff + restore))
        a_of.append(stiff * b_of[i])
    wide_shape = (tall_rows, cols + LANES)
    spread = lambda x: jnp.concatenate(
        [jnp.concatenate([x] * (wide_shape[1] // LANES), axis=1)] * (tall_rows // 8), axis=0
    )
    a_of = [spread(x) for x in a_of]
    b_of = [spread(x) for x in b_of]
    lane = iota((tall_rows, LANES), 1)
    global_row = iota(wide_shape, 0) + (index_ref[0] * rows - DEEP)
    inside = (global_row >= 0) & (global_row < total_lat)

    def widened(own, at, block, t):
        main = jnp.concatenate([above_ref[at], own, below_ref[at]], axis=0)
        right = roll(right_ref[block], LANES - t * DEEP, 1)
        left = roll(left_ref[block], LANES - (t + 1) * DEEP, 1)
        side = jnp.where(lane < DEEP, right, jnp.where(lane >= LANES - DEEP, left, 0.0))
        return jnp.concatenate([main, side], axis=1)

    blocks = layers // group
    clear_ends(now)
    clear_ends(other)
    load = widened(
        mask_ref[...].astype(jnp.float32) * height_ref[...], 2 * layers, 2 * blocks, 0
    )
    zero = jnp.zeros(wide_shape, jnp.float32)
    for k in range(layers):
        now[k + 1] = widened(u_ref[k], k, k // group, k % group)
        material = widened(
            mat_ref[k].astype(jnp.float32), layers + k, blocks + k // group, k % group
        )
        a_scr[k] = jnp.where(inside, pick(material, a_of), 0.0)
        b = jnp.where(inside, pick(material, b_of), 0.0)
        b_scr[k] = b
        f_scr[k] = b * load if k == 0 else zero
    run_sweeps(a_scr, f_scr, now, other)
    keep = pl.ds(DEEP - SHALLOW, rows + 2 * SHALLOW)
    for k in range(layers):
        u_out[k] = now[k + 1, keep, :]
        a_out[k] = a_scr[k, keep, :]
        b_out[k] = b_scr[k, keep, :]
    load_out[...] = load[DEEP - SHALLOW : rows + DEEP + SHALLOW]
    put_density(
        lambda k: mat_ref[k],
        lambda k: now[k + 1, pl.ds(DEEP, rows), pl.ds(0, cols)],
        contrast_ref,
        index_ref,
        lon_count,
        layers,
        d_scr,
        pieces,
    )


def second_sweeps_kernel(
    lon_count, index_ref, contrast_ref, mat_ref, u_ref, a_ref, b_ref, load_ref, *rest
):
    parts, rest = rest[:lon_count], rest[lon_count:]
    pieces, rest = rest[:lon_count], rest[lon_count:]
    field_out, now, other, f_scr, d_scr = rest
    layers, rows, cols = mat_ref.shape
    tall_rows = rows + 2 * SHALLOW
    share = layers // lon_count
    chunk = LANES // share
    lane = iota((tall_rows, LANES), 1)
    clear_ends(now)
    clear_ends(other)
    for s in range(lon_count):
        source = lax.rem(index_ref[1] + (lon_count - s), lon_count)
        packed = parts[s][share * tall_rows :]
        for t in range(share):
            k = source * share + t
            main = parts[s][t * tall_rows : (t + 1) * tall_rows]
            right = roll(packed, LANES - t * chunk, 1)
            left = roll(packed, LANES - (t + 1) * chunk, 1)
            side = jnp.where(lane < DEEP, right, left)
            f_scr[k] = b_ref[k] * jnp.concatenate([main, side], axis=1)
    f_scr[0] = f_scr[0] + b_ref[0] * load_ref[...]
    for k in range(layers):
        now[k + 1] = u_ref[k]
    run_sweeps(a_ref, f_scr, now, other)

    def field(k):
        return now[k + 1, pl.ds(SHALLOW, rows), pl.ds(0, cols)]

    for k in range(layers):
        field_out[k] = field(k)
    put_density(
        lambda k: mat_ref[k], field, contrast_ref, index_ref, lon_count, layers, d_scr, pieces
    )


def swap_chunks(blocks, chunk):
    blocks = list(blocks)
    lane = iota(blocks[0].shape, 1)
    step = 1
    while step < len(blocks):
        upper = (lane // (chunk * step)) % 2 == 1
        for i in range(len(blocks)):
            if i & step:
                continue
            a, b = blocks[i], blocks[i + step]
            blocks[i] = jnp.where(upper, roll(b, chunk * step, 1), a)
            blocks[i + step] = jnp.where(upper, b, roll(a, LANES - chunk * step, 1))
        step *= 2
    return blocks


def forward_kernel(lon_count, scale, index_ref, weight_ref, high_ref, low_ref, *rest):
    parts, (o_ref,) = rest[:lon_count], rest[lon_count:]
    share, rows, cols = parts[0].shape
    chunk = LANES // share
    product = None
    for s in range(lon_count):
        source = lax.rem(index_ref[1] + (lon_count - s), lon_count)
        at = pl.ds(pl.multiple_of(source * cols, cols), cols)
        term = dot3(
            halves(parts[s][...].reshape(share * rows, cols)), (high_ref[at, :], low_ref[at, :]), NN
        )
        product = term if product is None else product + term
    weight = weight_ref[...] * scale
    for g in range(product.shape[1] // LANES):
        blocks = swap_chunks(
            [
                product[k * rows : (k + 1) * rows, g * LANES : (g + 1) * LANES] * weight
                for k in range(share)
            ],
            chunk,
        )
        for i in range(share):
            o_ref[g * share + i] = blocks[i]


def spectral_kernel(margin, high_ref, low_ref, green_ref, x_ref, o_ref, turned, coeffs, pots):
    share, degrees, width = high_ref.shape
    lat_count, lon_count, rows, _ = x_ref.shape
    total_lat = lat_count * rows
    size = 2 * share
    layers = turned.shape[1] // size
    pad = jnp.zeros((width - total_lat, LANES), jnp.float32)
    for q in range(lon_count):
        x = x_ref[:, q].reshape(total_lat, LANES)
        x = jnp.concatenate([x, pad], axis=0)
        for c in range(width // LANES):
            turned[c, q * LANES : (q + 1) * LANES, :] = x[c * LANES : (c + 1) * LANES].T
    for m in range(share):
        x = halves(every(turned, m, share, 2 * layers))
        put_every(coeffs, m, share, dot3(x, (high_ref[m], low_ref[m]), NT))
    block = 4

    def targets(i, carry):
        for c in range(degrees // LANES):
            sums = [jnp.zeros((size, LANES), jnp.float32) for _ in range(block)]
            for k in range(0, layers, 8):
                part = [
                    green_ref[
                        pl.ds(pl.multiple_of((i * block + t) * layers + k, 8), 8),
                        c * LANES : (c + 1) * LANES,
                    ]
                    for t in range(block)
                ]
                for e in range(8):
                    x = coeffs[c, (k + e) * size : (k + e + 1) * size, :]
                    for t in range(block):
                        sums[t] = sums[t] + part[t][e : e + 1] * x
            for t in range(block):
                pots[c, pl.ds(pl.multiple_of((i * block + t) * size, size), size), :] = sums[t]
        return carry

    lax.fori_loop(0, layers // block, targets, 0)
    for m in range(share):
        x = halves(every(pots, m, share, 2 * layers))
        put_every(turned, m, share, dot3(x, (high_ref[m], low_ref[m]), NN))
    for q in range(lon_count):
        x = [turned[c, q * LANES : (q + 1) * LANES, :].T for c in range(width // LANES)]
        x = jnp.concatenate(x, axis=0)[:total_lat]
        if margin > 0:
            edge = jnp.zeros((margin, LANES), jnp.float32)
            x = jnp.concatenate([edge, x, edge], axis=0)
        for i in range(lat_count):
            o_ref[i, q] = x[i * rows : (i + 1) * rows + 2 * margin]


def inverse_kernel(lon_count, margin, index_ref, high_ref, low_ref, x_ref, *rest):
    pieces, (columns,) = rest[:lon_count], rest[lon_count:]
    owners, rows, _ = x_ref.shape
    cols = high_ref.shape[0] // lon_count
    share = columns.shape[1] // rows
    chunk = LANES // share
    groups = [
        swap_chunks([x_ref[g * share + i] for i in range(share)], chunk)
        for g in range(owners // share)
    ]
    terms = jnp.concatenate(
        [jnp.concatenate([group[k] for group in groups], axis=1) for k in range(share)], axis=0
    )
    terms = halves(terms)
    for q in range(lon_count):
        at = slice(q * cols, (q + 1) * cols)
        columns[q] = dot3(terms, (high_ref[at, :], low_ref[at, :]), NT)
    lane = iota((rows, LANES), 1)
    for s in range(lon_count):
        dest = lax.rem(index_ref[1] + s, lon_count)
        pieces[s][0 : share * rows] = columns[dest]
        if margin == 0:
            continue
        after = lax.rem(dest + 1, lon_count)
        before = lax.rem(dest + lon_count - 1, lon_count)
        packed = jnp.zeros((rows, LANES), jnp.float32)
        for k in range(share):
            right = roll(columns[after, k * rows : (k + 1) * rows, :], k * chunk, 1)
            left = roll(columns[before, k * rows : (k + 1) * rows, :], (k + 1) * chunk, 1)
            packed = jnp.where(
                lane // DEEP == 2 * k, right, jnp.where(lane // DEEP == 2 * k + 1, left, packed)
            )
        pieces[s][share * rows :] = packed


def assemble_kernel(lon_count, index_ref, *rest):
    parts, (o_ref,) = rest[:lon_count], rest[lon_count:]
    share = o_ref.shape[1]
    for s in range(lon_count):
        source = lax.rem(index_ref[1] + (lon_count - s), lon_count)
        o_ref[source] = parts[s][...].reshape(o_ref.shape[1:])


def exchange(pieces):
    count = len(pieces)
    return [pieces[0]] + [
        lax.ppermute(pieces[s], "lon", [(i, (i + s) % count) for i in range(count)])
        for s in range(1, count)
    ]


def on_device(displacement, materials, ice_mask, ice_height, shear, restoring, contrast, green):
    layers, rows, cols = displacement.shape
    lat_count, lon_count = lax.axis_size("lat"), lax.axis_size("lon")
    total_lat, total_lon = rows * lat_count, cols * lon_count
    owners = lat_count * lon_count
    share, orders = layers // lon_count, LMAX // owners
    width = -(-total_lat // LANES) * LANES
    tall = rows + 2 * SHALLOW
    lat_index = lax.axis_index("lat")
    index = jnp.stack([lat_index, lax.axis_index("lon")]).astype(jnp.int32)
    owner = (index[0] * lon_count + index[1])[None]

    down = [(i, i + 1) for i in range(lat_count - 1)]
    up = [(i + 1, i) for i in range(lat_count - 1)]

    def slab(at):
        return jnp.concatenate(
            [
                displacement[:, at],
                materials[:, at].astype(jnp.float32),
                (ice_mask[at].astype(jnp.float32) * ice_height[at])[None],
            ],
            axis=0,
        )

    above = lax.ppermute(slab(slice(rows - DEEP, rows)), "lat", down)
    below = lax.ppermute(slab(slice(0, DEEP)), "lat", up)
    all_green = lax.all_gather(
        green.reshape(green.shape[0], layers * layers), "lat", axis=0, tiled=True
    )
    table = call(
        functools.partial(fourier_kernel, total_lon, orders),
        (jax.ShapeDtypeStruct((total_lon, 2 * LMAX), HALF),) * 2,
        cost=100_000_000,
    )()
    blocks = 2 * (layers * DEEP // LANES) + 1
    first, last = call(
        pack_kernel, (f32(blocks, rows + 2 * DEEP, cols),) * 2, cost=10_000_000
    )(displacement, materials, ice_mask, ice_height, above, below)
    left = lax.ppermute(last, "lon", [(i, (i + 1) % lon_count) for i in range(lon_count)])
    right = lax.ppermute(first, "lon", [((i + 1) % lon_count, i) for i in range(lon_count)])
    legendre_table = call(
        functools.partial(legendre_kernel, total_lat, orders),
        (jax.ShapeDtypeStruct((orders, LMAX, width), HALF),) * 2,
        scratch=[pltpu.VMEM((width // LANES, LMAX * orders, LANES), jnp.float32)],
        cost=100_000_000,
        smem=(0,),
    )(owner)
    theta = ((lat_index * rows + jnp.arange(rows)).astype(jnp.float32) + 0.5) * (
        jnp.pi / total_lat
    )
    weight = jnp.broadcast_to((jnp.sin(theta) / (4.0 * total_lat))[:, None], (rows, LANES))

    deep = pltpu.VMEM((layers + 2, rows + 2 * DEEP, cols + LANES), jnp.float32)
    deep_in = pltpu.VMEM((layers, rows + 2 * DEEP, cols + LANES), jnp.float32)
    flat = pltpu.VMEM((lon_count, share, rows, cols), jnp.float32)
    kept = f32(layers, tall, cols + LANES)
    out = call(
        functools.partial(first_sweeps_kernel, lon_count, total_lat),
        (f32(share, rows, cols),) * lon_count + (kept,) * 3 + (f32(tall, cols + LANES),),
        scratch=[deep, deep, deep_in, deep_in, deep_in, flat],
        cost=100_000_000,
        smem=(0, 1, 2, 3),
    )(
        index, shear, restoring, contrast, displacement, materials, ice_mask, ice_height, above,
        below, left, right,
    )
    pieces, state = out[:lon_count], out[lon_count:]
    turned_green = call(turn_kernel, f32(layers * layers, LMAX), cost=1_000_000)(all_green)

    for iteration in range(ITERS):
        margin = SHALLOW if iteration < ITERS - 1 else 0
        spectrum = call(
            functools.partial(forward_kernel, lon_count, 2.0 * math.pi / total_lon),
            f32(owners, rows, LANES),
            cost=300_000_000,
            smem=(0,),
        )(index, weight, *table, *exchange(pieces))
        spectrum = lax.all_to_all(spectrum, BOTH, 0, 0, tiled=True)
        square = pltpu.VMEM((width // LANES, lon_count * LANES, LANES), jnp.float32)
        coeff_shape = pltpu.VMEM((LMAX // LANES, lon_count * LANES, LANES), jnp.float32)
        synth = call(
            functools.partial(spectral_kernel, margin),
            f32(lat_count, lon_count, rows + 2 * margin, LANES),
            scratch=[square, coeff_shape, coeff_shape],
            cost=300_000_000,
        )(
            *legendre_table,
            turned_green,
            spectrum.reshape(lat_count, lon_count, rows, LANES),
        )
        synth = lax.all_to_all(
            synth.reshape(owners, rows + 2 * margin, LANES), BOTH, 0, 0, tiled=True
        )
        high = rows + 2 * margin
        sent = share * high + (high if margin > 0 else 0)
        parts = call(
            functools.partial(inverse_kernel, lon_count, margin),
            (f32(sent, cols),) * lon_count,
            scratch=[pltpu.VMEM((lon_count, share * high, cols), jnp.float32)],
            cost=300_000_000,
            smem=(0,),
        )(index, *table, synth)
        parts = exchange(parts)
        if iteration < ITERS - 1:
            wide = pltpu.VMEM((layers + 2, tall, cols + LANES), jnp.float32)
            wide_in = pltpu.VMEM((layers, tall, cols + LANES), jnp.float32)
            out = call(
                functools.partial(second_sweeps_kernel, lon_count),
                (f32(share, rows, cols),) * lon_count + (f32(layers, rows, cols),),
                scratch=[wide, wide, wide_in, flat],
                cost=100_000_000,
                smem=(0, 1),
            )(index, contrast, materials, *state, *parts)
            pieces, field = out[:lon_count], out[lon_count]
    potential = call(
        functools.partial(assemble_kernel, lon_count),
        f32(lon_count, share, rows, cols),
        cost=1_000_000,
        smem=(0,),
    )(index, *parts)
    return (field, potential.reshape(layers, rows, cols))


def aligned(mesh, displacement):
    lat_count, lon_count = mesh.shape["lat"], mesh.shape["lon"]
    layers, total_lat, total_lon = displacement.shape
    rows, cols = total_lat // lat_count, total_lon // lon_count
    owners = lat_count * lon_count
    return (
        ITERS == 2
        and cols == LANES
        and rows % 8 == 0
        and layers % (LANES // DEEP) == 0
        and layers % lon_count == 0
        and LMAX % owners == 0
        and 2 * (LMAX // owners) * (layers // lon_count) == LANES
        and 2 * (LMAX // owners) == 2 * DEEP
        and LMAX % LANES == 0
    )


def solution(mesh):
    in_specs = (
        P(None, "lat", "lon"),
        P(None, "lat", "lon"),
        P("lat", "lon"),
        P("lat", "lon"),
        P(),
        P(),
        P(),
        P("lat", None, None),
    )
    out_specs = (P(None, "lat", "lon"), P(None, "lat", "lon"))

    def step(displacement, *others):
        device = on_device if aligned(mesh, displacement) else general_device
        return jax.shard_map(
            device, mesh=mesh, in_specs=in_specs, out_specs=out_specs, check_vma=False
        )(displacement, *others)

    return step
```

```python
import functools
import math

import jax
import jax.numpy as jnp
from jax import lax
from jax.experimental import pallas as pl
from jax.experimental.pallas import tpu as pltpu
from jax.sharding import PartitionSpec as P

LMAX = 256
NMAT = 4
ITERS = 2
SWEEPS = 4
LANES = 128
DEEP = 8
SHALLOW = 4
HALF = jnp.bfloat16
VMEM_LIMIT = 16 * 1024 * 1024
BOTH = ("lat", "lon")


def extended(cells, sides, width, closed):
    for axis, dim in sides:
        count = lax.axis_size(axis)
        ends = count if closed else count - 1
        head = lax.slice_in_dim(cells, 0, width, axis=dim)
        tail = lax.slice_in_dim(cells, cells.shape[dim] - width, cells.shape[dim], axis=dim)
        cells = jnp.concatenate(
            [
                lax.ppermute(tail, axis, [(i, (i + 1) % count) for i in range(ends)]),
                cells,
                lax.ppermute(head, axis, [((i + 1) % count, i) for i in range(ends)]),
            ],
            axis=dim,
        )
    return cells


def legendre(theta):
    orders = jnp.arange(LMAX)
    order_f = orders.astype(jnp.float32)
    cosine = jnp.cos(theta)[:, None]
    sine = jnp.sin(theta)[:, None]
    safe = jnp.maximum(order_f, 1.0)
    growth = jnp.where(orders >= 2, 0.5 * jnp.log((2.0 * safe + 1.0) / (2.0 * safe)), 0.0)
    log_diag = jnp.where(orders >= 1, 0.5 * jnp.log(3.0) + jnp.cumsum(growth), 0.0)
    diagonal = jnp.exp(log_diag[None, :] + order_f[None, :] * jnp.log(sine))

    def advance(carry, degree):
        prev_one, prev_two = carry
        deg_f = degree.astype(jnp.float32)
        first = jnp.sqrt(
            (4.0 * deg_f * deg_f - 1.0) / jnp.maximum(deg_f * deg_f - order_f * order_f, 1.0)
        )
        second = jnp.sqrt(
            jnp.maximum((deg_f - 1.0) ** 2 - order_f * order_f, 0.0)
            / jnp.maximum(4.0 * (deg_f - 1.0) ** 2 - 1.0, 1.0)
        )
        general = first * (cosine * prev_one - second * prev_two)
        start_next = jnp.sqrt(2.0 * order_f + 3.0) * cosine * diagonal
        value = jnp.where(
            orders == degree,
            diagonal,
            jnp.where(
                orders == degree - 1, start_next, jnp.where(orders < degree - 1, general, 0.0)
            ),
        )
        return ((value, prev_one), value)

    zeros = jnp.zeros((theta.shape[0], LMAX), jnp.float32)
    _, table = lax.scan(advance, (zeros, zeros), jnp.arange(LMAX), unroll=8)
    return table


def fourier_tables(columns, total):
    orders = jnp.arange(LMAX)
    phase = columns[:, None] * orders[None, :] % total
    angle = 2.0 * jnp.pi / total * phase.astype(jnp.float32)
    forward = jnp.concatenate([jnp.cos(angle), jnp.sin(angle)], axis=1) * (2.0 * jnp.pi / total)
    inverse = jnp.concatenate([jnp.cos(angle), jnp.sin(angle)], axis=1).T
    return (forward, inverse)


def lookup(materials, table):
    result = jnp.zeros(materials.shape, jnp.float32)
    for material in range(NMAT):
        result = result + jnp.where(materials == material, table[material], 0.0)
    return result


def crop_block(block, margin):
    return block[:, margin : block.shape[1] - margin, margin : block.shape[2] - margin]


def margin_sweeps(field, force, stiff, restore, depth, lat_first, total_lat):
    stacked = jnp.stack([field, force, stiff, restore], axis=0)
    lat_wide = extended(stacked, (("lat", 2),), depth, False)
    wide = extended(lat_wide, (("lon", 3),), depth, True)
    current = wide[0]
    rows_wide = wide.shape[2]
    global_rows = lat_first - depth + jnp.arange(rows_wide)
    inside = ((global_rows >= 0) & (global_rows < total_lat))[None, :, None]
    for step in range(depth):
        margin = step + 1
        inner = current[:, 1:-1, 1:-1]
        beside_all = (
            current[:, 2:, 1:-1]
            + current[:, :-2, 1:-1]
            + current[:, 1:-1, 2:]
            + current[:, 1:-1, :-2]
        )
        layer_pad = jnp.pad(inner, ((1, 1), (0, 0), (0, 0)))
        beside_all = beside_all + layer_pad[2:] + layer_pad[:-2]
        force_part = crop_block(wide[1], margin)
        stiff_part = crop_block(wide[2], margin)
        restore_part = crop_block(wide[3], margin)
        valid = inside[:, margin : rows_wide - margin, :]
        denominator = jnp.where(valid, 6.0 * stiff_part + restore_part, 1.0)
        current = jnp.where(valid, (force_part + stiff_part * beside_all) / denominator, 0.0)
    return current


def general_device(displacement, materials, ice_mask, ice_height, shear, restoring, contrast, green):
    highest = lax.Precision.HIGHEST
    layers, lat_rows, lon_cols = displacement.shape
    lon_count = lax.axis_size("lon")
    lat_count = lax.axis_size("lat")
    total_lat = lat_rows * lat_count
    total_lon = lon_cols * lon_count
    layer_share = layers // lon_count
    stiff = lookup(materials, shear)
    restore = lookup(materials, restoring)
    rho_scale = lookup(materials, contrast)
    surface = (ice_mask.astype(jnp.float32) * ice_height)[None]
    load = jnp.concatenate(
        [surface, jnp.zeros((layers - 1, lat_rows, lon_cols), jnp.float32)], axis=0
    )
    lat_first = lax.axis_index("lat") * lat_rows
    theta = ((lat_first + jnp.arange(lat_rows)).astype(jnp.float32) + 0.5) * (jnp.pi / total_lat)
    table = legendre(theta)
    weights = jnp.sin(theta) / (4.0 * total_lat)
    own_columns = lax.axis_index("lon") * lon_cols + jnp.arange(lon_cols)
    layer_first = lax.axis_index("lon") * layer_share
    depth = 1
    for candidate in range(1, SWEEPS + 1):
        if SWEEPS % candidate == 0 and candidate <= min(lat_rows, lon_cols):
            depth = candidate
    forward, inverse = fourier_tables(own_columns, total_lon)
    field = displacement
    potential = jnp.zeros((layers, lat_rows, lon_cols), jnp.float32)
    for iteration in range(ITERS):
        force = load + potential
        field = margin_sweeps(field, force, stiff, restore, depth, lat_first, total_lat)
        density = rho_scale * field
        product = jnp.dot(
            density.reshape(layer_share * lax.axis_size("lon") * lat_rows, lon_cols),
            forward,
            precision=highest,
            preferred_element_type=jnp.float32,
        )
        spectrum = lax.psum_scatter(
            product.reshape(layer_share * lax.axis_size("lon"), lat_rows, 2 * LMAX),
            "lon",
            scatter_dimension=0,
            tiled=True,
        )
        weighted = spectrum.reshape(layer_share, lat_rows, 2, LMAX) * weights[None, :, None, None]
        coeffs = lax.psum_scatter(
            jnp.einsum("lam,kacm->lkcm", table, weighted, precision=highest),
            "lat",
            scatter_dimension=0,
            tiled=True,
        )
        green_part = lax.dynamic_slice_in_dim(green, layer_first, layer_share, 2)
        partial_pot = jnp.einsum("lkj,ljcm->lkcm", green_part, coeffs, precision=highest)
        pot_coeffs = lax.psum_scatter(partial_pot, "lon", scatter_dimension=1, tiled=True)
        synth = jnp.einsum(
            "lam,lkcm->kacm",
            table,
            lax.all_gather(pot_coeffs, "lat", axis=0, tiled=True),
            precision=highest,
        )
        synth = synth.reshape(layer_share, lat_rows, 2 * LMAX)
        piece = lax.all_gather(synth, "lon", axis=0, tiled=True)
        synth_product = jnp.dot(
            piece.reshape(piece.shape[0] * lat_rows, 2 * LMAX),
            inverse,
            precision=highest,
            preferred_element_type=jnp.float32,
        )
        potential = synth_product.reshape(piece.shape[0], lat_rows, lon_cols)
    return (field, potential)


def call(kernel, outs, scratch=(), smem=(), hbm=()):
    def space(i):
        return pl.BlockSpec(memory_space=pl.ANY if i in hbm else pltpu.VMEM)

    def run(*args):
        return pl.pallas_call(
            kernel,
            out_shape=outs,
            in_specs=[
                pl.BlockSpec(memory_space=pltpu.SMEM if i in smem else pltpu.VMEM)
                for i in range(len(args))
            ],
            out_specs=tuple(space(i) for i in range(len(outs))) if type(outs) is tuple else space(0),
            scratch_shapes=list(scratch),
            compiler_params=pltpu.CompilerParams(vmem_limit_bytes=VMEM_LIMIT),
            cost_estimate=pl.CostEstimate(flops=1, bytes_accessed=1, transcendentals=0),
        )(*args)

    return run


def f32(*shape):
    return jax.ShapeDtypeStruct(shape, jnp.float32)


def halves(x):
    high = x.astype(HALF)
    return high, (x - high.astype(jnp.float32)).astype(HALF)


def dot(a, b, dims):
    return lax.dot_general(a, b, (dims, ((), ())), preferred_element_type=jnp.float32)


def dot3(a, b, dims):
    return dot(a[0], b[0], dims) + (dot(a[0], b[1], dims) + dot(a[1], b[0], dims))


def every(ref, start, stride, count):
    at = pl.ds(start, count, stride=stride)
    return jnp.concatenate([ref[c, at, :] for c in range(ref.shape[0])], axis=1)


def put_every(ref, start, stride, value):
    at = pl.ds(start, value.shape[0], stride=stride)
    for c in range(ref.shape[0]):
        ref[c, at, :] = value[:, c * LANES : (c + 1) * LANES]


NN = ((1,), (0,))
NT = ((1,), (1,))


def iota(shape, dim):
    return lax.broadcasted_iota(jnp.int32, shape, dim)


def fourier_kernel(total, share, high_ref, low_ref):
    shape = (16, 2 * LMAX)
    column = iota(shape, 1)
    order = column // (2 * share) * share + column % share
    shift = (column // share) % 2 * (total - total // 4)
    first = iota(shape, 0) * order + shift
    quarter, half = total // 4, total // 2

    def block(i, carry):
        phase = first + order * (i * shape[0])
        phase = phase & (total - 1) if total & (total - 1) == 0 else lax.rem(phase, total)
        near = jnp.minimum(phase, total - phase)
        beyond = near > quarter
        angle = jnp.where(beyond, half - near, near).astype(jnp.float32) * (2.0 * math.pi / total)
        square = angle * angle
        value = jnp.full(shape, 1.0 / math.factorial(14), jnp.float32)
        for n in range(12, -1, -2):
            value = 1.0 / math.factorial(n) - square * value
        high, low = halves(jnp.where(beyond, -value, value))
        at = pl.ds(pl.multiple_of(i * shape[0], shape[0]), shape[0])
        high_ref[at, :] = high
        low_ref[at, :] = low
        return carry

    lax.fori_loop(0, total // shape[0], block, 0, unroll=2)


def legendre_kernel(total_lat, share, index_ref, high_out, low_out, table, high_ref, low_ref, sem):
    width = table.shape[0] * LANES
    base = index_ref[0] * share
    shape = (share, width)
    order = iota(shape, 0) + base
    order_f = order.astype(jnp.float32)
    row = iota(shape, 1)
    theta = (row.astype(jnp.float32) + 0.5) * (math.pi / total_lat)
    cosine = jnp.cos(theta)
    sine = jnp.where(row < total_lat, jnp.sin(theta), 1.0)
    terms = (share, LMAX)
    term = iota(terms, 1)
    term_f = jnp.maximum(term.astype(jnp.float32), 1.0)
    growth = 0.5 * jnp.log((2.0 * term_f + 1.0) / (2.0 * term_f))
    used = (term >= 2) & (term <= iota(terms, 0) + base)
    total = jnp.sum(jnp.where(used, growth, 0.0), axis=1, keepdims=True)
    log_diag = jnp.where(order >= 1, 0.5 * math.log(3.0) + total, 0.0)
    diagonal = jnp.exp(log_diag + order_f * jnp.log(sine))
    diagonal = jnp.where(row < total_lat, diagonal, 0.0)
    start_next = jnp.sqrt(2.0 * order_f + 3.0) * cosine * diagonal
    narrow = (share, LANES)
    square = ((iota(narrow, 0) + base).astype(jnp.float32)) ** 2

    def wide(x):
        return jnp.concatenate([x] * (width // LANES), axis=1)

    def advance(degree, carry):
        prev_one, prev_two = carry
        deg = jnp.full(narrow, degree, jnp.int32).astype(jnp.float32)
        first = jnp.sqrt((4.0 * deg * deg - 1.0) / jnp.maximum(deg * deg - square, 1.0))
        below = (deg - 1.0) * (deg - 1.0)
        second = jnp.sqrt(jnp.maximum(below - square, 0.0) / jnp.maximum(4.0 * below - 1.0, 1.0))
        general = wide(first) * (cosine * prev_one - wide(second) * prev_two)
        value = jnp.where(
            order == degree,
            diagonal,
            jnp.where(
                order == degree - 1, start_next, jnp.where(order < degree - 1, general, 0.0)
            ),
        )
        for c in range(width // LANES):
            at = pl.ds(pl.multiple_of(degree * share, share), share)
            table[c, at, :] = value[:, c * LANES : (c + 1) * LANES]
        return (value, prev_one)

    table[:, 0:share, :] = jnp.zeros((width // LANES, share, LANES), jnp.float32)
    zeros = jnp.concatenate([table[c, 0:share, :] for c in range(width // LANES)], axis=1)
    lax.fori_loop(0, LMAX, advance, (zeros, zeros), unroll=8)
    for m in range(share):
        high, low = halves(every(table, m, share, LMAX))
        high_ref[m] = high
        low_ref[m] = low
    copies = [
        pltpu.make_async_copy(high_ref, high_out, sem.at[0]),
        pltpu.make_async_copy(low_ref, low_out, sem.at[1]),
    ]
    for copy in copies:
        copy.start()
    for copy in copies:
        copy.wait()


def turn_kernel(size, index_ref, *rest):
    blocks, (o_ref, ordered) = rest[:-2], rest[-2:]
    near = blocks[0].shape[0] // size
    width = blocks[0].shape[1]
    order, step = [0], near
    while step > 0:
        order, step = order + [i ^ step for i in order], step // 2
    for half in range(2):
        for i in range(2 * near):
            at = pl.ds(pl.multiple_of((index_ref[0] ^ order[i]) * size, size), size)
            block = blocks[2 * half + i // near]
            ordered[at, :] = block[(i % near) * size : (i % near + 1) * size, :]
        first = (index_ref[1] ^ half) % 2 * width
        o_ref[pl.ds(pl.multiple_of(first, width), width), :] = ordered[...].T


def slab_kernel(u_ref, mat_ref, mask_ref, height_ref, first_ref, last_ref):
    rows = mask_ref.shape[0]
    layers = u_ref.shape[0] // rows
    for k in range(layers):
        for ref, at in ((first_ref, 0), (last_ref, rows - DEEP)):
            source = slice(k * rows + at, k * rows + at + DEEP)
            ref[k * DEEP : (k + 1) * DEEP, :] = u_ref[source, :]
            to = (layers + k) * DEEP
            ref[to : to + DEEP, :] = mat_ref[source, :].astype(jnp.float32)
    surface = mask_ref[...].astype(jnp.float32) * height_ref[...]
    first_ref[2 * layers * DEEP :, :] = surface[:DEEP]
    last_ref[2 * layers * DEEP :, :] = surface[rows - DEEP :]


SUB = 8


def roll(x, shift, axis):
    shift = shift % x.shape[axis]
    return x if shift == 0 else pltpu.roll(x, shift, axis)


def pick(material, table):
    value = jnp.full(material.shape, table[NMAT - 1], jnp.float32)
    for i in range(NMAT - 1):
        value = jnp.where(material == i, table[i], value)
    return value


def tile(row):
    return pl.ds(pl.multiple_of(row * SUB, SUB), SUB)


def by_layer(ref, rows, first, t, steps, row):
    return ref[pl.ds((first + t) * rows + row, SUB, stride=steps * rows), :].astype(jnp.float32)


def for_rows(rows, own, above, below, body):
    u_ref, mat_ref, mask_ref, height_ref = own
    steps = u_ref.shape[0] // rows // SUB
    layers = SUB * steps

    def margin(ref, offset):
        def one(i, carry):
            body(
                i + offset,
                lambda t: by_layer(ref, DEEP, 0, t, steps, i),
                lambda t: by_layer(ref, DEEP, layers, t, steps, i),
                ref[pl.ds(2 * layers * DEEP + i, 1), :],
            )
            return carry

        lax.fori_loop(0, DEEP, one, 0, unroll=8)

    def inner(i, carry):
        at = pl.ds(i, 1)
        body(
            i + DEEP,
            lambda t: by_layer(u_ref, rows, 0, t, steps, i),
            lambda t: by_layer(mat_ref, rows, 0, t, steps, i),
            mask_ref[at, :].astype(jnp.float32) * height_ref[at, :],
        )
        return carry

    margin(above, 0)
    lax.fori_loop(0, rows, inner, 0, unroll=8)
    margin(below, rows + DEEP)


def pack_kernel(
    u_ref, mat_ref, mask_ref, height_ref, above_ref, below_ref, first_ref, last_ref
):
    rows = mask_ref.shape[0]
    steps = u_ref.shape[0] // rows // SUB
    slot = iota((SUB, LANES), 1) // DEEP

    def body(row, u, mat, load):
        first = jnp.zeros((SUB, LANES), jnp.float32)
        last = first
        fields = [u(t) for t in range(steps)] + [mat(t) for t in range(steps)]
        fields.append(jnp.broadcast_to(load, (SUB, LANES)))
        for i, x in enumerate(fields):
            first = jnp.where(slot == i, roll(x, i * DEEP, 1), first)
            last = jnp.where(slot == i, roll(x, (i + 1) * DEEP, 1), last)
        first_ref[tile(row), :] = first
        last_ref[tile(row), :] = last

    for_rows(rows, (u_ref, mat_ref, mask_ref, height_ref), above_ref, below_ref, body)


def run_sweeps(src, offset, a_ref, f_ref, two):
    steps = a_ref.shape[0]
    rows = a_ref.shape[2] // SUB - 2 * offset
    lane = iota((SUB, LANES), 1)
    sub = iota((SUB, LANES), 0)
    cells = [(t, c) for t in range(steps) for c in range(2)]
    for sweep in range(SWEEPS):
        dst = two[sweep % 2]
        shift = offset if sweep == 0 else 0

        def load(row, src=src, shift=shift):
            return {cell: src[cell[0], cell[1], tile(row + shift), :] for cell in cells}

        def one(row, carry, load=load, dst=dst):
            before, x = ({cell: carry[j][i] for i, cell in enumerate(cells)} for j in range(2))
            after = load(row + 1)
            for t in range(steps):
                to_right = [roll(x[t, c], 1, 1) for c in range(2)]
                to_left = [roll(x[t, c], LANES - 1, 1) for c in range(2)]
                for c in range(2):
                    total = jnp.where(lane == 0, to_right[1 - c], to_right[c])
                    total = total + jnp.where(lane == LANES - 1, to_left[1 - c], to_left[c])
                    total = total + (before[t, c] + after[t, c])
                    if t > 0:
                        under = x[t - 1, c]
                    else:
                        under = jnp.where(sub == 0, 0.0, roll(x[steps - 1, c], 1, 0))
                    if t < steps - 1:
                        over = x[t + 1, c]
                    else:
                        over = jnp.where(sub == SUB - 1, 0.0, roll(x[0, c], SUB - 1, 0))
                    total = total + (under + over)
                    value = a_ref[t, c, tile(row + offset), :] * total
                    if t < f_ref.shape[0]:
                        value = value + f_ref[t, c, tile(row), :]
                    dst[t, c, tile(row), :] = value
            return (
                tuple(x[cell] for cell in cells),
                tuple(after[cell] for cell in cells),
            )

        start = (tuple(load(sweep).values()), tuple(load(sweep + 1).values()))
        lax.fori_loop(sweep + 1, rows - 1 - sweep, one, start, unroll=8)
        src = dst


def put_density(mat_ref, contrast, field, index_ref, scratch, pieces):
    lon_count = len(pieces)
    share, rows, _ = pieces[0].shape
    for k in range(lon_count * share):
        material = mat_ref[k * rows : (k + 1) * rows, :]
        scratch[k // share, k % share] = pick(material, contrast) * field(k)
    for s in range(lon_count):
        pieces[s][...] = scratch[lax.rem(index_ref[1] + s, lon_count)]


def layer_of(ref, k, margin, rows):
    steps = ref.shape[0]
    return ref[k % steps, 0, pl.ds(margin * SUB + k // steps, rows, stride=SUB), :]


def first_sweeps_kernel(
    lon_count, total_lat, index_ref, shear_ref, restoring_ref, contrast_ref, u_ref, mat_ref, mask_ref,
    height_ref, above_ref, below_ref, left_ref, right_ref, *rest,
):
    pieces, rest = rest[:lon_count], rest[lon_count:]
    u_hbm, a_hbm, b_hbm, load_hbm, first, middle, u_out, a_out, b_out, load_out, f_scr, d_scr, sem = rest
    rows = mask_ref.shape[0]
    steps = u_out.shape[0]
    a_of, b_of = [], []
    for i in range(NMAT):
        stiff = jnp.full((SUB, LANES), shear_ref[i], jnp.float32)
        restore = jnp.full((SUB, LANES), restoring_ref[i], jnp.float32)
        b_of.append(1.0 / (6.0 * stiff + restore))
        a_of.append(stiff * b_of[i])
    lane = iota((SUB, LANES), 1)
    sub = iota((SUB, LANES), 0)

    def body(row, u, mat, load):
        at = tile(row)
        left, right = left_ref[at, :], right_ref[at, :]
        global_row = index_ref[0] * rows - DEEP + row
        inside = ((global_row >= 0) & (global_row < total_lat)).astype(jnp.float32)

        def side(i):
            after = roll(right, LANES - i * DEEP, 1)
            before = roll(left, LANES - (i + 1) * DEEP, 1)
            return jnp.where(lane < DEEP, after, jnp.where(lane >= LANES - DEEP, before, 0.0))

        loads = (jnp.broadcast_to(load, (SUB, LANES)), side(2 * steps))
        for t in range(steps):
            fields = ((u(t), mat(t)), (side(t), side(steps + t)))
            for c in range(2):
                value, material = fields[c]
                first[t, c, at, :] = value
                a_out[t, c, at, :] = pick(material, a_of) * inside
                b = pick(material, b_of) * inside
                b_out[t, c, at, :] = b
                if t == 0:
                    surface = jnp.where(sub == 0, loads[c], 0.0)
                    load_out[0, c, at, :] = surface
                    f_scr[0, c, at, :] = b * surface

    for_rows(rows, (u_ref, mat_ref, mask_ref, height_ref), above_ref, below_ref, body)
    kept = ((a_out, a_hbm), (b_out, b_hbm), (load_out, load_hbm), (u_out, u_hbm))
    copies = [pltpu.make_async_copy(*pair, sem.at[i]) for i, pair in enumerate(kept)]
    for copy in copies[:-1]:
        copy.start()
    run_sweeps(first, 0, a_out, f_scr, (middle, u_out))
    copies[-1].start()
    put_density(
        mat_ref, contrast_ref, lambda k: layer_of(u_out, k, DEEP, rows), index_ref, d_scr, pieces
    )
    for copy in copies:
        copy.wait()


def second_sweeps_kernel(
    lon_count, index_ref, contrast_ref, mat_ref, u_ref, a_ref, b_ref, load_ref, *rest
):
    parts, rest = rest[:lon_count], rest[lon_count:]
    pieces, rest = rest[:lon_count], rest[lon_count:]
    field_out, middle, last, f_scr, pot, edge, d_scr = rest
    layers, rows, _ = field_out.shape
    steps = u_ref.shape[0]
    tall = rows + 2 * SHALLOW
    share = layers // lon_count
    spread = share // steps
    chunk = LANES // share
    lane = iota((SUB, LANES), 1)
    for s in range(lon_count):
        source = lax.rem(index_ref[1] + (lon_count - s), lon_count)
        for k in range(share):
            at = pl.ds(source * spread + k // steps, tall, stride=SUB)
            pot[k % steps, at, :] = parts[s][k * tall : (k + 1) * tall, :]
        packed = parts[s][share * tall :, :]
        for e in range(spread):
            at = pl.ds(source * spread + e, tall, stride=SUB)
            edge[at, :] = roll(packed, LANES - e * steps * chunk, 1)

    def force(row, carry):
        at, deep = tile(row), tile(row + DEEP - SHALLOW)
        ends = edge[at, :]
        for t in range(steps):
            after = roll(ends, LANES - t * chunk, 1)
            before = roll(ends, LANES - (t + 1) * chunk, 1)
            potential = (pot[t, at, :], jnp.where(lane < DEEP, after, before))
            for c in range(2):
                value = potential[c]
                if t == 0:
                    value = value + load_ref[0, c, deep, :]
                f_scr[t, c, at, :] = b_ref[t, c, deep, :] * value
        return carry

    lax.fori_loop(0, tall, force, 0, unroll=8)
    run_sweeps(u_ref, DEEP - SHALLOW, a_ref, f_scr, (middle, last))
    for k in range(layers):
        field_out[k] = layer_of(last, k, SHALLOW, rows)
    put_density(mat_ref, contrast_ref, lambda k: field_out[k], index_ref, d_scr, pieces)


def swap_chunks(blocks, chunk):
    blocks = list(blocks)
    lane = iota(blocks[0].shape, 1)
    step = 1
    while step < len(blocks):
        upper = (lane // (chunk * step)) % 2 == 1
        for i in range(len(blocks)):
            if i & step:
                continue
            a, b = blocks[i], blocks[i + step]
            blocks[i] = jnp.where(upper, roll(b, chunk * step, 1), a)
            blocks[i + step] = jnp.where(upper, b, roll(a, LANES - chunk * step, 1))
        step *= 2
    return blocks


def forward_kernel(lon_count, scale, index_ref, weight_ref, high_ref, low_ref, *rest):
    parts, (o_ref,) = rest[:lon_count], rest[lon_count:]
    share, rows, cols = parts[0].shape
    chunk = LANES // share
    product = None
    for s in range(lon_count):
        source = lax.rem(index_ref[1] + (lon_count - s), lon_count)
        at = pl.ds(pl.multiple_of(source * cols, cols), cols)
        term = dot3(
            halves(parts[s][...].reshape(share * rows, cols)), (high_ref[at, :], low_ref[at, :]), NN
        )
        product = term if product is None else product + term
    weight = weight_ref[...] * scale
    for g in range(product.shape[1] // LANES):
        blocks = swap_chunks(
            [
                product[k * rows : (k + 1) * rows, g * LANES : (g + 1) * LANES] * weight
                for k in range(share)
            ],
            chunk,
        )
        for i in range(share):
            o_ref[g * share + i] = blocks[i]


def spectral_kernel(margin, high_ref, low_ref, green_ref, x_ref, o_ref, turned, coeffs, pots):
    share, degrees, width = high_ref.shape
    lat_count, lon_count, rows, _ = x_ref.shape
    total_lat = lat_count * rows
    size = 2 * share
    layers = turned.shape[1] // size
    pad = jnp.zeros((width - total_lat, LANES), jnp.float32)
    for q in range(lon_count):
        x = x_ref[:, q].reshape(total_lat, LANES)
        x = jnp.concatenate([x, pad], axis=0)
        for c in range(width // LANES):
            turned[c, q * LANES : (q + 1) * LANES, :] = x[c * LANES : (c + 1) * LANES].T
    for m in range(share):
        x = halves(every(turned, m, share, 2 * layers))
        put_every(coeffs, m, share, dot3(x, (high_ref[m], low_ref[m]), NT))
    block = 4

    def targets(i, carry):
        for c in range(degrees // LANES):
            sums = [jnp.zeros((size, LANES), jnp.float32) for _ in range(block)]
            for k in range(0, layers, 8):
                part = [
                    green_ref[
                        pl.ds(pl.multiple_of((i * block + t) * layers + k, 8), 8),
                        c * LANES : (c + 1) * LANES,
                    ]
                    for t in range(block)
                ]
                for e in range(8):
                    x = coeffs[c, (k + e) * size : (k + e + 1) * size, :]
                    for t in range(block):
                        sums[t] = sums[t] + part[t][e : e + 1] * x
            for t in range(block):
                pots[c, pl.ds(pl.multiple_of((i * block + t) * size, size), size), :] = sums[t]
        return carry

    lax.fori_loop(0, layers // block, targets, 0)
    for m in range(share):
        x = halves(every(pots, m, share, 2 * layers))
        put_every(turned, m, share, dot3(x, (high_ref[m], low_ref[m]), NN))
    for q in range(lon_count):
        x = [turned[c, q * LANES : (q + 1) * LANES, :].T for c in range(width // LANES)]
        x = jnp.concatenate(x, axis=0)[:total_lat]
        if margin > 0:
            edge = jnp.zeros((margin, LANES), jnp.float32)
            x = jnp.concatenate([edge, x, edge], axis=0)
        for i in range(lat_count):
            o_ref[i, q] = x[i * rows : (i + 1) * rows + 2 * margin]


def inverse_kernel(lon_count, margin, index_ref, high_ref, low_ref, x_ref, *rest):
    pieces, (columns,) = rest[:lon_count], rest[lon_count:]
    owners, rows, _ = x_ref.shape
    cols = high_ref.shape[0] // lon_count
    share = columns.shape[1] // rows
    chunk = LANES // share
    groups = [
        swap_chunks([x_ref[g * share + i] for i in range(share)], chunk)
        for g in range(owners // share)
    ]
    terms = jnp.concatenate(
        [jnp.concatenate([group[k] for group in groups], axis=1) for k in range(share)], axis=0
    )
    terms = halves(terms)
    for q in range(lon_count):
        at = slice(q * cols, (q + 1) * cols)
        columns[q] = dot3(terms, (high_ref[at, :], low_ref[at, :]), NT)
    lane = iota((rows, LANES), 1)
    for s in range(lon_count):
        dest = lax.rem(index_ref[1] + s, lon_count)
        pieces[s][0 : share * rows] = columns[dest]
        if margin == 0:
            continue
        after = lax.rem(dest + 1, lon_count)
        before = lax.rem(dest + lon_count - 1, lon_count)
        packed = jnp.zeros((rows, LANES), jnp.float32)
        for k in range(share):
            right = roll(columns[after, k * rows : (k + 1) * rows, :], k * chunk, 1)
            left = roll(columns[before, k * rows : (k + 1) * rows, :], (k + 1) * chunk, 1)
            packed = jnp.where(
                lane // DEEP == 2 * k, right, jnp.where(lane // DEEP == 2 * k + 1, left, packed)
            )
        pieces[s][share * rows :] = packed


def assemble_kernel(lon_count, index_ref, *rest):
    parts, (o_ref,) = rest[:lon_count], rest[lon_count:]
    share = o_ref.shape[1]
    for s in range(lon_count):
        source = lax.rem(index_ref[1] + (lon_count - s), lon_count)
        o_ref[source] = parts[s][...].reshape(o_ref.shape[1:])


def exchange(pieces):
    count = len(pieces)
    return [pieces[0]] + [
        lax.ppermute(pieces[s], "lon", [(i, (i + s) % count) for i in range(count)])
        for s in range(1, count)
    ]


def on_device(displacement, materials, ice_mask, ice_height, shear, restoring, contrast, green):
    layers, rows, cols = displacement.shape
    lat_count, lon_count = lax.axis_size("lat"), lax.axis_size("lon")
    total_lat, total_lon = rows * lat_count, cols * lon_count
    owners = lat_count * lon_count
    share, orders = layers // lon_count, LMAX // owners
    width = -(-total_lat // LANES) * LANES
    tall = rows + 2 * SHALLOW
    lat_index = lax.axis_index("lat")
    index = jnp.stack([lat_index, lax.axis_index("lon")]).astype(jnp.int32)
    owner = (index[0] * lon_count + index[1])[None]

    own = (
        displacement.reshape(layers * rows, cols),
        materials.reshape(layers * rows, cols),
        ice_mask,
        ice_height,
    )
    first, last = call(slab_kernel, (f32((2 * layers + 1) * DEEP, cols),) * 2)(*own)
    above = lax.ppermute(last, "lat", [(i, i + 1) for i in range(lat_count - 1)])
    below = lax.ppermute(first, "lat", [(i + 1, i) for i in range(lat_count - 1)])
    table = call(
        functools.partial(fourier_kernel, total_lon, orders),
        (jax.ShapeDtypeStruct((total_lon, 2 * LMAX), HALF),) * 2,
    )()
    def partner(x, axis, step):
        return lax.ppermute(x, axis, [(i, i ^ step) for i in range(lax.axis_size(axis))])

    half = layers * layers // 2
    near = lax.dynamic_slice_in_dim(
        green.reshape(green.shape[0], layers * layers), index[1] % 2 * half, half, 1
    )
    step = lat_count // 2
    far = partner(near, "lat", step)
    above, below, far, table = lax.optimization_barrier((above, below, far, table))
    first, last = call(pack_kernel, (f32((rows + 2 * DEEP) * SUB, cols),) * 2)(
        *own, above, below
    )
    left = lax.ppermute(last, "lon", [(i, (i + 1) % lon_count) for i in range(lon_count)])
    right = lax.ppermute(first, "lon", [((i + 1) % lon_count, i) for i in range(lon_count)])
    stage = 0
    while step > 1:
        step //= 2
        near = jnp.concatenate([near, far], axis=0)
        far = partner(near, "lat", step)
        if stage == 0:
            left, right, far = lax.optimization_barrier((left, right, far))
        stage += 1
    theta = ((lat_index * rows + jnp.arange(rows)).astype(jnp.float32) + 0.5) * (
        jnp.pi / total_lat
    )
    weight = jnp.broadcast_to((jnp.sin(theta) / (4.0 * total_lat))[:, None], (rows, LANES))

    steps = layers // SUB

    def worked(t, height):
        return (t, 2, height * SUB, LANES)

    deep = rows + 2 * DEEP
    flat = pltpu.VMEM((lon_count, share, rows, cols), jnp.float32)
    out = call(
        functools.partial(first_sweeps_kernel, lon_count, total_lat),
        (f32(share, rows, cols),) * lon_count
        + (f32(*worked(steps, deep)),) * 3
        + (f32(*worked(1, deep)),),
        scratch=[pltpu.VMEM(worked(steps, deep), jnp.float32)] * 5
        + [pltpu.VMEM(worked(1, deep), jnp.float32)] * 2
        + [flat, pltpu.SemaphoreType.DMA((4,))],
        smem=(0, 1, 2, 3),
        hbm=range(lon_count, lon_count + 4),
    )(index, shear, restoring, contrast, *own, above, below, left, right)
    pieces, state = out[:lon_count], out[lon_count:]
    for iteration in range(ITERS):
        margin = SHALLOW if iteration < ITERS - 1 else 0
        parts = exchange(pieces)
        if iteration == 0:
            parts, near, far = lax.optimization_barrier((parts, near, far))
        spectrum = call(
            functools.partial(forward_kernel, lon_count, 2.0 * math.pi / total_lon),
            f32(owners, rows, LANES),
            smem=(0,),
        )(index, weight, *table, *parts)
        if iteration == 0:
            owner, spectrum = lax.optimization_barrier((owner, spectrum))
            half_table = (orders, LMAX, width)
            legendre_table = call(
                functools.partial(legendre_kernel, total_lat, orders),
                (jax.ShapeDtypeStruct(half_table, HALF),) * 2,
                scratch=[
                    pltpu.VMEM((width // LANES, LMAX * orders, LANES), jnp.float32),
                    pltpu.VMEM(half_table, HALF),
                    pltpu.VMEM(half_table, HALF),
                    pltpu.SemaphoreType.DMA((2,)),
                ],
                smem=(0,),
                hbm=(0, 1),
            )(owner)
            blocks = (near, far, partner(near, "lon", 1), partner(far, "lon", 1))
            turned_green = call(
                functools.partial(turn_kernel, green.shape[0]),
                f32(layers * layers, LMAX),
                scratch=[pltpu.VMEM((LMAX, half), jnp.float32)],
                smem=(0,),
            )(index, *blocks)
        spectrum = lax.all_to_all(spectrum, BOTH, 0, 0, tiled=True)
        square = pltpu.VMEM((width // LANES, lon_count * LANES, LANES), jnp.float32)
        coeff_shape = pltpu.VMEM((LMAX // LANES, lon_count * LANES, LANES), jnp.float32)
        synth = call(
            functools.partial(spectral_kernel, margin),
            f32(lat_count, lon_count, rows + 2 * margin, LANES),
            scratch=[square, coeff_shape, coeff_shape],
        )(
            *legendre_table,
            turned_green,
            spectrum.reshape(lat_count, lon_count, rows, LANES),
        )
        synth = lax.all_to_all(
            synth.reshape(owners, rows + 2 * margin, LANES), BOTH, 0, 0, tiled=True
        )
        high = rows + 2 * margin
        sent = share * high + (high if margin > 0 else 0)
        parts = call(
            functools.partial(inverse_kernel, lon_count, margin),
            (f32(sent, cols),) * lon_count,
            scratch=[pltpu.VMEM((lon_count, share * high, cols), jnp.float32)],
            smem=(0,),
        )(index, *table, synth)
        parts = exchange(parts)
        if iteration < ITERS - 1:
            out = call(
                functools.partial(second_sweeps_kernel, lon_count),
                (f32(share, rows, cols),) * lon_count + (f32(layers, rows, cols),),
                scratch=[pltpu.VMEM(worked(steps, tall), jnp.float32)] * 3
                + [
                    pltpu.VMEM((steps, tall * SUB, LANES), jnp.float32),
                    pltpu.VMEM((tall * SUB, LANES), jnp.float32),
                    flat,
                ],
                smem=(0, 1),
            )(index, contrast, own[1], *state, *parts)
            pieces, field = out[:lon_count], out[lon_count]
    potential = call(
        functools.partial(assemble_kernel, lon_count),
        f32(lon_count, share, rows, cols),
        smem=(0,),
    )(index, *parts)
    return (field, potential.reshape(layers, rows, cols))


def aligned(mesh, displacement):
    lat_count, lon_count = mesh.shape["lat"], mesh.shape["lon"]
    layers, total_lat, total_lon = displacement.shape
    rows, cols = total_lat // lat_count, total_lon // lon_count
    owners = lat_count * lon_count
    return (
        ITERS == 2
        and cols == LANES
        and rows % 8 == 0
        and layers % SUB == 0
        and (2 * (layers // SUB) + 1) * DEEP <= LANES
        and (layers // lon_count) % (layers // SUB) == 0
        and lat_count > 2
        and lon_count % 2 == 0
        and lat_count & (lat_count - 1) == 0
        and layers % lon_count == 0
        and LMAX % owners == 0
        and 2 * (LMAX // owners) * (layers // lon_count) == LANES
        and 2 * (LMAX // owners) == 2 * DEEP
        and LMAX % LANES == 0
    )


def solution(mesh):
    in_specs = (
        P(None, "lat", "lon"),
        P(None, "lat", "lon"),
        P("lat", "lon"),
        P("lat", "lon"),
        P(),
        P(),
        P(),
        P("lat", None, None),
    )
    out_specs = (P(None, "lat", "lon"), P(None, "lat", "lon"))

    def step(displacement, *others):
        device = on_device if aligned(mesh, displacement) else general_device
        return jax.shard_map(
            device, mesh=mesh, in_specs=in_specs, out_specs=out_specs, check_vma=False
        )(displacement, *others)

    return step
```

```python
import functools
import math

import jax
import jax.numpy as jnp
from jax import lax
from jax.experimental import pallas as pl
from jax.experimental.pallas import tpu as pltpu
from jax.sharding import PartitionSpec as P

LMAX = 256
NMAT = 4
ITERS = 2
SWEEPS = 4
LANES = 128
DEEP = 8
SHALLOW = 4
HALF = jnp.bfloat16
VMEM_LIMIT = 16 * 1024 * 1024
BOTH = ("lat", "lon")


def extended(cells, sides, width, closed):
    for axis, dim in sides:
        count = lax.axis_size(axis)
        ends = count if closed else count - 1
        head = lax.slice_in_dim(cells, 0, width, axis=dim)
        tail = lax.slice_in_dim(cells, cells.shape[dim] - width, cells.shape[dim], axis=dim)
        cells = jnp.concatenate(
            [
                lax.ppermute(tail, axis, [(i, (i + 1) % count) for i in range(ends)]),
                cells,
                lax.ppermute(head, axis, [((i + 1) % count, i) for i in range(ends)]),
            ],
            axis=dim,
        )
    return cells


def legendre(theta):
    orders = jnp.arange(LMAX)
    order_f = orders.astype(jnp.float32)
    cosine = jnp.cos(theta)[:, None]
    sine = jnp.sin(theta)[:, None]
    safe = jnp.maximum(order_f, 1.0)
    growth = jnp.where(orders >= 2, 0.5 * jnp.log((2.0 * safe + 1.0) / (2.0 * safe)), 0.0)
    log_diag = jnp.where(orders >= 1, 0.5 * jnp.log(3.0) + jnp.cumsum(growth), 0.0)
    diagonal = jnp.exp(log_diag[None, :] + order_f[None, :] * jnp.log(sine))

    def advance(carry, degree):
        prev_one, prev_two = carry
        deg_f = degree.astype(jnp.float32)
        first = jnp.sqrt(
            (4.0 * deg_f * deg_f - 1.0) / jnp.maximum(deg_f * deg_f - order_f * order_f, 1.0)
        )
        second = jnp.sqrt(
            jnp.maximum((deg_f - 1.0) ** 2 - order_f * order_f, 0.0)
            / jnp.maximum(4.0 * (deg_f - 1.0) ** 2 - 1.0, 1.0)
        )
        general = first * (cosine * prev_one - second * prev_two)
        start_next = jnp.sqrt(2.0 * order_f + 3.0) * cosine * diagonal
        value = jnp.where(
            orders == degree,
            diagonal,
            jnp.where(
                orders == degree - 1, start_next, jnp.where(orders < degree - 1, general, 0.0)
            ),
        )
        return ((value, prev_one), value)

    zeros = jnp.zeros((theta.shape[0], LMAX), jnp.float32)
    _, table = lax.scan(advance, (zeros, zeros), jnp.arange(LMAX), unroll=8)
    return table


def fourier_tables(columns, total):
    orders = jnp.arange(LMAX)
    phase = columns[:, None] * orders[None, :] % total
    angle = 2.0 * jnp.pi / total * phase.astype(jnp.float32)
    forward = jnp.concatenate([jnp.cos(angle), jnp.sin(angle)], axis=1) * (2.0 * jnp.pi / total)
    inverse = jnp.concatenate([jnp.cos(angle), jnp.sin(angle)], axis=1).T
    return (forward, inverse)


def lookup(materials, table):
    result = jnp.zeros(materials.shape, jnp.float32)
    for material in range(NMAT):
        result = result + jnp.where(materials == material, table[material], 0.0)
    return result


def crop_block(block, margin):
    return block[:, margin : block.shape[1] - margin, margin : block.shape[2] - margin]


def margin_sweeps(field, force, stiff, restore, depth, lat_first, total_lat):
    stacked = jnp.stack([field, force, stiff, restore], axis=0)
    lat_wide = extended(stacked, (("lat", 2),), depth, False)
    wide = extended(lat_wide, (("lon", 3),), depth, True)
    current = wide[0]
    rows_wide = wide.shape[2]
    global_rows = lat_first - depth + jnp.arange(rows_wide)
    inside = ((global_rows >= 0) & (global_rows < total_lat))[None, :, None]
    for step in range(depth):
        margin = step + 1
        inner = current[:, 1:-1, 1:-1]
        beside_all = (
            current[:, 2:, 1:-1]
            + current[:, :-2, 1:-1]
            + current[:, 1:-1, 2:]
            + current[:, 1:-1, :-2]
        )
        layer_pad = jnp.pad(inner, ((1, 1), (0, 0), (0, 0)))
        beside_all = beside_all + layer_pad[2:] + layer_pad[:-2]
        force_part = crop_block(wide[1], margin)
        stiff_part = crop_block(wide[2], margin)
        restore_part = crop_block(wide[3], margin)
        valid = inside[:, margin : rows_wide - margin, :]
        denominator = jnp.where(valid, 6.0 * stiff_part + restore_part, 1.0)
        current = jnp.where(valid, (force_part + stiff_part * beside_all) / denominator, 0.0)
    return current


def general_device(displacement, materials, ice_mask, ice_height, shear, restoring, contrast, green):
    highest = lax.Precision.HIGHEST
    layers, lat_rows, lon_cols = displacement.shape
    lon_count = lax.axis_size("lon")
    lat_count = lax.axis_size("lat")
    total_lat = lat_rows * lat_count
    total_lon = lon_cols * lon_count
    layer_share = layers // lon_count
    stiff = lookup(materials, shear)
    restore = lookup(materials, restoring)
    rho_scale = lookup(materials, contrast)
    surface = (ice_mask.astype(jnp.float32) * ice_height)[None]
    load = jnp.concatenate(
        [surface, jnp.zeros((layers - 1, lat_rows, lon_cols), jnp.float32)], axis=0
    )
    lat_first = lax.axis_index("lat") * lat_rows
    theta = ((lat_first + jnp.arange(lat_rows)).astype(jnp.float32) + 0.5) * (jnp.pi / total_lat)
    table = legendre(theta)
    weights = jnp.sin(theta) / (4.0 * total_lat)
    own_columns = lax.axis_index("lon") * lon_cols + jnp.arange(lon_cols)
    layer_first = lax.axis_index("lon") * layer_share
    depth = 1
    for candidate in range(1, SWEEPS + 1):
        if SWEEPS % candidate == 0 and candidate <= min(lat_rows, lon_cols):
            depth = candidate
    forward, inverse = fourier_tables(own_columns, total_lon)
    field = displacement
    potential = jnp.zeros((layers, lat_rows, lon_cols), jnp.float32)
    for iteration in range(ITERS):
        force = load + potential
        field = margin_sweeps(field, force, stiff, restore, depth, lat_first, total_lat)
        density = rho_scale * field
        product = jnp.dot(
            density.reshape(layer_share * lax.axis_size("lon") * lat_rows, lon_cols),
            forward,
            precision=highest,
            preferred_element_type=jnp.float32,
        )
        spectrum = lax.psum_scatter(
            product.reshape(layer_share * lax.axis_size("lon"), lat_rows, 2 * LMAX),
            "lon",
            scatter_dimension=0,
            tiled=True,
        )
        weighted = spectrum.reshape(layer_share, lat_rows, 2, LMAX) * weights[None, :, None, None]
        coeffs = lax.psum_scatter(
            jnp.einsum("lam,kacm->lkcm", table, weighted, precision=highest),
            "lat",
            scatter_dimension=0,
            tiled=True,
        )
        green_part = lax.dynamic_slice_in_dim(green, layer_first, layer_share, 2)
        partial_pot = jnp.einsum("lkj,ljcm->lkcm", green_part, coeffs, precision=highest)
        pot_coeffs = lax.psum_scatter(partial_pot, "lon", scatter_dimension=1, tiled=True)
        synth = jnp.einsum(
            "lam,lkcm->kacm",
            table,
            lax.all_gather(pot_coeffs, "lat", axis=0, tiled=True),
            precision=highest,
        )
        synth = synth.reshape(layer_share, lat_rows, 2 * LMAX)
        piece = lax.all_gather(synth, "lon", axis=0, tiled=True)
        synth_product = jnp.dot(
            piece.reshape(piece.shape[0] * lat_rows, 2 * LMAX),
            inverse,
            precision=highest,
            preferred_element_type=jnp.float32,
        )
        potential = synth_product.reshape(piece.shape[0], lat_rows, lon_cols)
    return (field, potential)


def call(kernel, outs, micros, scratch=(), smem=(), far=(), hbm=()):
    def place(i, scalars, away):
        space = pltpu.SMEM if i in scalars else pltpu.HBM if i in away else pltpu.VMEM
        return pl.BlockSpec(memory_space=space)

    def run(*args):
        return pl.pallas_call(
            kernel,
            out_shape=outs,
            in_specs=[place(i, smem, far) for i in range(len(args))],
            out_specs=tuple(place(i, (), hbm) for i in range(len(outs)))
            if type(outs) is tuple
            else place(0, (), hbm),
            scratch_shapes=list(scratch),
            compiler_params=pltpu.CompilerParams(vmem_limit_bytes=VMEM_LIMIT),
            cost_estimate=pl.CostEstimate(
                flops=int(micros * 1e9), bytes_accessed=1, transcendentals=0
            ),
        )(*args)

    return run


def copy_all(sem, *pairs):
    copies = [pltpu.make_async_copy(*pair, sem.at[i]) for i, pair in enumerate(pairs)]
    for copy in copies:
        copy.start()
    for copy in copies:
        copy.wait()


def f32(*shape):
    return jax.ShapeDtypeStruct(shape, jnp.float32)


def halves(x):
    high = x.astype(HALF)
    return high, (x - high.astype(jnp.float32)).astype(HALF)


def dot(a, b, dims):
    return lax.dot_general(a, b, (dims, ((), ())), preferred_element_type=jnp.float32)


def dot3(a, b, dims):
    return dot(a[0], b[0], dims) + (dot(a[0], b[1], dims) + dot(a[1], b[0], dims))


def every(ref, start, stride, count):
    at = pl.ds(start, count, stride=stride)
    return jnp.concatenate([ref[c, at, :] for c in range(ref.shape[0])], axis=1)


def put_every(ref, start, stride, value):
    at = pl.ds(start, value.shape[0], stride=stride)
    for c in range(ref.shape[0]):
        ref[c, at, :] = value[:, c * LANES : (c + 1) * LANES]


NN = ((1,), (0,))
NT = ((1,), (1,))


def iota(shape, dim):
    return lax.broadcasted_iota(jnp.int32, shape, dim)


def fourier_kernel(total, share, high_ref, low_ref):
    shape = (16, 2 * LMAX)
    column = iota(shape, 1)
    order = column // (2 * share) * share + column % share
    shift = (column // share) % 2 * (total - total // 4)
    first = iota(shape, 0) * order + shift
    quarter, half = total // 4, total // 2

    def block(i, carry):
        phase = first + order * (i * shape[0])
        phase = phase & (total - 1) if total & (total - 1) == 0 else lax.rem(phase, total)
        near = jnp.minimum(phase, total - phase)
        beyond = near > quarter
        angle = jnp.where(beyond, half - near, near).astype(jnp.float32) * (2.0 * math.pi / total)
        square = angle * angle
        value = jnp.full(shape, 1.0 / math.factorial(14), jnp.float32)
        for n in range(12, -1, -2):
            value = 1.0 / math.factorial(n) - square * value
        high, low = halves(jnp.where(beyond, -value, value))
        at = pl.ds(pl.multiple_of(i * shape[0], shape[0]), shape[0])
        high_ref[at, :] = high
        low_ref[at, :] = low
        return carry

    lax.fori_loop(0, total // shape[0], block, 0, unroll=2)


def legendre_kernel(total_lat, share, index_ref, high_out, low_out, table, high_ref, low_ref, sem):
    width = table.shape[0] * LANES
    base = index_ref[0] * share
    shape = (share, width)
    order = iota(shape, 0) + base
    order_f = order.astype(jnp.float32)
    row = iota(shape, 1)
    theta = (row.astype(jnp.float32) + 0.5) * (math.pi / total_lat)
    cosine = jnp.cos(theta)
    sine = jnp.where(row < total_lat, jnp.sin(theta), 1.0)
    terms = (share, LMAX)
    term = iota(terms, 1)
    term_f = jnp.maximum(term.astype(jnp.float32), 1.0)
    growth = 0.5 * jnp.log((2.0 * term_f + 1.0) / (2.0 * term_f))
    used = (term >= 2) & (term <= iota(terms, 0) + base)
    total = jnp.sum(jnp.where(used, growth, 0.0), axis=1, keepdims=True)
    log_diag = jnp.where(order >= 1, 0.5 * math.log(3.0) + total, 0.0)
    diagonal = jnp.exp(log_diag + order_f * jnp.log(sine))
    diagonal = jnp.where(row < total_lat, diagonal, 0.0)
    start_next = jnp.sqrt(2.0 * order_f + 3.0) * cosine * diagonal
    narrow = (share, LANES)
    square = ((iota(narrow, 0) + base).astype(jnp.float32)) ** 2

    def wide(x):
        return jnp.concatenate([x] * (width // LANES), axis=1)

    def advance(degree, carry):
        prev_one, prev_two = carry
        deg = jnp.full(narrow, degree, jnp.int32).astype(jnp.float32)
        first = jnp.sqrt((4.0 * deg * deg - 1.0) / jnp.maximum(deg * deg - square, 1.0))
        below = (deg - 1.0) * (deg - 1.0)
        second = jnp.sqrt(jnp.maximum(below - square, 0.0) / jnp.maximum(4.0 * below - 1.0, 1.0))
        general = wide(first) * (cosine * prev_one - wide(second) * prev_two)
        value = jnp.where(
            order == degree,
            diagonal,
            jnp.where(
                order == degree - 1, start_next, jnp.where(order < degree - 1, general, 0.0)
            ),
        )
        for c in range(width // LANES):
            at = pl.ds(pl.multiple_of(degree * share, share), share)
            table[c, at, :] = value[:, c * LANES : (c + 1) * LANES]
        return (value, prev_one)

    table[:, 0:share, :] = jnp.zeros((width // LANES, share, LANES), jnp.float32)
    zeros = jnp.concatenate([table[c, 0:share, :] for c in range(width // LANES)], axis=1)
    lax.fori_loop(0, LMAX, advance, (zeros, zeros), unroll=8)
    for m in range(share):
        high, low = halves(every(table, m, share, LMAX))
        high_ref[m] = high
        low_ref[m] = low
    copy_all(sem, (high_ref, high_out), (low_ref, low_out))


def turn_kernel(size, index_ref, near_ref, far_ref, o_ref, ordered):
    count = 2 * near_ref.shape[0] // size
    for i in range(count):
        partner = 2 * i if 2 * i < count else 2 * i - count + 1
        block = near_ref if 2 * i < count else far_ref
        first = i % (count // 2) * size
        at = pl.ds(pl.multiple_of((index_ref[0] ^ partner) * size, size), size)
        ordered[at, :] = block[first : first + size, :]
    o_ref[...] = ordered[...].T


def slab_kernel(u_ref, mat_ref, surface_ref, first_ref, last_ref):
    layers, rows, _ = u_ref.shape
    for ref, at in ((first_ref, pl.ds(0, DEEP)), (last_ref, pl.ds(rows - DEEP, DEEP))):
        for k in range(layers):
            ref[k] = u_ref[k, at, :]
            ref[layers + k] = mat_ref[k, at, :].astype(jnp.float32)
        ref[2 * layers] = surface_ref[at, :]


SUB = 8


def roll(x, shift, axis):
    shift = shift % x.shape[axis]
    return x if shift == 0 else pltpu.roll(x, shift, axis)


def pick(material, table):
    value = jnp.full(material.shape, table[NMAT - 1], jnp.float32)
    for i in range(NMAT - 1):
        value = jnp.where(material == i, table[i], value)
    return value


def tile(row):
    return pl.ds(pl.multiple_of(row * SUB, SUB), SUB)


def by_layer(ref, rows, first, t, steps, row):
    return ref[pl.ds((first + t) * rows + row, SUB, stride=steps * rows), :].astype(jnp.float32)


def for_rows(rows, own, above, below, body):
    u_ref, mat_ref, surface_ref = own
    steps = u_ref.shape[0] // rows // SUB
    layers = SUB * steps

    def margin(ref, offset):
        def one(i, carry):
            body(
                i + offset,
                lambda t: by_layer(ref, DEEP, 0, t, steps, i),
                lambda t: by_layer(ref, DEEP, layers, t, steps, i),
                ref[pl.ds(2 * layers * DEEP + i, 1), :],
            )
            return carry

        lax.fori_loop(0, DEEP, one, 0, unroll=8)

    def inner(i, carry):
        body(
            i + DEEP,
            lambda t: by_layer(u_ref, rows, 0, t, steps, i),
            lambda t: by_layer(mat_ref, rows, 0, t, steps, i),
            surface_ref[pl.ds(i, 1), :],
        )
        return carry

    margin(above, 0)
    lax.fori_loop(0, rows, inner, 0, unroll=8)
    margin(below, rows + DEEP)


def pack_kernel(
    u_ref, mat_ref, surface_ref, above_ref, below_ref, first_ref, last_ref
):
    rows = surface_ref.shape[0]
    steps = u_ref.shape[0] // rows // SUB
    slot = iota((SUB, LANES), 1) // DEEP

    def body(row, u, mat, load):
        first = jnp.zeros((SUB, LANES), jnp.float32)
        last = first
        fields = [u(t) for t in range(steps)] + [mat(t) for t in range(steps)]
        fields.append(jnp.broadcast_to(load, (SUB, LANES)))
        for i, x in enumerate(fields):
            first = jnp.where(slot == i, roll(x, i * DEEP, 1), first)
            last = jnp.where(slot == i, roll(x, (i + 1) * DEEP, 1), last)
        first_ref[tile(row), :] = first
        last_ref[tile(row), :] = last

    for_rows(rows, (u_ref, mat_ref, surface_ref), above_ref, below_ref, body)


def run_sweeps(src, offset, a_ref, f_ref, two):
    steps = a_ref.shape[0]
    rows = a_ref.shape[2] // SUB - 2 * offset
    lane = iota((SUB, LANES), 1)
    sub = iota((SUB, LANES), 0)
    cells = [(t, c) for t in range(steps) for c in range(2)]
    for sweep in range(SWEEPS):
        dst = two[sweep % 2]
        shift = offset if sweep == 0 else 0

        def load(row, src=src, shift=shift):
            return {cell: src[cell[0], cell[1], tile(row + shift), :] for cell in cells}

        def one(row, carry, load=load, dst=dst):
            before, x = ({cell: carry[j][i] for i, cell in enumerate(cells)} for j in range(2))
            after = load(row + 1)
            for t in range(steps):
                to_right = [roll(x[t, c], 1, 1) for c in range(2)]
                to_left = [roll(x[t, c], LANES - 1, 1) for c in range(2)]
                for c in range(2):
                    total = jnp.where(lane == 0, to_right[1 - c], to_right[c])
                    total = total + jnp.where(lane == LANES - 1, to_left[1 - c], to_left[c])
                    total = total + (before[t, c] + after[t, c])
                    if t > 0:
                        under = x[t - 1, c]
                    else:
                        under = jnp.where(sub == 0, 0.0, roll(x[steps - 1, c], 1, 0))
                    if t < steps - 1:
                        over = x[t + 1, c]
                    else:
                        over = jnp.where(sub == SUB - 1, 0.0, roll(x[0, c], SUB - 1, 0))
                    total = total + (under + over)
                    value = a_ref[t, c, tile(row + offset), :] * total
                    if t < f_ref.shape[0]:
                        value = value + f_ref[t, c, tile(row), :]
                    dst[t, c, tile(row), :] = value
            return (
                tuple(x[cell] for cell in cells),
                tuple(after[cell] for cell in cells),
            )

        start = (tuple(load(sweep).values()), tuple(load(sweep + 1).values()))
        lax.fori_loop(sweep + 1, rows - 1 - sweep, one, start, unroll=8)
        src = dst


def put_density(mat_ref, contrast, field, index_ref, scratch, pieces):
    lon_count = len(pieces)
    share, rows, _ = pieces[0].shape
    for k in range(lon_count * share):
        material = mat_ref[k * rows : (k + 1) * rows, :]
        scratch[k // share, k % share] = pick(material, contrast) * field(k)
    for s in range(lon_count):
        pieces[s][...] = scratch[lax.rem(index_ref[1] + s, lon_count)]


def layer_of(ref, k, margin, rows):
    steps = ref.shape[0]
    return ref[k % steps, 0, pl.ds(margin * SUB + k // steps, rows, stride=SUB), :]


def first_sweeps_kernel(
    lon_count, total_lat, index_ref, shear_ref, restoring_ref, contrast_ref, u_ref, mat_ref,
    surface_ref, above_ref, below_ref, left_ref, right_ref, *rest,
):
    pieces, rest = rest[:lon_count], rest[lon_count:]
    u_hbm, a_hbm, b_hbm, load_hbm, first, middle, u_out, a_out, b_out, load_out, f_scr, d_scr, sem = rest
    rows = surface_ref.shape[0]
    steps = u_out.shape[0]
    a_of, b_of = [], []
    for i in range(NMAT):
        stiff = jnp.full((SUB, LANES), shear_ref[i], jnp.float32)
        restore = jnp.full((SUB, LANES), restoring_ref[i], jnp.float32)
        b_of.append(1.0 / (6.0 * stiff + restore))
        a_of.append(stiff * b_of[i])
    lane = iota((SUB, LANES), 1)
    sub = iota((SUB, LANES), 0)

    def body(row, u, mat, load):
        at = tile(row)
        left, right = left_ref[at, :], right_ref[at, :]
        global_row = index_ref[0] * rows - DEEP + row
        inside = ((global_row >= 0) & (global_row < total_lat)).astype(jnp.float32)

        def side(i):
            after = roll(right, LANES - i * DEEP, 1)
            before = roll(left, LANES - (i + 1) * DEEP, 1)
            return jnp.where(lane < DEEP, after, jnp.where(lane >= LANES - DEEP, before, 0.0))

        loads = (jnp.broadcast_to(load, (SUB, LANES)), side(2 * steps))
        for t in range(steps):
            fields = ((u(t), mat(t)), (side(t), side(steps + t)))
            for c in range(2):
                value, material = fields[c]
                first[t, c, at, :] = value
                a_out[t, c, at, :] = pick(material, a_of) * inside
                b = pick(material, b_of) * inside
                b_out[t, c, at, :] = b
                if t == 0:
                    surface = jnp.where(sub == 0, loads[c], 0.0)
                    load_out[0, c, at, :] = surface
                    f_scr[0, c, at, :] = b * surface

    for_rows(rows, (u_ref, mat_ref, surface_ref), above_ref, below_ref, body)
    kept = ((a_out, a_hbm), (b_out, b_hbm), (load_out, load_hbm), (u_out, u_hbm))
    copies = [pltpu.make_async_copy(*pair, sem.at[i]) for i, pair in enumerate(kept)]
    for copy in copies[:-1]:
        copy.start()
    run_sweeps(first, 0, a_out, f_scr, (middle, u_out))
    copies[-1].start()
    put_density(
        mat_ref, contrast_ref, lambda k: layer_of(u_out, k, DEEP, rows), index_ref, d_scr, pieces
    )
    for copy in copies:
        copy.wait()


def second_sweeps_kernel(
    lon_count, index_ref, contrast_ref, mat_ref, u_ref, a_ref, b_ref, load_ref, *rest
):
    parts, rest = rest[:lon_count], rest[lon_count:]
    pieces, rest = rest[:lon_count], rest[lon_count:]
    field_out, middle, last, f_scr, pot, edge, d_scr = rest
    layers, rows, _ = field_out.shape
    steps = u_ref.shape[0]
    tall = rows + 2 * SHALLOW
    share = layers // lon_count
    spread = share // steps
    chunk = LANES // share
    lane = iota((SUB, LANES), 1)
    for s in range(lon_count):
        source = lax.rem(index_ref[1] + (lon_count - s), lon_count)
        for k in range(share):
            at = pl.ds(source * spread + k // steps, tall, stride=SUB)
            pot[k % steps, at, :] = parts[s][k * tall : (k + 1) * tall, :]
        packed = parts[s][share * tall :, :]
        for e in range(spread):
            at = pl.ds(source * spread + e, tall, stride=SUB)
            edge[at, :] = roll(packed, LANES - e * steps * chunk, 1)

    def force(row, carry):
        at, deep = tile(row), tile(row + DEEP - SHALLOW)
        ends = edge[at, :]
        for t in range(steps):
            after = roll(ends, LANES - t * chunk, 1)
            before = roll(ends, LANES - (t + 1) * chunk, 1)
            potential = (pot[t, at, :], jnp.where(lane < DEEP, after, before))
            for c in range(2):
                value = potential[c]
                if t == 0:
                    value = value + load_ref[0, c, deep, :]
                f_scr[t, c, at, :] = b_ref[t, c, deep, :] * value
        return carry

    lax.fori_loop(0, tall, force, 0, unroll=8)
    run_sweeps(u_ref, DEEP - SHALLOW, a_ref, f_scr, (middle, last))
    for k in range(layers):
        field_out[k] = layer_of(last, k, SHALLOW, rows)
    put_density(mat_ref, contrast_ref, lambda k: field_out[k], index_ref, d_scr, pieces)


def swap_chunks(blocks, chunk):
    blocks = list(blocks)
    lane = iota(blocks[0].shape, 1)
    step = 1
    while step < len(blocks):
        upper = (lane // (chunk * step)) % 2 == 1
        for i in range(len(blocks)):
            if i & step:
                continue
            a, b = blocks[i], blocks[i + step]
            blocks[i] = jnp.where(upper, roll(b, chunk * step, 1), a)
            blocks[i + step] = jnp.where(upper, b, roll(a, LANES - chunk * step, 1))
        step *= 2
    return blocks


def forward_kernel(lon_count, scale, index_ref, weight_ref, high_ref, low_ref, *rest):
    parts, (o_ref,) = rest[:lon_count], rest[lon_count:]
    share, rows, cols = parts[0].shape
    chunk = LANES // share
    product = None
    for s in range(lon_count):
        source = lax.rem(index_ref[1] + (lon_count - s), lon_count)
        at = pl.ds(pl.multiple_of(source * cols, cols), cols)
        term = dot3(
            halves(parts[s][...].reshape(share * rows, cols)), (high_ref[at, :], low_ref[at, :]), NN
        )
        product = term if product is None else product + term
    weight = weight_ref[...] * scale
    for g in range(product.shape[1] // LANES):
        blocks = swap_chunks(
            [
                product[k * rows : (k + 1) * rows, g * LANES : (g + 1) * LANES] * weight
                for k in range(share)
            ],
            chunk,
        )
        for i in range(share):
            o_ref[g * share + i] = blocks[i]


def spectral_kernel(margin, high_ref, low_ref, green_ref, x_ref, o_ref, turned, coeffs, pots):
    share, degrees, width = high_ref.shape
    lat_count, lon_count, rows, _ = x_ref.shape
    total_lat = lat_count * rows
    size = 2 * share
    layers = turned.shape[1] // size
    pad = jnp.zeros((width - total_lat, LANES), jnp.float32)
    for q in range(lon_count):
        x = x_ref[:, q].reshape(total_lat, LANES)
        x = jnp.concatenate([x, pad], axis=0)
        for c in range(width // LANES):
            turned[c, q * LANES : (q + 1) * LANES, :] = x[c * LANES : (c + 1) * LANES].T
    for m in range(share):
        x = halves(every(turned, m, share, 2 * layers))
        put_every(coeffs, m, share, dot3(x, (high_ref[m], low_ref[m]), NT))
    block = 4

    def targets(i, carry):
        for c in range(degrees // LANES):
            sums = [jnp.zeros((size, LANES), jnp.float32) for _ in range(block)]
            for k in range(0, layers, 8):
                part = [
                    green_ref[
                        pl.ds(pl.multiple_of((i * block + t) * layers + k, 8), 8),
                        c * LANES : (c + 1) * LANES,
                    ]
                    for t in range(block)
                ]
                for e in range(8):
                    x = coeffs[c, (k + e) * size : (k + e + 1) * size, :]
                    for t in range(block):
                        sums[t] = sums[t] + part[t][e : e + 1] * x
            for t in range(block):
                pots[c, pl.ds(pl.multiple_of((i * block + t) * size, size), size), :] = sums[t]
        return carry

    lax.fori_loop(0, layers // block, targets, 0)
    for m in range(share):
        x = halves(every(pots, m, share, 2 * layers))
        put_every(turned, m, share, dot3(x, (high_ref[m], low_ref[m]), NN))
    for q in range(lon_count):
        x = [turned[c, q * LANES : (q + 1) * LANES, :].T for c in range(width // LANES)]
        x = jnp.concatenate(x, axis=0)[:total_lat]
        if margin > 0:
            edge = jnp.zeros((margin, LANES), jnp.float32)
            x = jnp.concatenate([edge, x, edge], axis=0)
        for i in range(lat_count):
            o_ref[i, q] = x[i * rows : (i + 1) * rows + 2 * margin]


def inverse_kernel(lon_count, margin, index_ref, high_ref, low_ref, x_ref, *rest):
    pieces, (columns,) = rest[:lon_count], rest[lon_count:]
    owners, rows, _ = x_ref.shape
    cols = high_ref.shape[0] // lon_count
    share = columns.shape[1] // rows
    chunk = LANES // share
    groups = [
        swap_chunks([x_ref[g * share + i] for i in range(share)], chunk)
        for g in range(owners // share)
    ]
    terms = jnp.concatenate(
        [jnp.concatenate([group[k] for group in groups], axis=1) for k in range(share)], axis=0
    )
    terms = halves(terms)
    for q in range(lon_count):
        at = slice(q * cols, (q + 1) * cols)
        columns[q] = dot3(terms, (high_ref[at, :], low_ref[at, :]), NT)
    lane = iota((rows, LANES), 1)
    for s in range(lon_count):
        dest = lax.rem(index_ref[1] + s, lon_count)
        pieces[s][0 : share * rows] = columns[dest]
        if margin == 0:
            continue
        after = lax.rem(dest + 1, lon_count)
        before = lax.rem(dest + lon_count - 1, lon_count)
        packed = jnp.zeros((rows, LANES), jnp.float32)
        for k in range(share):
            right = roll(columns[after, k * rows : (k + 1) * rows, :], k * chunk, 1)
            left = roll(columns[before, k * rows : (k + 1) * rows, :], (k + 1) * chunk, 1)
            packed = jnp.where(
                lane // DEEP == 2 * k, right, jnp.where(lane // DEEP == 2 * k + 1, left, packed)
            )
        pieces[s][share * rows :] = packed


def assemble_kernel(lon_count, index_ref, *rest):
    parts, o_hbm, sem = rest[:lon_count], rest[lon_count], rest[lon_count + 1]
    sources = [lax.rem(index_ref[1] + (lon_count - s), lon_count) for s in range(lon_count)]
    copy_all(sem, *((part, o_hbm.at[source]) for part, source in zip(parts, sources)))


def exchange(pieces):
    count = len(pieces)
    return [pieces[0]] + [
        lax.ppermute(pieces[s], "lon", [(i, (i + s) % count) for i in range(count)])
        for s in range(1, count)
    ]


def on_device(displacement, materials, ice_mask, ice_height, shear, restoring, contrast, green):
    layers, rows, cols = displacement.shape
    lat_count, lon_count = lax.axis_size("lat"), lax.axis_size("lon")
    total_lat, total_lon = rows * lat_count, cols * lon_count
    owners = lat_count * lon_count
    share, orders = layers // lon_count, LMAX // owners
    width = -(-total_lat // LANES) * LANES
    tall = rows + 2 * SHALLOW
    lat_index = lax.axis_index("lat")
    index = jnp.stack([lat_index, lax.axis_index("lon")]).astype(jnp.int32)
    owner = (index[0] * lon_count + index[1])[None]

    surface = ice_mask.astype(jnp.float32) * ice_height
    own = (
        displacement.reshape(layers * rows, cols),
        materials.reshape(layers * rows, cols),
        surface,
    )
    first, last = call(
        slab_kernel,
        (f32(2 * layers + 1, DEEP, cols),) * 2,
        1.0,
    )(displacement, materials, surface)
    green, first, last = lax.optimization_barrier((green, first, last))
    first, last = (x.reshape(-1, cols) for x in (first, last))
    above = lax.ppermute(last, "lat", [(i, i + 1) for i in range(lat_count - 1)])
    below = lax.ppermute(first, "lat", [(i + 1, i) for i in range(lat_count - 1)])
    table = call(
        functools.partial(fourier_kernel, total_lon, orders),
        (jax.ShapeDtypeStruct((total_lon, 2 * LMAX), HALF),) * 2,
        1.2,
    )()
    def partner(x, step):
        return lax.ppermute(x, "lat", [(i, i ^ step) for i in range(lat_count)])

    near = green.reshape(green.shape[0], layers * layers)
    near, table = lax.optimization_barrier((near, table))
    others = [partner(near, i) for i in range(2, lat_count, 2)]
    half_table = (orders, LMAX, width)
    legendre_table = call(
        functools.partial(legendre_kernel, total_lat, orders),
        (jax.ShapeDtypeStruct(half_table, HALF),) * 2,
        2.9,
        scratch=[
            pltpu.VMEM((width // LANES, LMAX * orders, LANES), jnp.float32),
            pltpu.VMEM(half_table, HALF),
            pltpu.VMEM(half_table, HALF),
            pltpu.SemaphoreType.DMA((2,)),
        ],
        smem=(0,),
        hbm=(0, 1),
    )(owner)
    above, below, others, table, legendre_table = lax.optimization_barrier(
        (above, below, others, table, legendre_table)
    )
    near = jnp.concatenate([near, *others], axis=0)
    far = partner(near, 1)
    first, last = call(pack_kernel, (f32((rows + 2 * DEEP) * SUB, cols),) * 2, 1.5)(
        *own, above, below
    )
    left = lax.ppermute(last, "lon", [(i, (i + 1) % lon_count) for i in range(lon_count)])
    right = lax.ppermute(first, "lon", [((i + 1) % lon_count, i) for i in range(lon_count)])
    theta = ((lat_index * rows + jnp.arange(rows)).astype(jnp.float32) + 0.5) * (
        jnp.pi / total_lat
    )
    weight = jnp.broadcast_to((jnp.sin(theta) / (4.0 * total_lat))[:, None], (rows, LANES))

    steps = layers // SUB

    def worked(t, height):
        return (t, 2, height * SUB, LANES)

    deep = rows + 2 * DEEP
    flat = pltpu.VMEM((lon_count, share, rows, cols), jnp.float32)
    out = call(
        functools.partial(first_sweeps_kernel, lon_count, total_lat),
        (f32(share, rows, cols),) * lon_count
        + (f32(*worked(steps, deep)),) * 3
        + (f32(*worked(1, deep)),),
        6.6,
        scratch=[pltpu.VMEM(worked(steps, deep), jnp.float32)] * 5
        + [pltpu.VMEM(worked(1, deep), jnp.float32)] * 2
        + [flat, pltpu.SemaphoreType.DMA((4,))],
        smem=(0, 1, 2, 3),
        hbm=range(lon_count, lon_count + 4),
    )(index, shear, restoring, contrast, *own, above, below, left, right)
    pieces, state = out[:lon_count], out[lon_count:]
    for iteration in range(ITERS):
        margin = SHALLOW if iteration < ITERS - 1 else 0
        parts = exchange(pieces)
        if iteration == 0:
            turned_green = call(
                functools.partial(turn_kernel, green.shape[0]),
                f32(layers * layers, LMAX),
                1.4,
                scratch=[pltpu.VMEM((LMAX, layers * layers), jnp.float32)],
                smem=(0,),
            )(index, near, far)
            parts, turned_green = lax.optimization_barrier((parts, turned_green))
        spectrum = call(
            functools.partial(forward_kernel, lon_count, 2.0 * math.pi / total_lon),
            f32(owners, rows, LANES),
            2.0,
            smem=(0,),
        )(index, weight, *table, *parts)
        spectrum = lax.all_to_all(spectrum, BOTH, 0, 0, tiled=True)
        square = pltpu.VMEM((width // LANES, lon_count * LANES, LANES), jnp.float32)
        coeff_shape = pltpu.VMEM((LMAX // LANES, lon_count * LANES, LANES), jnp.float32)
        synth = call(
            functools.partial(spectral_kernel, margin),
            f32(lat_count, lon_count, rows + 2 * margin, LANES),
            4.0,
            scratch=[square, coeff_shape, coeff_shape],
        )(
            *legendre_table,
            turned_green,
            spectrum.reshape(lat_count, lon_count, rows, LANES),
        )
        synth = lax.all_to_all(
            synth.reshape(owners, rows + 2 * margin, LANES), BOTH, 0, 0, tiled=True
        )
        high = rows + 2 * margin
        sent = share * high + (high if margin > 0 else 0)
        parts = call(
            functools.partial(inverse_kernel, lon_count, margin),
            (f32(sent, cols),) * lon_count,
            2.0,
            scratch=[pltpu.VMEM((lon_count, share * high, cols), jnp.float32)],
            smem=(0,),
        )(index, *table, synth)
        parts = exchange(parts)
        if iteration < ITERS - 1:
            out = call(
                functools.partial(second_sweeps_kernel, lon_count),
                (f32(share, rows, cols),) * lon_count + (f32(layers, rows, cols),),
                5.4,
                scratch=[pltpu.VMEM(worked(steps, tall), jnp.float32)] * 3
                + [
                    pltpu.VMEM((steps, tall * SUB, LANES), jnp.float32),
                    pltpu.VMEM((tall * SUB, LANES), jnp.float32),
                    flat,
                ],
                smem=(0, 1),
            )(index, contrast, own[1], *state, *parts)
            pieces, field = out[:lon_count], out[lon_count]
    potential = call(
        functools.partial(assemble_kernel, lon_count),
        f32(lon_count, share * rows, cols),
        1.0,
        scratch=[pltpu.SemaphoreType.DMA((lon_count,))],
        smem=(0,),
        hbm=(0,),
    )(index, *parts)
    return (field, potential.reshape(layers, rows, cols))


def aligned(mesh, displacement):
    lat_count, lon_count = mesh.shape["lat"], mesh.shape["lon"]
    layers, total_lat, total_lon = displacement.shape
    rows, cols = total_lat // lat_count, total_lon // lon_count
    owners = lat_count * lon_count
    return (
        ITERS == 2
        and cols == LANES
        and rows % 8 == 0
        and layers % SUB == 0
        and (2 * (layers // SUB) + 1) * DEEP <= LANES
        and (layers // lon_count) % (layers // SUB) == 0
        and lat_count > 2
        and lat_count & (lat_count - 1) == 0
        and layers % lon_count == 0
        and LMAX % owners == 0
        and 2 * (LMAX // owners) * (layers // lon_count) == LANES
        and 2 * (LMAX // owners) == 2 * DEEP
        and LMAX % LANES == 0
    )


def solution(mesh):
    in_specs = (
        P(None, "lat", "lon"),
        P(None, "lat", "lon"),
        P("lat", "lon"),
        P("lat", "lon"),
        P(),
        P(),
        P(),
        P("lat", None, None),
    )
    out_specs = (P(None, "lat", "lon"), P(None, "lat", "lon"))

    def step(displacement, *others):
        device = on_device if aligned(mesh, displacement) else general_device
        return jax.shard_map(
            device, mesh=mesh, in_specs=in_specs, out_specs=out_specs, check_vma=False
        )(displacement, *others)

    return step
```

```python
import functools
import math

import jax
import jax.numpy as jnp
from jax import lax
from jax.experimental import pallas as pl
from jax.experimental.pallas import tpu as pltpu
from jax.sharding import PartitionSpec as P

LMAX = 256
NMAT = 4
ITERS = 2
SWEEPS = 4
LANES = 128
DEEP = 8
SHALLOW = 4
HALF = jnp.bfloat16
VMEM_LIMIT = 16 * 1024 * 1024
BOTH = ("lat", "lon")


def extended(cells, sides, width, closed):
    for axis, dim in sides:
        count = lax.axis_size(axis)
        ends = count if closed else count - 1
        head = lax.slice_in_dim(cells, 0, width, axis=dim)
        tail = lax.slice_in_dim(cells, cells.shape[dim] - width, cells.shape[dim], axis=dim)
        cells = jnp.concatenate(
            [
                lax.ppermute(tail, axis, [(i, (i + 1) % count) for i in range(ends)]),
                cells,
                lax.ppermute(head, axis, [((i + 1) % count, i) for i in range(ends)]),
            ],
            axis=dim,
        )
    return cells


def legendre(theta):
    orders = jnp.arange(LMAX)
    order_f = orders.astype(jnp.float32)
    cosine = jnp.cos(theta)[:, None]
    sine = jnp.sin(theta)[:, None]
    safe = jnp.maximum(order_f, 1.0)
    growth = jnp.where(orders >= 2, 0.5 * jnp.log((2.0 * safe + 1.0) / (2.0 * safe)), 0.0)
    log_diag = jnp.where(orders >= 1, 0.5 * jnp.log(3.0) + jnp.cumsum(growth), 0.0)
    diagonal = jnp.exp(log_diag[None, :] + order_f[None, :] * jnp.log(sine))

    def advance(carry, degree):
        prev_one, prev_two = carry
        deg_f = degree.astype(jnp.float32)
        first = jnp.sqrt(
            (4.0 * deg_f * deg_f - 1.0) / jnp.maximum(deg_f * deg_f - order_f * order_f, 1.0)
        )
        second = jnp.sqrt(
            jnp.maximum((deg_f - 1.0) ** 2 - order_f * order_f, 0.0)
            / jnp.maximum(4.0 * (deg_f - 1.0) ** 2 - 1.0, 1.0)
        )
        general = first * (cosine * prev_one - second * prev_two)
        start_next = jnp.sqrt(2.0 * order_f + 3.0) * cosine * diagonal
        value = jnp.where(
            orders == degree,
            diagonal,
            jnp.where(
                orders == degree - 1, start_next, jnp.where(orders < degree - 1, general, 0.0)
            ),
        )
        return ((value, prev_one), value)

    zeros = jnp.zeros((theta.shape[0], LMAX), jnp.float32)
    _, table = lax.scan(advance, (zeros, zeros), jnp.arange(LMAX), unroll=8)
    return table


def fourier_tables(columns, total):
    orders = jnp.arange(LMAX)
    phase = columns[:, None] * orders[None, :] % total
    angle = 2.0 * jnp.pi / total * phase.astype(jnp.float32)
    forward = jnp.concatenate([jnp.cos(angle), jnp.sin(angle)], axis=1) * (2.0 * jnp.pi / total)
    inverse = jnp.concatenate([jnp.cos(angle), jnp.sin(angle)], axis=1).T
    return (forward, inverse)


def lookup(materials, table):
    result = jnp.zeros(materials.shape, jnp.float32)
    for material in range(NMAT):
        result = result + jnp.where(materials == material, table[material], 0.0)
    return result


def crop_block(block, margin):
    return block[:, margin : block.shape[1] - margin, margin : block.shape[2] - margin]


def margin_sweeps(field, force, stiff, restore, depth, lat_first, total_lat):
    stacked = jnp.stack([field, force, stiff, restore], axis=0)
    lat_wide = extended(stacked, (("lat", 2),), depth, False)
    wide = extended(lat_wide, (("lon", 3),), depth, True)
    current = wide[0]
    rows_wide = wide.shape[2]
    global_rows = lat_first - depth + jnp.arange(rows_wide)
    inside = ((global_rows >= 0) & (global_rows < total_lat))[None, :, None]
    for step in range(depth):
        margin = step + 1
        inner = current[:, 1:-1, 1:-1]
        beside_all = (
            current[:, 2:, 1:-1]
            + current[:, :-2, 1:-1]
            + current[:, 1:-1, 2:]
            + current[:, 1:-1, :-2]
        )
        layer_pad = jnp.pad(inner, ((1, 1), (0, 0), (0, 0)))
        beside_all = beside_all + layer_pad[2:] + layer_pad[:-2]
        force_part = crop_block(wide[1], margin)
        stiff_part = crop_block(wide[2], margin)
        restore_part = crop_block(wide[3], margin)
        valid = inside[:, margin : rows_wide - margin, :]
        denominator = jnp.where(valid, 6.0 * stiff_part + restore_part, 1.0)
        current = jnp.where(valid, (force_part + stiff_part * beside_all) / denominator, 0.0)
    return current


def general_device(displacement, materials, ice_mask, ice_height, shear, restoring, contrast, green):
    highest = lax.Precision.HIGHEST
    layers, lat_rows, lon_cols = displacement.shape
    lon_count = lax.axis_size("lon")
    lat_count = lax.axis_size("lat")
    total_lat = lat_rows * lat_count
    total_lon = lon_cols * lon_count
    layer_share = layers // lon_count
    stiff = lookup(materials, shear)
    restore = lookup(materials, restoring)
    rho_scale = lookup(materials, contrast)
    surface = (ice_mask.astype(jnp.float32) * ice_height)[None]
    load = jnp.concatenate(
        [surface, jnp.zeros((layers - 1, lat_rows, lon_cols), jnp.float32)], axis=0
    )
    lat_first = lax.axis_index("lat") * lat_rows
    theta = ((lat_first + jnp.arange(lat_rows)).astype(jnp.float32) + 0.5) * (jnp.pi / total_lat)
    table = legendre(theta)
    weights = jnp.sin(theta) / (4.0 * total_lat)
    own_columns = lax.axis_index("lon") * lon_cols + jnp.arange(lon_cols)
    layer_first = lax.axis_index("lon") * layer_share
    depth = 1
    for candidate in range(1, SWEEPS + 1):
        if SWEEPS % candidate == 0 and candidate <= min(lat_rows, lon_cols):
            depth = candidate
    forward, inverse = fourier_tables(own_columns, total_lon)
    field = displacement
    potential = jnp.zeros((layers, lat_rows, lon_cols), jnp.float32)
    for iteration in range(ITERS):
        force = load + potential
        field = margin_sweeps(field, force, stiff, restore, depth, lat_first, total_lat)
        density = rho_scale * field
        product = jnp.dot(
            density.reshape(layer_share * lax.axis_size("lon") * lat_rows, lon_cols),
            forward,
            precision=highest,
            preferred_element_type=jnp.float32,
        )
        spectrum = lax.psum_scatter(
            product.reshape(layer_share * lax.axis_size("lon"), lat_rows, 2 * LMAX),
            "lon",
            scatter_dimension=0,
            tiled=True,
        )
        weighted = spectrum.reshape(layer_share, lat_rows, 2, LMAX) * weights[None, :, None, None]
        coeffs = lax.psum_scatter(
            jnp.einsum("lam,kacm->lkcm", table, weighted, precision=highest),
            "lat",
            scatter_dimension=0,
            tiled=True,
        )
        green_part = lax.dynamic_slice_in_dim(green, layer_first, layer_share, 2)
        partial_pot = jnp.einsum("lkj,ljcm->lkcm", green_part, coeffs, precision=highest)
        pot_coeffs = lax.psum_scatter(partial_pot, "lon", scatter_dimension=1, tiled=True)
        synth = jnp.einsum(
            "lam,lkcm->kacm",
            table,
            lax.all_gather(pot_coeffs, "lat", axis=0, tiled=True),
            precision=highest,
        )
        synth = synth.reshape(layer_share, lat_rows, 2 * LMAX)
        piece = lax.all_gather(synth, "lon", axis=0, tiled=True)
        synth_product = jnp.dot(
            piece.reshape(piece.shape[0] * lat_rows, 2 * LMAX),
            inverse,
            precision=highest,
            preferred_element_type=jnp.float32,
        )
        potential = synth_product.reshape(piece.shape[0], lat_rows, lon_cols)
    return (field, potential)


def call(kernel, outs, micros, scratch=(), smem=(), far=(), hbm=()):
    def place(i, scalars, away):
        space = pltpu.SMEM if i in scalars else pltpu.HBM if i in away else pltpu.VMEM
        return pl.BlockSpec(memory_space=space)

    def run(*args):
        return pl.pallas_call(
            kernel,
            out_shape=outs,
            in_specs=[place(i, smem, far) for i in range(len(args))],
            out_specs=tuple(place(i, (), hbm) for i in range(len(outs)))
            if type(outs) is tuple
            else place(0, (), hbm),
            scratch_shapes=list(scratch),
            compiler_params=pltpu.CompilerParams(vmem_limit_bytes=VMEM_LIMIT),
            cost_estimate=pl.CostEstimate(
                flops=int(micros * 1e9), bytes_accessed=1, transcendentals=0
            ),
        )(*args)

    return run


def copy_all(sem, *pairs):
    copies = [pltpu.make_async_copy(*pair, sem.at[i]) for i, pair in enumerate(pairs)]
    for copy in copies:
        copy.start()
    for copy in copies:
        copy.wait()


def f32(*shape):
    return jax.ShapeDtypeStruct(shape, jnp.float32)


def halves(x):
    high = x.astype(HALF)
    return high, (x - high.astype(jnp.float32)).astype(HALF)


def dot(a, b, dims):
    return lax.dot_general(a, b, (dims, ((), ())), preferred_element_type=jnp.float32)


def dot3(a, b, dims):
    rows = a[0].shape[0]
    both = dot(jnp.concatenate(a, axis=0), b[0], dims)
    return both[:rows] + (both[rows:] + dot(a[0], b[1], dims))


def every(ref, start, stride, count):
    at = pl.ds(start, count, stride=stride)
    return jnp.concatenate([ref[c, at, :] for c in range(ref.shape[0])], axis=1)


def put_every(ref, start, stride, value):
    at = pl.ds(start, value.shape[0], stride=stride)
    for c in range(ref.shape[0]):
        ref[c, at, :] = value[:, c * LANES : (c + 1) * LANES]


NN = ((1,), (0,))
NT = ((1,), (1,))


def iota(shape, dim):
    return lax.broadcasted_iota(jnp.int32, shape, dim)


def fourier_kernel(total, share, high_ref, low_ref):
    shape = (16, 2 * LMAX)
    column = iota(shape, 1)
    order = column // (2 * share) * share + column % share
    shift = (column // share) % 2 * (total - total // 4)
    first = iota(shape, 0) * order + shift
    quarter, half = total // 4, total // 2

    def block(i, carry):
        phase = first + order * (i * shape[0])
        phase = phase & (total - 1) if total & (total - 1) == 0 else lax.rem(phase, total)
        near = jnp.minimum(phase, total - phase)
        beyond = near > quarter
        angle = jnp.where(beyond, half - near, near).astype(jnp.float32) * (2.0 * math.pi / total)
        square = angle * angle
        value = jnp.full(shape, 1.0 / math.factorial(14), jnp.float32)
        for n in range(12, -1, -2):
            value = 1.0 / math.factorial(n) - square * value
        high, low = halves(jnp.where(beyond, -value, value))
        at = pl.ds(pl.multiple_of(i * shape[0], shape[0]), shape[0])
        high_ref[at, :] = high
        low_ref[at, :] = low
        return carry

    lax.fori_loop(0, total // shape[0], block, 0, unroll=2)


def legendre_kernel(total_lat, share, index_ref, high_out, low_out, table, high_ref, low_ref, sem):
    width = table.shape[0] * LANES
    base = index_ref[0] * share
    shape = (share, width)
    order = iota(shape, 0) + base
    order_f = order.astype(jnp.float32)
    row = iota(shape, 1)
    theta = (row.astype(jnp.float32) + 0.5) * (math.pi / total_lat)
    cosine = jnp.cos(theta)
    sine = jnp.where(row < total_lat, jnp.sin(theta), 1.0)
    terms = (share, LMAX)
    term = iota(terms, 1)
    term_f = jnp.maximum(term.astype(jnp.float32), 1.0)
    growth = 0.5 * jnp.log((2.0 * term_f + 1.0) / (2.0 * term_f))
    used = (term >= 2) & (term <= iota(terms, 0) + base)
    total = jnp.sum(jnp.where(used, growth, 0.0), axis=1, keepdims=True)
    log_diag = jnp.where(order >= 1, 0.5 * math.log(3.0) + total, 0.0)
    diagonal = jnp.exp(log_diag + order_f * jnp.log(sine))
    diagonal = jnp.where(row < total_lat, diagonal, 0.0)
    start_next = jnp.sqrt(2.0 * order_f + 3.0) * cosine * diagonal
    narrow = (share, LANES)
    square = ((iota(narrow, 0) + base).astype(jnp.float32)) ** 2

    def wide(x):
        return jnp.concatenate([x] * (width // LANES), axis=1)

    def advance(degree, carry):
        prev_one, prev_two = carry
        deg = jnp.full(narrow, degree, jnp.int32).astype(jnp.float32)
        first = jnp.sqrt((4.0 * deg * deg - 1.0) / jnp.maximum(deg * deg - square, 1.0))
        below = (deg - 1.0) * (deg - 1.0)
        second = jnp.sqrt(jnp.maximum(below - square, 0.0) / jnp.maximum(4.0 * below - 1.0, 1.0))
        general = wide(first) * (cosine * prev_one - wide(second) * prev_two)
        value = jnp.where(
            order == degree,
            diagonal,
            jnp.where(
                order == degree - 1, start_next, jnp.where(order < degree - 1, general, 0.0)
            ),
        )
        for c in range(width // LANES):
            at = pl.ds(pl.multiple_of(degree * share, share), share)
            table[c, at, :] = value[:, c * LANES : (c + 1) * LANES]
        return (value, prev_one)

    table[:, 0:share, :] = jnp.zeros((width // LANES, share, LANES), jnp.float32)
    zeros = jnp.concatenate([table[c, 0:share, :] for c in range(width // LANES)], axis=1)
    lax.fori_loop(0, LMAX, advance, (zeros, zeros), unroll=8)
    for m in range(share):
        high, low = halves(every(table, m, share, LMAX))
        high_ref[m] = high
        low_ref[m] = low
    copy_all(sem, (high_ref, high_out), (low_ref, low_out))


def turn_kernel(size, index_ref, near_ref, far_ref, o_ref, ordered):
    count = 2 * near_ref.shape[0] // size
    for i in range(count):
        partner = 2 * i if 2 * i < count else 2 * i - count + 1
        block = near_ref if 2 * i < count else far_ref
        first = i % (count // 2) * size
        at = pl.ds(pl.multiple_of((index_ref[0] ^ partner) * size, size), size)
        ordered[at, :] = block[first : first + size, :]
    o_ref[...] = ordered[...].T


def slab_kernel(u_ref, mat_ref, surface_ref, first_ref, last_ref):
    layers, rows, _ = u_ref.shape
    for ref, at in ((first_ref, pl.ds(0, DEEP)), (last_ref, pl.ds(rows - DEEP, DEEP))):
        for k in range(layers):
            ref[k] = u_ref[k, at, :]
            ref[layers + k] = mat_ref[k, at, :].astype(jnp.float32)
        ref[2 * layers] = surface_ref[at, :]


SUB = 8
PARTS = 2
UNROLL = True


def roll(x, shift, axis):
    shift = shift % x.shape[axis]
    return x if shift == 0 else pltpu.roll(x, shift, axis)


def pick(material, table):
    value = jnp.full(material.shape, table[NMAT - 1], jnp.float32)
    for i in range(NMAT - 1):
        value = jnp.where(material == i, table[i], value)
    return value


def tile(row):
    return pl.ds(pl.multiple_of(row * SUB, SUB), SUB)


def by_layer(ref, rows, first, t, steps, row):
    return ref[pl.ds((first + t) * rows + row, SUB, stride=steps * rows), :].astype(jnp.float32)


def for_rows(rows, own, above, below, body):
    u_ref, mat_ref, surface_ref = own
    steps = u_ref.shape[0] // rows // SUB
    layers = SUB * steps

    def margin(ref, offset):
        def one(i, carry):
            body(
                i + offset,
                lambda t: by_layer(ref, DEEP, 0, t, steps, i),
                lambda t: by_layer(ref, DEEP, layers, t, steps, i),
                ref[pl.ds(2 * layers * DEEP + i, 1), :],
            )
            return carry

        lax.fori_loop(0, DEEP, one, 0, unroll=8)

    def inner(i, carry):
        body(
            i + DEEP,
            lambda t: by_layer(u_ref, rows, 0, t, steps, i),
            lambda t: by_layer(mat_ref, rows, 0, t, steps, i),
            surface_ref[pl.ds(i, 1), :],
        )
        return carry

    margin(above, 0)
    lax.fori_loop(0, rows, inner, 0, unroll=8)
    margin(below, rows + DEEP)


def pack_kernel(
    u_ref, mat_ref, surface_ref, above_ref, below_ref, first_ref, last_ref
):
    rows = surface_ref.shape[0]
    steps = u_ref.shape[0] // rows // SUB
    slot = iota((SUB, LANES), 1) // DEEP

    def body(row, u, mat, load):
        first = jnp.zeros((SUB, LANES), jnp.float32)
        last = first
        fields = [u(t) for t in range(steps)] + [mat(t) for t in range(steps)]
        fields.append(jnp.broadcast_to(load, (SUB, LANES)))
        for i, x in enumerate(fields):
            first = jnp.where(slot == i, roll(x, i * DEEP, 1), first)
            last = jnp.where(slot == i, roll(x, (i + 1) * DEEP, 1), last)
        first_ref[tile(row), :] = first
        last_ref[tile(row), :] = last

    for_rows(rows, (u_ref, mat_ref, surface_ref), above_ref, below_ref, body)


def lon_neighbours(near):
    width = near.shape[0]
    apart = iota(near.shape, 0) - iota(near.shape, 1)
    apart = jnp.where(apart < 0, apart + width, apart)
    near[...] = ((apart == 1) | (apart == width - 1)).astype(jnp.float32).astype(HALF)


def run_sweeps(src, offset, a_ref, f_ref, two, near):
    steps = a_ref.shape[0]
    rows = a_ref.shape[2] // SUB - 2 * offset
    for sweep in range(SWEEPS):
        dst = two[sweep % 2]
        shift = offset if sweep == 0 else 0
        size = (rows - 2 - 2 * sweep) // PARTS

        def block(i, carry, src=src, dst=dst, shift=shift, size=size, sweep=sweep):
            first = sweep + 1 + i * size

            def at(row):
                return pl.ds(pl.multiple_of(row * SUB, SUB), size * SUB)

            def tiles(t, c, move):
                return src[t, c, at(first + shift + move), :].reshape(size, SUB, LANES)

            sub = iota((size, SUB, LANES), 1)
            x = [[tiles(t, c, 0) for c in range(2)] for t in range(steps)]
            for t in range(steps):
                both = jnp.concatenate([x[t][c].reshape(size * SUB, LANES) for c in range(2)], axis=1)
                high, low = halves(both)
                beside = dot(high, near[...], NN) + dot(low, near[...], NN)
                for c in range(2):
                    total = beside[:, c * LANES : (c + 1) * LANES].reshape(size, SUB, LANES)
                    total = total + (tiles(t, c, -1) + tiles(t, c, 1))
                    if t > 0:
                        under = x[t - 1][c]
                    else:
                        under = jnp.where(sub == 0, 0.0, roll(x[steps - 1][c], 1, 1))
                    if t < steps - 1:
                        over = x[t + 1][c]
                    else:
                        over = jnp.where(sub == SUB - 1, 0.0, roll(x[0][c], SUB - 1, 1))
                    total = (total + (under + over)).reshape(size * SUB, LANES)
                    value = a_ref[t, c, at(first + offset), :] * total
                    if t < f_ref.shape[0]:
                        value = value + f_ref[t, c, at(first), :]
                    dst[t, c, at(first), :] = value
            return carry

        lax.fori_loop(0, PARTS, block, 0, unroll=UNROLL)
        src = dst


def put_density(mat_ref, contrast, field, index_ref, scratch, pieces):
    lon_count = len(pieces)
    share, rows, _ = pieces[0].shape
    for k in range(lon_count * share):
        material = mat_ref[k * rows : (k + 1) * rows, :]
        scratch[k // share, k % share] = pick(material, contrast) * field(k)
    for s in range(lon_count):
        pieces[s][...] = scratch[lax.rem(index_ref[1] + s, lon_count)]


def layer_of(ref, k, margin, rows):
    steps = ref.shape[0]
    return ref[k % steps, 0, pl.ds(margin * SUB + k // steps, rows, stride=SUB), :]


def first_sweeps_kernel(
    lon_count, total_lat, index_ref, shear_ref, restoring_ref, contrast_ref, u_ref, mat_ref,
    surface_ref, above_ref, below_ref, left_ref, right_ref, *rest,
):
    pieces, rest = rest[:lon_count], rest[lon_count:]
    u_hbm, a_hbm, b_hbm, load_hbm, first, middle, u_out, a_out, b_out, load_out, f_scr, d_scr, near, sem = rest
    rows = surface_ref.shape[0]
    steps = u_out.shape[0]
    a_of, b_of = [], []
    for i in range(NMAT):
        stiff = jnp.full((SUB, LANES), shear_ref[i], jnp.float32)
        restore = jnp.full((SUB, LANES), restoring_ref[i], jnp.float32)
        b_of.append(1.0 / (6.0 * stiff + restore))
        a_of.append(stiff * b_of[i])
    lane = iota((SUB, LANES), 1)
    sub = iota((SUB, LANES), 0)

    def body(row, u, mat, load):
        at = tile(row)
        left, right = left_ref[at, :], right_ref[at, :]
        global_row = index_ref[0] * rows - DEEP + row
        inside = ((global_row >= 0) & (global_row < total_lat)).astype(jnp.float32)

        def side(i):
            after = roll(right, LANES - i * DEEP, 1)
            before = roll(left, LANES - (i + 1) * DEEP, 1)
            return jnp.where(lane < DEEP, after, jnp.where(lane >= LANES - DEEP, before, 0.0))

        loads = (jnp.broadcast_to(load, (SUB, LANES)), side(2 * steps))
        for t in range(steps):
            fields = ((u(t), mat(t)), (side(t), side(steps + t)))
            for c in range(2):
                value, material = fields[c]
                first[t, c, at, :] = value
                a_out[t, c, at, :] = pick(material, a_of) * inside
                b = pick(material, b_of) * inside
                b_out[t, c, at, :] = b
                if t == 0:
                    surface = jnp.where(sub == 0, loads[c], 0.0)
                    load_out[0, c, at, :] = surface
                    f_scr[0, c, at, :] = b * surface

    for_rows(rows, (u_ref, mat_ref, surface_ref), above_ref, below_ref, body)
    kept = ((a_out, a_hbm), (b_out, b_hbm), (load_out, load_hbm), (u_out, u_hbm))
    copies = [pltpu.make_async_copy(*pair, sem.at[i]) for i, pair in enumerate(kept)]
    for copy in copies[:-1]:
        copy.start()
    lon_neighbours(near)
    run_sweeps(first, 0, a_out, f_scr, (middle, u_out), near)
    copies[-1].start()
    put_density(
        mat_ref, contrast_ref, lambda k: layer_of(u_out, k, DEEP, rows), index_ref, d_scr, pieces
    )
    for copy in copies:
        copy.wait()


def second_sweeps_kernel(
    lon_count, index_ref, contrast_ref, mat_ref, u_ref, a_ref, b_ref, load_ref, *rest
):
    parts, rest = rest[:lon_count], rest[lon_count:]
    pieces, rest = rest[:lon_count], rest[lon_count:]
    field_out, middle, last, f_scr, pot, edge, d_scr, near = rest
    layers, rows, _ = field_out.shape
    steps = u_ref.shape[0]
    tall = rows + 2 * SHALLOW
    share = layers // lon_count
    spread = share // steps
    chunk = LANES // share
    lane = iota((SUB, LANES), 1)
    for s in range(lon_count):
        source = lax.rem(index_ref[1] + (lon_count - s), lon_count)
        for k in range(share):
            at = pl.ds(source * spread + k // steps, tall, stride=SUB)
            pot[k % steps, at, :] = parts[s][k * tall : (k + 1) * tall, :]
        packed = parts[s][share * tall :, :]
        for e in range(spread):
            at = pl.ds(source * spread + e, tall, stride=SUB)
            edge[at, :] = roll(packed, LANES - e * steps * chunk, 1)

    def force(row, carry):
        at, deep = tile(row), tile(row + DEEP - SHALLOW)
        ends = edge[at, :]
        for t in range(steps):
            after = roll(ends, LANES - t * chunk, 1)
            before = roll(ends, LANES - (t + 1) * chunk, 1)
            potential = (pot[t, at, :], jnp.where(lane < DEEP, after, before))
            for c in range(2):
                value = potential[c]
                if t == 0:
                    value = value + load_ref[0, c, deep, :]
                f_scr[t, c, at, :] = b_ref[t, c, deep, :] * value
        return carry

    lax.fori_loop(0, tall, force, 0, unroll=8)
    lon_neighbours(near)
    run_sweeps(u_ref, DEEP - SHALLOW, a_ref, f_scr, (middle, last), near)
    for k in range(layers):
        field_out[k] = layer_of(last, k, SHALLOW, rows)
    put_density(mat_ref, contrast_ref, lambda k: field_out[k], index_ref, d_scr, pieces)


def swap_chunks(blocks, chunk):
    blocks = list(blocks)
    lane = iota(blocks[0].shape, 1)
    step = 1
    while step < len(blocks):
        upper = (lane // (chunk * step)) % 2 == 1
        for i in range(len(blocks)):
            if i & step:
                continue
            a, b = blocks[i], blocks[i + step]
            blocks[i] = jnp.where(upper, roll(b, chunk * step, 1), a)
            blocks[i + step] = jnp.where(upper, b, roll(a, LANES - chunk * step, 1))
        step *= 2
    return blocks


def forward_kernel(lon_count, scale, index_ref, weight_ref, high_ref, low_ref, *rest):
    parts, (o_ref,) = rest[:lon_count], rest[lon_count:]
    share, rows, cols = parts[0].shape
    chunk = LANES // share
    product = None
    for s in range(lon_count):
        source = lax.rem(index_ref[1] + (lon_count - s), lon_count)
        at = pl.ds(pl.multiple_of(source * cols, cols), cols)
        term = dot3(
            halves(parts[s][...].reshape(share * rows, cols)), (high_ref[at, :], low_ref[at, :]), NN
        )
        product = term if product is None else product + term
    weight = weight_ref[...] * scale
    for g in range(product.shape[1] // LANES):
        blocks = swap_chunks(
            [
                product[k * rows : (k + 1) * rows, g * LANES : (g + 1) * LANES] * weight
                for k in range(share)
            ],
            chunk,
        )
        for i in range(share):
            o_ref[g * share + i] = blocks[i]


def spectral_kernel(margin, high_ref, low_ref, green_ref, x_ref, o_ref, turned, coeffs, pots):
    share, degrees, width = high_ref.shape
    lat_count, lon_count, rows, _ = x_ref.shape
    total_lat = lat_count * rows
    size = 2 * share
    layers = turned.shape[1] // size
    pad = jnp.zeros((width - total_lat, LANES), jnp.float32)
    for q in range(lon_count):
        x = x_ref[:, q].reshape(total_lat, LANES)
        x = jnp.concatenate([x, pad], axis=0)
        for c in range(width // LANES):
            turned[c, q * LANES : (q + 1) * LANES, :] = x[c * LANES : (c + 1) * LANES].T
    for m in range(share):
        x = halves(every(turned, m, share, 2 * layers))
        put_every(coeffs, m, share, dot3(x, (high_ref[m], low_ref[m]), NT))
    block = 4

    def targets(i, carry):
        for c in range(degrees // LANES):
            sums = [jnp.zeros((size, LANES), jnp.float32) for _ in range(block)]
            for k in range(0, layers, 8):
                part = [
                    green_ref[
                        pl.ds(pl.multiple_of((i * block + t) * layers + k, 8), 8),
                        c * LANES : (c + 1) * LANES,
                    ]
                    for t in range(block)
                ]
                for e in range(8):
                    x = coeffs[c, (k + e) * size : (k + e + 1) * size, :]
                    for t in range(block):
                        sums[t] = sums[t] + part[t][e : e + 1] * x
            for t in range(block):
                pots[c, pl.ds(pl.multiple_of((i * block + t) * size, size), size), :] = sums[t]
        return carry

    lax.fori_loop(0, layers // block, targets, 0)
    for m in range(share):
        x = halves(every(pots, m, share, 2 * layers))
        put_every(turned, m, share, dot3(x, (high_ref[m], low_ref[m]), NN))
    for q in range(lon_count):
        x = [turned[c, q * LANES : (q + 1) * LANES, :].T for c in range(width // LANES)]
        x = jnp.concatenate(x, axis=0)[:total_lat]
        if margin > 0:
            edge = jnp.zeros((margin, LANES), jnp.float32)
            x = jnp.concatenate([edge, x, edge], axis=0)
        for i in range(lat_count):
            o_ref[i, q] = x[i * rows : (i + 1) * rows + 2 * margin]


def inverse_kernel(lon_count, margin, index_ref, high_ref, low_ref, x_ref, *rest):
    pieces, (columns,) = rest[:lon_count], rest[lon_count:]
    owners, rows, _ = x_ref.shape
    cols = high_ref.shape[0] // lon_count
    share = columns.shape[1] // rows
    chunk = LANES // share
    groups = [
        swap_chunks([x_ref[g * share + i] for i in range(share)], chunk)
        for g in range(owners // share)
    ]
    terms = jnp.concatenate(
        [jnp.concatenate([group[k] for group in groups], axis=1) for k in range(share)], axis=0
    )
    terms = halves(terms)
    for q in range(lon_count):
        at = slice(q * cols, (q + 1) * cols)
        columns[q] = dot3(terms, (high_ref[at, :], low_ref[at, :]), NT)
    lane = iota((rows, LANES), 1)
    for s in range(lon_count):
        dest = lax.rem(index_ref[1] + s, lon_count)
        pieces[s][0 : share * rows] = columns[dest]
        if margin == 0:
            continue
        after = lax.rem(dest + 1, lon_count)
        before = lax.rem(dest + lon_count - 1, lon_count)
        packed = jnp.zeros((rows, LANES), jnp.float32)
        for k in range(share):
            right = roll(columns[after, k * rows : (k + 1) * rows, :], k * chunk, 1)
            left = roll(columns[before, k * rows : (k + 1) * rows, :], (k + 1) * chunk, 1)
            packed = jnp.where(
                lane // DEEP == 2 * k, right, jnp.where(lane // DEEP == 2 * k + 1, left, packed)
            )
        pieces[s][share * rows :] = packed


def assemble_kernel(lon_count, index_ref, *rest):
    parts, o_hbm, sem = rest[:lon_count], rest[lon_count], rest[lon_count + 1]
    sources = [lax.rem(index_ref[1] + (lon_count - s), lon_count) for s in range(lon_count)]
    copy_all(sem, *((part, o_hbm.at[source]) for part, source in zip(parts, sources)))


def exchange(pieces):
    count = len(pieces)
    return [pieces[0]] + [
        lax.ppermute(pieces[s], "lon", [(i, (i + s) % count) for i in range(count)])
        for s in range(1, count)
    ]


def on_device(displacement, materials, ice_mask, ice_height, shear, restoring, contrast, green):
    layers, rows, cols = displacement.shape
    lat_count, lon_count = lax.axis_size("lat"), lax.axis_size("lon")
    total_lat, total_lon = rows * lat_count, cols * lon_count
    owners = lat_count * lon_count
    share, orders = layers // lon_count, LMAX // owners
    width = -(-total_lat // LANES) * LANES
    tall = rows + 2 * SHALLOW
    lat_index = lax.axis_index("lat")
    index = jnp.stack([lat_index, lax.axis_index("lon")]).astype(jnp.int32)
    owner = (index[0] * lon_count + index[1])[None]

    surface = ice_mask.astype(jnp.float32) * ice_height
    own = (
        displacement.reshape(layers * rows, cols),
        materials.reshape(layers * rows, cols),
        surface,
    )
    first, last = call(
        slab_kernel,
        (f32(2 * layers + 1, DEEP, cols),) * 2,
        1.0,
    )(displacement, materials, surface)
    green, first, last = lax.optimization_barrier((green, first, last))
    first, last = (x.reshape(-1, cols) for x in (first, last))
    above = lax.ppermute(last, "lat", [(i, i + 1) for i in range(lat_count - 1)])
    below = lax.ppermute(first, "lat", [(i + 1, i) for i in range(lat_count - 1)])
    table = call(
        functools.partial(fourier_kernel, total_lon, orders),
        (jax.ShapeDtypeStruct((total_lon, 2 * LMAX), HALF),) * 2,
        1.2,
    )()
    def partner(x, step):
        return lax.ppermute(x, "lat", [(i, i ^ step) for i in range(lat_count)])

    near = green.reshape(green.shape[0], layers * layers)
    near, table = lax.optimization_barrier((near, table))
    others = [partner(near, i) for i in range(2, lat_count, 2)]
    half_table = (orders, LMAX, width)
    legendre_table = call(
        functools.partial(legendre_kernel, total_lat, orders),
        (jax.ShapeDtypeStruct(half_table, HALF),) * 2,
        2.9,
        scratch=[
            pltpu.VMEM((width // LANES, LMAX * orders, LANES), jnp.float32),
            pltpu.VMEM(half_table, HALF),
            pltpu.VMEM(half_table, HALF),
            pltpu.SemaphoreType.DMA((2,)),
        ],
        smem=(0,),
        hbm=(0, 1),
    )(owner)
    above, below, others, table, legendre_table = lax.optimization_barrier(
        (above, below, others, table, legendre_table)
    )
    near = jnp.concatenate([near, *others], axis=0)
    far = partner(near, 1)
    first, last = call(pack_kernel, (f32((rows + 2 * DEEP) * SUB, cols),) * 2, 1.5)(
        *own, above, below
    )
    left = lax.ppermute(last, "lon", [(i, (i + 1) % lon_count) for i in range(lon_count)])
    right = lax.ppermute(first, "lon", [((i + 1) % lon_count, i) for i in range(lon_count)])
    theta = ((lat_index * rows + jnp.arange(rows)).astype(jnp.float32) + 0.5) * (
        jnp.pi / total_lat
    )
    weight = jnp.broadcast_to((jnp.sin(theta) / (4.0 * total_lat))[:, None], (rows, LANES))

    steps = layers // SUB

    def worked(t, height):
        return (t, 2, height * SUB, LANES)

    deep = rows + 2 * DEEP
    flat = pltpu.VMEM((lon_count, share, rows, cols), jnp.float32)
    near_shape = pltpu.VMEM((2 * LANES, 2 * LANES), HALF)
    out = call(
        functools.partial(first_sweeps_kernel, lon_count, total_lat),
        (f32(share, rows, cols),) * lon_count
        + (f32(*worked(steps, deep)),) * 3
        + (f32(*worked(1, deep)),),
        6.6,
        scratch=[pltpu.VMEM(worked(steps, deep), jnp.float32)] * 5
        + [pltpu.VMEM(worked(1, deep), jnp.float32)] * 2
        + [flat, near_shape, pltpu.SemaphoreType.DMA((4,))],
        smem=(0, 1, 2, 3),
        hbm=range(lon_count, lon_count + 4),
    )(index, shear, restoring, contrast, *own, above, below, left, right)
    pieces, state = out[:lon_count], out[lon_count:]
    for iteration in range(ITERS):
        margin = SHALLOW if iteration < ITERS - 1 else 0
        parts = exchange(pieces)
        if iteration == 0:
            turned_green = call(
                functools.partial(turn_kernel, green.shape[0]),
                f32(layers * layers, LMAX),
                1.4,
                scratch=[pltpu.VMEM((LMAX, layers * layers), jnp.float32)],
                smem=(0,),
            )(index, near, far)
            parts, turned_green = lax.optimization_barrier((parts, turned_green))
        spectrum = call(
            functools.partial(forward_kernel, lon_count, 2.0 * math.pi / total_lon),
            f32(owners, rows, LANES),
            2.0,
            smem=(0,),
        )(index, weight, *table, *parts)
        spectrum = lax.all_to_all(spectrum, BOTH, 0, 0, tiled=True)
        square = pltpu.VMEM((width // LANES, lon_count * LANES, LANES), jnp.float32)
        coeff_shape = pltpu.VMEM((LMAX // LANES, lon_count * LANES, LANES), jnp.float32)
        synth = call(
            functools.partial(spectral_kernel, margin),
            f32(lat_count, lon_count, rows + 2 * margin, LANES),
            4.0,
            scratch=[square, coeff_shape, coeff_shape],
        )(
            *legendre_table,
            turned_green,
            spectrum.reshape(lat_count, lon_count, rows, LANES),
        )
        synth = lax.all_to_all(
            synth.reshape(owners, rows + 2 * margin, LANES), BOTH, 0, 0, tiled=True
        )
        high = rows + 2 * margin
        sent = share * high + (high if margin > 0 else 0)
        parts = call(
            functools.partial(inverse_kernel, lon_count, margin),
            (f32(sent, cols),) * lon_count,
            2.0,
            scratch=[pltpu.VMEM((lon_count, share * high, cols), jnp.float32)],
            smem=(0,),
        )(index, *table, synth)
        parts = exchange(parts)
        if iteration < ITERS - 1:
            out = call(
                functools.partial(second_sweeps_kernel, lon_count),
                (f32(share, rows, cols),) * lon_count + (f32(layers, rows, cols),),
                5.4,
                scratch=[pltpu.VMEM(worked(steps, tall), jnp.float32)] * 3
                + [
                    pltpu.VMEM((steps, tall * SUB, LANES), jnp.float32),
                    pltpu.VMEM((tall * SUB, LANES), jnp.float32),
                    flat,
                    near_shape,
                ],
                smem=(0, 1),
            )(index, contrast, own[1], *state, *parts)
            pieces, field = out[:lon_count], out[lon_count]
    potential = call(
        functools.partial(assemble_kernel, lon_count),
        f32(lon_count, share * rows, cols),
        1.0,
        scratch=[pltpu.SemaphoreType.DMA((lon_count,))],
        smem=(0,),
        hbm=(0,),
    )(index, *parts)
    return (field, potential.reshape(layers, rows, cols))


def aligned(mesh, displacement):
    lat_count, lon_count = mesh.shape["lat"], mesh.shape["lon"]
    layers, total_lat, total_lon = displacement.shape
    rows, cols = total_lat // lat_count, total_lon // lon_count
    owners = lat_count * lon_count
    return (
        ITERS == 2
        and cols == LANES
        and rows % 8 == 0
        and layers % SUB == 0
        and (2 * (layers // SUB) + 1) * DEEP <= LANES
        and (layers // lon_count) % (layers // SUB) == 0
        and lat_count > 2
        and lat_count & (lat_count - 1) == 0
        and layers % lon_count == 0
        and LMAX % owners == 0
        and 2 * (LMAX // owners) * (layers // lon_count) == LANES
        and 2 * (LMAX // owners) == 2 * DEEP
        and LMAX % LANES == 0
    )


def solution(mesh):
    in_specs = (
        P(None, "lat", "lon"),
        P(None, "lat", "lon"),
        P("lat", "lon"),
        P("lat", "lon"),
        P(),
        P(),
        P(),
        P("lat", None, None),
    )
    out_specs = (P(None, "lat", "lon"), P(None, "lat", "lon"))

    def step(displacement, *others):
        device = on_device if aligned(mesh, displacement) else general_device
        return jax.shard_map(
            device, mesh=mesh, in_specs=in_specs, out_specs=out_specs, check_vma=False
        )(displacement, *others)

    return step
```

```python
import functools
import math

import jax
import jax.numpy as jnp
from jax import lax
from jax.experimental import pallas as pl
from jax.experimental.pallas import tpu as pltpu
from jax.sharding import PartitionSpec as P

LMAX = 256
NMAT = 4
ITERS = 2
SWEEPS = 4
LANES = 128
DEEP = 8
SHALLOW = 4
HALF = jnp.bfloat16
VMEM_LIMIT = 16 * 1024 * 1024
BOTH = ("lat", "lon")


def extended(cells, sides, width, closed):
    for axis, dim in sides:
        count = lax.axis_size(axis)
        ends = count if closed else count - 1
        head = lax.slice_in_dim(cells, 0, width, axis=dim)
        tail = lax.slice_in_dim(cells, cells.shape[dim] - width, cells.shape[dim], axis=dim)
        cells = jnp.concatenate(
            [
                lax.ppermute(tail, axis, [(i, (i + 1) % count) for i in range(ends)]),
                cells,
                lax.ppermute(head, axis, [((i + 1) % count, i) for i in range(ends)]),
            ],
            axis=dim,
        )
    return cells


def legendre(theta):
    orders = jnp.arange(LMAX)
    order_f = orders.astype(jnp.float32)
    cosine = jnp.cos(theta)[:, None]
    sine = jnp.sin(theta)[:, None]
    safe = jnp.maximum(order_f, 1.0)
    growth = jnp.where(orders >= 2, 0.5 * jnp.log((2.0 * safe + 1.0) / (2.0 * safe)), 0.0)
    log_diag = jnp.where(orders >= 1, 0.5 * jnp.log(3.0) + jnp.cumsum(growth), 0.0)
    diagonal = jnp.exp(log_diag[None, :] + order_f[None, :] * jnp.log(sine))

    def advance(carry, degree):
        prev_one, prev_two = carry
        deg_f = degree.astype(jnp.float32)
        first = jnp.sqrt(
            (4.0 * deg_f * deg_f - 1.0) / jnp.maximum(deg_f * deg_f - order_f * order_f, 1.0)
        )
        second = jnp.sqrt(
            jnp.maximum((deg_f - 1.0) ** 2 - order_f * order_f, 0.0)
            / jnp.maximum(4.0 * (deg_f - 1.0) ** 2 - 1.0, 1.0)
        )
        general = first * (cosine * prev_one - second * prev_two)
        start_next = jnp.sqrt(2.0 * order_f + 3.0) * cosine * diagonal
        value = jnp.where(
            orders == degree,
            diagonal,
            jnp.where(
                orders == degree - 1, start_next, jnp.where(orders < degree - 1, general, 0.0)
            ),
        )
        return ((value, prev_one), value)

    zeros = jnp.zeros((theta.shape[0], LMAX), jnp.float32)
    _, table = lax.scan(advance, (zeros, zeros), jnp.arange(LMAX), unroll=8)
    return table


def fourier_tables(columns, total):
    orders = jnp.arange(LMAX)
    phase = columns[:, None] * orders[None, :] % total
    angle = 2.0 * jnp.pi / total * phase.astype(jnp.float32)
    forward = jnp.concatenate([jnp.cos(angle), jnp.sin(angle)], axis=1) * (2.0 * jnp.pi / total)
    inverse = jnp.concatenate([jnp.cos(angle), jnp.sin(angle)], axis=1).T
    return (forward, inverse)


def lookup(materials, table):
    result = jnp.zeros(materials.shape, jnp.float32)
    for material in range(NMAT):
        result = result + jnp.where(materials == material, table[material], 0.0)
    return result


def crop_block(block, margin):
    return block[:, margin : block.shape[1] - margin, margin : block.shape[2] - margin]


def margin_sweeps(field, force, stiff, restore, depth, lat_first, total_lat):
    stacked = jnp.stack([field, force, stiff, restore], axis=0)
    lat_wide = extended(stacked, (("lat", 2),), depth, False)
    wide = extended(lat_wide, (("lon", 3),), depth, True)
    current = wide[0]
    rows_wide = wide.shape[2]
    global_rows = lat_first - depth + jnp.arange(rows_wide)
    inside = ((global_rows >= 0) & (global_rows < total_lat))[None, :, None]
    for step in range(depth):
        margin = step + 1
        inner = current[:, 1:-1, 1:-1]
        beside_all = (
            current[:, 2:, 1:-1]
            + current[:, :-2, 1:-1]
            + current[:, 1:-1, 2:]
            + current[:, 1:-1, :-2]
        )
        layer_pad = jnp.pad(inner, ((1, 1), (0, 0), (0, 0)))
        beside_all = beside_all + layer_pad[2:] + layer_pad[:-2]
        force_part = crop_block(wide[1], margin)
        stiff_part = crop_block(wide[2], margin)
        restore_part = crop_block(wide[3], margin)
        valid = inside[:, margin : rows_wide - margin, :]
        denominator = jnp.where(valid, 6.0 * stiff_part + restore_part, 1.0)
        current = jnp.where(valid, (force_part + stiff_part * beside_all) / denominator, 0.0)
    return current


def general_device(displacement, materials, ice_mask, ice_height, shear, restoring, contrast, green):
    highest = lax.Precision.HIGHEST
    layers, lat_rows, lon_cols = displacement.shape
    lon_count = lax.axis_size("lon")
    lat_count = lax.axis_size("lat")
    total_lat = lat_rows * lat_count
    total_lon = lon_cols * lon_count
    layer_share = layers // lon_count
    stiff = lookup(materials, shear)
    restore = lookup(materials, restoring)
    rho_scale = lookup(materials, contrast)
    surface = (ice_mask.astype(jnp.float32) * ice_height)[None]
    load = jnp.concatenate(
        [surface, jnp.zeros((layers - 1, lat_rows, lon_cols), jnp.float32)], axis=0
    )
    lat_first = lax.axis_index("lat") * lat_rows
    theta = ((lat_first + jnp.arange(lat_rows)).astype(jnp.float32) + 0.5) * (jnp.pi / total_lat)
    table = legendre(theta)
    weights = jnp.sin(theta) / (4.0 * total_lat)
    own_columns = lax.axis_index("lon") * lon_cols + jnp.arange(lon_cols)
    layer_first = lax.axis_index("lon") * layer_share
    depth = 1
    for candidate in range(1, SWEEPS + 1):
        if SWEEPS % candidate == 0 and candidate <= min(lat_rows, lon_cols):
            depth = candidate
    forward, inverse = fourier_tables(own_columns, total_lon)
    field = displacement
    potential = jnp.zeros((layers, lat_rows, lon_cols), jnp.float32)
    for iteration in range(ITERS):
        force = load + potential
        field = margin_sweeps(field, force, stiff, restore, depth, lat_first, total_lat)
        density = rho_scale * field
        product = jnp.dot(
            density.reshape(layer_share * lax.axis_size("lon") * lat_rows, lon_cols),
            forward,
            precision=highest,
            preferred_element_type=jnp.float32,
        )
        spectrum = lax.psum_scatter(
            product.reshape(layer_share * lax.axis_size("lon"), lat_rows, 2 * LMAX),
            "lon",
            scatter_dimension=0,
            tiled=True,
        )
        weighted = spectrum.reshape(layer_share, lat_rows, 2, LMAX) * weights[None, :, None, None]
        coeffs = lax.psum_scatter(
            jnp.einsum("lam,kacm->lkcm", table, weighted, precision=highest),
            "lat",
            scatter_dimension=0,
            tiled=True,
        )
        green_part = lax.dynamic_slice_in_dim(green, layer_first, layer_share, 2)
        partial_pot = jnp.einsum("lkj,ljcm->lkcm", green_part, coeffs, precision=highest)
        pot_coeffs = lax.psum_scatter(partial_pot, "lon", scatter_dimension=1, tiled=True)
        synth = jnp.einsum(
            "lam,lkcm->kacm",
            table,
            lax.all_gather(pot_coeffs, "lat", axis=0, tiled=True),
            precision=highest,
        )
        synth = synth.reshape(layer_share, lat_rows, 2 * LMAX)
        piece = lax.all_gather(synth, "lon", axis=0, tiled=True)
        synth_product = jnp.dot(
            piece.reshape(piece.shape[0] * lat_rows, 2 * LMAX),
            inverse,
            precision=highest,
            preferred_element_type=jnp.float32,
        )
        potential = synth_product.reshape(piece.shape[0], lat_rows, lon_cols)
    return (field, potential)


def call(kernel, outs, micros, scratch=(), smem=(), far=(), hbm=()):
    def place(i, scalars, away):
        space = pltpu.SMEM if i in scalars else pltpu.HBM if i in away else pltpu.VMEM
        return pl.BlockSpec(memory_space=space)

    def run(*args):
        return pl.pallas_call(
            kernel,
            out_shape=outs,
            in_specs=[place(i, smem, far) for i in range(len(args))],
            out_specs=tuple(place(i, (), hbm) for i in range(len(outs)))
            if type(outs) is tuple
            else place(0, (), hbm),
            scratch_shapes=list(scratch),
            compiler_params=pltpu.CompilerParams(vmem_limit_bytes=VMEM_LIMIT),
            cost_estimate=pl.CostEstimate(
                flops=int(micros * 1e9), bytes_accessed=1, transcendentals=0
            ),
        )(*args)

    return run


def copy_all(sem, *pairs):
    copies = [pltpu.make_async_copy(*pair, sem.at[i]) for i, pair in enumerate(pairs)]
    for copy in copies:
        copy.start()
    for copy in copies:
        copy.wait()


def f32(*shape):
    return jax.ShapeDtypeStruct(shape, jnp.float32)


def halves(x):
    high = x.astype(HALF)
    return high, (x - high.astype(jnp.float32)).astype(HALF)


def dot(a, b, dims):
    return lax.dot_general(a, b, (dims, ((), ())), preferred_element_type=jnp.float32)


def dot3(a, b, dims):
    rows = a[0].shape[0]
    both = dot(jnp.concatenate(a, axis=0), b[0], dims)
    return both[:rows] + (both[rows:] + dot(a[0], b[1], dims))


def every(ref, start, stride, count):
    at = pl.ds(start, count, stride=stride)
    return jnp.concatenate([ref[c, at, :] for c in range(ref.shape[0])], axis=1)


def put_every(ref, start, stride, value):
    at = pl.ds(start, value.shape[0], stride=stride)
    for c in range(ref.shape[0]):
        ref[c, at, :] = value[:, c * LANES : (c + 1) * LANES]


NN = ((1,), (0,))
NT = ((1,), (1,))


def iota(shape, dim):
    return lax.broadcasted_iota(jnp.int32, shape, dim)


def fourier_kernel(total, share, high_ref, low_ref):
    shape = (16, 2 * LMAX)
    column = iota(shape, 1)
    order = column // (2 * share) * share + column % share
    shift = (column // share) % 2 * (total - total // 4)
    first = iota(shape, 0) * order + shift
    quarter, half = total // 4, total // 2

    def block(i, carry):
        phase = first + order * (i * shape[0])
        phase = phase & (total - 1) if total & (total - 1) == 0 else lax.rem(phase, total)
        near = jnp.minimum(phase, total - phase)
        beyond = near > quarter
        angle = jnp.where(beyond, half - near, near).astype(jnp.float32) * (2.0 * math.pi / total)
        square = angle * angle
        value = jnp.full(shape, 1.0 / math.factorial(14), jnp.float32)
        for n in range(12, -1, -2):
            value = 1.0 / math.factorial(n) - square * value
        high, low = halves(jnp.where(beyond, -value, value))
        at = pl.ds(pl.multiple_of(i * shape[0], shape[0]), shape[0])
        high_ref[at, :] = high
        low_ref[at, :] = low
        return carry

    lax.fori_loop(0, total // shape[0], block, 0, unroll=2)


def legendre_kernel(total_lat, share, index_ref, high_ref, low_ref, table):
    width = table.shape[0] * LANES
    base = index_ref[0] * share
    shape = (share, width)
    order = iota(shape, 0) + base
    order_f = order.astype(jnp.float32)
    row = iota(shape, 1)
    theta = (row.astype(jnp.float32) + 0.5) * (math.pi / total_lat)
    cosine = jnp.cos(theta)
    sine = jnp.where(row < total_lat, jnp.sin(theta), 1.0)
    terms = (share, LMAX)
    term = iota(terms, 1)
    term_f = jnp.maximum(term.astype(jnp.float32), 1.0)
    growth = 0.5 * jnp.log((2.0 * term_f + 1.0) / (2.0 * term_f))
    used = (term >= 2) & (term <= iota(terms, 0) + base)
    total = jnp.sum(jnp.where(used, growth, 0.0), axis=1, keepdims=True)
    log_diag = jnp.where(order >= 1, 0.5 * math.log(3.0) + total, 0.0)
    diagonal = jnp.exp(log_diag + order_f * jnp.log(sine))
    diagonal = jnp.where(row < total_lat, diagonal, 0.0)
    start_next = jnp.sqrt(2.0 * order_f + 3.0) * cosine * diagonal
    narrow = (share, LANES)
    square = ((iota(narrow, 0) + base).astype(jnp.float32)) ** 2

    def wide(x):
        return jnp.concatenate([x] * (width // LANES), axis=1)

    def advance(degree, carry):
        prev_one, prev_two = carry
        deg = jnp.full(narrow, degree, jnp.int32).astype(jnp.float32)
        first = jnp.sqrt((4.0 * deg * deg - 1.0) / jnp.maximum(deg * deg - square, 1.0))
        below = (deg - 1.0) * (deg - 1.0)
        second = jnp.sqrt(jnp.maximum(below - square, 0.0) / jnp.maximum(4.0 * below - 1.0, 1.0))
        general = wide(first) * (cosine * prev_one - wide(second) * prev_two)
        value = jnp.where(
            order == degree,
            diagonal,
            jnp.where(
                order == degree - 1, start_next, jnp.where(order < degree - 1, general, 0.0)
            ),
        )
        for c in range(width // LANES):
            at = pl.ds(pl.multiple_of(degree * share, share), share)
            table[c, at, :] = value[:, c * LANES : (c + 1) * LANES]
        return (value, prev_one)

    table[:, 0:share, :] = jnp.zeros((width // LANES, share, LANES), jnp.float32)
    zeros = jnp.concatenate([table[c, 0:share, :] for c in range(width // LANES)], axis=1)
    lax.fori_loop(0, LMAX, advance, (zeros, zeros), unroll=8)
    for m in range(share):
        high, low = halves(every(table, m, share, LMAX))
        high_ref[m] = high
        low_ref[m] = low


def turn_kernel(size, index_ref, near_ref, far_ref, o_ref, ordered):
    count = 2 * near_ref.shape[0] // size
    for i in range(count):
        partner = 2 * i if 2 * i < count else 2 * i - count + 1
        block = near_ref if 2 * i < count else far_ref
        first = i % (count // 2) * size
        at = pl.ds(pl.multiple_of((index_ref[0] ^ partner) * size, size), size)
        ordered[at, :] = block[first : first + size, :]
    for c in range(o_ref.shape[0]):
        o_ref[c] = ordered[c * LANES : (c + 1) * LANES, :].T


def slab_kernel(u_ref, mat_ref, surface_ref, first_ref, last_ref):
    layers, rows, _ = u_ref.shape
    for ref, at in ((first_ref, pl.ds(0, DEEP)), (last_ref, pl.ds(rows - DEEP, DEEP))):
        for k in range(layers):
            ref[k] = u_ref[k, at, :]
            ref[layers + k] = mat_ref[k, at, :].astype(jnp.float32)
        ref[2 * layers] = surface_ref[at, :]


SUB = 8
PARTS = 2
UNROLL = True


def roll(x, shift, axis):
    shift = shift % x.shape[axis]
    return x if shift == 0 else pltpu.roll(x, shift, axis)


def pick(material, table):
    value = jnp.full(material.shape, table[NMAT - 1], jnp.float32)
    for i in range(NMAT - 1):
        value = jnp.where(material == i, table[i], value)
    return value


def tile(row):
    return pl.ds(pl.multiple_of(row * SUB, SUB), SUB)


def by_layer(ref, rows, first, t, steps, row):
    return ref[pl.ds((first + t) * rows + row, SUB, stride=steps * rows), :].astype(jnp.float32)


def for_rows(rows, own, above, below, body):
    u_ref, mat_ref, surface_ref = own
    steps = u_ref.shape[0] // rows // SUB
    layers = SUB * steps

    def margin(ref, offset):
        def one(i, carry):
            body(
                i + offset,
                lambda t: by_layer(ref, DEEP, 0, t, steps, i),
                lambda t: by_layer(ref, DEEP, layers, t, steps, i),
                ref[pl.ds(2 * layers * DEEP + i, 1), :],
            )
            return carry

        lax.fori_loop(0, DEEP, one, 0, unroll=8)

    def inner(i, carry):
        body(
            i + DEEP,
            lambda t: by_layer(u_ref, rows, 0, t, steps, i),
            lambda t: by_layer(mat_ref, rows, 0, t, steps, i),
            surface_ref[pl.ds(i, 1), :],
        )
        return carry

    margin(above, 0)
    lax.fori_loop(0, rows, inner, 0, unroll=8)
    margin(below, rows + DEEP)


def pack_kernel(
    u_ref, mat_ref, surface_ref, above_ref, below_ref, first_ref, last_ref
):
    rows = surface_ref.shape[0]
    steps = u_ref.shape[0] // rows // SUB
    slot = iota((SUB, LANES), 1) // DEEP

    def body(row, u, mat, load):
        first = jnp.zeros((SUB, LANES), jnp.float32)
        last = first
        fields = [u(t) for t in range(steps)] + [mat(t) for t in range(steps)]
        fields.append(jnp.broadcast_to(load, (SUB, LANES)))
        for i, x in enumerate(fields):
            first = jnp.where(slot == i, roll(x, i * DEEP, 1), first)
            last = jnp.where(slot == i, roll(x, (i + 1) * DEEP, 1), last)
        first_ref[tile(row), :] = first
        last_ref[tile(row), :] = last

    for_rows(rows, (u_ref, mat_ref, surface_ref), above_ref, below_ref, body)


def lon_neighbours(near):
    width = near.shape[0]
    apart = iota(near.shape, 0) - iota(near.shape, 1)
    apart = jnp.where(apart < 0, apart + width, apart)
    near[...] = ((apart == 1) | (apart == width - 1)).astype(jnp.float32).astype(HALF)


def run_sweeps(src, offset, a_ref, f_ref, two, near):
    steps = a_ref.shape[0]
    rows = a_ref.shape[2] // SUB - 2 * offset
    for sweep in range(SWEEPS):
        dst = two[sweep % 2]
        shift = offset if sweep == 0 else 0
        size = (rows - 2 - 2 * sweep) // PARTS

        def block(i, carry, src=src, dst=dst, shift=shift, size=size, sweep=sweep):
            first = sweep + 1 + i * size

            def at(row):
                return pl.ds(pl.multiple_of(row * SUB, SUB), size * SUB)

            def tiles(t, c, move):
                return src[t, c, at(first + shift + move), :].reshape(size, SUB, LANES)

            sub = iota((size, SUB, LANES), 1)
            x = [[tiles(t, c, 0) for c in range(2)] for t in range(steps)]
            for t in range(steps):
                both = jnp.concatenate([x[t][c].reshape(size * SUB, LANES) for c in range(2)], axis=1)
                high, low = halves(both)
                beside = dot(high, near[...], NN) + dot(low, near[...], NN)
                for c in range(2):
                    total = beside[:, c * LANES : (c + 1) * LANES].reshape(size, SUB, LANES)
                    total = total + (tiles(t, c, -1) + tiles(t, c, 1))
                    if t > 0:
                        under = x[t - 1][c]
                    else:
                        under = jnp.where(sub == 0, 0.0, roll(x[steps - 1][c], 1, 1))
                    if t < steps - 1:
                        over = x[t + 1][c]
                    else:
                        over = jnp.where(sub == SUB - 1, 0.0, roll(x[0][c], SUB - 1, 1))
                    total = (total + (under + over)).reshape(size * SUB, LANES)
                    value = a_ref[t, c, at(first + offset), :] * total
                    if t < f_ref.shape[0]:
                        value = value + f_ref[t, c, at(first), :]
                    dst[t, c, at(first), :] = value
            return carry

        lax.fori_loop(0, PARTS, block, 0, unroll=UNROLL)
        src = dst


def put_density(mat_ref, contrast, field, index_ref, scratch, pieces):
    lon_count = len(pieces)
    share, rows, _ = pieces[0].shape
    for k in range(lon_count * share):
        material = mat_ref[k * rows : (k + 1) * rows, :]
        scratch[k // share, k % share] = pick(material, contrast) * field(k)
    for s in range(lon_count):
        pieces[s][...] = scratch[lax.rem(index_ref[1] + s, lon_count)]


def layer_of(ref, k, margin, rows):
    steps = ref.shape[0]
    return ref[k % steps, 0, pl.ds(margin * SUB + k // steps, rows, stride=SUB), :]


def first_sweeps_kernel(
    lon_count, total_lat, index_ref, shear_ref, restoring_ref, contrast_ref, u_ref, mat_ref,
    surface_ref, above_ref, below_ref, left_ref, right_ref, *rest,
):
    pieces, rest = rest[:lon_count], rest[lon_count:]
    u_out, a_out, b_out, load_out, first, middle, f_scr, d_scr, near = rest
    rows = surface_ref.shape[0]
    steps = u_out.shape[0]
    a_of, b_of = [], []
    for i in range(NMAT):
        stiff = jnp.full((SUB, LANES), shear_ref[i], jnp.float32)
        restore = jnp.full((SUB, LANES), restoring_ref[i], jnp.float32)
        b_of.append(1.0 / (6.0 * stiff + restore))
        a_of.append(stiff * b_of[i])
    lane = iota((SUB, LANES), 1)
    sub = iota((SUB, LANES), 0)

    def body(row, u, mat, load):
        at = tile(row)
        left, right = left_ref[at, :], right_ref[at, :]
        global_row = index_ref[0] * rows - DEEP + row
        inside = ((global_row >= 0) & (global_row < total_lat)).astype(jnp.float32)

        def side(i):
            after = roll(right, LANES - i * DEEP, 1)
            before = roll(left, LANES - (i + 1) * DEEP, 1)
            return jnp.where(lane < DEEP, after, jnp.where(lane >= LANES - DEEP, before, 0.0))

        loads = (jnp.broadcast_to(load, (SUB, LANES)), side(2 * steps))
        for t in range(steps):
            fields = ((u(t), mat(t)), (side(t), side(steps + t)))
            for c in range(2):
                value, material = fields[c]
                first[t, c, at, :] = value
                a_out[t, c, at, :] = pick(material, a_of) * inside
                b = pick(material, b_of) * inside
                b_out[t, c, at, :] = b
                if t == 0:
                    surface = jnp.where(sub == 0, loads[c], 0.0)
                    load_out[0, c, at, :] = surface
                    f_scr[0, c, at, :] = b * surface

    for_rows(rows, (u_ref, mat_ref, surface_ref), above_ref, below_ref, body)
    lon_neighbours(near)
    run_sweeps(first, 0, a_out, f_scr, (middle, u_out), near)
    put_density(
        mat_ref, contrast_ref, lambda k: layer_of(u_out, k, DEEP, rows), index_ref, d_scr, pieces
    )


def second_sweeps_kernel(
    lon_count, index_ref, contrast_ref, mat_ref, u_ref, a_ref, b_ref, load_ref, *rest
):
    parts, rest = rest[:lon_count], rest[lon_count:]
    pieces, rest = rest[:lon_count], rest[lon_count:]
    field_out, middle, last, f_scr, pot, edge, d_scr, near = rest
    layers, rows, _ = field_out.shape
    steps = u_ref.shape[0]
    tall = rows + 2 * SHALLOW
    share = layers // lon_count
    spread = share // steps
    chunk = LANES // share
    lane = iota((SUB, LANES), 1)
    for s in range(lon_count):
        source = lax.rem(index_ref[1] + (lon_count - s), lon_count)
        for k in range(share):
            at = pl.ds(source * spread + k // steps, tall, stride=SUB)
            pot[k % steps, at, :] = parts[s][k * tall : (k + 1) * tall, :]
        packed = parts[s][share * tall :, :]
        for e in range(spread):
            at = pl.ds(source * spread + e, tall, stride=SUB)
            edge[at, :] = roll(packed, LANES - e * steps * chunk, 1)

    def force(row, carry):
        at, deep = tile(row), tile(row + DEEP - SHALLOW)
        ends = edge[at, :]
        for t in range(steps):
            after = roll(ends, LANES - t * chunk, 1)
            before = roll(ends, LANES - (t + 1) * chunk, 1)
            potential = (pot[t, at, :], jnp.where(lane < DEEP, after, before))
            for c in range(2):
                value = potential[c]
                if t == 0:
                    value = value + load_ref[0, c, deep, :]
                f_scr[t, c, at, :] = b_ref[t, c, deep, :] * value
        return carry

    lax.fori_loop(0, tall, force, 0, unroll=8)
    lon_neighbours(near)
    run_sweeps(u_ref, DEEP - SHALLOW, a_ref, f_scr, (middle, last), near)
    for k in range(layers):
        field_out[k] = layer_of(last, k, SHALLOW, rows)
    put_density(mat_ref, contrast_ref, lambda k: field_out[k], index_ref, d_scr, pieces)


def swap_chunks(blocks, chunk):
    blocks = list(blocks)
    lane = iota(blocks[0].shape, 1)
    step = 1
    while step < len(blocks):
        upper = (lane // (chunk * step)) % 2 == 1
        for i in range(len(blocks)):
            if i & step:
                continue
            a, b = blocks[i], blocks[i + step]
            blocks[i] = jnp.where(upper, roll(b, chunk * step, 1), a)
            blocks[i + step] = jnp.where(upper, b, roll(a, LANES - chunk * step, 1))
        step *= 2
    return blocks


def forward_kernel(lon_count, scale, index_ref, weight_ref, high_ref, low_ref, *rest):
    parts, (o_ref,) = rest[:lon_count], rest[lon_count:]
    share, rows, cols = parts[0].shape
    chunk = LANES // share
    product = None
    for pair in zip(range(0, lon_count, 2), range(1, lon_count, 2)):
        x = jnp.concatenate([parts[s][...].reshape(share * rows, cols) for s in pair], axis=1)
        places = []
        for s in pair:
            source = lax.rem(index_ref[1] + (lon_count - s), lon_count)
            places.append(pl.ds(pl.multiple_of(source * cols, cols), cols))
        tables = [
            jnp.concatenate([ref[at, :] for at in places], axis=0) for ref in (high_ref, low_ref)
        ]
        term = dot3(halves(x), tables, NN)
        product = term if product is None else product + term
    weight = weight_ref[...] * scale
    for g in range(product.shape[1] // LANES):
        blocks = swap_chunks(
            [
                product[k * rows : (k + 1) * rows, g * LANES : (g + 1) * LANES] * weight
                for k in range(share)
            ],
            chunk,
        )
        for i in range(share):
            o_ref[g * share + i] = blocks[i]


def spectral_kernel(margin, high_ref, low_ref, green_ref, x_ref, o_ref, turned, coeffs, pots):
    share, degrees, width = high_ref.shape
    lat_count, lon_count, rows, _ = x_ref.shape
    total_lat = lat_count * rows
    size = 2 * share
    layers = turned.shape[1] // size
    pad = jnp.zeros((width - total_lat, LANES), jnp.float32)
    for q in range(lon_count):
        x = x_ref[:, q].reshape(total_lat, LANES)
        x = jnp.concatenate([x, pad], axis=0)
        for c in range(width // LANES):
            turned[c, q * LANES : (q + 1) * LANES, :] = x[c * LANES : (c + 1) * LANES].T
    for m in range(share):
        x = halves(every(turned, m, share, 2 * layers))
        put_every(coeffs, m, share, dot3(x, (high_ref[m], low_ref[m]), NT))
    block = 8

    def targets(i, carry):
        for c in range(degrees // LANES):
            sums = [jnp.zeros((size, LANES), jnp.float32) for _ in range(block)]
            for k in range(layers):
                x = coeffs[c, k * size : (k + 1) * size, :]
                for t in range(block):
                    row = green_ref[c, pl.ds((i * block + t) * layers + k, 1), :]
                    sums[t] = sums[t] + row * x
            for t in range(block):
                pots[c, pl.ds(pl.multiple_of((i * block + t) * size, size), size), :] = sums[t]
        return carry

    lax.fori_loop(0, layers // block, targets, 0)
    for m in range(share):
        x = halves(every(pots, m, share, 2 * layers))
        put_every(turned, m, share, dot3(x, (high_ref[m], low_ref[m]), NN))
    for q in range(lon_count):
        x = [turned[c, q * LANES : (q + 1) * LANES, :].T for c in range(width // LANES)]
        x = jnp.concatenate(x, axis=0)[:total_lat]
        if margin > 0:
            edge = jnp.zeros((margin, LANES), jnp.float32)
            x = jnp.concatenate([edge, x, edge], axis=0)
        for i in range(lat_count):
            o_ref[i, q] = x[i * rows : (i + 1) * rows + 2 * margin]


def inverse_kernel(lon_count, margin, index_ref, high_ref, low_ref, x_ref, *rest):
    pieces, (columns,) = rest[:lon_count], rest[lon_count:]
    owners, rows, _ = x_ref.shape
    cols = high_ref.shape[0] // lon_count
    share = columns.shape[1] // rows
    chunk = LANES // share
    groups = [
        swap_chunks([x_ref[g * share + i] for i in range(share)], chunk)
        for g in range(owners // share)
    ]
    terms = jnp.concatenate(
        [jnp.concatenate([group[k] for group in groups], axis=1) for k in range(share)], axis=0
    )
    terms = halves(terms)
    for q in range(0, lon_count, 2):
        at = slice(q * cols, (q + 2) * cols)
        both = dot3(terms, (high_ref[at, :], low_ref[at, :]), NT)
        columns[q] = both[:, :cols]
        columns[q + 1] = both[:, cols:]
    lane = iota((rows, LANES), 1)
    for s in range(lon_count):
        dest = lax.rem(index_ref[1] + s, lon_count)
        pieces[s][0 : share * rows] = columns[dest]
        if margin == 0:
            continue
        after = lax.rem(dest + 1, lon_count)
        before = lax.rem(dest + lon_count - 1, lon_count)
        packed = jnp.zeros((rows, LANES), jnp.float32)
        for k in range(share):
            right = roll(columns[after, k * rows : (k + 1) * rows, :], k * chunk, 1)
            left = roll(columns[before, k * rows : (k + 1) * rows, :], (k + 1) * chunk, 1)
            packed = jnp.where(
                lane // DEEP == 2 * k, right, jnp.where(lane // DEEP == 2 * k + 1, left, packed)
            )
        pieces[s][share * rows :] = packed


def assemble_kernel(lon_count, index_ref, *rest):
    parts, o_hbm, sem = rest[:lon_count], rest[lon_count], rest[lon_count + 1]
    sources = [lax.rem(index_ref[1] + (lon_count - s), lon_count) for s in range(lon_count)]
    copy_all(sem, *((part, o_hbm.at[source]) for part, source in zip(parts, sources)))


def exchange(pieces):
    count = len(pieces)
    return [pieces[0]] + [
        lax.ppermute(pieces[s], "lon", [(i, (i + s) % count) for i in range(count)])
        for s in range(1, count)
    ]


def on_device(displacement, materials, ice_mask, ice_height, shear, restoring, contrast, green):
    layers, rows, cols = displacement.shape
    lat_count, lon_count = lax.axis_size("lat"), lax.axis_size("lon")
    total_lat, total_lon = rows * lat_count, cols * lon_count
    owners = lat_count * lon_count
    share, orders = layers // lon_count, LMAX // owners
    width = -(-total_lat // LANES) * LANES
    tall = rows + 2 * SHALLOW
    lat_index = lax.axis_index("lat")
    index = jnp.stack([lat_index, lax.axis_index("lon")]).astype(jnp.int32)
    owner = (index[0] * lon_count + index[1])[None]

    surface = ice_mask.astype(jnp.float32) * ice_height
    own = (
        displacement.reshape(layers * rows, cols),
        materials.reshape(layers * rows, cols),
        surface,
    )
    first, last = call(
        slab_kernel,
        (f32(2 * layers + 1, DEEP, cols),) * 2,
        1.0,
    )(displacement, materials, surface)
    green, first, last = lax.optimization_barrier((green, first, last))
    first, last = (x.reshape(-1, cols) for x in (first, last))
    above = lax.ppermute(last, "lat", [(i, i + 1) for i in range(lat_count - 1)])
    below = lax.ppermute(first, "lat", [(i + 1, i) for i in range(lat_count - 1)])
    table = call(
        functools.partial(fourier_kernel, total_lon, orders),
        (jax.ShapeDtypeStruct((total_lon, 2 * LMAX), HALF),) * 2,
        1.2,
    )()
    def partner(x, step):
        return lax.ppermute(x, "lat", [(i, i ^ step) for i in range(lat_count)])

    near = green.reshape(green.shape[0], layers * layers)
    near, table = lax.optimization_barrier((near, table))
    others = [partner(near, i) for i in range(2, lat_count, 2)]
    half_table = (orders, LMAX, width)
    legendre_table = call(
        functools.partial(legendre_kernel, total_lat, orders),
        (jax.ShapeDtypeStruct(half_table, HALF),) * 2,
        2.9,
        scratch=[pltpu.VMEM((width // LANES, LMAX * orders, LANES), jnp.float32)],
        smem=(0,),
    )(owner)
    above, below, others, table, legendre_table = lax.optimization_barrier(
        (above, below, others, table, legendre_table)
    )
    near = jnp.concatenate([near, *others], axis=0)
    far = partner(near, 1)
    first, last = call(pack_kernel, (f32((rows + 2 * DEEP) * SUB, cols),) * 2, 1.5)(
        *own, above, below
    )
    left = lax.ppermute(last, "lon", [(i, (i + 1) % lon_count) for i in range(lon_count)])
    right = lax.ppermute(first, "lon", [((i + 1) % lon_count, i) for i in range(lon_count)])
    theta = ((lat_index * rows + jnp.arange(rows)).astype(jnp.float32) + 0.5) * (
        jnp.pi / total_lat
    )
    weight = jnp.broadcast_to((jnp.sin(theta) / (4.0 * total_lat))[:, None], (rows, LANES))

    steps = layers // SUB

    def worked(t, height):
        return (t, 2, height * SUB, LANES)

    deep = rows + 2 * DEEP
    flat = pltpu.VMEM((lon_count, share, rows, cols), jnp.float32)
    near_shape = pltpu.VMEM((2 * LANES, 2 * LANES), HALF)
    out = call(
        functools.partial(first_sweeps_kernel, lon_count, total_lat),
        (f32(share, rows, cols),) * lon_count
        + (f32(*worked(steps, deep)),) * 3
        + (f32(*worked(1, deep)),),
        6.6,
        scratch=[pltpu.VMEM(worked(steps, deep), jnp.float32)] * 2
        + [pltpu.VMEM(worked(1, deep), jnp.float32), flat, near_shape],
        smem=(0, 1, 2, 3),
    )(index, shear, restoring, contrast, *own, above, below, left, right)
    pieces, state = out[:lon_count], out[lon_count:]
    for iteration in range(ITERS):
        margin = SHALLOW if iteration < ITERS - 1 else 0
        parts = exchange(pieces)
        if iteration == 0:
            turned_green = call(
                functools.partial(turn_kernel, green.shape[0]),
                f32(LMAX // LANES, layers * layers, LANES),
                1.4,
                scratch=[pltpu.VMEM((LMAX, layers * layers), jnp.float32)],
                smem=(0,),
            )(index, near, far)
            parts, turned_green = lax.optimization_barrier((parts, turned_green))
        spectrum = call(
            functools.partial(forward_kernel, lon_count, 2.0 * math.pi / total_lon),
            f32(owners, rows, LANES),
            2.0,
            smem=(0,),
        )(index, weight, *table, *parts)
        spectrum = lax.all_to_all(spectrum, BOTH, 0, 0, tiled=True)
        square = pltpu.VMEM((width // LANES, lon_count * LANES, LANES), jnp.float32)
        coeff_shape = pltpu.VMEM((LMAX // LANES, lon_count * LANES, LANES), jnp.float32)
        synth = call(
            functools.partial(spectral_kernel, margin),
            f32(lat_count, lon_count, rows + 2 * margin, LANES),
            4.0,
            scratch=[square, coeff_shape, coeff_shape],
        )(
            *legendre_table,
            turned_green,
            spectrum.reshape(lat_count, lon_count, rows, LANES),
        )
        synth = lax.all_to_all(
            synth.reshape(owners, rows + 2 * margin, LANES), BOTH, 0, 0, tiled=True
        )
        high = rows + 2 * margin
        sent = share * high + (high if margin > 0 else 0)
        parts = call(
            functools.partial(inverse_kernel, lon_count, margin),
            (f32(sent, cols),) * lon_count,
            2.0,
            scratch=[pltpu.VMEM((lon_count, share * high, cols), jnp.float32)],
            smem=(0,),
        )(index, *table, synth)
        parts = exchange(parts)
        if iteration < ITERS - 1:
            out = call(
                functools.partial(second_sweeps_kernel, lon_count),
                (f32(share, rows, cols),) * lon_count + (f32(layers, rows, cols),),
                5.4,
                scratch=[pltpu.VMEM(worked(steps, tall), jnp.float32)] * 3
                + [
                    pltpu.VMEM((steps, tall * SUB, LANES), jnp.float32),
                    pltpu.VMEM((tall * SUB, LANES), jnp.float32),
                    flat,
                    near_shape,
                ],
                smem=(0, 1),
            )(index, contrast, own[1], *state, *parts)
            pieces, field = out[:lon_count], out[lon_count]
    potential = call(
        functools.partial(assemble_kernel, lon_count),
        f32(lon_count, share * rows, cols),
        1.0,
        scratch=[pltpu.SemaphoreType.DMA((lon_count,))],
        smem=(0,),
        hbm=(0,),
    )(index, *parts)
    return (field, potential.reshape(layers, rows, cols))


def aligned(mesh, displacement):
    lat_count, lon_count = mesh.shape["lat"], mesh.shape["lon"]
    layers, total_lat, total_lon = displacement.shape
    rows, cols = total_lat // lat_count, total_lon // lon_count
    owners = lat_count * lon_count
    return (
        ITERS == 2
        and cols == LANES
        and rows % 8 == 0
        and layers % SUB == 0
        and (2 * (layers // SUB) + 1) * DEEP <= LANES
        and (layers // lon_count) % (layers // SUB) == 0
        and lat_count > 2
        and lon_count % 2 == 0
        and lat_count & (lat_count - 1) == 0
        and layers % lon_count == 0
        and LMAX % owners == 0
        and 2 * (LMAX // owners) * (layers // lon_count) == LANES
        and 2 * (LMAX // owners) == 2 * DEEP
        and LMAX % LANES == 0
    )


def solution(mesh):
    in_specs = (
        P(None, "lat", "lon"),
        P(None, "lat", "lon"),
        P("lat", "lon"),
        P("lat", "lon"),
        P(),
        P(),
        P(),
        P("lat", None, None),
    )
    out_specs = (P(None, "lat", "lon"), P(None, "lat", "lon"))

    def step(displacement, *others):
        device = on_device if aligned(mesh, displacement) else general_device
        return jax.shard_map(
            device, mesh=mesh, in_specs=in_specs, out_specs=out_specs, check_vma=False
        )(displacement, *others)

    return step
```

```python
import functools
import math

import jax
import jax.numpy as jnp
from jax import lax
from jax.experimental import pallas as pl
from jax.experimental.pallas import tpu as pltpu
from jax.sharding import PartitionSpec as P

LMAX = 256
NMAT = 4
ITERS = 2
SWEEPS = 4
LANES = 128
DEEP = 8
SHALLOW = 4
HALF = jnp.bfloat16
VMEM_LIMIT = 16 * 1024 * 1024
BOTH = ("lat", "lon")


def extended(cells, sides, width, closed):
    for axis, dim in sides:
        count = lax.axis_size(axis)
        ends = count if closed else count - 1
        head = lax.slice_in_dim(cells, 0, width, axis=dim)
        tail = lax.slice_in_dim(cells, cells.shape[dim] - width, cells.shape[dim], axis=dim)
        cells = jnp.concatenate(
            [
                lax.ppermute(tail, axis, [(i, (i + 1) % count) for i in range(ends)]),
                cells,
                lax.ppermute(head, axis, [((i + 1) % count, i) for i in range(ends)]),
            ],
            axis=dim,
        )
    return cells


def legendre(theta):
    orders = jnp.arange(LMAX)
    order_f = orders.astype(jnp.float32)
    cosine = jnp.cos(theta)[:, None]
    sine = jnp.sin(theta)[:, None]
    safe = jnp.maximum(order_f, 1.0)
    growth = jnp.where(orders >= 2, 0.5 * jnp.log((2.0 * safe + 1.0) / (2.0 * safe)), 0.0)
    log_diag = jnp.where(orders >= 1, 0.5 * jnp.log(3.0) + jnp.cumsum(growth), 0.0)
    diagonal = jnp.exp(log_diag[None, :] + order_f[None, :] * jnp.log(sine))

    def advance(carry, degree):
        prev_one, prev_two = carry
        deg_f = degree.astype(jnp.float32)
        first = jnp.sqrt(
            (4.0 * deg_f * deg_f - 1.0) / jnp.maximum(deg_f * deg_f - order_f * order_f, 1.0)
        )
        second = jnp.sqrt(
            jnp.maximum((deg_f - 1.0) ** 2 - order_f * order_f, 0.0)
            / jnp.maximum(4.0 * (deg_f - 1.0) ** 2 - 1.0, 1.0)
        )
        general = first * (cosine * prev_one - second * prev_two)
        start_next = jnp.sqrt(2.0 * order_f + 3.0) * cosine * diagonal
        value = jnp.where(
            orders == degree,
            diagonal,
            jnp.where(
                orders == degree - 1, start_next, jnp.where(orders < degree - 1, general, 0.0)
            ),
        )
        return ((value, prev_one), value)

    zeros = jnp.zeros((theta.shape[0], LMAX), jnp.float32)
    _, table = lax.scan(advance, (zeros, zeros), jnp.arange(LMAX), unroll=8)
    return table


def fourier_tables(columns, total):
    orders = jnp.arange(LMAX)
    phase = columns[:, None] * orders[None, :] % total
    angle = 2.0 * jnp.pi / total * phase.astype(jnp.float32)
    forward = jnp.concatenate([jnp.cos(angle), jnp.sin(angle)], axis=1) * (2.0 * jnp.pi / total)
    inverse = jnp.concatenate([jnp.cos(angle), jnp.sin(angle)], axis=1).T
    return (forward, inverse)


def lookup(materials, table):
    result = jnp.zeros(materials.shape, jnp.float32)
    for material in range(NMAT):
        result = result + jnp.where(materials == material, table[material], 0.0)
    return result


def crop_block(block, margin):
    return block[:, margin : block.shape[1] - margin, margin : block.shape[2] - margin]


def margin_sweeps(field, force, stiff, restore, depth, lat_first, total_lat):
    stacked = jnp.stack([field, force, stiff, restore], axis=0)
    lat_wide = extended(stacked, (("lat", 2),), depth, False)
    wide = extended(lat_wide, (("lon", 3),), depth, True)
    current = wide[0]
    rows_wide = wide.shape[2]
    global_rows = lat_first - depth + jnp.arange(rows_wide)
    inside = ((global_rows >= 0) & (global_rows < total_lat))[None, :, None]
    for step in range(depth):
        margin = step + 1
        inner = current[:, 1:-1, 1:-1]
        beside_all = (
            current[:, 2:, 1:-1]
            + current[:, :-2, 1:-1]
            + current[:, 1:-1, 2:]
            + current[:, 1:-1, :-2]
        )
        layer_pad = jnp.pad(inner, ((1, 1), (0, 0), (0, 0)))
        beside_all = beside_all + layer_pad[2:] + layer_pad[:-2]
        force_part = crop_block(wide[1], margin)
        stiff_part = crop_block(wide[2], margin)
        restore_part = crop_block(wide[3], margin)
        valid = inside[:, margin : rows_wide - margin, :]
        denominator = jnp.where(valid, 6.0 * stiff_part + restore_part, 1.0)
        current = jnp.where(valid, (force_part + stiff_part * beside_all) / denominator, 0.0)
    return current


def general_device(displacement, materials, ice_mask, ice_height, shear, restoring, contrast, green):
    highest = lax.Precision.HIGHEST
    layers, lat_rows, lon_cols = displacement.shape
    lon_count = lax.axis_size("lon")
    lat_count = lax.axis_size("lat")
    total_lat = lat_rows * lat_count
    total_lon = lon_cols * lon_count
    layer_share = layers // lon_count
    stiff = lookup(materials, shear)
    restore = lookup(materials, restoring)
    rho_scale = lookup(materials, contrast)
    surface = (ice_mask.astype(jnp.float32) * ice_height)[None]
    load = jnp.concatenate(
        [surface, jnp.zeros((layers - 1, lat_rows, lon_cols), jnp.float32)], axis=0
    )
    lat_first = lax.axis_index("lat") * lat_rows
    theta = ((lat_first + jnp.arange(lat_rows)).astype(jnp.float32) + 0.5) * (jnp.pi / total_lat)
    table = legendre(theta)
    weights = jnp.sin(theta) / (4.0 * total_lat)
    own_columns = lax.axis_index("lon") * lon_cols + jnp.arange(lon_cols)
    layer_first = lax.axis_index("lon") * layer_share
    depth = 1
    for candidate in range(1, SWEEPS + 1):
        if SWEEPS % candidate == 0 and candidate <= min(lat_rows, lon_cols):
            depth = candidate
    forward, inverse = fourier_tables(own_columns, total_lon)
    field = displacement
    potential = jnp.zeros((layers, lat_rows, lon_cols), jnp.float32)
    for iteration in range(ITERS):
        force = load + potential
        field = margin_sweeps(field, force, stiff, restore, depth, lat_first, total_lat)
        density = rho_scale * field
        product = jnp.dot(
            density.reshape(layer_share * lax.axis_size("lon") * lat_rows, lon_cols),
            forward,
            precision=highest,
            preferred_element_type=jnp.float32,
        )
        spectrum = lax.psum_scatter(
            product.reshape(layer_share * lax.axis_size("lon"), lat_rows, 2 * LMAX),
            "lon",
            scatter_dimension=0,
            tiled=True,
        )
        weighted = spectrum.reshape(layer_share, lat_rows, 2, LMAX) * weights[None, :, None, None]
        coeffs = lax.psum_scatter(
            jnp.einsum("lam,kacm->lkcm", table, weighted, precision=highest),
            "lat",
            scatter_dimension=0,
            tiled=True,
        )
        green_part = lax.dynamic_slice_in_dim(green, layer_first, layer_share, 2)
        partial_pot = jnp.einsum("lkj,ljcm->lkcm", green_part, coeffs, precision=highest)
        pot_coeffs = lax.psum_scatter(partial_pot, "lon", scatter_dimension=1, tiled=True)
        synth = jnp.einsum(
            "lam,lkcm->kacm",
            table,
            lax.all_gather(pot_coeffs, "lat", axis=0, tiled=True),
            precision=highest,
        )
        synth = synth.reshape(layer_share, lat_rows, 2 * LMAX)
        piece = lax.all_gather(synth, "lon", axis=0, tiled=True)
        synth_product = jnp.dot(
            piece.reshape(piece.shape[0] * lat_rows, 2 * LMAX),
            inverse,
            precision=highest,
            preferred_element_type=jnp.float32,
        )
        potential = synth_product.reshape(piece.shape[0], lat_rows, lon_cols)
    return (field, potential)


def call(kernel, outs, micros, scratch=(), smem=(), far=(), hbm=()):
    def place(i, scalars, away):
        space = pltpu.SMEM if i in scalars else pltpu.HBM if i in away else pltpu.VMEM
        return pl.BlockSpec(memory_space=space)

    def run(*args):
        return pl.pallas_call(
            kernel,
            out_shape=outs,
            in_specs=[place(i, smem, far) for i in range(len(args))],
            out_specs=tuple(place(i, (), hbm) for i in range(len(outs)))
            if type(outs) is tuple
            else place(0, (), hbm),
            scratch_shapes=list(scratch),
            compiler_params=pltpu.CompilerParams(vmem_limit_bytes=VMEM_LIMIT),
            cost_estimate=pl.CostEstimate(
                flops=int(micros * 1e9), bytes_accessed=1, transcendentals=0
            ),
        )(*args)

    return run


def copy_all(sem, *pairs):
    copies = [pltpu.make_async_copy(*pair, sem.at[i]) for i, pair in enumerate(pairs)]
    for copy in copies:
        copy.start()
    for copy in copies:
        copy.wait()


def f32(*shape):
    return jax.ShapeDtypeStruct(shape, jnp.float32)


def halves(x):
    high = x.astype(HALF)
    return high, (x - high.astype(jnp.float32)).astype(HALF)


def dot(a, b, dims):
    return lax.dot_general(a, b, (dims, ((), ())), preferred_element_type=jnp.float32)


def dot3(a, b, dims):
    rows = a[0].shape[0]
    both = dot(jnp.concatenate(a, axis=0), b[0], dims)
    return both[:rows] + (both[rows:] + dot(a[0], b[1], dims))


def every(ref, start, stride, count):
    at = pl.ds(start, count, stride=stride)
    return jnp.concatenate([ref[c, at, :] for c in range(ref.shape[0])], axis=1)


def put_every(ref, start, stride, value):
    at = pl.ds(start, value.shape[0], stride=stride)
    for c in range(ref.shape[0]):
        ref[c, at, :] = value[:, c * LANES : (c + 1) * LANES]


NN = ((1,), (0,))
NT = ((1,), (1,))


def iota(shape, dim):
    return lax.broadcasted_iota(jnp.int32, shape, dim)


def fourier_kernel(total, share, high_ref, low_ref):
    shape = (16, 2 * LMAX)
    column = iota(shape, 1)
    part = share // 2
    order = column // share % 2 * (LMAX // 2) + column // (2 * share) * part + column % part
    shift = column // part % 2 * (total - total // 4)
    first = iota(shape, 0) * order + shift
    quarter, half = total // 4, total // 2

    def block(i, carry):
        phase = first + order * (i * shape[0])
        phase = phase & (total - 1) if total & (total - 1) == 0 else lax.rem(phase, total)
        near = jnp.minimum(phase, total - phase)
        beyond = near > quarter
        angle = jnp.where(beyond, half - near, near).astype(jnp.float32) * (2.0 * math.pi / total)
        square = angle * angle
        value = jnp.full(shape, 1.0 / math.factorial(14), jnp.float32)
        for n in range(12, -1, -2):
            value = 1.0 / math.factorial(n) - square * value
        high, low = halves(jnp.where(beyond, -value, value))
        at = pl.ds(pl.multiple_of(i * shape[0], shape[0]), shape[0])
        high_ref[at, :] = high
        low_ref[at, :] = low
        return carry

    lax.fori_loop(0, total // shape[0], block, 0, unroll=2)


def legendre_kernel(total_lat, share, index_ref, high_ref, low_ref, table):
    width = table.shape[0] * LANES
    part = share // 2
    shape = (share, width)

    def orders(shape):
        i = iota(shape, 0)
        return i // part * (LMAX // 2) + index_ref[0] * part + i % part

    order = orders(shape)
    order_f = order.astype(jnp.float32)
    row = iota(shape, 1)
    theta = (row.astype(jnp.float32) + 0.5) * (math.pi / total_lat)
    cosine = jnp.cos(theta)
    sine = jnp.where(row < total_lat, jnp.sin(theta), 1.0)
    terms = (share, LMAX)
    term = iota(terms, 1)
    term_f = jnp.maximum(term.astype(jnp.float32), 1.0)
    growth = 0.5 * jnp.log((2.0 * term_f + 1.0) / (2.0 * term_f))
    used = (term >= 2) & (term <= orders(terms))
    total = jnp.sum(jnp.where(used, growth, 0.0), axis=1, keepdims=True)
    log_diag = jnp.where(order >= 1, 0.5 * math.log(3.0) + total, 0.0)
    diagonal = jnp.exp(log_diag + order_f * jnp.log(sine))
    diagonal = jnp.where(row < total_lat, diagonal, 0.0)
    start_next = jnp.sqrt(2.0 * order_f + 3.0) * cosine * diagonal
    narrow = (share, LANES)
    square = orders(narrow).astype(jnp.float32) ** 2

    def wide(x):
        return jnp.concatenate([x] * (width // LANES), axis=1)

    def advance(degree, carry):
        prev_one, prev_two = carry
        deg = jnp.full(narrow, degree, jnp.int32).astype(jnp.float32)
        first = jnp.sqrt((4.0 * deg * deg - 1.0) / jnp.maximum(deg * deg - square, 1.0))
        below = (deg - 1.0) * (deg - 1.0)
        second = jnp.sqrt(jnp.maximum(below - square, 0.0) / jnp.maximum(4.0 * below - 1.0, 1.0))
        general = wide(first) * (cosine * prev_one - wide(second) * prev_two)
        value = jnp.where(
            order == degree,
            diagonal,
            jnp.where(
                order == degree - 1, start_next, jnp.where(order < degree - 1, general, 0.0)
            ),
        )
        for c in range(width // LANES):
            at = pl.ds(pl.multiple_of(degree * share, share), share)
            table[c, at, :] = value[:, c * LANES : (c + 1) * LANES]
        return (value, prev_one)

    table[:, 0:share, :] = jnp.zeros((width // LANES, share, LANES), jnp.float32)
    zeros = jnp.concatenate([table[c, 0:share, :] for c in range(width // LANES)], axis=1)
    lax.fori_loop(0, LMAX, advance, (zeros, zeros), unroll=8)
    for m in range(share):
        high, low = halves(every(table, m, share, LMAX))
        high_ref[m] = high
        low_ref[m] = low


def turn_kernel(size, index_ref, near_ref, far_ref, o_ref, ordered):
    count = 2 * near_ref.shape[0] // size
    for i in range(count):
        partner = 2 * i if 2 * i < count else 2 * i - count + 1
        block = near_ref if 2 * i < count else far_ref
        first = i % (count // 2) * size
        at = pl.ds(pl.multiple_of((index_ref[0] ^ partner) * size, size), size)
        ordered[at, :] = block[first : first + size, :]
    for c in range(o_ref.shape[0]):
        o_ref[c] = ordered[c * LANES : (c + 1) * LANES, :].T


def slab_kernel(u_ref, mat_ref, surface_ref, first_ref, last_ref):
    layers, rows, _ = u_ref.shape
    for ref, at in ((first_ref, pl.ds(0, DEEP)), (last_ref, pl.ds(rows - DEEP, DEEP))):
        for k in range(layers):
            ref[k] = u_ref[k, at, :]
            ref[layers + k] = mat_ref[k, at, :].astype(jnp.float32)
        ref[2 * layers] = surface_ref[at, :]


SUB = 8
PARTS = 2
UNROLL = True


def roll(x, shift, axis):
    shift = shift % x.shape[axis]
    return x if shift == 0 else pltpu.roll(x, shift, axis)


def pick(material, table):
    value = jnp.full(material.shape, table[NMAT - 1], jnp.float32)
    for i in range(NMAT - 1):
        value = jnp.where(material == i, table[i], value)
    return value


def tile(row):
    return pl.ds(pl.multiple_of(row * SUB, SUB), SUB)


def by_layer(ref, rows, first, t, steps, row):
    return ref[pl.ds((first + t) * rows + row, SUB, stride=steps * rows), :].astype(jnp.float32)


def for_rows(rows, own, above, below, body):
    u_ref, mat_ref, surface_ref = own
    steps = u_ref.shape[0] // rows // SUB
    layers = SUB * steps

    def margin(ref, offset):
        def one(i, carry):
            body(
                i + offset,
                lambda t: by_layer(ref, DEEP, 0, t, steps, i),
                lambda t: by_layer(ref, DEEP, layers, t, steps, i),
                ref[pl.ds(2 * layers * DEEP + i, 1), :],
            )
            return carry

        lax.fori_loop(0, DEEP, one, 0, unroll=8)

    def inner(i, carry):
        body(
            i + DEEP,
            lambda t: by_layer(u_ref, rows, 0, t, steps, i),
            lambda t: by_layer(mat_ref, rows, 0, t, steps, i),
            surface_ref[pl.ds(i, 1), :],
        )
        return carry

    margin(above, 0)
    lax.fori_loop(0, rows, inner, 0, unroll=8)
    margin(below, rows + DEEP)


def pack_kernel(
    u_ref, mat_ref, surface_ref, above_ref, below_ref, first_ref, last_ref
):
    rows = surface_ref.shape[0]
    steps = u_ref.shape[0] // rows // SUB
    lane = iota((SUB, LANES), 1)
    chunk = 2 * DEEP

    def body(row, u, mat, load):
        both = jnp.zeros((SUB, LANES), jnp.float32)
        fields = [u(t) for t in range(steps)] + [mat(t) for t in range(steps)]
        for i, x in enumerate(fields):
            both = jnp.where(lane // chunk == i, roll(x, i * chunk + DEEP, 1), both)
        load = jnp.broadcast_to(load, (SUB, LANES))
        is_last = lane % chunk < DEEP
        first_ref[tile(row), :] = jnp.where(is_last, load, both)
        last_ref[tile(row), :] = jnp.where(is_last, both, roll(load, chunk, 1))

    for_rows(rows, (u_ref, mat_ref, surface_ref), above_ref, below_ref, body)


def lon_neighbours(near):
    width = near.shape[0]
    apart = iota(near.shape, 0) - iota(near.shape, 1)
    apart = jnp.where(apart < 0, apart + width, apart)
    near[...] = ((apart == 1) | (apart == width - 1)).astype(jnp.float32).astype(HALF)


def run_sweeps(src, offset, a_ref, f_ref, two, near):
    steps = a_ref.shape[0]
    rows = a_ref.shape[2] // SUB - 2 * offset
    for sweep in range(SWEEPS):
        dst = two[sweep % 2]
        shift = offset if sweep == 0 else 0
        size = (rows - 2 - 2 * sweep) // PARTS

        def block(i, carry, src=src, dst=dst, shift=shift, size=size, sweep=sweep):
            first = sweep + 1 + i * size

            def at(row):
                return pl.ds(pl.multiple_of(row * SUB, SUB), size * SUB)

            def tiles(t, c, move):
                return src[t, c, at(first + shift + move), :].reshape(size, SUB, LANES)

            sub = iota((size, SUB, LANES), 1)
            x = [[tiles(t, c, 0) for c in range(2)] for t in range(steps)]
            for t in range(steps):
                both = jnp.concatenate([x[t][c].reshape(size * SUB, LANES) for c in range(2)], axis=1)
                high, low = halves(both)
                beside = dot(high, near[...], NN) + dot(low, near[...], NN)
                for c in range(2):
                    total = beside[:, c * LANES : (c + 1) * LANES].reshape(size, SUB, LANES)
                    total = total + (tiles(t, c, -1) + tiles(t, c, 1))
                    if t > 0:
                        under = x[t - 1][c]
                    else:
                        under = jnp.where(sub == 0, 0.0, roll(x[steps - 1][c], 1, 1))
                    if t < steps - 1:
                        over = x[t + 1][c]
                    else:
                        over = jnp.where(sub == SUB - 1, 0.0, roll(x[0][c], SUB - 1, 1))
                    total = (total + (under + over)).reshape(size * SUB, LANES)
                    value = a_ref[t, c, at(first + offset), :] * total
                    if t < f_ref.shape[0]:
                        value = value + f_ref[t, c, at(first), :]
                    dst[t, c, at(first), :] = value
            return carry

        lax.fori_loop(0, PARTS, block, 0, unroll=UNROLL)
        src = dst


def put_density(mat_ref, contrast, field, index_ref, scratch, pieces):
    lon_count = len(pieces)
    share, rows, _ = pieces[0].shape
    for k in range(lon_count * share):
        material = mat_ref[k * rows : (k + 1) * rows, :]
        scratch[k // share, k % share] = pick(material, contrast) * field(k)
    for s in range(lon_count):
        pieces[s][...] = scratch[lax.rem(index_ref[1] + s, lon_count)]


def layer_of(ref, k, margin, rows):
    steps = ref.shape[0]
    return ref[k % steps, 0, pl.ds(margin * SUB + k // steps, rows, stride=SUB), :]


def first_sweeps_kernel(
    lon_count, total_lat, index_ref, shear_ref, restoring_ref, contrast_ref, u_ref, mat_ref,
    surface_ref, above_ref, below_ref, left_ref, right_ref, *rest,
):
    pieces, rest = rest[:lon_count], rest[lon_count:]
    u_out, a_out, b_out, load_out, first, middle, f_scr, d_scr, near = rest
    rows = surface_ref.shape[0]
    steps = u_out.shape[0]
    a_of, b_of = [], []
    for i in range(NMAT):
        stiff = jnp.full((SUB, LANES), shear_ref[i], jnp.float32)
        restore = jnp.full((SUB, LANES), restoring_ref[i], jnp.float32)
        b_of.append(1.0 / (6.0 * stiff + restore))
        a_of.append(stiff * b_of[i])
    lane = iota((SUB, LANES), 1)
    sub = iota((SUB, LANES), 0)

    def body(row, u, mat, load):
        at = tile(row)
        left, right = left_ref[at, :], right_ref[at, :]
        global_row = index_ref[0] * rows - DEEP + row
        inside = ((global_row >= 0) & (global_row < total_lat)).astype(jnp.float32)

        ends = jnp.where(lane % (2 * DEEP) < DEEP, left, right)

        def side(i):
            return roll(ends, LANES - (2 * i + 1) * DEEP, 1)

        load_side = jnp.where(lane < DEEP, right, roll(left, LANES - 2 * DEEP, 1))
        loads = (jnp.broadcast_to(load, (SUB, LANES)), load_side)
        for t in range(steps):
            fields = ((u(t), mat(t)), (side(t), side(steps + t)))
            for c in range(2):
                value, material = fields[c]
                first[t, c, at, :] = value
                a_out[t, c, at, :] = pick(material, a_of) * inside
                b = pick(material, b_of) * inside
                b_out[t, c, at, :] = b
                if t == 0:
                    surface = jnp.where(sub == 0, loads[c], 0.0)
                    load_out[0, c, at, :] = surface
                    f_scr[0, c, at, :] = b * surface

    for_rows(rows, (u_ref, mat_ref, surface_ref), above_ref, below_ref, body)
    lon_neighbours(near)
    run_sweeps(first, 0, a_out, f_scr, (middle, u_out), near)
    put_density(
        mat_ref, contrast_ref, lambda k: layer_of(u_out, k, DEEP, rows), index_ref, d_scr, pieces
    )


def second_sweeps_kernel(
    lon_count, index_ref, contrast_ref, mat_ref, u_ref, a_ref, b_ref, load_ref, *rest
):
    parts, rest = rest[:lon_count], rest[lon_count:]
    pieces, rest = rest[:lon_count], rest[lon_count:]
    field_hbm, middle, last, f_scr, pot, edge, d_scr, near, field_out, sem = rest
    layers, rows, _ = field_out.shape
    steps = u_ref.shape[0]
    tall = rows + 2 * SHALLOW
    share = layers // lon_count
    spread = share // steps
    chunk = LANES // share
    lane = iota((SUB, LANES), 1)
    for s in range(lon_count):
        source = lax.rem(index_ref[1] + (lon_count - s), lon_count)
        for k in range(share):
            at = pl.ds(source * spread + k // steps, tall, stride=SUB)
            pot[k % steps, at, :] = parts[s][k * tall : (k + 1) * tall, :]
        packed = parts[s][share * tall :, :]
        for e in range(spread):
            at = pl.ds(source * spread + e, tall, stride=SUB)
            edge[at, :] = roll(packed, LANES - e * steps * chunk, 1)

    def force(row, carry):
        at, deep = tile(row), tile(row + DEEP - SHALLOW)
        ends = edge[at, :]
        for t in range(steps):
            potential = (pot[t, at, :], roll(ends, LANES - t * chunk - DEEP, 1))
            for c in range(2):
                value = potential[c]
                if t == 0:
                    value = value + load_ref[0, c, deep, :]
                f_scr[t, c, at, :] = b_ref[t, c, deep, :] * value
        return carry

    lax.fori_loop(0, tall, force, 0, unroll=8)
    lon_neighbours(near)
    run_sweeps(u_ref, DEEP - SHALLOW, a_ref, f_scr, (middle, last), near)
    for k in range(layers):
        field_out[k] = layer_of(last, k, SHALLOW, rows)
    copy = pltpu.make_async_copy(field_out, field_hbm, sem)
    copy.start()
    put_density(mat_ref, contrast_ref, lambda k: field_out[k], index_ref, d_scr, pieces)
    copy.wait()


def swap_chunks(blocks, chunk):
    blocks = list(blocks)
    lane = iota(blocks[0].shape, 1)
    step = 1
    while step < len(blocks):
        upper = (lane // (chunk * step)) % 2 == 1
        for i in range(len(blocks)):
            if i & step:
                continue
            a, b = blocks[i], blocks[i + step]
            blocks[i] = jnp.where(upper, roll(b, chunk * step, 1), a)
            blocks[i + step] = jnp.where(upper, b, roll(a, LANES - chunk * step, 1))
        step *= 2
    return blocks


def forward_kernel(lon_count, scale, index_ref, weight_ref, high_ref, low_ref, *rest):
    parts, (o_ref,) = rest[:lon_count], rest[lon_count:]
    share, rows, cols = parts[0].shape
    chunk = LANES // share
    product = None
    for pair in zip(range(0, lon_count, 2), range(1, lon_count, 2)):
        x = jnp.concatenate([parts[s][...].reshape(share * rows, cols) for s in pair], axis=1)
        places = []
        for s in pair:
            source = lax.rem(index_ref[1] + (lon_count - s), lon_count)
            places.append(pl.ds(pl.multiple_of(source * cols, cols), cols))
        tables = [
            jnp.concatenate([ref[at, :] for at in places], axis=0) for ref in (high_ref, low_ref)
        ]
        term = dot3(halves(x), tables, NN)
        product = term if product is None else product + term
    weight = weight_ref[...] * scale
    for g in range(product.shape[1] // LANES):
        blocks = swap_chunks(
            [
                product[k * rows : (k + 1) * rows, g * LANES : (g + 1) * LANES] * weight
                for k in range(share)
            ],
            chunk,
        )
        for i in range(share):
            o_ref[g * share + i] = blocks[i]


def spectral_kernel(margin, high_ref, low_ref, green_ref, x_ref, o_ref, turned, coeffs, pots):
    share, degrees, width = high_ref.shape
    lat_count, lon_count, rows, _ = x_ref.shape
    total_lat = lat_count * rows
    size = 2 * share
    layers = turned.shape[1] // size
    part = share // 2
    spots = [[m // part * share + c * part + m % part for c in range(2)] for m in range(share)]
    skip = [m // part for m in range(share)]
    used = [slice(first * LANES, degrees) for first in skip]

    def put(ref, m, y):
        first = ref.shape[0] - y.shape[1] // LANES
        for i, r in enumerate(spots[m]):
            put_every(ref.at[first:], r, size, y[i * layers : (i + 1) * layers, :])

    pad = jnp.zeros((width - total_lat, LANES), jnp.float32)
    for q in range(lon_count):
        x = x_ref[:, q].reshape(total_lat, LANES)
        x = jnp.concatenate([x, pad], axis=0)
        for c in range(width // LANES):
            turned[c, q * LANES : (q + 1) * LANES, :] = x[c * LANES : (c + 1) * LANES].T
    for m in range(share):
        x = halves(jnp.concatenate([every(turned, r, size, layers) for r in spots[m]], axis=0))
        y = dot3(x, [ref[m, used[m], :] for ref in (high_ref, low_ref)], NT)
        put(coeffs, m, y)
    block = 8

    def targets(i, carry):
        for c in range(degrees // LANES):
            live = size if c > 0 else share
            sums = [jnp.zeros((live, LANES), jnp.float32) for _ in range(block)]
            for k in range(layers):
                x = coeffs[c, k * size : k * size + live, :]
                for t in range(block):
                    row = green_ref[c, pl.ds((i * block + t) * layers + k, 1), :]
                    sums[t] = sums[t] + row * x
            for t in range(block):
                pots[c, pl.ds(pl.multiple_of((i * block + t) * size, size), live), :] = sums[t]
        return carry

    lax.fori_loop(0, layers // block, targets, 0)
    for m in range(share):
        x = [every(pots.at[skip[m] :], r, size, layers) for r in spots[m]]
        x = halves(jnp.concatenate(x, axis=0))
        y = dot3(x, [ref[m, used[m], :] for ref in (high_ref, low_ref)], NN)
        put(turned, m, y)
    for q in range(lon_count):
        x = [turned[c, q * LANES : (q + 1) * LANES, :].T for c in range(width // LANES)]
        x = jnp.concatenate(x, axis=0)[:total_lat]
        if margin > 0:
            edge = jnp.zeros((margin, LANES), jnp.float32)
            x = jnp.concatenate([edge, x, edge], axis=0)
        for i in range(lat_count):
            o_ref[i, q] = x[i * rows : (i + 1) * rows + 2 * margin]


def inverse_kernel(lon_count, margin, index_ref, high_ref, low_ref, x_ref, *rest):
    pieces, (columns,) = rest[:lon_count], rest[lon_count:]
    owners, rows, _ = x_ref.shape
    cols = high_ref.shape[0] // lon_count
    share = columns.shape[1] // rows
    chunk = LANES // share
    groups = [
        swap_chunks([x_ref[g * share + i] for i in range(share)], chunk)
        for g in range(owners // share)
    ]
    terms = jnp.concatenate(
        [jnp.concatenate([group[k] for group in groups], axis=1) for k in range(share)], axis=0
    )
    terms = halves(terms)
    for q in range(0, lon_count, 2):
        at = slice(q * cols, (q + 2) * cols)
        both = dot3(terms, (high_ref[at, :], low_ref[at, :]), NT)
        columns[q] = both[:, :cols]
        columns[q + 1] = both[:, cols:]
    lane = iota((rows, LANES), 1)
    for s in range(lon_count):
        dest = lax.rem(index_ref[1] + s, lon_count)
        pieces[s][0 : share * rows] = columns[dest]
        if margin == 0:
            continue
        after = lax.rem(dest + 1, lon_count)
        before = lax.rem(dest + lon_count - 1, lon_count)
        packed = jnp.zeros((rows, LANES), jnp.float32)
        for k in range(share):
            at = slice(k * rows, (k + 1) * rows)
            ends = jnp.where(lane < LANES - DEEP, columns[after, at, :], columns[before, at, :])
            packed = jnp.where(lane // chunk == k, roll(ends, k * chunk + DEEP, 1), packed)
        pieces[s][share * rows :] = packed


def assemble_kernel(lon_count, index_ref, *rest):
    parts, o_hbm, sem = rest[:lon_count], rest[lon_count], rest[lon_count + 1]
    sources = [lax.rem(index_ref[1] + (lon_count - s), lon_count) for s in range(lon_count)]
    copy_all(sem, *((part, o_hbm.at[source]) for part, source in zip(parts, sources)))


def exchange(pieces):
    count = len(pieces)
    return [pieces[0]] + [
        lax.ppermute(pieces[s], "lon", [(i, (i + s) % count) for i in range(count)])
        for s in range(1, count)
    ]


def on_device(displacement, materials, ice_mask, ice_height, shear, restoring, contrast, green):
    layers, rows, cols = displacement.shape
    lat_count, lon_count = lax.axis_size("lat"), lax.axis_size("lon")
    total_lat, total_lon = rows * lat_count, cols * lon_count
    owners = lat_count * lon_count
    share, orders = layers // lon_count, LMAX // owners
    width = -(-total_lat // LANES) * LANES
    tall = rows + 2 * SHALLOW
    lat_index = lax.axis_index("lat")
    index = jnp.stack([lat_index, lax.axis_index("lon")]).astype(jnp.int32)
    owner = (index[0] * lon_count + index[1])[None]

    surface = ice_mask.astype(jnp.float32) * ice_height
    own = (
        displacement.reshape(layers * rows, cols),
        materials.reshape(layers * rows, cols),
        surface,
    )
    first, last = call(
        slab_kernel,
        (f32(2 * layers + 1, DEEP, cols),) * 2,
        1.0,
    )(displacement, materials, surface)
    green, first, last = lax.optimization_barrier((green, first, last))
    first, last = (x.reshape(-1, cols) for x in (first, last))
    above = lax.ppermute(last, "lat", [(i, i + 1) for i in range(lat_count - 1)])
    below = lax.ppermute(first, "lat", [(i + 1, i) for i in range(lat_count - 1)])
    table = call(
        functools.partial(fourier_kernel, total_lon, orders),
        (jax.ShapeDtypeStruct((total_lon, 2 * LMAX), HALF),) * 2,
        1.2,
    )()
    def partner(x, step):
        return lax.ppermute(x, "lat", [(i, i ^ step) for i in range(lat_count)])

    near = green.reshape(green.shape[0], layers * layers)
    near, table = lax.optimization_barrier((near, table))
    others = [partner(near, i) for i in range(2, lat_count, 2)]
    half_table = (orders, LMAX, width)
    legendre_table = call(
        functools.partial(legendre_kernel, total_lat, orders),
        (jax.ShapeDtypeStruct(half_table, HALF),) * 2,
        2.9,
        scratch=[pltpu.VMEM((width // LANES, LMAX * orders, LANES), jnp.float32)],
        smem=(0,),
    )(owner)
    above, below, others, table, legendre_table = lax.optimization_barrier(
        (above, below, others, table, legendre_table)
    )
    near = jnp.concatenate([near, *others], axis=0)
    far = partner(near, 1)
    first, last = call(pack_kernel, (f32((rows + 2 * DEEP) * SUB, cols),) * 2, 1.5)(
        *own, above, below
    )
    left = lax.ppermute(last, "lon", [(i, (i + 1) % lon_count) for i in range(lon_count)])
    right = lax.ppermute(first, "lon", [((i + 1) % lon_count, i) for i in range(lon_count)])
    theta = ((lat_index * rows + jnp.arange(rows)).astype(jnp.float32) + 0.5) * (
        jnp.pi / total_lat
    )
    weight = jnp.broadcast_to((jnp.sin(theta) / (4.0 * total_lat))[:, None], (rows, LANES))

    steps = layers // SUB

    def worked(t, height):
        return (t, 2, height * SUB, LANES)

    deep = rows + 2 * DEEP
    flat = pltpu.VMEM((lon_count, share, rows, cols), jnp.float32)
    near_shape = pltpu.VMEM((2 * LANES, 2 * LANES), HALF)
    out = call(
        functools.partial(first_sweeps_kernel, lon_count, total_lat),
        (f32(share, rows, cols),) * lon_count
        + (f32(*worked(steps, deep)),) * 3
        + (f32(*worked(1, deep)),),
        6.6,
        scratch=[pltpu.VMEM(worked(steps, deep), jnp.float32)] * 2
        + [pltpu.VMEM(worked(1, deep), jnp.float32), flat, near_shape],
        smem=(0, 1, 2, 3),
    )(index, shear, restoring, contrast, *own, above, below, left, right)
    pieces, state = out[:lon_count], out[lon_count:]
    for iteration in range(ITERS):
        margin = SHALLOW if iteration < ITERS - 1 else 0
        parts = exchange(pieces)
        if iteration == 0:
            turned_green = call(
                functools.partial(turn_kernel, green.shape[0]),
                f32(LMAX // LANES, layers * layers, LANES),
                1.4,
                scratch=[pltpu.VMEM((LMAX, layers * layers), jnp.float32)],
                smem=(0,),
            )(index, near, far)
            parts, turned_green = lax.optimization_barrier((parts, turned_green))
        spectrum = call(
            functools.partial(forward_kernel, lon_count, 2.0 * math.pi / total_lon),
            f32(owners, rows, LANES),
            2.0,
            smem=(0,),
        )(index, weight, *table, *parts)
        spectrum = lax.all_to_all(spectrum, BOTH, 0, 0, tiled=True)
        square = pltpu.VMEM((width // LANES, lon_count * LANES, LANES), jnp.float32)
        coeff_shape = pltpu.VMEM((LMAX // LANES, lon_count * LANES, LANES), jnp.float32)
        synth = call(
            functools.partial(spectral_kernel, margin),
            f32(lat_count, lon_count, rows + 2 * margin, LANES),
            4.0,
            scratch=[square, coeff_shape, coeff_shape],
        )(
            *legendre_table,
            turned_green,
            spectrum.reshape(lat_count, lon_count, rows, LANES),
        )
        synth = lax.all_to_all(
            synth.reshape(owners, rows + 2 * margin, LANES), BOTH, 0, 0, tiled=True
        )
        high = rows + 2 * margin
        sent = share * high + (high if margin > 0 else 0)
        parts = call(
            functools.partial(inverse_kernel, lon_count, margin),
            (f32(sent, cols),) * lon_count,
            2.0,
            scratch=[pltpu.VMEM((lon_count, share * high, cols), jnp.float32)],
            smem=(0,),
        )(index, *table, synth)
        parts = exchange(parts)
        if iteration < ITERS - 1:
            out = call(
                functools.partial(second_sweeps_kernel, lon_count),
                (f32(share, rows, cols),) * lon_count + (f32(layers, rows, cols),),
                5.4,
                scratch=[pltpu.VMEM(worked(steps, tall), jnp.float32)] * 3
                + [
                    pltpu.VMEM((steps, tall * SUB, LANES), jnp.float32),
                    pltpu.VMEM((tall * SUB, LANES), jnp.float32),
                    flat,
                    near_shape,
                    pltpu.VMEM((layers, rows, cols), jnp.float32),
                    pltpu.SemaphoreType.DMA,
                ],
                smem=(0, 1),
                hbm=(lon_count,),
            )(index, contrast, own[1], *state, *parts)
            pieces, field = out[:lon_count], out[lon_count]
    potential = call(
        functools.partial(assemble_kernel, lon_count),
        f32(lon_count, share * rows, cols),
        1.0,
        scratch=[pltpu.SemaphoreType.DMA((lon_count,))],
        smem=(0,),
        hbm=(0,),
    )(index, *parts)
    return (field, potential.reshape(layers, rows, cols))


def aligned(mesh, displacement):
    lat_count, lon_count = mesh.shape["lat"], mesh.shape["lon"]
    layers, total_lat, total_lon = displacement.shape
    rows, cols = total_lat // lat_count, total_lon // lon_count
    owners = lat_count * lon_count
    return (
        ITERS == 2
        and cols == LANES
        and rows % 8 == 0
        and layers % SUB == 0
        and 2 * (layers // SUB) * 2 * DEEP <= LANES
        and (layers // lon_count) % (layers // SUB) == 0
        and lat_count > 2
        and lon_count % 2 == 0
        and lat_count & (lat_count - 1) == 0
        and layers % lon_count == 0
        and LMAX % owners == 0
        and 2 * (LMAX // owners) * (layers // lon_count) == LANES
        and 2 * (LMAX // owners) == 2 * DEEP
        and LMAX == 2 * LANES
    )


def solution(mesh):
    in_specs = (
        P(None, "lat", "lon"),
        P(None, "lat", "lon"),
        P("lat", "lon"),
        P("lat", "lon"),
        P(),
        P(),
        P(),
        P("lat", None, None),
    )
    out_specs = (P(None, "lat", "lon"), P(None, "lat", "lon"))

    def step(displacement, *others):
        device = on_device if aligned(mesh, displacement) else general_device
        return jax.shard_map(
            device, mesh=mesh, in_specs=in_specs, out_specs=out_specs, check_vma=False
        )(displacement, *others)

    return step
```

```python
import functools
import math

import jax
import jax.numpy as jnp
from jax import lax
from jax.experimental import pallas as pl
from jax.experimental.pallas import tpu as pltpu
from jax.sharding import PartitionSpec as P

LMAX = 256
NMAT = 4
ITERS = 2
SWEEPS = 4
LANES = 128
DEEP = 8
SHALLOW = 4
HALF = jnp.bfloat16
VMEM_LIMIT = 16 * 1024 * 1024
BOTH = ("lat", "lon")


def extended(cells, sides, width, closed):
    for axis, dim in sides:
        count = lax.axis_size(axis)
        ends = count if closed else count - 1
        head = lax.slice_in_dim(cells, 0, width, axis=dim)
        tail = lax.slice_in_dim(cells, cells.shape[dim] - width, cells.shape[dim], axis=dim)
        cells = jnp.concatenate(
            [
                lax.ppermute(tail, axis, [(i, (i + 1) % count) for i in range(ends)]),
                cells,
                lax.ppermute(head, axis, [((i + 1) % count, i) for i in range(ends)]),
            ],
            axis=dim,
        )
    return cells


def legendre(theta):
    orders = jnp.arange(LMAX)
    order_f = orders.astype(jnp.float32)
    cosine = jnp.cos(theta)[:, None]
    sine = jnp.sin(theta)[:, None]
    safe = jnp.maximum(order_f, 1.0)
    growth = jnp.where(orders >= 2, 0.5 * jnp.log((2.0 * safe + 1.0) / (2.0 * safe)), 0.0)
    log_diag = jnp.where(orders >= 1, 0.5 * jnp.log(3.0) + jnp.cumsum(growth), 0.0)
    diagonal = jnp.exp(log_diag[None, :] + order_f[None, :] * jnp.log(sine))

    def advance(carry, degree):
        prev_one, prev_two = carry
        deg_f = degree.astype(jnp.float32)
        first = jnp.sqrt(
            (4.0 * deg_f * deg_f - 1.0) / jnp.maximum(deg_f * deg_f - order_f * order_f, 1.0)
        )
        second = jnp.sqrt(
            jnp.maximum((deg_f - 1.0) ** 2 - order_f * order_f, 0.0)
            / jnp.maximum(4.0 * (deg_f - 1.0) ** 2 - 1.0, 1.0)
        )
        general = first * (cosine * prev_one - second * prev_two)
        start_next = jnp.sqrt(2.0 * order_f + 3.0) * cosine * diagonal
        value = jnp.where(
            orders == degree,
            diagonal,
            jnp.where(
                orders == degree - 1, start_next, jnp.where(orders < degree - 1, general, 0.0)
            ),
        )
        return ((value, prev_one), value)

    zeros = jnp.zeros((theta.shape[0], LMAX), jnp.float32)
    _, table = lax.scan(advance, (zeros, zeros), jnp.arange(LMAX), unroll=8)
    return table


def fourier_tables(columns, total):
    orders = jnp.arange(LMAX)
    phase = columns[:, None] * orders[None, :] % total
    angle = 2.0 * jnp.pi / total * phase.astype(jnp.float32)
    forward = jnp.concatenate([jnp.cos(angle), jnp.sin(angle)], axis=1) * (2.0 * jnp.pi / total)
    inverse = jnp.concatenate([jnp.cos(angle), jnp.sin(angle)], axis=1).T
    return (forward, inverse)


def lookup(materials, table):
    result = jnp.zeros(materials.shape, jnp.float32)
    for material in range(NMAT):
        result = result + jnp.where(materials == material, table[material], 0.0)
    return result


def crop_block(block, margin):
    return block[:, margin : block.shape[1] - margin, margin : block.shape[2] - margin]


def margin_sweeps(field, force, stiff, restore, depth, lat_first, total_lat):
    stacked = jnp.stack([field, force, stiff, restore], axis=0)
    lat_wide = extended(stacked, (("lat", 2),), depth, False)
    wide = extended(lat_wide, (("lon", 3),), depth, True)
    current = wide[0]
    rows_wide = wide.shape[2]
    global_rows = lat_first - depth + jnp.arange(rows_wide)
    inside = ((global_rows >= 0) & (global_rows < total_lat))[None, :, None]
    for step in range(depth):
        margin = step + 1
        inner = current[:, 1:-1, 1:-1]
        beside_all = (
            current[:, 2:, 1:-1]
            + current[:, :-2, 1:-1]
            + current[:, 1:-1, 2:]
            + current[:, 1:-1, :-2]
        )
        layer_pad = jnp.pad(inner, ((1, 1), (0, 0), (0, 0)))
        beside_all = beside_all + layer_pad[2:] + layer_pad[:-2]
        force_part = crop_block(wide[1], margin)
        stiff_part = crop_block(wide[2], margin)
        restore_part = crop_block(wide[3], margin)
        valid = inside[:, margin : rows_wide - margin, :]
        denominator = jnp.where(valid, 6.0 * stiff_part + restore_part, 1.0)
        current = jnp.where(valid, (force_part + stiff_part * beside_all) / denominator, 0.0)
    return current


def general_device(displacement, materials, ice_mask, ice_height, shear, restoring, contrast, green):
    highest = lax.Precision.HIGHEST
    layers, lat_rows, lon_cols = displacement.shape
    lon_count = lax.axis_size("lon")
    lat_count = lax.axis_size("lat")
    total_lat = lat_rows * lat_count
    total_lon = lon_cols * lon_count
    layer_share = layers // lon_count
    stiff = lookup(materials, shear)
    restore = lookup(materials, restoring)
    rho_scale = lookup(materials, contrast)
    surface = (ice_mask.astype(jnp.float32) * ice_height)[None]
    load = jnp.concatenate(
        [surface, jnp.zeros((layers - 1, lat_rows, lon_cols), jnp.float32)], axis=0
    )
    lat_first = lax.axis_index("lat") * lat_rows
    theta = ((lat_first + jnp.arange(lat_rows)).astype(jnp.float32) + 0.5) * (jnp.pi / total_lat)
    table = legendre(theta)
    weights = jnp.sin(theta) / (4.0 * total_lat)
    own_columns = lax.axis_index("lon") * lon_cols + jnp.arange(lon_cols)
    layer_first = lax.axis_index("lon") * layer_share
    depth = 1
    for candidate in range(1, SWEEPS + 1):
        if SWEEPS % candidate == 0 and candidate <= min(lat_rows, lon_cols):
            depth = candidate
    forward, inverse = fourier_tables(own_columns, total_lon)
    field = displacement
    potential = jnp.zeros((layers, lat_rows, lon_cols), jnp.float32)
    for iteration in range(ITERS):
        force = load + potential
        field = margin_sweeps(field, force, stiff, restore, depth, lat_first, total_lat)
        density = rho_scale * field
        product = jnp.dot(
            density.reshape(layer_share * lax.axis_size("lon") * lat_rows, lon_cols),
            forward,
            precision=highest,
            preferred_element_type=jnp.float32,
        )
        spectrum = lax.psum_scatter(
            product.reshape(layer_share * lax.axis_size("lon"), lat_rows, 2 * LMAX),
            "lon",
            scatter_dimension=0,
            tiled=True,
        )
        weighted = spectrum.reshape(layer_share, lat_rows, 2, LMAX) * weights[None, :, None, None]
        coeffs = lax.psum_scatter(
            jnp.einsum("lam,kacm->lkcm", table, weighted, precision=highest),
            "lat",
            scatter_dimension=0,
            tiled=True,
        )
        green_part = lax.dynamic_slice_in_dim(green, layer_first, layer_share, 2)
        partial_pot = jnp.einsum("lkj,ljcm->lkcm", green_part, coeffs, precision=highest)
        pot_coeffs = lax.psum_scatter(partial_pot, "lon", scatter_dimension=1, tiled=True)
        synth = jnp.einsum(
            "lam,lkcm->kacm",
            table,
            lax.all_gather(pot_coeffs, "lat", axis=0, tiled=True),
            precision=highest,
        )
        synth = synth.reshape(layer_share, lat_rows, 2 * LMAX)
        piece = lax.all_gather(synth, "lon", axis=0, tiled=True)
        synth_product = jnp.dot(
            piece.reshape(piece.shape[0] * lat_rows, 2 * LMAX),
            inverse,
            precision=highest,
            preferred_element_type=jnp.float32,
        )
        potential = synth_product.reshape(piece.shape[0], lat_rows, lon_cols)
    return (field, potential)


def call(kernel, outs, micros, scratch=(), smem=(), far=(), hbm=()):
    def place(i, scalars, away):
        space = pltpu.SMEM if i in scalars else pltpu.HBM if i in away else pltpu.VMEM
        return pl.BlockSpec(memory_space=space)

    def run(*args):
        return pl.pallas_call(
            kernel,
            out_shape=outs,
            in_specs=[place(i, smem, far) for i in range(len(args))],
            out_specs=tuple(place(i, (), hbm) for i in range(len(outs)))
            if type(outs) is tuple
            else place(0, (), hbm),
            scratch_shapes=list(scratch),
            compiler_params=pltpu.CompilerParams(vmem_limit_bytes=VMEM_LIMIT),
            cost_estimate=pl.CostEstimate(
                flops=int(micros * 1e9), bytes_accessed=1, transcendentals=0
            ),
        )(*args)

    return run


def copy_all(sem, *pairs):
    copies = [pltpu.make_async_copy(*pair, sem.at[i]) for i, pair in enumerate(pairs)]
    for copy in copies:
        copy.start()
    for copy in copies:
        copy.wait()


def f32(*shape):
    return jax.ShapeDtypeStruct(shape, jnp.float32)


def halves(x):
    high = x.astype(HALF)
    return high, (x - high.astype(jnp.float32)).astype(HALF)


def dot(a, b, dims):
    return lax.dot_general(a, b, (dims, ((), ())), preferred_element_type=jnp.float32)


def dot3(a, b, dims):
    rows = a[0].shape[0]
    both = dot(jnp.concatenate(a, axis=0), b[0], dims)
    return both[:rows] + (both[rows:] + dot(a[0], b[1], dims))


def every(ref, start, stride, count):
    at = pl.ds(start, count, stride=stride)
    return jnp.concatenate([ref[c, at, :] for c in range(ref.shape[0])], axis=1)


def put_every(ref, start, stride, value):
    at = pl.ds(start, value.shape[0], stride=stride)
    for c in range(ref.shape[0]):
        ref[c, at, :] = value[:, c * LANES : (c + 1) * LANES]


NN = ((1,), (0,))
NT = ((1,), (1,))


def iota(shape, dim):
    return lax.broadcasted_iota(jnp.int32, shape, dim)


def fourier_kernel(total, share, high_ref, low_ref):
    shape = (16, 2 * LMAX)
    column = iota(shape, 1)
    part = share // 2
    order = column // share % 2 * (LMAX // 2) + column // (2 * share) * part + column % part
    shift = column // part % 2 * (total - total // 4)
    first = iota(shape, 0) * order + shift
    quarter, half = total // 4, total // 2

    def block(i, carry):
        phase = first + order * (i * shape[0])
        phase = phase & (total - 1) if total & (total - 1) == 0 else lax.rem(phase, total)
        near = jnp.minimum(phase, total - phase)
        beyond = near > quarter
        angle = jnp.where(beyond, half - near, near).astype(jnp.float32) * (2.0 * math.pi / total)
        square = angle * angle
        value = jnp.full(shape, 1.0 / math.factorial(14), jnp.float32)
        for n in range(12, -1, -2):
            value = 1.0 / math.factorial(n) - square * value
        high, low = halves(jnp.where(beyond, -value, value))
        at = pl.ds(pl.multiple_of(i * shape[0], shape[0]), shape[0])
        high_ref[at, :] = high
        low_ref[at, :] = low
        return carry

    lax.fori_loop(0, total // shape[0], block, 0, unroll=2)


def legendre_kernel(total_lat, share, index_ref, high_ref, low_ref, table):
    width = table.shape[0] * LANES
    part = share // 2
    shape = (share, width)

    def orders(shape):
        i = iota(shape, 0)
        return i // part * (LMAX // 2) + index_ref[0] * part + i % part

    order = orders(shape)
    order_f = order.astype(jnp.float32)
    row = iota(shape, 1)
    theta = (row.astype(jnp.float32) + 0.5) * (math.pi / total_lat)
    cosine = jnp.cos(theta)
    sine = jnp.where(row < total_lat, jnp.sin(theta), 1.0)
    terms = (share, LMAX)
    term = iota(terms, 1)
    term_f = jnp.maximum(term.astype(jnp.float32), 1.0)
    growth = 0.5 * jnp.log((2.0 * term_f + 1.0) / (2.0 * term_f))
    used = (term >= 2) & (term <= orders(terms))
    total = jnp.sum(jnp.where(used, growth, 0.0), axis=1, keepdims=True)
    log_diag = jnp.where(order >= 1, 0.5 * math.log(3.0) + total, 0.0)
    diagonal = jnp.exp(log_diag + order_f * jnp.log(sine))
    diagonal = jnp.where(row < total_lat, diagonal, 0.0)
    start_next = jnp.sqrt(2.0 * order_f + 3.0) * cosine * diagonal
    narrow = (share, LANES)
    square = orders(narrow).astype(jnp.float32) ** 2

    def wide(x):
        return jnp.concatenate([x] * (width // LANES), axis=1)

    def advance(degree, carry):
        prev_one, prev_two = carry
        deg = jnp.full(narrow, degree, jnp.int32).astype(jnp.float32)
        first = jnp.sqrt((4.0 * deg * deg - 1.0) / jnp.maximum(deg * deg - square, 1.0))
        below = (deg - 1.0) * (deg - 1.0)
        second = jnp.sqrt(jnp.maximum(below - square, 0.0) / jnp.maximum(4.0 * below - 1.0, 1.0))
        general = wide(first) * (cosine * prev_one - wide(second) * prev_two)
        value = jnp.where(
            order == degree,
            diagonal,
            jnp.where(
                order == degree - 1, start_next, jnp.where(order < degree - 1, general, 0.0)
            ),
        )
        for c in range(width // LANES):
            at = pl.ds(pl.multiple_of(degree * share, share), share)
            table[c, at, :] = value[:, c * LANES : (c + 1) * LANES]
        return (value, prev_one)

    table[:, 0:share, :] = jnp.zeros((width // LANES, share, LANES), jnp.float32)
    zeros = jnp.concatenate([table[c, 0:share, :] for c in range(width // LANES)], axis=1)
    lax.fori_loop(0, LMAX, advance, (zeros, zeros), unroll=8)
    for m in range(share):
        high, low = halves(every(table, m, share, LMAX))
        high_ref[m] = high
        low_ref[m] = low


def turn_kernel(size, index_ref, near_ref, far_ref, o_ref, ordered):
    count = 2 * near_ref.shape[0] // size
    for i in range(count):
        partner = 2 * i if 2 * i < count else 2 * i - count + 1
        block = near_ref if 2 * i < count else far_ref
        first = i % (count // 2) * size
        at = pl.ds(pl.multiple_of((index_ref[0] ^ partner) * size, size), size)
        ordered[at, :] = block[first : first + size, :]
    for c in range(o_ref.shape[0]):
        o_ref[c] = ordered[c * LANES : (c + 1) * LANES, :].T


def slab_kernel(u_ref, mat_ref, surface_ref, first_ref, last_ref):
    layers, rows, _ = u_ref.shape
    for ref, at in ((first_ref, pl.ds(0, DEEP)), (last_ref, pl.ds(rows - DEEP, DEEP))):
        for k in range(layers):
            ref[k] = u_ref[k, at, :]
            ref[layers + k] = mat_ref[k, at, :].astype(jnp.float32)
        ref[2 * layers] = surface_ref[at, :]


SUB = 8
PARTS = 2
UNROLL = True


def roll(x, shift, axis):
    shift = shift % x.shape[axis]
    return x if shift == 0 else pltpu.roll(x, shift, axis)


def pick(material, table):
    value = jnp.full(material.shape, table[NMAT - 1], jnp.float32)
    for i in range(NMAT - 1):
        value = jnp.where(material == i, table[i], value)
    return value


def tile(row):
    return pl.ds(pl.multiple_of(row * SUB, SUB), SUB)


def by_layer(ref, rows, first, t, steps, row):
    return ref[pl.ds((first + t) * rows + row, SUB, stride=steps * rows), :].astype(jnp.float32)


def for_rows(rows, own, above, below, body):
    u_ref, mat_ref, surface_ref = own
    steps = u_ref.shape[0] // rows // SUB
    layers = SUB * steps

    def margin(ref, offset):
        def one(i, carry):
            body(
                i + offset,
                lambda t: by_layer(ref, DEEP, 0, t, steps, i),
                lambda t: by_layer(ref, DEEP, layers, t, steps, i),
                ref[pl.ds(2 * layers * DEEP + i, 1), :],
            )
            return carry

        lax.fori_loop(0, DEEP, one, 0, unroll=8)

    def inner(i, carry):
        body(
            i + DEEP,
            lambda t: by_layer(u_ref, rows, 0, t, steps, i),
            lambda t: by_layer(mat_ref, rows, 0, t, steps, i),
            surface_ref[pl.ds(i, 1), :],
        )
        return carry

    margin(above, 0)
    lax.fori_loop(0, rows, inner, 0, unroll=8)
    margin(below, rows + DEEP)


def pack_kernel(
    u_ref, mat_ref, surface_ref, above_ref, below_ref, first_ref, last_ref, ends, loads
):
    rows = surface_ref.shape[0]
    steps = u_ref.shape[0] // rows // SUB
    lane = iota((SUB, LANES), 1)
    chunk = 2 * DEEP

    def body(row, u, mat, load):
        both = jnp.zeros((SUB, LANES), jnp.float32)
        fields = [u(t) for t in range(steps)] + [mat(t) for t in range(steps)]
        for i, x in enumerate(fields):
            both = jnp.where(lane // chunk == i, roll(x, i * chunk + DEEP, 1), both)
        ends[tile(row), :] = both
        loads[tile(row), :] = jnp.broadcast_to(load, (SUB, LANES))

    for_rows(rows, (u_ref, mat_ref, surface_ref), above_ref, below_ref, body)
    is_last = lane % chunk < DEEP
    half = ends.shape[0] // 2
    for j in range(0, half, SUB):
        low, high = ends[j : j + SUB, :], ends[half + j : half + j + SUB, :]
        first_ref[j : j + SUB, :] = jnp.where(is_last, roll(high, LANES - DEEP, 1), low)
        last_ref[j : j + SUB, :] = jnp.where(is_last, low, roll(high, DEEP, 1))
    sub = iota((SUB, LANES), 0)
    first = jnp.zeros((SUB, LANES), jnp.float32)
    last = first
    tall = loads.shape[0] // SUB
    for i in range(SUB):
        x = first
        for r in range(i, tall, SUB):
            x = jnp.where(sub == r // SUB, loads[r * SUB : (r + 1) * SUB, :], x)
        chosen = lane // chunk == i
        first = jnp.where(chosen, roll(x, i * chunk, 1), first)
        last = jnp.where(chosen, roll(x, i * chunk + DEEP, 1), last)
    first_ref[half:, :] = first
    last_ref[half:, :] = last


def lon_neighbours(near):
    width = near.shape[0]
    apart = iota(near.shape, 0) - iota(near.shape, 1)
    apart = jnp.where(apart < 0, apart + width, apart)
    near[...] = ((apart == 1) | (apart == width - 1)).astype(jnp.float32).astype(HALF)


def run_sweeps(src, offset, a_ref, f_ref, two, near):
    steps = a_ref.shape[0]
    rows = a_ref.shape[2] // SUB - 2 * offset
    for sweep in range(SWEEPS):
        dst = two[sweep % 2]
        shift = offset if sweep == 0 else 0
        size = (rows - 2 - 2 * sweep) // PARTS

        def block(i, carry, src=src, dst=dst, shift=shift, size=size, sweep=sweep):
            first = sweep + 1 + i * size

            def at(row):
                return pl.ds(pl.multiple_of(row * SUB, SUB), size * SUB)

            def tiles(t, c, move):
                return src[t, c, at(first + shift + move), :].reshape(size, SUB, LANES)

            sub = iota((size, SUB, LANES), 1)
            x = [[tiles(t, c, 0) for c in range(2)] for t in range(steps)]
            for t in range(steps):
                both = jnp.concatenate([x[t][c].reshape(size * SUB, LANES) for c in range(2)], axis=1)
                high, low = halves(both)
                beside = dot(high, near[...], NN) + dot(low, near[...], NN)
                for c in range(2):
                    total = beside[:, c * LANES : (c + 1) * LANES].reshape(size, SUB, LANES)
                    total = total + (tiles(t, c, -1) + tiles(t, c, 1))
                    if t > 0:
                        under = x[t - 1][c]
                    else:
                        under = jnp.where(sub == 0, 0.0, roll(x[steps - 1][c], 1, 1))
                    if t < steps - 1:
                        over = x[t + 1][c]
                    else:
                        over = jnp.where(sub == SUB - 1, 0.0, roll(x[0][c], SUB - 1, 1))
                    total = (total + (under + over)).reshape(size * SUB, LANES)
                    value = a_ref[t, c, at(first + offset), :] * total
                    if t < f_ref.shape[0]:
                        value = value + f_ref[t, c, at(first), :]
                    dst[t, c, at(first), :] = value
            return carry

        lax.fori_loop(0, PARTS, block, 0, unroll=UNROLL)
        src = dst


def put_density(mat_ref, contrast, field, index_ref, scratch, pieces):
    lon_count = len(pieces)
    share, rows, _ = pieces[0].shape
    for k in range(lon_count * share):
        material = mat_ref[k * rows : (k + 1) * rows, :]
        scratch[k // share, k % share] = pick(material, contrast) * field(k)
    for s in range(lon_count):
        pieces[s][...] = scratch[lax.rem(index_ref[1] + s, lon_count)]


def layer_of(ref, k, margin, rows):
    steps = ref.shape[0]
    return ref[k % steps, 0, pl.ds(margin * SUB + k // steps, rows, stride=SUB), :]


def first_sweeps_kernel(
    lon_count, total_lat, index_ref, shear_ref, restoring_ref, contrast_ref, u_ref, mat_ref,
    surface_ref, above_ref, below_ref, left_ref, right_ref, *rest,
):
    pieces, rest = rest[:lon_count], rest[lon_count:]
    u_out, a_out, b_out, load_out, first, middle, f_scr, d_scr, near = rest
    rows = surface_ref.shape[0]
    steps = u_out.shape[0]
    a_of, b_of = [], []
    for i in range(NMAT):
        stiff = jnp.full((SUB, LANES), shear_ref[i], jnp.float32)
        restore = jnp.full((SUB, LANES), restoring_ref[i], jnp.float32)
        b_of.append(1.0 / (6.0 * stiff + restore))
        a_of.append(stiff * b_of[i])
    lane = iota((SUB, LANES), 1)
    sub = iota((SUB, LANES), 0)

    half = rows // 2 + DEEP

    def body(row, u, mat, load):
        at = tile(row)
        upper = row >= half
        ends_at = tile(row - jnp.where(upper, half, 0))
        left, right = left_ref[ends_at, :], right_ref[ends_at, :]
        left = jnp.where(upper, roll(left, LANES - DEEP, 1), left)
        right = jnp.where(upper, roll(right, DEEP, 1), right)
        global_row = index_ref[0] * rows - DEEP + row
        inside = ((global_row >= 0) & (global_row < total_lat)).astype(jnp.float32)

        ends = jnp.where(lane % (2 * DEEP) < DEEP, left, right)

        def side(i):
            return roll(ends, LANES - (2 * i + 1) * DEEP, 1)

        load_at = pl.ds(half * SUB + row // SUB, 1)
        place = row % SUB * 2 * DEEP
        after = jnp.broadcast_to(right_ref[load_at, :], (SUB, LANES))
        after = pltpu.roll(after, (LANES - place) % LANES, 1)
        before = jnp.broadcast_to(left_ref[load_at, :], (SUB, LANES))
        before = pltpu.roll(before, (2 * LANES - DEEP - place) % LANES, 1)
        load_side = jnp.where(lane < DEEP, after, before)
        loads = (jnp.broadcast_to(load, (SUB, LANES)), load_side)
        for t in range(steps):
            fields = ((u(t), mat(t)), (side(t), side(steps + t)))
            for c in range(2):
                value, material = fields[c]
                first[t, c, at, :] = value
                a_out[t, c, at, :] = pick(material, a_of) * inside
                b = pick(material, b_of) * inside
                b_out[t, c, at, :] = b
                if t == 0:
                    surface = jnp.where(sub == 0, loads[c], 0.0)
                    load_out[0, c, at, :] = surface
                    f_scr[0, c, at, :] = b * surface

    for_rows(rows, (u_ref, mat_ref, surface_ref), above_ref, below_ref, body)
    lon_neighbours(near)
    run_sweeps(first, 0, a_out, f_scr, (middle, u_out), near)
    put_density(
        mat_ref, contrast_ref, lambda k: layer_of(u_out, k, DEEP, rows), index_ref, d_scr, pieces
    )


def second_sweeps_kernel(
    lon_count, index_ref, contrast_ref, mat_ref, u_ref, a_ref, b_ref, load_ref, *rest
):
    parts, rest = rest[:lon_count], rest[lon_count:]
    pieces, rest = rest[:lon_count], rest[lon_count:]
    field_hbm, middle, last, f_scr, pot, edge, d_scr, near, field_out, sem = rest
    layers, rows, _ = field_out.shape
    steps = u_ref.shape[0]
    tall = rows + 2 * SHALLOW
    share = layers // lon_count
    spread = share // steps
    chunk = LANES // share
    lane = iota((SUB, LANES), 1)
    for s in range(lon_count):
        source = lax.rem(index_ref[1] + (lon_count - s), lon_count)
        for k in range(share):
            at = pl.ds(source * spread + k // steps, tall, stride=SUB)
            pot[k % steps, at, :] = parts[s][k * tall : (k + 1) * tall, :]
        packed = parts[s][share * tall :, :]
        for e in range(spread):
            at = pl.ds(source * spread + e, tall, stride=SUB)
            edge[at, :] = roll(packed, LANES - e * steps * chunk, 1)

    def force(row, carry):
        at, deep = tile(row), tile(row + DEEP - SHALLOW)
        ends = edge[at, :]
        for t in range(steps):
            potential = (pot[t, at, :], roll(ends, LANES - t * chunk - DEEP, 1))
            for c in range(2):
                value = potential[c]
                if t == 0:
                    value = value + load_ref[0, c, deep, :]
                f_scr[t, c, at, :] = b_ref[t, c, deep, :] * value
        return carry

    lax.fori_loop(0, tall, force, 0, unroll=8)
    lon_neighbours(near)
    run_sweeps(u_ref, DEEP - SHALLOW, a_ref, f_scr, (middle, last), near)
    for k in range(layers):
        field_out[k] = layer_of(last, k, SHALLOW, rows)
    copy = pltpu.make_async_copy(field_out, field_hbm, sem)
    copy.start()
    put_density(mat_ref, contrast_ref, lambda k: field_out[k], index_ref, d_scr, pieces)
    copy.wait()


def swap_chunks(blocks, chunk):
    blocks = list(blocks)
    lane = iota(blocks[0].shape, 1)
    step = 1
    while step < len(blocks):
        upper = (lane // (chunk * step)) % 2 == 1
        for i in range(len(blocks)):
            if i & step:
                continue
            a, b = blocks[i], blocks[i + step]
            blocks[i] = jnp.where(upper, roll(b, chunk * step, 1), a)
            blocks[i + step] = jnp.where(upper, b, roll(a, LANES - chunk * step, 1))
        step *= 2
    return blocks


def forward_kernel(lon_count, scale, index_ref, weight_ref, high_ref, low_ref, *rest):
    parts, (o_ref,) = rest[:lon_count], rest[lon_count:]
    share, rows, cols = parts[0].shape
    chunk = LANES // share
    product = None
    for pair in zip(range(0, lon_count, 2), range(1, lon_count, 2)):
        x = jnp.concatenate([parts[s][...].reshape(share * rows, cols) for s in pair], axis=1)
        places = []
        for s in pair:
            source = lax.rem(index_ref[1] + (lon_count - s), lon_count)
            places.append(pl.ds(pl.multiple_of(source * cols, cols), cols))
        tables = [
            jnp.concatenate([ref[at, :] for at in places], axis=0) for ref in (high_ref, low_ref)
        ]
        term = dot3(halves(x), tables, NN)
        product = term if product is None else product + term
    weight = weight_ref[...] * scale
    for g in range(product.shape[1] // LANES):
        blocks = swap_chunks(
            [
                product[k * rows : (k + 1) * rows, g * LANES : (g + 1) * LANES] * weight
                for k in range(share)
            ],
            chunk,
        )
        for i in range(share):
            o_ref[g * share + i] = blocks[i]


def spectral_kernel(margin, high_ref, low_ref, green_ref, x_ref, o_ref, turned, coeffs, pots):
    share, degrees, width = high_ref.shape
    lat_count, lon_count, rows, _ = x_ref.shape
    total_lat = lat_count * rows
    size = 2 * share
    layers = turned.shape[1] // size
    part = share // 2
    spots = [[m // part * share + c * part + m % part for c in range(2)] for m in range(share)]
    skip = [m // part for m in range(share)]
    used = [slice(first * LANES, degrees) for first in skip]

    def put(ref, m, y):
        first = ref.shape[0] - y.shape[1] // LANES
        for i, r in enumerate(spots[m]):
            put_every(ref.at[first:], r, size, y[i * layers : (i + 1) * layers, :])

    pad = jnp.zeros((width - total_lat, LANES), jnp.float32)
    for q in range(lon_count):
        x = x_ref[:, q].reshape(total_lat, LANES)
        x = jnp.concatenate([x, pad], axis=0)
        for c in range(width // LANES):
            turned[c, q * LANES : (q + 1) * LANES, :] = x[c * LANES : (c + 1) * LANES].T
    for m in range(share):
        x = halves(jnp.concatenate([every(turned, r, size, layers) for r in spots[m]], axis=0))
        y = dot3(x, [ref[m, used[m], :] for ref in (high_ref, low_ref)], NT)
        put(coeffs, m, y)
    block = 8

    def targets(i, carry):
        for c in range(degrees // LANES):
            live = size if c > 0 else share
            sums = [jnp.zeros((live, LANES), jnp.float32) for _ in range(block)]
            for k in range(layers):
                x = coeffs[c, k * size : k * size + live, :]
                for t in range(block):
                    row = green_ref[c, pl.ds((i * block + t) * layers + k, 1), :]
                    sums[t] = sums[t] + row * x
            for t in range(block):
                pots[c, pl.ds(pl.multiple_of((i * block + t) * size, size), live), :] = sums[t]
        return carry

    lax.fori_loop(0, layers // block, targets, 0)
    for m in range(share):
        x = [every(pots.at[skip[m] :], r, size, layers) for r in spots[m]]
        x = halves(jnp.concatenate(x, axis=0))
        y = dot3(x, [ref[m, used[m], :] for ref in (high_ref, low_ref)], NN)
        put(turned, m, y)
    for q in range(lon_count):
        x = [turned[c, q * LANES : (q + 1) * LANES, :].T for c in range(width // LANES)]
        x = jnp.concatenate(x, axis=0)[:total_lat]
        if margin > 0:
            edge = jnp.zeros((margin, LANES), jnp.float32)
            x = jnp.concatenate([edge, x, edge], axis=0)
        for i in range(lat_count):
            o_ref[i, q] = x[i * rows : (i + 1) * rows + 2 * margin]


def inverse_kernel(lon_count, margin, index_ref, high_ref, low_ref, x_ref, *rest):
    pieces, (columns,) = rest[:lon_count], rest[lon_count:]
    owners, rows, _ = x_ref.shape
    cols = high_ref.shape[0] // lon_count
    share = columns.shape[1] // rows
    chunk = LANES // share
    groups = [
        swap_chunks([x_ref[g * share + i] for i in range(share)], chunk)
        for g in range(owners // share)
    ]
    terms = jnp.concatenate(
        [jnp.concatenate([group[k] for group in groups], axis=1) for k in range(share)], axis=0
    )
    terms = halves(terms)
    for q in range(0, lon_count, 2):
        at = slice(q * cols, (q + 2) * cols)
        both = dot3(terms, (high_ref[at, :], low_ref[at, :]), NT)
        columns[q] = both[:, :cols]
        columns[q + 1] = both[:, cols:]
    lane = iota((rows, LANES), 1)
    for s in range(lon_count):
        dest = lax.rem(index_ref[1] + s, lon_count)
        pieces[s][0 : share * rows] = columns[dest]
        if margin == 0:
            continue
        after = lax.rem(dest + 1, lon_count)
        before = lax.rem(dest + lon_count - 1, lon_count)
        packed = jnp.zeros((rows, LANES), jnp.float32)
        for k in range(share):
            at = slice(k * rows, (k + 1) * rows)
            ends = jnp.where(lane < LANES - DEEP, columns[after, at, :], columns[before, at, :])
            packed = jnp.where(lane // chunk == k, roll(ends, k * chunk + DEEP, 1), packed)
        pieces[s][share * rows :] = packed


def assemble_kernel(lon_count, index_ref, *rest):
    parts, o_hbm, sem = rest[:lon_count], rest[lon_count], rest[lon_count + 1]
    sources = [lax.rem(index_ref[1] + (lon_count - s), lon_count) for s in range(lon_count)]
    copy_all(sem, *((part, o_hbm.at[source]) for part, source in zip(parts, sources)))


def exchange(pieces):
    count = len(pieces)
    got = {0: pieces[0]}
    for s in (2, 1, 3) if count == 4 else range(1, count):
        got[s] = lax.ppermute(pieces[s], "lon", [(i, (i + s) % count) for i in range(count)])
    return [got[s] for s in range(count)]


def on_device(displacement, materials, ice_mask, ice_height, shear, restoring, contrast, green):
    layers, rows, cols = displacement.shape
    lat_count, lon_count = lax.axis_size("lat"), lax.axis_size("lon")
    total_lat, total_lon = rows * lat_count, cols * lon_count
    owners = lat_count * lon_count
    share, orders = layers // lon_count, LMAX // owners
    width = -(-total_lat // LANES) * LANES
    tall = rows + 2 * SHALLOW
    lat_index = lax.axis_index("lat")
    index = jnp.stack([lat_index, lax.axis_index("lon")]).astype(jnp.int32)
    owner = (index[0] * lon_count + index[1])[None]

    surface = ice_mask.astype(jnp.float32) * ice_height
    own = (
        displacement.reshape(layers * rows, cols),
        materials.reshape(layers * rows, cols),
        surface,
    )
    first, last = call(
        slab_kernel,
        (f32(2 * layers + 1, DEEP, cols),) * 2,
        1.0,
    )(displacement, materials, surface)
    green, first, last = lax.optimization_barrier((green, first, last))
    first, last = (x.reshape(-1, cols) for x in (first, last))
    above = lax.ppermute(last, "lat", [(i, i + 1) for i in range(lat_count - 1)])
    below = lax.ppermute(first, "lat", [(i + 1, i) for i in range(lat_count - 1)])
    table = call(
        functools.partial(fourier_kernel, total_lon, orders),
        (jax.ShapeDtypeStruct((total_lon, 2 * LMAX), HALF),) * 2,
        1.2,
    )()
    def partner(x, step):
        return lax.ppermute(x, "lat", [(i, i ^ step) for i in range(lat_count)])

    near = green.reshape(green.shape[0], layers * layers)
    near, table = lax.optimization_barrier((near, table))
    others = [partner(near, i) for i in range(2, lat_count, 2)]
    half_table = (orders, LMAX, width)
    legendre_table = call(
        functools.partial(legendre_kernel, total_lat, orders),
        (jax.ShapeDtypeStruct(half_table, HALF),) * 2,
        2.9,
        scratch=[pltpu.VMEM((width // LANES, LMAX * orders, LANES), jnp.float32)],
        smem=(0,),
    )(owner)
    above, below, others, table, legendre_table = lax.optimization_barrier(
        (above, below, others, table, legendre_table)
    )
    near = jnp.concatenate([near, *others], axis=0)
    far = partner(near, 1)
    deep = rows + 2 * DEEP
    edge_tiles = f32((deep // 2 + 1) * SUB, cols)
    whole = pltpu.VMEM((deep * SUB, cols), jnp.float32)
    first, last = call(pack_kernel, (edge_tiles,) * 2, 1.5, scratch=[whole, whole])(
        *own, above, below
    )
    left = lax.ppermute(last, "lon", [(i, (i + 1) % lon_count) for i in range(lon_count)])
    right = lax.ppermute(first, "lon", [((i + 1) % lon_count, i) for i in range(lon_count)])
    theta = ((lat_index * rows + jnp.arange(rows)).astype(jnp.float32) + 0.5) * (
        jnp.pi / total_lat
    )
    weight = jnp.broadcast_to((jnp.sin(theta) / (4.0 * total_lat))[:, None], (rows, LANES))

    steps = layers // SUB

    def worked(t, height):
        return (t, 2, height * SUB, LANES)

    flat = pltpu.VMEM((lon_count, share, rows, cols), jnp.float32)
    near_shape = pltpu.VMEM((2 * LANES, 2 * LANES), HALF)
    out = call(
        functools.partial(first_sweeps_kernel, lon_count, total_lat),
        (f32(share, rows, cols),) * lon_count
        + (f32(*worked(steps, deep)),) * 3
        + (f32(*worked(1, deep)),),
        6.6,
        scratch=[pltpu.VMEM(worked(steps, deep), jnp.float32)] * 2
        + [pltpu.VMEM(worked(1, deep), jnp.float32), flat, near_shape],
        smem=(0, 1, 2, 3),
    )(index, shear, restoring, contrast, *own, above, below, left, right)
    pieces, state = out[:lon_count], out[lon_count:]
    for iteration in range(ITERS):
        margin = SHALLOW if iteration < ITERS - 1 else 0
        parts = exchange(pieces)
        if iteration == 0:
            turned_green = call(
                functools.partial(turn_kernel, green.shape[0]),
                f32(LMAX // LANES, layers * layers, LANES),
                1.4,
                scratch=[pltpu.VMEM((LMAX, layers * layers), jnp.float32)],
                smem=(0,),
            )(index, near, far)
            parts, turned_green = lax.optimization_barrier((parts, turned_green))
        spectrum = call(
            functools.partial(forward_kernel, lon_count, 2.0 * math.pi / total_lon),
            f32(owners, rows, LANES),
            2.0,
            smem=(0,),
        )(index, weight, *table, *parts)
        spectrum = lax.all_to_all(spectrum, BOTH, 0, 0, tiled=True)
        square = pltpu.VMEM((width // LANES, lon_count * LANES, LANES), jnp.float32)
        coeff_shape = pltpu.VMEM((LMAX // LANES, lon_count * LANES, LANES), jnp.float32)
        synth = call(
            functools.partial(spectral_kernel, margin),
            f32(lat_count, lon_count, rows + 2 * margin, LANES),
            4.0,
            scratch=[square, coeff_shape, coeff_shape],
        )(
            *legendre_table,
            turned_green,
            spectrum.reshape(lat_count, lon_count, rows, LANES),
        )
        synth = lax.all_to_all(
            synth.reshape(owners, rows + 2 * margin, LANES), BOTH, 0, 0, tiled=True
        )
        high = rows + 2 * margin
        sent = share * high + (high if margin > 0 else 0)
        parts = call(
            functools.partial(inverse_kernel, lon_count, margin),
            (f32(sent, cols),) * lon_count,
            2.0,
            scratch=[pltpu.VMEM((lon_count, share * high, cols), jnp.float32)],
            smem=(0,),
        )(index, *table, synth)
        parts = exchange(parts)
        if iteration < ITERS - 1:
            out = call(
                functools.partial(second_sweeps_kernel, lon_count),
                (f32(share, rows, cols),) * lon_count + (f32(layers, rows, cols),),
                5.4,
                scratch=[pltpu.VMEM(worked(steps, tall), jnp.float32)] * 3
                + [
                    pltpu.VMEM((steps, tall * SUB, LANES), jnp.float32),
                    pltpu.VMEM((tall * SUB, LANES), jnp.float32),
                    flat,
                    near_shape,
                    pltpu.VMEM((layers, rows, cols), jnp.float32),
                    pltpu.SemaphoreType.DMA,
                ],
                smem=(0, 1),
                hbm=(lon_count,),
            )(index, contrast, own[1], *state, *parts)
            pieces, field = out[:lon_count], out[lon_count]
    potential = call(
        functools.partial(assemble_kernel, lon_count),
        f32(lon_count, share * rows, cols),
        1.0,
        scratch=[pltpu.SemaphoreType.DMA((lon_count,))],
        smem=(0,),
        hbm=(0,),
    )(index, *parts)
    return (field, potential.reshape(layers, rows, cols))


def aligned(mesh, displacement):
    lat_count, lon_count = mesh.shape["lat"], mesh.shape["lon"]
    layers, total_lat, total_lon = displacement.shape
    rows, cols = total_lat // lat_count, total_lon // lon_count
    owners = lat_count * lon_count
    return (
        ITERS == 2
        and cols == LANES
        and rows % 8 == 0
        and rows + 2 * DEEP <= SUB * SUB
        and layers % SUB == 0
        and 2 * (layers // SUB) * 2 * DEEP <= LANES
        and (layers // lon_count) % (layers // SUB) == 0
        and lat_count > 2
        and lon_count % 2 == 0
        and lat_count & (lat_count - 1) == 0
        and layers % lon_count == 0
        and LMAX % owners == 0
        and 2 * (LMAX // owners) * (layers // lon_count) == LANES
        and 2 * (LMAX // owners) == 2 * DEEP
        and LMAX == 2 * LANES
    )


def solution(mesh):
    in_specs = (
        P(None, "lat", "lon"),
        P(None, "lat", "lon"),
        P("lat", "lon"),
        P("lat", "lon"),
        P(),
        P(),
        P(),
        P("lat", None, None),
    )
    out_specs = (P(None, "lat", "lon"), P(None, "lat", "lon"))

    def step(displacement, *others):
        device = on_device if aligned(mesh, displacement) else general_device
        return jax.shard_map(
            device, mesh=mesh, in_specs=in_specs, out_specs=out_specs, check_vma=False
        )(displacement, *others)

    return step
```

```python
import functools
import math

import jax
import jax.numpy as jnp
from jax import lax
from jax.experimental import pallas as pl
from jax.experimental.pallas import tpu as pltpu
from jax.sharding import PartitionSpec as P

LMAX = 256
NMAT = 4
ITERS = 2
SWEEPS = 4
LANES = 128
DEEP = 8
SHALLOW = 4
HALF = jnp.bfloat16
VMEM_LIMIT = 16 * 1024 * 1024
BOTH = ("lat", "lon")


def extended(cells, sides, width, closed):
    for axis, dim in sides:
        count = lax.axis_size(axis)
        ends = count if closed else count - 1
        head = lax.slice_in_dim(cells, 0, width, axis=dim)
        tail = lax.slice_in_dim(cells, cells.shape[dim] - width, cells.shape[dim], axis=dim)
        cells = jnp.concatenate(
            [
                lax.ppermute(tail, axis, [(i, (i + 1) % count) for i in range(ends)]),
                cells,
                lax.ppermute(head, axis, [((i + 1) % count, i) for i in range(ends)]),
            ],
            axis=dim,
        )
    return cells


def legendre(theta):
    orders = jnp.arange(LMAX)
    order_f = orders.astype(jnp.float32)
    cosine = jnp.cos(theta)[:, None]
    sine = jnp.sin(theta)[:, None]
    safe = jnp.maximum(order_f, 1.0)
    growth = jnp.where(orders >= 2, 0.5 * jnp.log((2.0 * safe + 1.0) / (2.0 * safe)), 0.0)
    log_diag = jnp.where(orders >= 1, 0.5 * jnp.log(3.0) + jnp.cumsum(growth), 0.0)
    diagonal = jnp.exp(log_diag[None, :] + order_f[None, :] * jnp.log(sine))

    def advance(carry, degree):
        prev_one, prev_two = carry
        deg_f = degree.astype(jnp.float32)
        first = jnp.sqrt(
            (4.0 * deg_f * deg_f - 1.0) / jnp.maximum(deg_f * deg_f - order_f * order_f, 1.0)
        )
        second = jnp.sqrt(
            jnp.maximum((deg_f - 1.0) ** 2 - order_f * order_f, 0.0)
            / jnp.maximum(4.0 * (deg_f - 1.0) ** 2 - 1.0, 1.0)
        )
        general = first * (cosine * prev_one - second * prev_two)
        start_next = jnp.sqrt(2.0 * order_f + 3.0) * cosine * diagonal
        value = jnp.where(
            orders == degree,
            diagonal,
            jnp.where(
                orders == degree - 1, start_next, jnp.where(orders < degree - 1, general, 0.0)
            ),
        )
        return ((value, prev_one), value)

    zeros = jnp.zeros((theta.shape[0], LMAX), jnp.float32)
    _, table = lax.scan(advance, (zeros, zeros), jnp.arange(LMAX), unroll=8)
    return table


def fourier_tables(columns, total):
    orders = jnp.arange(LMAX)
    phase = columns[:, None] * orders[None, :] % total
    angle = 2.0 * jnp.pi / total * phase.astype(jnp.float32)
    forward = jnp.concatenate([jnp.cos(angle), jnp.sin(angle)], axis=1) * (2.0 * jnp.pi / total)
    inverse = jnp.concatenate([jnp.cos(angle), jnp.sin(angle)], axis=1).T
    return (forward, inverse)


def lookup(materials, table):
    result = jnp.zeros(materials.shape, jnp.float32)
    for material in range(NMAT):
        result = result + jnp.where(materials == material, table[material], 0.0)
    return result


def crop_block(block, margin):
    return block[:, margin : block.shape[1] - margin, margin : block.shape[2] - margin]


def margin_sweeps(field, force, stiff, restore, depth, lat_first, total_lat):
    stacked = jnp.stack([field, force, stiff, restore], axis=0)
    lat_wide = extended(stacked, (("lat", 2),), depth, False)
    wide = extended(lat_wide, (("lon", 3),), depth, True)
    current = wide[0]
    rows_wide = wide.shape[2]
    global_rows = lat_first - depth + jnp.arange(rows_wide)
    inside = ((global_rows >= 0) & (global_rows < total_lat))[None, :, None]
    for step in range(depth):
        margin = step + 1
        inner = current[:, 1:-1, 1:-1]
        beside_all = (
            current[:, 2:, 1:-1]
            + current[:, :-2, 1:-1]
            + current[:, 1:-1, 2:]
            + current[:, 1:-1, :-2]
        )
        layer_pad = jnp.pad(inner, ((1, 1), (0, 0), (0, 0)))
        beside_all = beside_all + layer_pad[2:] + layer_pad[:-2]
        force_part = crop_block(wide[1], margin)
        stiff_part = crop_block(wide[2], margin)
        restore_part = crop_block(wide[3], margin)
        valid = inside[:, margin : rows_wide - margin, :]
        denominator = jnp.where(valid, 6.0 * stiff_part + restore_part, 1.0)
        current = jnp.where(valid, (force_part + stiff_part * beside_all) / denominator, 0.0)
    return current


def general_device(displacement, materials, ice_mask, ice_height, shear, restoring, contrast, green):
    highest = lax.Precision.HIGHEST
    layers, lat_rows, lon_cols = displacement.shape
    lon_count = lax.axis_size("lon")
    lat_count = lax.axis_size("lat")
    total_lat = lat_rows * lat_count
    total_lon = lon_cols * lon_count
    layer_share = layers // lon_count
    stiff = lookup(materials, shear)
    restore = lookup(materials, restoring)
    rho_scale = lookup(materials, contrast)
    surface = (ice_mask.astype(jnp.float32) * ice_height)[None]
    load = jnp.concatenate(
        [surface, jnp.zeros((layers - 1, lat_rows, lon_cols), jnp.float32)], axis=0
    )
    lat_first = lax.axis_index("lat") * lat_rows
    theta = ((lat_first + jnp.arange(lat_rows)).astype(jnp.float32) + 0.5) * (jnp.pi / total_lat)
    table = legendre(theta)
    weights = jnp.sin(theta) / (4.0 * total_lat)
    own_columns = lax.axis_index("lon") * lon_cols + jnp.arange(lon_cols)
    layer_first = lax.axis_index("lon") * layer_share
    depth = 1
    for candidate in range(1, SWEEPS + 1):
        if SWEEPS % candidate == 0 and candidate <= min(lat_rows, lon_cols):
            depth = candidate
    forward, inverse = fourier_tables(own_columns, total_lon)
    field = displacement
    potential = jnp.zeros((layers, lat_rows, lon_cols), jnp.float32)
    for iteration in range(ITERS):
        force = load + potential
        field = margin_sweeps(field, force, stiff, restore, depth, lat_first, total_lat)
        density = rho_scale * field
        product = jnp.dot(
            density.reshape(layer_share * lax.axis_size("lon") * lat_rows, lon_cols),
            forward,
            precision=highest,
            preferred_element_type=jnp.float32,
        )
        spectrum = lax.psum_scatter(
            product.reshape(layer_share * lax.axis_size("lon"), lat_rows, 2 * LMAX),
            "lon",
            scatter_dimension=0,
            tiled=True,
        )
        weighted = spectrum.reshape(layer_share, lat_rows, 2, LMAX) * weights[None, :, None, None]
        coeffs = lax.psum_scatter(
            jnp.einsum("lam,kacm->lkcm", table, weighted, precision=highest),
            "lat",
            scatter_dimension=0,
            tiled=True,
        )
        green_part = lax.dynamic_slice_in_dim(green, layer_first, layer_share, 2)
        partial_pot = jnp.einsum("lkj,ljcm->lkcm", green_part, coeffs, precision=highest)
        pot_coeffs = lax.psum_scatter(partial_pot, "lon", scatter_dimension=1, tiled=True)
        synth = jnp.einsum(
            "lam,lkcm->kacm",
            table,
            lax.all_gather(pot_coeffs, "lat", axis=0, tiled=True),
            precision=highest,
        )
        synth = synth.reshape(layer_share, lat_rows, 2 * LMAX)
        piece = lax.all_gather(synth, "lon", axis=0, tiled=True)
        synth_product = jnp.dot(
            piece.reshape(piece.shape[0] * lat_rows, 2 * LMAX),
            inverse,
            precision=highest,
            preferred_element_type=jnp.float32,
        )
        potential = synth_product.reshape(piece.shape[0], lat_rows, lon_cols)
    return (field, potential)


def call(kernel, outs, micros, scratch=(), smem=(), far=(), hbm=()):
    def place(i, scalars, away):
        space = pltpu.SMEM if i in scalars else pltpu.HBM if i in away else pltpu.VMEM
        return pl.BlockSpec(memory_space=space)

    def run(*args):
        return pl.pallas_call(
            kernel,
            out_shape=outs,
            in_specs=[place(i, smem, far) for i in range(len(args))],
            out_specs=tuple(place(i, (), hbm) for i in range(len(outs)))
            if type(outs) is tuple
            else place(0, (), hbm),
            scratch_shapes=list(scratch),
            compiler_params=pltpu.CompilerParams(vmem_limit_bytes=VMEM_LIMIT),
            cost_estimate=pl.CostEstimate(
                flops=int(micros * 1e9), bytes_accessed=1, transcendentals=0
            ),
        )(*args)

    return run


def copy_all(sem, *pairs):
    copies = [pltpu.make_async_copy(*pair, sem.at[i]) for i, pair in enumerate(pairs)]
    for copy in copies:
        copy.start()
    for copy in copies:
        copy.wait()


def f32(*shape):
    return jax.ShapeDtypeStruct(shape, jnp.float32)


def halves(x):
    high = x.astype(HALF)
    return high, (x - high.astype(jnp.float32)).astype(HALF)


def dot(a, b, dims):
    return lax.dot_general(a, b, (dims, ((), ())), preferred_element_type=jnp.float32)


def dot3(a, b, dims):
    rows = a[0].shape[0]
    both = dot(jnp.concatenate(a, axis=0), b[0], dims)
    return both[:rows] + (both[rows:] + dot(a[0], b[1], dims))


def every(ref, start, stride, count):
    at = pl.ds(start, count, stride=stride)
    return jnp.concatenate([ref[c, at, :] for c in range(ref.shape[0])], axis=1)


def put_every(ref, start, stride, value):
    at = pl.ds(start, value.shape[0], stride=stride)
    for c in range(ref.shape[0]):
        ref[c, at, :] = value[:, c * LANES : (c + 1) * LANES]


NN = ((1,), (0,))
NT = ((1,), (1,))


def iota(shape, dim):
    return lax.broadcasted_iota(jnp.int32, shape, dim)


def fourier_kernel(total, share, high_ref, low_ref):
    shape = (16, 2 * LMAX)
    column = iota(shape, 1)
    part = share // 2
    order = column // share % 2 * (LMAX // 2) + column // (2 * share) * part + column % part
    shift = column // part % 2 * (total - total // 4)
    first = iota(shape, 0) * order + shift
    quarter, half = total // 4, total // 2

    def block(i, carry):
        phase = first + order * (i * shape[0])
        phase = phase & (total - 1) if total & (total - 1) == 0 else lax.rem(phase, total)
        near = jnp.minimum(phase, total - phase)
        beyond = near > quarter
        angle = jnp.where(beyond, half - near, near).astype(jnp.float32) * (2.0 * math.pi / total)
        square = angle * angle
        value = jnp.full(shape, 1.0 / math.factorial(14), jnp.float32)
        for n in range(12, -1, -2):
            value = 1.0 / math.factorial(n) - square * value
        high, low = halves(jnp.where(beyond, -value, value))
        at = pl.ds(pl.multiple_of(i * shape[0], shape[0]), shape[0])
        high_ref[at, :] = high
        low_ref[at, :] = low
        return carry

    lax.fori_loop(0, total // shape[0], block, 0, unroll=2)


def legendre_kernel(total_lat, share, index_ref, high_ref, low_ref, table):
    width = table.shape[0] * LANES
    part = share // 2
    shape = (share, width)

    def orders(shape):
        i = iota(shape, 0)
        return i // part * (LMAX // 2) + index_ref[0] * part + i % part

    order = orders(shape)
    order_f = order.astype(jnp.float32)
    row = iota(shape, 1)
    theta = (row.astype(jnp.float32) + 0.5) * (math.pi / total_lat)
    cosine = jnp.cos(theta)
    sine = jnp.where(row < total_lat, jnp.sin(theta), 1.0)
    terms = (share, LMAX)
    term = iota(terms, 1)
    term_f = jnp.maximum(term.astype(jnp.float32), 1.0)
    growth = 0.5 * jnp.log((2.0 * term_f + 1.0) / (2.0 * term_f))
    used = (term >= 2) & (term <= orders(terms))
    total = jnp.sum(jnp.where(used, growth, 0.0), axis=1, keepdims=True)
    log_diag = jnp.where(order >= 1, 0.5 * math.log(3.0) + total, 0.0)
    diagonal = jnp.exp(log_diag + order_f * jnp.log(sine))
    diagonal = jnp.where(row < total_lat, diagonal, 0.0)
    start_next = jnp.sqrt(2.0 * order_f + 3.0) * cosine * diagonal
    narrow = (share, LANES)
    square = orders(narrow).astype(jnp.float32) ** 2

    def wide(x):
        return jnp.concatenate([x] * (width // LANES), axis=1)

    def advance(degree, carry):
        prev_one, prev_two = carry
        deg = jnp.full(narrow, degree, jnp.int32).astype(jnp.float32)
        first = jnp.sqrt((4.0 * deg * deg - 1.0) / jnp.maximum(deg * deg - square, 1.0))
        below = (deg - 1.0) * (deg - 1.0)
        second = jnp.sqrt(jnp.maximum(below - square, 0.0) / jnp.maximum(4.0 * below - 1.0, 1.0))
        general = wide(first) * (cosine * prev_one - wide(second) * prev_two)
        value = jnp.where(
            order == degree,
            diagonal,
            jnp.where(
                order == degree - 1, start_next, jnp.where(order < degree - 1, general, 0.0)
            ),
        )
        for c in range(width // LANES):
            at = pl.ds(pl.multiple_of(degree * share, share), share)
            table[c, at, :] = value[:, c * LANES : (c + 1) * LANES]
        return (value, prev_one)

    table[:, 0:share, :] = jnp.zeros((width // LANES, share, LANES), jnp.float32)
    zeros = jnp.concatenate([table[c, 0:share, :] for c in range(width // LANES)], axis=1)
    lax.fori_loop(0, LMAX, advance, (zeros, zeros), unroll=8)
    for m in range(share):
        high, low = halves(every(table, m, share, LMAX))
        high_ref[m] = high
        low_ref[m] = low


def turn_kernel(size, index_ref, near_ref, far_ref, o_ref, ordered):
    count = 2 * near_ref.shape[0] // size
    for i in range(count):
        partner = 2 * i if 2 * i < count else 2 * i - count + 1
        block = near_ref if 2 * i < count else far_ref
        first = i % (count // 2) * size
        at = pl.ds(pl.multiple_of((index_ref[0] ^ partner) * size, size), size)
        ordered[at, :] = block[first : first + size, :]
    for c in range(o_ref.shape[0]):
        o_ref[c] = ordered[c * LANES : (c + 1) * LANES, :].T


def slab_kernel(u_ref, mat_ref, surface_ref, first_ref, last_ref):
    layers, rows, _ = u_ref.shape
    for ref, at in ((first_ref, pl.ds(0, DEEP)), (last_ref, pl.ds(rows - DEEP, DEEP))):
        for k in range(layers):
            ref[k] = u_ref[k, at, :]
            ref[layers + k] = mat_ref[k, at, :].astype(jnp.float32)
        ref[2 * layers] = surface_ref[at, :]


SUB = 8
PARTS = 2
UNROLL = True


def roll(x, shift, axis):
    shift = shift % x.shape[axis]
    return x if shift == 0 else pltpu.roll(x, shift, axis)


def pick(material, table):
    value = jnp.full(material.shape, table[NMAT - 1], jnp.float32)
    for i in range(NMAT - 1):
        value = jnp.where(material == i, table[i], value)
    return value


def tile(row):
    return pl.ds(pl.multiple_of(row * SUB, SUB), SUB)


def by_layer(ref, rows, first, t, steps, row):
    return ref[pl.ds((first + t) * rows + row, SUB, stride=steps * rows), :].astype(jnp.float32)


def for_rows(rows, own, above, below, body):
    u_ref, mat_ref, surface_ref = own
    steps = u_ref.shape[0] // rows // SUB
    layers = SUB * steps

    def margin(ref, offset):
        def one(i, carry):
            body(
                i + offset,
                lambda t: by_layer(ref, DEEP, 0, t, steps, i),
                lambda t: by_layer(ref, DEEP, layers, t, steps, i),
                ref[pl.ds(2 * layers * DEEP + i, 1), :],
            )
            return carry

        lax.fori_loop(0, DEEP, one, 0, unroll=8)

    def inner(i, carry):
        body(
            i + DEEP,
            lambda t: by_layer(u_ref, rows, 0, t, steps, i),
            lambda t: by_layer(mat_ref, rows, 0, t, steps, i),
            surface_ref[pl.ds(i, 1), :],
        )
        return carry

    margin(above, 0)
    lax.fori_loop(0, rows, inner, 0, unroll=True)
    margin(below, rows + DEEP)


def pack_kernel(
    u_ref, mat_ref, surface_ref, above_ref, below_ref, first_ref, last_ref, ends, loads
):
    rows = surface_ref.shape[0]
    steps = u_ref.shape[0] // rows // SUB
    lane = iota((SUB, LANES), 1)
    chunk = 2 * DEEP

    def body(row, u, mat, load):
        both = jnp.zeros((SUB, LANES), jnp.float32)
        fields = [u(t) for t in range(steps)] + [mat(t) for t in range(steps)]
        for i, x in enumerate(fields):
            both = jnp.where(lane // chunk == i, roll(x, i * chunk + DEEP, 1), both)
        ends[tile(row), :] = both
        loads[tile(row), :] = jnp.broadcast_to(load, (SUB, LANES))

    for_rows(rows, (u_ref, mat_ref, surface_ref), above_ref, below_ref, body)
    is_last = lane % chunk < DEEP
    half = ends.shape[0] // 2
    for j in range(0, half, SUB):
        low, high = ends[j : j + SUB, :], ends[half + j : half + j + SUB, :]
        first_ref[j : j + SUB, :] = jnp.where(is_last, roll(high, LANES - DEEP, 1), low)
        last_ref[j : j + SUB, :] = jnp.where(is_last, low, roll(high, DEEP, 1))
    sub = iota((SUB, LANES), 0)
    first = jnp.zeros((SUB, LANES), jnp.float32)
    last = first
    tall = loads.shape[0] // SUB
    for i in range(SUB):
        x = first
        for r in range(i, tall, SUB):
            x = jnp.where(sub == r // SUB, loads[r * SUB : (r + 1) * SUB, :], x)
        chosen = lane // chunk == i
        first = jnp.where(chosen, roll(x, i * chunk, 1), first)
        last = jnp.where(chosen, roll(x, i * chunk + DEEP, 1), last)
    first_ref[half:, :] = first
    last_ref[half:, :] = last


def lon_neighbours(near):
    width = near.shape[0]
    apart = iota(near.shape, 0) - iota(near.shape, 1)
    apart = jnp.where(apart < 0, apart + width, apart)
    near[...] = ((apart == 1) | (apart == width - 1)).astype(jnp.float32).astype(HALF)


def run_sweeps(src, offset, a_ref, f_ref, two, near):
    steps = a_ref.shape[0]
    rows = a_ref.shape[2] // SUB - 2 * offset
    for sweep in range(SWEEPS):
        dst = two[sweep % 2]
        shift = offset if sweep == 0 else 0
        size = (rows - 2 - 2 * sweep) // PARTS

        def block(i, carry, src=src, dst=dst, shift=shift, size=size, sweep=sweep):
            first = sweep + 1 + i * size

            def at(row):
                return pl.ds(pl.multiple_of(row * SUB, SUB), size * SUB)

            def tiles(t, c, move):
                return src[t, c, at(first + shift + move), :].reshape(size, SUB, LANES)

            sub = iota((size, SUB, LANES), 1)
            x = [[tiles(t, c, 0) for c in range(2)] for t in range(steps)]
            for t in range(steps):
                both = jnp.concatenate([x[t][c].reshape(size * SUB, LANES) for c in range(2)], axis=1)
                high, low = halves(both)
                beside = dot(high, near[...], NN) + dot(low, near[...], NN)
                for c in range(2):
                    total = beside[:, c * LANES : (c + 1) * LANES].reshape(size, SUB, LANES)
                    total = total + (tiles(t, c, -1) + tiles(t, c, 1))
                    if t > 0:
                        under = x[t - 1][c]
                    else:
                        under = jnp.where(sub == 0, 0.0, roll(x[steps - 1][c], 1, 1))
                    if t < steps - 1:
                        over = x[t + 1][c]
                    else:
                        over = jnp.where(sub == SUB - 1, 0.0, roll(x[0][c], SUB - 1, 1))
                    total = (total + (under + over)).reshape(size * SUB, LANES)
                    value = a_ref[t, c, at(first + offset), :] * total
                    if t < f_ref.shape[0]:
                        value = value + f_ref[t, c, at(first), :]
                    dst[t, c, at(first), :] = value
            return carry

        lax.fori_loop(0, PARTS, block, 0, unroll=UNROLL)
        src = dst


def put_density(mat_ref, contrast, field, index_ref, scratch, pieces):
    lon_count = len(pieces)
    share, rows, _ = pieces[0].shape
    for k in range(lon_count * share):
        material = mat_ref[k * rows : (k + 1) * rows, :]
        scratch[k // share, k % share] = pick(material, contrast) * field(k)
    for s in range(lon_count):
        pieces[s][...] = scratch[lax.rem(index_ref[1] + s, lon_count)]


def layer_of(ref, k, margin, rows):
    steps = ref.shape[0]
    return ref[k % steps, 0, pl.ds(margin * SUB + k // steps, rows, stride=SUB), :]


def first_sweeps_kernel(
    lon_count, total_lat, index_ref, shear_ref, restoring_ref, contrast_ref, u_ref, mat_ref,
    surface_ref, above_ref, below_ref, left_ref, right_ref, *rest,
):
    pieces, rest = rest[:lon_count], rest[lon_count:]
    u_out, a_out, b_out, load_out, first, middle, f_scr, d_scr, near = rest
    rows = surface_ref.shape[0]
    steps = u_out.shape[0]
    a_of, b_of = [], []
    for i in range(NMAT):
        stiff = jnp.full((SUB, LANES), shear_ref[i], jnp.float32)
        restore = jnp.full((SUB, LANES), restoring_ref[i], jnp.float32)
        b_of.append(1.0 / (6.0 * stiff + restore))
        a_of.append(stiff * b_of[i])
    lane = iota((SUB, LANES), 1)
    sub = iota((SUB, LANES), 0)

    half = rows // 2 + DEEP

    def body(row, u, mat, load):
        at = tile(row)
        upper = row >= half
        ends_at = tile(row - jnp.where(upper, half, 0))
        left, right = left_ref[ends_at, :], right_ref[ends_at, :]
        left = jnp.where(upper, roll(left, LANES - DEEP, 1), left)
        right = jnp.where(upper, roll(right, DEEP, 1), right)
        global_row = index_ref[0] * rows - DEEP + row
        inside = ((global_row >= 0) & (global_row < total_lat)).astype(jnp.float32)

        ends = jnp.where(lane % (2 * DEEP) < DEEP, left, right)

        def side(i):
            return roll(ends, LANES - (2 * i + 1) * DEEP, 1)

        load_at = pl.ds(half * SUB + row // SUB, 1)
        place = row % SUB * 2 * DEEP
        after = jnp.broadcast_to(right_ref[load_at, :], (SUB, LANES))
        after = pltpu.roll(after, (LANES - place) % LANES, 1)
        before = jnp.broadcast_to(left_ref[load_at, :], (SUB, LANES))
        before = pltpu.roll(before, (2 * LANES - DEEP - place) % LANES, 1)
        load_side = jnp.where(lane < DEEP, after, before)
        loads = (jnp.broadcast_to(load, (SUB, LANES)), load_side)
        for t in range(steps):
            fields = ((u(t), mat(t)), (side(t), side(steps + t)))
            for c in range(2):
                value, material = fields[c]
                first[t, c, at, :] = value
                a_out[t, c, at, :] = pick(material, a_of) * inside
                b = pick(material, b_of) * inside
                b_out[t, c, at, :] = b
                if t == 0:
                    surface = jnp.where(sub == 0, loads[c], 0.0)
                    load_out[0, c, at, :] = surface
                    f_scr[0, c, at, :] = b * surface

    for_rows(rows, (u_ref, mat_ref, surface_ref), above_ref, below_ref, body)
    lon_neighbours(near)
    run_sweeps(first, 0, a_out, f_scr, (middle, u_out), near)
    put_density(
        mat_ref, contrast_ref, lambda k: layer_of(u_out, k, DEEP, rows), index_ref, d_scr, pieces
    )


def second_sweeps_kernel(
    lon_count, index_ref, contrast_ref, mat_ref, u_ref, a_ref, b_ref, load_ref, *rest
):
    parts, rest = rest[:lon_count], rest[lon_count:]
    pieces, rest = rest[:lon_count], rest[lon_count:]
    field_out, middle, last, f_scr, pot, edge, d_scr, near = rest
    layers, rows, _ = field_out.shape
    steps = u_ref.shape[0]
    tall = rows + 2 * SHALLOW
    share = layers // lon_count
    spread = share // steps
    chunk = LANES // share
    lane = iota((SUB, LANES), 1)
    for s in range(lon_count):
        source = lax.rem(index_ref[1] + (lon_count - s), lon_count)
        for k in range(share):
            at = pl.ds(source * spread + k // steps, tall, stride=SUB)
            pot[k % steps, at, :] = parts[s][k * tall : (k + 1) * tall, :]
        packed = parts[s][share * tall :, :]
        for e in range(spread):
            at = pl.ds(source * spread + e, tall, stride=SUB)
            edge[at, :] = roll(packed, LANES - e * steps * chunk, 1)

    def force(row, carry):
        at, deep = tile(row), tile(row + DEEP - SHALLOW)
        ends = edge[at, :]
        for t in range(steps):
            potential = (pot[t, at, :], roll(ends, LANES - t * chunk - DEEP, 1))
            for c in range(2):
                value = potential[c]
                if t == 0:
                    value = value + load_ref[0, c, deep, :]
                f_scr[t, c, at, :] = b_ref[t, c, deep, :] * value
        return carry

    lax.fori_loop(0, tall, force, 0, unroll=True)
    lon_neighbours(near)
    run_sweeps(u_ref, DEEP - SHALLOW, a_ref, f_scr, (middle, last), near)
    for k in range(layers):
        field_out[k] = layer_of(last, k, SHALLOW, rows)
    put_density(mat_ref, contrast_ref, lambda k: field_out[k], index_ref, d_scr, pieces)


def swap_chunks(blocks, chunk):
    blocks = list(blocks)
    lane = iota(blocks[0].shape, 1)
    step = 1
    while step < len(blocks):
        upper = (lane // (chunk * step)) % 2 == 1
        for i in range(len(blocks)):
            if i & step:
                continue
            a, b = blocks[i], blocks[i + step]
            blocks[i] = jnp.where(upper, roll(b, chunk * step, 1), a)
            blocks[i + step] = jnp.where(upper, b, roll(a, LANES - chunk * step, 1))
        step *= 2
    return blocks


def forward_kernel(lon_count, scale, index_ref, weight_ref, high_ref, low_ref, *rest):
    parts, (o_ref,) = rest[:lon_count], rest[lon_count:]
    share, rows, cols = parts[0].shape
    chunk = LANES // share
    product = None
    for pair in zip(range(0, lon_count, 2), range(1, lon_count, 2)):
        x = jnp.concatenate([parts[s][...].reshape(share * rows, cols) for s in pair], axis=1)
        places = []
        for s in pair:
            source = lax.rem(index_ref[1] + (lon_count - s), lon_count)
            places.append(pl.ds(pl.multiple_of(source * cols, cols), cols))
        tables = [
            jnp.concatenate([ref[at, :] for at in places], axis=0) for ref in (high_ref, low_ref)
        ]
        term = dot3(halves(x), tables, NN)
        product = term if product is None else product + term
    weight = weight_ref[...] * scale
    for g in range(product.shape[1] // LANES):
        blocks = swap_chunks(
            [
                product[k * rows : (k + 1) * rows, g * LANES : (g + 1) * LANES] * weight
                for k in range(share)
            ],
            chunk,
        )
        for i in range(share):
            o_ref[g * share + i] = blocks[i]


def spectral_kernel(margin, high_ref, low_ref, green_ref, x_ref, o_ref, turned, coeffs, pots):
    share, degrees, width = high_ref.shape
    lat_count, lon_count, rows, _ = x_ref.shape
    total_lat = lat_count * rows
    size = 2 * share
    layers = turned.shape[1] // size
    part = share // 2
    spots = [[m // part * share + c * part + m % part for c in range(2)] for m in range(share)]
    skip = [m // part for m in range(share)]
    used = [slice(first * LANES, degrees) for first in skip]

    def put(ref, m, y):
        first = ref.shape[0] - y.shape[1] // LANES
        for i, r in enumerate(spots[m]):
            put_every(ref.at[first:], r, size, y[i * layers : (i + 1) * layers, :])

    pad = jnp.zeros((width - total_lat, LANES), jnp.float32)
    for q in range(lon_count):
        x = x_ref[:, q].reshape(total_lat, LANES)
        x = jnp.concatenate([x, pad], axis=0)
        for c in range(width // LANES):
            turned[c, q * LANES : (q + 1) * LANES, :] = x[c * LANES : (c + 1) * LANES].T
    for m in range(share):
        x = halves(jnp.concatenate([every(turned, r, size, layers) for r in spots[m]], axis=0))
        y = dot3(x, [ref[m, used[m], :] for ref in (high_ref, low_ref)], NT)
        put(coeffs, m, y)
    block = 8

    def targets(i, carry):
        for c in range(degrees // LANES):
            live = size if c > 0 else share
            sums = [jnp.zeros((live, LANES), jnp.float32) for _ in range(block)]
            for k in range(layers):
                x = coeffs[c, k * size : k * size + live, :]
                for t in range(block):
                    row = green_ref[c, pl.ds((i * block + t) * layers + k, 1), :]
                    sums[t] = sums[t] + row * x
            for t in range(block):
                pots[c, pl.ds(pl.multiple_of((i * block + t) * size, size), live), :] = sums[t]
        return carry

    lax.fori_loop(0, layers // block, targets, 0)
    for m in range(share):
        x = [every(pots.at[skip[m] :], r, size, layers) for r in spots[m]]
        x = halves(jnp.concatenate(x, axis=0))
        y = dot3(x, [ref[m, used[m], :] for ref in (high_ref, low_ref)], NN)
        put(turned, m, y)
    for q in range(lon_count):
        x = [turned[c, q * LANES : (q + 1) * LANES, :].T for c in range(width // LANES)]
        x = jnp.concatenate(x, axis=0)[:total_lat]
        if margin > 0:
            edge = jnp.zeros((margin, LANES), jnp.float32)
            x = jnp.concatenate([edge, x, edge], axis=0)
        for i in range(lat_count):
            o_ref[i, q] = x[i * rows : (i + 1) * rows + 2 * margin]


def inverse_kernel(lon_count, margin, index_ref, high_ref, low_ref, x_ref, *rest):
    pieces, (columns,) = rest[:lon_count], rest[lon_count:]
    owners, rows, _ = x_ref.shape
    cols = high_ref.shape[0] // lon_count
    share = columns.shape[1] // rows
    chunk = LANES // share
    groups = [
        swap_chunks([x_ref[g * share + i] for i in range(share)], chunk)
        for g in range(owners // share)
    ]
    terms = jnp.concatenate(
        [jnp.concatenate([group[k] for group in groups], axis=1) for k in range(share)], axis=0
    )
    terms = halves(terms)
    for q in range(0, lon_count, 2):
        at = slice(q * cols, (q + 2) * cols)
        both = dot3(terms, (high_ref[at, :], low_ref[at, :]), NT)
        columns[q] = both[:, :cols]
        columns[q + 1] = both[:, cols:]
    lane = iota((rows, LANES), 1)
    for s in range(lon_count):
        dest = lax.rem(index_ref[1] + s, lon_count)
        pieces[s][0 : share * rows] = columns[dest]
        if margin == 0:
            continue
        after = lax.rem(dest + 1, lon_count)
        before = lax.rem(dest + lon_count - 1, lon_count)
        packed = jnp.zeros((rows, LANES), jnp.float32)
        for k in range(share):
            at = slice(k * rows, (k + 1) * rows)
            ends = jnp.where(lane < LANES - DEEP, columns[after, at, :], columns[before, at, :])
            packed = jnp.where(lane // chunk == k, roll(ends, k * chunk + DEEP, 1), packed)
        pieces[s][share * rows :] = packed


def assemble_kernel(lon_count, index_ref, *rest):
    parts, o_hbm, sem = rest[:lon_count], rest[lon_count], rest[lon_count + 1]
    sources = [lax.rem(index_ref[1] + (lon_count - s), lon_count) for s in range(lon_count)]
    copy_all(sem, *((part, o_hbm.at[source]) for part, source in zip(parts, sources)))


def exchange(pieces):
    count = len(pieces)
    got = {0: pieces[0]}
    for s in (2, 1, 3) if count == 4 else range(1, count):
        got[s] = lax.ppermute(pieces[s], "lon", [(i, (i + s) % count) for i in range(count)])
    return [got[s] for s in range(count)]


def on_device(displacement, materials, ice_mask, ice_height, shear, restoring, contrast, green):
    layers, rows, cols = displacement.shape
    lat_count, lon_count = lax.axis_size("lat"), lax.axis_size("lon")
    total_lat, total_lon = rows * lat_count, cols * lon_count
    owners = lat_count * lon_count
    share, orders = layers // lon_count, LMAX // owners
    width = -(-total_lat // LANES) * LANES
    tall = rows + 2 * SHALLOW
    lat_index = lax.axis_index("lat")
    index = jnp.stack([lat_index, lax.axis_index("lon")]).astype(jnp.int32)
    owner = (index[0] * lon_count + index[1])[None]

    surface = ice_mask.astype(jnp.float32) * ice_height
    own = (
        displacement.reshape(layers * rows, cols),
        materials.reshape(layers * rows, cols),
        surface,
    )
    first, last = call(
        slab_kernel,
        (f32(2 * layers + 1, DEEP, cols),) * 2,
        1.0,
    )(displacement, materials, surface)
    green, first, last = lax.optimization_barrier((green, first, last))
    first, last = (x.reshape(-1, cols) for x in (first, last))
    above = lax.ppermute(last, "lat", [(i, i + 1) for i in range(lat_count - 1)])
    below = lax.ppermute(first, "lat", [(i + 1, i) for i in range(lat_count - 1)])
    table = call(
        functools.partial(fourier_kernel, total_lon, orders),
        (jax.ShapeDtypeStruct((total_lon, 2 * LMAX), HALF),) * 2,
        1.2,
    )()
    def partner(x, step):
        return lax.ppermute(x, "lat", [(i, i ^ step) for i in range(lat_count)])

    near = green.reshape(green.shape[0], layers * layers)
    near, table = lax.optimization_barrier((near, table))
    others = [partner(near, i) for i in range(2, lat_count, 2)]
    half_table = (orders, LMAX, width)
    legendre_table = call(
        functools.partial(legendre_kernel, total_lat, orders),
        (jax.ShapeDtypeStruct(half_table, HALF),) * 2,
        2.9,
        scratch=[pltpu.VMEM((width // LANES, LMAX * orders, LANES), jnp.float32)],
        smem=(0,),
    )(owner)
    above, below, others, table, legendre_table = lax.optimization_barrier(
        (above, below, others, table, legendre_table)
    )
    near = jnp.concatenate([near, *others], axis=0)
    far = partner(near, 1)
    deep = rows + 2 * DEEP
    edge_tiles = f32((deep // 2 + 1) * SUB, cols)
    whole = pltpu.VMEM((deep * SUB, cols), jnp.float32)
    first, last = call(pack_kernel, (edge_tiles,) * 2, 1.5, scratch=[whole, whole])(
        *own, above, below
    )
    left = lax.ppermute(last, "lon", [(i, (i + 1) % lon_count) for i in range(lon_count)])
    right = lax.ppermute(first, "lon", [((i + 1) % lon_count, i) for i in range(lon_count)])
    theta = ((lat_index * rows + jnp.arange(rows)).astype(jnp.float32) + 0.5) * (
        jnp.pi / total_lat
    )
    weight = jnp.broadcast_to((jnp.sin(theta) / (4.0 * total_lat))[:, None], (rows, LANES))

    steps = layers // SUB

    def worked(t, height):
        return (t, 2, height * SUB, LANES)

    flat = pltpu.VMEM((lon_count, share, rows, cols), jnp.float32)
    near_shape = pltpu.VMEM((2 * LANES, 2 * LANES), HALF)
    out = call(
        functools.partial(first_sweeps_kernel, lon_count, total_lat),
        (f32(share, rows, cols),) * lon_count
        + (f32(*worked(steps, deep)),) * 3
        + (f32(*worked(1, deep)),),
        6.6,
        scratch=[pltpu.VMEM(worked(steps, deep), jnp.float32)] * 2
        + [pltpu.VMEM(worked(1, deep), jnp.float32), flat, near_shape],
        smem=(0, 1, 2, 3),
    )(index, shear, restoring, contrast, *own, above, below, left, right)
    pieces, state = out[:lon_count], out[lon_count:]
    for iteration in range(ITERS):
        margin = SHALLOW if iteration < ITERS - 1 else 0
        parts = exchange(pieces)
        if iteration == 0:
            turned_green = call(
                functools.partial(turn_kernel, green.shape[0]),
                f32(LMAX // LANES, layers * layers, LANES),
                1.4,
                scratch=[pltpu.VMEM((LMAX, layers * layers), jnp.float32)],
                smem=(0,),
            )(index, near, far)
            parts, turned_green = lax.optimization_barrier((parts, turned_green))
        spectrum = call(
            functools.partial(forward_kernel, lon_count, 2.0 * math.pi / total_lon),
            f32(owners, rows, LANES),
            2.0,
            smem=(0,),
        )(index, weight, *table, *parts)
        spectrum = lax.all_to_all(spectrum, BOTH, 0, 0, tiled=True)
        square = pltpu.VMEM((width // LANES, lon_count * LANES, LANES), jnp.float32)
        coeff_shape = pltpu.VMEM((LMAX // LANES, lon_count * LANES, LANES), jnp.float32)
        synth = call(
            functools.partial(spectral_kernel, margin),
            f32(lat_count, lon_count, rows + 2 * margin, LANES),
            4.0,
            scratch=[square, coeff_shape, coeff_shape],
        )(
            *legendre_table,
            turned_green,
            spectrum.reshape(lat_count, lon_count, rows, LANES),
        )
        synth = lax.all_to_all(
            synth.reshape(owners, rows + 2 * margin, LANES), BOTH, 0, 0, tiled=True
        )
        high = rows + 2 * margin
        sent = share * high + (high if margin > 0 else 0)
        parts = call(
            functools.partial(inverse_kernel, lon_count, margin),
            (f32(sent, cols),) * lon_count,
            2.0,
            scratch=[pltpu.VMEM((lon_count, share * high, cols), jnp.float32)],
            smem=(0,),
        )(index, *table, synth)
        parts = exchange(parts)
        if iteration < ITERS - 1:
            out = call(
                functools.partial(second_sweeps_kernel, lon_count),
                (f32(share, rows, cols),) * lon_count + (f32(layers, rows, cols),),
                5.4,
                scratch=[pltpu.VMEM(worked(steps, tall), jnp.float32)] * 3
                + [
                    pltpu.VMEM((steps, tall * SUB, LANES), jnp.float32),
                    pltpu.VMEM((tall * SUB, LANES), jnp.float32),
                    flat,
                    near_shape,
                ],
                smem=(0, 1),
            )(index, contrast, own[1], *state, *parts)
            pieces, field = out[:lon_count], out[lon_count]
    potential = call(
        functools.partial(assemble_kernel, lon_count),
        f32(lon_count, share * rows, cols),
        1.0,
        scratch=[pltpu.SemaphoreType.DMA((lon_count,))],
        smem=(0,),
        hbm=(0,),
    )(index, *parts)
    return (field, potential.reshape(layers, rows, cols))


def aligned(mesh, displacement):
    lat_count, lon_count = mesh.shape["lat"], mesh.shape["lon"]
    layers, total_lat, total_lon = displacement.shape
    rows, cols = total_lat // lat_count, total_lon // lon_count
    owners = lat_count * lon_count
    return (
        ITERS == 2
        and cols == LANES
        and rows % 8 == 0
        and rows + 2 * DEEP <= SUB * SUB
        and layers % SUB == 0
        and 2 * (layers // SUB) * 2 * DEEP <= LANES
        and (layers // lon_count) % (layers // SUB) == 0
        and lat_count > 2
        and lon_count % 2 == 0
        and lat_count & (lat_count - 1) == 0
        and layers % lon_count == 0
        and LMAX % owners == 0
        and 2 * (LMAX // owners) * (layers // lon_count) == LANES
        and 2 * (LMAX // owners) == 2 * DEEP
        and LMAX == 2 * LANES
    )


def solution(mesh):
    in_specs = (
        P(None, "lat", "lon"),
        P(None, "lat", "lon"),
        P("lat", "lon"),
        P("lat", "lon"),
        P(),
        P(),
        P(),
        P("lat", None, None),
    )
    out_specs = (P(None, "lat", "lon"), P(None, "lat", "lon"))

    def step(displacement, *others):
        device = on_device if aligned(mesh, displacement) else general_device
        return jax.shard_map(
            device, mesh=mesh, in_specs=in_specs, out_specs=out_specs, check_vma=False
        )(displacement, *others)

    return step
```

```python
import functools
import math

import jax
import jax.numpy as jnp
from jax import lax
from jax.experimental import pallas as pl
from jax.experimental.pallas import tpu as pltpu
from jax.sharding import PartitionSpec as P

LMAX = 256
NMAT = 4
ITERS = 2
SWEEPS = 4
LANES = 128
DEEP = 8
SHALLOW = 4
HALF = jnp.bfloat16
VMEM_LIMIT = 16 * 1024 * 1024
BOTH = ("lat", "lon")


def extended(cells, sides, width, closed):
    for axis, dim in sides:
        count = lax.axis_size(axis)
        ends = count if closed else count - 1
        head = lax.slice_in_dim(cells, 0, width, axis=dim)
        tail = lax.slice_in_dim(cells, cells.shape[dim] - width, cells.shape[dim], axis=dim)
        cells = jnp.concatenate(
            [
                lax.ppermute(tail, axis, [(i, (i + 1) % count) for i in range(ends)]),
                cells,
                lax.ppermute(head, axis, [((i + 1) % count, i) for i in range(ends)]),
            ],
            axis=dim,
        )
    return cells


def legendre(theta):
    orders = jnp.arange(LMAX)
    order_f = orders.astype(jnp.float32)
    cosine = jnp.cos(theta)[:, None]
    sine = jnp.sin(theta)[:, None]
    safe = jnp.maximum(order_f, 1.0)
    growth = jnp.where(orders >= 2, 0.5 * jnp.log((2.0 * safe + 1.0) / (2.0 * safe)), 0.0)
    log_diag = jnp.where(orders >= 1, 0.5 * jnp.log(3.0) + jnp.cumsum(growth), 0.0)
    diagonal = jnp.exp(log_diag[None, :] + order_f[None, :] * jnp.log(sine))

    def advance(carry, degree):
        prev_one, prev_two = carry
        deg_f = degree.astype(jnp.float32)
        first = jnp.sqrt(
            (4.0 * deg_f * deg_f - 1.0) / jnp.maximum(deg_f * deg_f - order_f * order_f, 1.0)
        )
        second = jnp.sqrt(
            jnp.maximum((deg_f - 1.0) ** 2 - order_f * order_f, 0.0)
            / jnp.maximum(4.0 * (deg_f - 1.0) ** 2 - 1.0, 1.0)
        )
        general = first * (cosine * prev_one - second * prev_two)
        start_next = jnp.sqrt(2.0 * order_f + 3.0) * cosine * diagonal
        value = jnp.where(
            orders == degree,
            diagonal,
            jnp.where(
                orders == degree - 1, start_next, jnp.where(orders < degree - 1, general, 0.0)
            ),
        )
        return ((value, prev_one), value)

    zeros = jnp.zeros((theta.shape[0], LMAX), jnp.float32)
    _, table = lax.scan(advance, (zeros, zeros), jnp.arange(LMAX), unroll=8)
    return table


def fourier_tables(columns, total):
    orders = jnp.arange(LMAX)
    phase = columns[:, None] * orders[None, :] % total
    angle = 2.0 * jnp.pi / total * phase.astype(jnp.float32)
    forward = jnp.concatenate([jnp.cos(angle), jnp.sin(angle)], axis=1) * (2.0 * jnp.pi / total)
    inverse = jnp.concatenate([jnp.cos(angle), jnp.sin(angle)], axis=1).T
    return (forward, inverse)


def lookup(materials, table):
    result = jnp.zeros(materials.shape, jnp.float32)
    for material in range(NMAT):
        result = result + jnp.where(materials == material, table[material], 0.0)
    return result


def crop_block(block, margin):
    return block[:, margin : block.shape[1] - margin, margin : block.shape[2] - margin]


def margin_sweeps(field, force, stiff, restore, depth, lat_first, total_lat):
    stacked = jnp.stack([field, force, stiff, restore], axis=0)
    lat_wide = extended(stacked, (("lat", 2),), depth, False)
    wide = extended(lat_wide, (("lon", 3),), depth, True)
    current = wide[0]
    rows_wide = wide.shape[2]
    global_rows = lat_first - depth + jnp.arange(rows_wide)
    inside = ((global_rows >= 0) & (global_rows < total_lat))[None, :, None]
    for step in range(depth):
        margin = step + 1
        inner = current[:, 1:-1, 1:-1]
        beside_all = (
            current[:, 2:, 1:-1]
            + current[:, :-2, 1:-1]
            + current[:, 1:-1, 2:]
            + current[:, 1:-1, :-2]
        )
        layer_pad = jnp.pad(inner, ((1, 1), (0, 0), (0, 0)))
        beside_all = beside_all + layer_pad[2:] + layer_pad[:-2]
        force_part = crop_block(wide[1], margin)
        stiff_part = crop_block(wide[2], margin)
        restore_part = crop_block(wide[3], margin)
        valid = inside[:, margin : rows_wide - margin, :]
        denominator = jnp.where(valid, 6.0 * stiff_part + restore_part, 1.0)
        current = jnp.where(valid, (force_part + stiff_part * beside_all) / denominator, 0.0)
    return current


def general_device(displacement, materials, ice_mask, ice_height, shear, restoring, contrast, green):
    highest = lax.Precision.HIGHEST
    layers, lat_rows, lon_cols = displacement.shape
    lon_count = lax.axis_size("lon")
    lat_count = lax.axis_size("lat")
    total_lat = lat_rows * lat_count
    total_lon = lon_cols * lon_count
    layer_share = layers // lon_count
    stiff = lookup(materials, shear)
    restore = lookup(materials, restoring)
    rho_scale = lookup(materials, contrast)
    surface = (ice_mask.astype(jnp.float32) * ice_height)[None]
    load = jnp.concatenate(
        [surface, jnp.zeros((layers - 1, lat_rows, lon_cols), jnp.float32)], axis=0
    )
    lat_first = lax.axis_index("lat") * lat_rows
    theta = ((lat_first + jnp.arange(lat_rows)).astype(jnp.float32) + 0.5) * (jnp.pi / total_lat)
    table = legendre(theta)
    weights = jnp.sin(theta) / (4.0 * total_lat)
    own_columns = lax.axis_index("lon") * lon_cols + jnp.arange(lon_cols)
    layer_first = lax.axis_index("lon") * layer_share
    depth = 1
    for candidate in range(1, SWEEPS + 1):
        if SWEEPS % candidate == 0 and candidate <= min(lat_rows, lon_cols):
            depth = candidate
    forward, inverse = fourier_tables(own_columns, total_lon)
    field = displacement
    potential = jnp.zeros((layers, lat_rows, lon_cols), jnp.float32)
    for iteration in range(ITERS):
        force = load + potential
        field = margin_sweeps(field, force, stiff, restore, depth, lat_first, total_lat)
        density = rho_scale * field
        product = jnp.dot(
            density.reshape(layer_share * lax.axis_size("lon") * lat_rows, lon_cols),
            forward,
            precision=highest,
            preferred_element_type=jnp.float32,
        )
        spectrum = lax.psum_scatter(
            product.reshape(layer_share * lax.axis_size("lon"), lat_rows, 2 * LMAX),
            "lon",
            scatter_dimension=0,
            tiled=True,
        )
        weighted = spectrum.reshape(layer_share, lat_rows, 2, LMAX) * weights[None, :, None, None]
        coeffs = lax.psum_scatter(
            jnp.einsum("lam,kacm->lkcm", table, weighted, precision=highest),
            "lat",
            scatter_dimension=0,
            tiled=True,
        )
        green_part = lax.dynamic_slice_in_dim(green, layer_first, layer_share, 2)
        partial_pot = jnp.einsum("lkj,ljcm->lkcm", green_part, coeffs, precision=highest)
        pot_coeffs = lax.psum_scatter(partial_pot, "lon", scatter_dimension=1, tiled=True)
        synth = jnp.einsum(
            "lam,lkcm->kacm",
            table,
            lax.all_gather(pot_coeffs, "lat", axis=0, tiled=True),
            precision=highest,
        )
        synth = synth.reshape(layer_share, lat_rows, 2 * LMAX)
        piece = lax.all_gather(synth, "lon", axis=0, tiled=True)
        synth_product = jnp.dot(
            piece.reshape(piece.shape[0] * lat_rows, 2 * LMAX),
            inverse,
            precision=highest,
            preferred_element_type=jnp.float32,
        )
        potential = synth_product.reshape(piece.shape[0], lat_rows, lon_cols)
    return (field, potential)


def call(kernel, outs, micros, scratch=(), smem=(), far=(), hbm=()):
    def place(i, scalars, away):
        space = pltpu.SMEM if i in scalars else pltpu.HBM if i in away else pltpu.VMEM
        return pl.BlockSpec(memory_space=space)

    def run(*args):
        return pl.pallas_call(
            kernel,
            out_shape=outs,
            in_specs=[place(i, smem, far) for i in range(len(args))],
            out_specs=tuple(place(i, (), hbm) for i in range(len(outs)))
            if type(outs) is tuple
            else place(0, (), hbm),
            scratch_shapes=list(scratch),
            compiler_params=pltpu.CompilerParams(vmem_limit_bytes=VMEM_LIMIT),
            cost_estimate=pl.CostEstimate(
                flops=int(micros * 1e9), bytes_accessed=1, transcendentals=0
            ),
        )(*args)

    return run


def copy_all(sem, *pairs):
    copies = [pltpu.make_async_copy(*pair, sem.at[i]) for i, pair in enumerate(pairs)]
    for copy in copies:
        copy.start()
    for copy in copies:
        copy.wait()


def f32(*shape):
    return jax.ShapeDtypeStruct(shape, jnp.float32)


def halves(x):
    high = x.astype(HALF)
    return high, (x - high.astype(jnp.float32)).astype(HALF)


def dot(a, b, dims):
    return lax.dot_general(a, b, (dims, ((), ())), preferred_element_type=jnp.float32)


def dot3(a, b, dims):
    rows = a[0].shape[0]
    both = dot(jnp.concatenate(a, axis=0), b[0], dims)
    return both[:rows] + (both[rows:] + dot(a[0], b[1], dims))


def every(ref, start, stride, count):
    at = pl.ds(start, count, stride=stride)
    return jnp.concatenate([ref[c, at, :] for c in range(ref.shape[0])], axis=1)


def put_every(ref, start, stride, value):
    at = pl.ds(start, value.shape[0], stride=stride)
    for c in range(ref.shape[0]):
        ref[c, at, :] = value[:, c * LANES : (c + 1) * LANES]


NN = ((1,), (0,))
NT = ((1,), (1,))


def iota(shape, dim):
    return lax.broadcasted_iota(jnp.int32, shape, dim)


def fourier_kernel(total, share, high_ref, low_ref):
    shape = (16, 2 * LMAX)
    column = iota(shape, 1)
    part = share // 2
    order = column // share % 2 * (LMAX // 2) + column // (2 * share) * part + column % part
    shift = column // part % 2 * (total - total // 4)
    first = iota(shape, 0) * order + shift
    quarter, half = total // 4, total // 2

    def block(i, carry):
        phase = first + order * (i * shape[0])
        phase = phase & (total - 1) if total & (total - 1) == 0 else lax.rem(phase, total)
        near = jnp.minimum(phase, total - phase)
        beyond = near > quarter
        angle = jnp.where(beyond, half - near, near).astype(jnp.float32) * (2.0 * math.pi / total)
        square = angle * angle
        value = jnp.full(shape, 1.0 / math.factorial(14), jnp.float32)
        for n in range(12, -1, -2):
            value = 1.0 / math.factorial(n) - square * value
        high, low = halves(jnp.where(beyond, -value, value))
        at = pl.ds(pl.multiple_of(i * shape[0], shape[0]), shape[0])
        high_ref[at, :] = high
        low_ref[at, :] = low
        return carry

    lax.fori_loop(0, total // shape[0], block, 0, unroll=2)


def legendre_kernel(total_lat, share, index_ref, high_ref, low_ref, table):
    width = table.shape[0] * LANES
    part = share // 2
    shape = (share, width)

    def orders(shape):
        i = iota(shape, 0)
        return i // part * (LMAX // 2) + index_ref[0] * part + i % part

    order = orders(shape)
    order_f = order.astype(jnp.float32)
    row = iota(shape, 1)
    theta = (row.astype(jnp.float32) + 0.5) * (math.pi / total_lat)
    cosine = jnp.cos(theta)
    sine = jnp.where(row < total_lat, jnp.sin(theta), 1.0)
    terms = (share, LMAX)
    term = iota(terms, 1)
    term_f = jnp.maximum(term.astype(jnp.float32), 1.0)
    growth = 0.5 * jnp.log((2.0 * term_f + 1.0) / (2.0 * term_f))
    used = (term >= 2) & (term <= orders(terms))
    total = jnp.sum(jnp.where(used, growth, 0.0), axis=1, keepdims=True)
    log_diag = jnp.where(order >= 1, 0.5 * math.log(3.0) + total, 0.0)
    diagonal = jnp.exp(log_diag + order_f * jnp.log(sine))
    diagonal = jnp.where(row < total_lat, diagonal, 0.0)
    start_next = jnp.sqrt(2.0 * order_f + 3.0) * cosine * diagonal
    narrow = (share, LANES)
    square = orders(narrow).astype(jnp.float32) ** 2

    def wide(x):
        return jnp.concatenate([x] * (width // LANES), axis=1)

    def advance(degree, carry):
        prev_one, prev_two = carry
        deg = jnp.full(narrow, degree, jnp.int32).astype(jnp.float32)
        first = jnp.sqrt((4.0 * deg * deg - 1.0) / jnp.maximum(deg * deg - square, 1.0))
        below = (deg - 1.0) * (deg - 1.0)
        second = jnp.sqrt(jnp.maximum(below - square, 0.0) / jnp.maximum(4.0 * below - 1.0, 1.0))
        general = wide(first) * (cosine * prev_one - wide(second) * prev_two)
        value = jnp.where(
            order == degree,
            diagonal,
            jnp.where(
                order == degree - 1, start_next, jnp.where(order < degree - 1, general, 0.0)
            ),
        )
        for c in range(width // LANES):
            at = pl.ds(pl.multiple_of(degree * share, share), share)
            table[c, at, :] = value[:, c * LANES : (c + 1) * LANES]
        return (value, prev_one)

    table[:, 0:share, :] = jnp.zeros((width // LANES, share, LANES), jnp.float32)
    zeros = jnp.concatenate([table[c, 0:share, :] for c in range(width // LANES)], axis=1)
    lax.fori_loop(0, LMAX, advance, (zeros, zeros), unroll=8)
    for m in range(share):
        high, low = halves(every(table, m, share, LMAX))
        high_ref[m] = high
        low_ref[m] = low


def turn_kernel(size, index_ref, near_ref, far_ref, o_ref, ordered):
    count = 2 * near_ref.shape[0] // size
    for i in range(count):
        partner = 2 * i if 2 * i < count else 2 * i - count + 1
        block = near_ref if 2 * i < count else far_ref
        first = i % (count // 2) * size
        at = pl.ds(pl.multiple_of((index_ref[0] ^ partner) * size, size), size)
        ordered[at, :] = block[first : first + size, :]
    for c in range(o_ref.shape[0]):
        o_ref[c] = ordered[c * LANES : (c + 1) * LANES, :].T


def slab_kernel(u_ref, mat_ref, surface_ref, first_ref, last_ref):
    layers, rows, _ = u_ref.shape
    for ref, at in ((first_ref, pl.ds(0, DEEP)), (last_ref, pl.ds(rows - DEEP, DEEP))):
        for k in range(layers):
            ref[k] = u_ref[k, at, :]
            ref[layers + k] = mat_ref[k, at, :].astype(jnp.float32)
        ref[2 * layers] = surface_ref[at, :]


SUB = 8
PARTS = 1
UNROLL = True


def roll(x, shift, axis):
    shift = shift % x.shape[axis]
    return x if shift == 0 else pltpu.roll(x, shift, axis)


def pick(material, table):
    value = jnp.full(material.shape, table[NMAT - 1], jnp.float32)
    for i in range(NMAT - 1):
        value = jnp.where(material == i, table[i], value)
    return value


def tile(row):
    return pl.ds(pl.multiple_of(row * SUB, SUB), SUB)


def by_layer(ref, rows, first, t, steps, row):
    return ref[pl.ds((first + t) * rows + row, SUB, stride=steps * rows), :].astype(jnp.float32)


def for_rows(rows, own, above, below, body):
    u_ref, mat_ref, surface_ref = own
    steps = u_ref.shape[0] // rows // SUB
    layers = SUB * steps

    def margin(ref, offset):
        def one(i, carry):
            body(
                i + offset,
                lambda t: by_layer(ref, DEEP, 0, t, steps, i),
                lambda t: by_layer(ref, DEEP, layers, t, steps, i),
                ref[pl.ds(2 * layers * DEEP + i, 1), :],
            )
            return carry

        lax.fori_loop(0, DEEP, one, 0, unroll=8)

    def inner(i, carry):
        body(
            i + DEEP,
            lambda t: by_layer(u_ref, rows, 0, t, steps, i),
            lambda t: by_layer(mat_ref, rows, 0, t, steps, i),
            surface_ref[pl.ds(i, 1), :],
        )
        return carry

    margin(above, 0)
    lax.fori_loop(0, rows, inner, 0, unroll=True)
    margin(below, rows + DEEP)


def pack_kernel(
    u_ref, mat_ref, surface_ref, above_ref, below_ref, first_ref, last_ref, ends, loads
):
    rows = surface_ref.shape[0]
    steps = u_ref.shape[0] // rows // SUB
    lane = iota((SUB, LANES), 1)
    chunk = 2 * DEEP

    def body(row, u, mat, load):
        both = jnp.zeros((SUB, LANES), jnp.float32)
        fields = [u(t) for t in range(steps)] + [mat(t) for t in range(steps)]
        for i, x in enumerate(fields):
            both = jnp.where(lane // chunk == i, roll(x, i * chunk + DEEP, 1), both)
        ends[tile(row), :] = both
        loads[tile(row), :] = jnp.broadcast_to(load, (SUB, LANES))

    for_rows(rows, (u_ref, mat_ref, surface_ref), above_ref, below_ref, body)
    is_last = lane % chunk < DEEP
    half = ends.shape[0] // 2
    for j in range(0, half, SUB):
        low, high = ends[j : j + SUB, :], ends[half + j : half + j + SUB, :]
        first_ref[j : j + SUB, :] = jnp.where(is_last, roll(high, LANES - DEEP, 1), low)
        last_ref[j : j + SUB, :] = jnp.where(is_last, low, roll(high, DEEP, 1))
    sub = iota((SUB, LANES), 0)
    first = jnp.zeros((SUB, LANES), jnp.float32)
    last = first
    tall = loads.shape[0] // SUB
    for i in range(SUB):
        x = first
        for r in range(i, tall, SUB):
            x = jnp.where(sub == r // SUB, loads[r * SUB : (r + 1) * SUB, :], x)
        chosen = lane // chunk == i
        first = jnp.where(chosen, roll(x, i * chunk, 1), first)
        last = jnp.where(chosen, roll(x, i * chunk + DEEP, 1), last)
    first_ref[half:, :] = first
    last_ref[half:, :] = last


def lon_neighbours(near):
    width = near.shape[0]
    apart = iota(near.shape, 0) - iota(near.shape, 1)
    apart = jnp.where(apart < 0, apart + width, apart)
    near[...] = ((apart == 1) | (apart == width - 1)).astype(jnp.float32).astype(HALF)


def run_sweeps(src, offset, a_ref, f_ref, two, near):
    steps = a_ref.shape[0]
    rows = a_ref.shape[2] // SUB - 2 * offset
    for sweep in range(SWEEPS):
        dst = two[sweep % 2]
        shift = offset if sweep == 0 else 0
        size = (rows - 2 - 2 * sweep) // PARTS

        def block(i, carry, src=src, dst=dst, shift=shift, size=size, sweep=sweep):
            first = sweep + 1 + i * size

            def at(row):
                return pl.ds(pl.multiple_of(row * SUB, SUB), size * SUB)

            def tiles(t, c, move):
                return src[t, c, at(first + shift + move), :].reshape(size, SUB, LANES)

            sub = iota((size, SUB, LANES), 1)
            x = [[tiles(t, c, 0) for c in range(2)] for t in range(steps)]
            for t in range(steps):
                both = jnp.concatenate([x[t][c].reshape(size * SUB, LANES) for c in range(2)], axis=1)
                high, low = halves(both)
                beside = dot(high, near[...], NN) + dot(low, near[...], NN)
                for c in range(2):
                    total = beside[:, c * LANES : (c + 1) * LANES].reshape(size, SUB, LANES)
                    total = total + (tiles(t, c, -1) + tiles(t, c, 1))
                    if t > 0:
                        under = x[t - 1][c]
                    else:
                        under = jnp.where(sub == 0, 0.0, roll(x[steps - 1][c], 1, 1))
                    if t < steps - 1:
                        over = x[t + 1][c]
                    else:
                        over = jnp.where(sub == SUB - 1, 0.0, roll(x[0][c], SUB - 1, 1))
                    total = (total + (under + over)).reshape(size * SUB, LANES)
                    value = a_ref[t, c, at(first + offset), :] * total
                    if t < f_ref.shape[0]:
                        value = value + f_ref[t, c, at(first), :]
                    dst[t, c, at(first), :] = value
            return carry

        lax.fori_loop(0, PARTS, block, 0, unroll=UNROLL)
        src = dst


def put_density(mat_ref, contrast, field, index_ref, scratch, pieces):
    lon_count = len(pieces)
    share, rows, _ = pieces[0].shape
    for k in range(lon_count * share):
        material = mat_ref[k * rows : (k + 1) * rows, :]
        scratch[k // share, k % share] = pick(material, contrast) * field(k)
    for s in range(lon_count):
        pieces[s][...] = scratch[lax.rem(index_ref[1] + s, lon_count)]


def layer_of(ref, k, margin, rows):
    steps = ref.shape[0]
    return ref[k % steps, 0, pl.ds(margin * SUB + k // steps, rows, stride=SUB), :]


def first_sweeps_kernel(
    lon_count, total_lat, index_ref, shear_ref, restoring_ref, contrast_ref, u_ref, mat_ref,
    surface_ref, above_ref, below_ref, left_ref, right_ref, *rest,
):
    pieces, rest = rest[:lon_count], rest[lon_count:]
    u_out, a_out, b_out, load_out, first, middle, f_scr, d_scr, near = rest
    rows = surface_ref.shape[0]
    steps = u_out.shape[0]
    a_of, b_of = [], []
    for i in range(NMAT):
        stiff = jnp.full((SUB, LANES), shear_ref[i], jnp.float32)
        restore = jnp.full((SUB, LANES), restoring_ref[i], jnp.float32)
        b_of.append(1.0 / (6.0 * stiff + restore))
        a_of.append(stiff * b_of[i])
    lane = iota((SUB, LANES), 1)
    sub = iota((SUB, LANES), 0)

    half = rows // 2 + DEEP

    def body(row, u, mat, load):
        at = tile(row)
        upper = row >= half
        ends_at = tile(row - jnp.where(upper, half, 0))
        left, right = left_ref[ends_at, :], right_ref[ends_at, :]
        left = jnp.where(upper, roll(left, LANES - DEEP, 1), left)
        right = jnp.where(upper, roll(right, DEEP, 1), right)
        global_row = index_ref[0] * rows - DEEP + row
        inside = ((global_row >= 0) & (global_row < total_lat)).astype(jnp.float32)

        ends = jnp.where(lane % (2 * DEEP) < DEEP, left, right)

        def side(i):
            return roll(ends, LANES - (2 * i + 1) * DEEP, 1)

        load_at = pl.ds(half * SUB + row // SUB, 1)
        place = row % SUB * 2 * DEEP
        after = jnp.broadcast_to(right_ref[load_at, :], (SUB, LANES))
        after = pltpu.roll(after, (LANES - place) % LANES, 1)
        before = jnp.broadcast_to(left_ref[load_at, :], (SUB, LANES))
        before = pltpu.roll(before, (2 * LANES - DEEP - place) % LANES, 1)
        load_side = jnp.where(lane < DEEP, after, before)
        loads = (jnp.broadcast_to(load, (SUB, LANES)), load_side)
        for t in range(steps):
            fields = ((u(t), mat(t)), (side(t), side(steps + t)))
            for c in range(2):
                value, material = fields[c]
                first[t, c, at, :] = value
                a_out[t, c, at, :] = pick(material, a_of) * inside
                b = pick(material, b_of) * inside
                b_out[t, c, at, :] = b
                if t == 0:
                    surface = jnp.where(sub == 0, loads[c], 0.0)
                    load_out[0, c, at, :] = surface
                    f_scr[0, c, at, :] = b * surface

    for_rows(rows, (u_ref, mat_ref, surface_ref), above_ref, below_ref, body)
    lon_neighbours(near)
    run_sweeps(first, 0, a_out, f_scr, (middle, u_out), near)
    put_density(
        mat_ref, contrast_ref, lambda k: layer_of(u_out, k, DEEP, rows), index_ref, d_scr, pieces
    )


def second_sweeps_kernel(
    lon_count, index_ref, contrast_ref, mat_ref, u_ref, a_ref, b_ref, load_ref, *rest
):
    parts, rest = rest[:lon_count], rest[lon_count:]
    pieces, rest = rest[:lon_count], rest[lon_count:]
    field_out, middle, last, f_scr, pot, edge, d_scr, near = rest
    layers, rows, _ = field_out.shape
    steps = u_ref.shape[0]
    tall = rows + 2 * SHALLOW
    share = layers // lon_count
    spread = share // steps
    chunk = LANES // share
    lane = iota((SUB, LANES), 1)
    for s in range(lon_count):
        source = lax.rem(index_ref[1] + (lon_count - s), lon_count)
        for k in range(share):
            at = pl.ds(source * spread + k // steps, tall, stride=SUB)
            pot[k % steps, at, :] = parts[s][k * tall : (k + 1) * tall, :]
        packed = parts[s][share * tall :, :]
        for e in range(spread):
            at = pl.ds(source * spread + e, tall, stride=SUB)
            edge[at, :] = roll(packed, LANES - e * steps * chunk, 1)

    def force(row, carry):
        at, deep = tile(row), tile(row + DEEP - SHALLOW)
        ends = edge[at, :]
        for t in range(steps):
            potential = (pot[t, at, :], roll(ends, LANES - t * chunk - DEEP, 1))
            for c in range(2):
                value = potential[c]
                if t == 0:
                    value = value + load_ref[0, c, deep, :]
                f_scr[t, c, at, :] = b_ref[t, c, deep, :] * value
        return carry

    lax.fori_loop(0, tall, force, 0, unroll=True)
    lon_neighbours(near)
    run_sweeps(u_ref, DEEP - SHALLOW, a_ref, f_scr, (middle, last), near)
    for k in range(layers):
        field_out[k] = layer_of(last, k, SHALLOW, rows)
    put_density(mat_ref, contrast_ref, lambda k: field_out[k], index_ref, d_scr, pieces)


def swap_chunks(blocks, chunk):
    blocks = list(blocks)
    lane = iota(blocks[0].shape, 1)
    step = 1
    while step < len(blocks):
        upper = (lane // (chunk * step)) % 2 == 1
        for i in range(len(blocks)):
            if i & step:
                continue
            a, b = blocks[i], blocks[i + step]
            blocks[i] = jnp.where(upper, roll(b, chunk * step, 1), a)
            blocks[i + step] = jnp.where(upper, b, roll(a, LANES - chunk * step, 1))
        step *= 2
    return blocks


def forward_kernel(lon_count, scale, index_ref, weight_ref, high_ref, low_ref, *rest):
    parts, (o_ref,) = rest[:lon_count], rest[lon_count:]
    share, rows, cols = parts[0].shape
    chunk = LANES // share
    product = None
    for pair in zip(range(0, lon_count, 2), range(1, lon_count, 2)):
        x = jnp.concatenate([parts[s][...].reshape(share * rows, cols) for s in pair], axis=1)
        places = []
        for s in pair:
            source = lax.rem(index_ref[1] + (lon_count - s), lon_count)
            places.append(pl.ds(pl.multiple_of(source * cols, cols), cols))
        tables = [
            jnp.concatenate([ref[at, :] for at in places], axis=0) for ref in (high_ref, low_ref)
        ]
        term = dot3(halves(x), tables, NN)
        product = term if product is None else product + term
    weight = weight_ref[...] * scale
    for g in range(product.shape[1] // LANES):
        blocks = swap_chunks(
            [
                product[k * rows : (k + 1) * rows, g * LANES : (g + 1) * LANES] * weight
                for k in range(share)
            ],
            chunk,
        )
        for i in range(share):
            o_ref[g * share + i] = blocks[i]


def forward_and_turn_kernel(lon_count, scale, size, *refs):
    *inputs, near_ref, far_ref, o_ref, green_ref, ordered = refs
    turn_kernel(size, inputs[0], near_ref, far_ref, green_ref, ordered)
    forward_kernel(lon_count, scale, *inputs, o_ref)


def spectral_kernel(margin, high_ref, low_ref, green_ref, x_ref, o_ref, turned, coeffs, pots):
    share, degrees, width = high_ref.shape
    lat_count, lon_count, rows, _ = x_ref.shape
    total_lat = lat_count * rows
    size = 2 * share
    layers = turned.shape[1] // size
    part = share // 2
    spots = [[m // part * share + c * part + m % part for c in range(2)] for m in range(share)]
    skip = [m // part for m in range(share)]
    used = [slice(first * LANES, degrees) for first in skip]

    def put(ref, m, y):
        first = ref.shape[0] - y.shape[1] // LANES
        for i, r in enumerate(spots[m]):
            put_every(ref.at[first:], r, size, y[i * layers : (i + 1) * layers, :])

    pad = jnp.zeros((width - total_lat, LANES), jnp.float32)
    for q in range(lon_count):
        x = x_ref[:, q].reshape(total_lat, LANES)
        x = jnp.concatenate([x, pad], axis=0)
        for c in range(width // LANES):
            turned[c, q * LANES : (q + 1) * LANES, :] = x[c * LANES : (c + 1) * LANES].T
    for m in range(share):
        x = halves(jnp.concatenate([every(turned, r, size, layers) for r in spots[m]], axis=0))
        y = dot3(x, [ref[m, used[m], :] for ref in (high_ref, low_ref)], NT)
        put(coeffs, m, y)
    block = 8

    def targets(i, carry):
        for c in range(degrees // LANES):
            live = size if c > 0 else share
            sums = [jnp.zeros((live, LANES), jnp.float32) for _ in range(block)]
            for k in range(layers):
                x = coeffs[c, k * size : k * size + live, :]
                for t in range(block):
                    row = green_ref[c, pl.ds((i * block + t) * layers + k, 1), :]
                    sums[t] = sums[t] + row * x
            for t in range(block):
                pots[c, pl.ds(pl.multiple_of((i * block + t) * size, size), live), :] = sums[t]
        return carry

    lax.fori_loop(0, layers // block, targets, 0, unroll=True)
    for m in range(share):
        x = [every(pots.at[skip[m] :], r, size, layers) for r in spots[m]]
        x = halves(jnp.concatenate(x, axis=0))
        y = dot3(x, [ref[m, used[m], :] for ref in (high_ref, low_ref)], NN)
        put(turned, m, y)
    for q in range(lon_count):
        x = [turned[c, q * LANES : (q + 1) * LANES, :].T for c in range(width // LANES)]
        x = jnp.concatenate(x, axis=0)[:total_lat]
        if margin > 0:
            edge = jnp.zeros((margin, LANES), jnp.float32)
            x = jnp.concatenate([edge, x, edge], axis=0)
        for i in range(lat_count):
            o_ref[i, q] = x[i * rows : (i + 1) * rows + 2 * margin]


def inverse_kernel(lon_count, margin, index_ref, high_ref, low_ref, x_ref, *rest):
    pieces, (columns,) = rest[:lon_count], rest[lon_count:]
    owners, rows, _ = x_ref.shape
    cols = high_ref.shape[0] // lon_count
    share = columns.shape[1] // rows
    chunk = LANES // share
    groups = [
        swap_chunks([x_ref[g * share + i] for i in range(share)], chunk)
        for g in range(owners // share)
    ]
    terms = jnp.concatenate(
        [jnp.concatenate([group[k] for group in groups], axis=1) for k in range(share)], axis=0
    )
    terms = halves(terms)
    for q in range(0, lon_count, 2):
        at = slice(q * cols, (q + 2) * cols)
        both = dot3(terms, (high_ref[at, :], low_ref[at, :]), NT)
        columns[q] = both[:, :cols]
        columns[q + 1] = both[:, cols:]
    lane = iota((rows, LANES), 1)
    for s in range(lon_count):
        dest = lax.rem(index_ref[1] + s, lon_count)
        pieces[s][0 : share * rows] = columns[dest]
        if margin == 0:
            continue
        after = lax.rem(dest + 1, lon_count)
        before = lax.rem(dest + lon_count - 1, lon_count)
        packed = jnp.zeros((rows, LANES), jnp.float32)
        for k in range(share):
            at = slice(k * rows, (k + 1) * rows)
            ends = jnp.where(lane < LANES - DEEP, columns[after, at, :], columns[before, at, :])
            packed = jnp.where(lane // chunk == k, roll(ends, k * chunk + DEEP, 1), packed)
        pieces[s][share * rows :] = packed


def assemble_kernel(lon_count, index_ref, *rest):
    parts, o_hbm, sem = rest[:lon_count], rest[lon_count], rest[lon_count + 1]
    sources = [lax.rem(index_ref[1] + (lon_count - s), lon_count) for s in range(lon_count)]
    copy_all(sem, *((part, o_hbm.at[source]) for part, source in zip(parts, sources)))


def exchange(pieces):
    count = len(pieces)
    got = {0: pieces[0]}
    for s in (2, 1, 3) if count == 4 else range(1, count):
        got[s] = lax.ppermute(pieces[s], "lon", [(i, (i + s) % count) for i in range(count)])
    return [got[s] for s in range(count)]


def on_device(displacement, materials, ice_mask, ice_height, shear, restoring, contrast, green):
    layers, rows, cols = displacement.shape
    lat_count, lon_count = lax.axis_size("lat"), lax.axis_size("lon")
    total_lat, total_lon = rows * lat_count, cols * lon_count
    owners = lat_count * lon_count
    share, orders = layers // lon_count, LMAX // owners
    width = -(-total_lat // LANES) * LANES
    tall = rows + 2 * SHALLOW
    lat_index = lax.axis_index("lat")
    index = jnp.stack([lat_index, lax.axis_index("lon")]).astype(jnp.int32)
    owner = (index[0] * lon_count + index[1])[None]

    surface = ice_mask.astype(jnp.float32) * ice_height
    own = (
        displacement.reshape(layers * rows, cols),
        materials.reshape(layers * rows, cols),
        surface,
    )
    first, last = call(
        slab_kernel,
        (f32(2 * layers + 1, DEEP, cols),) * 2,
        1.0,
    )(displacement, materials, surface)
    green, first, last = lax.optimization_barrier((green, first, last))
    first, last = (x.reshape(-1, cols) for x in (first, last))
    above = lax.ppermute(last, "lat", [(i, i + 1) for i in range(lat_count - 1)])
    below = lax.ppermute(first, "lat", [(i + 1, i) for i in range(lat_count - 1)])
    table = call(
        functools.partial(fourier_kernel, total_lon, orders),
        (jax.ShapeDtypeStruct((total_lon, 2 * LMAX), HALF),) * 2,
        1.2,
    )()
    def partner(x, step):
        return lax.ppermute(x, "lat", [(i, i ^ step) for i in range(lat_count)])

    near = green.reshape(green.shape[0], layers * layers)
    near, table = lax.optimization_barrier((near, table))
    others = [partner(near, i) for i in range(2, lat_count, 2)]
    half_table = (orders, LMAX, width)
    legendre_table = call(
        functools.partial(legendre_kernel, total_lat, orders),
        (jax.ShapeDtypeStruct(half_table, HALF),) * 2,
        2.9,
        scratch=[pltpu.VMEM((width // LANES, LMAX * orders, LANES), jnp.float32)],
        smem=(0,),
    )(owner)
    above, below, others, table, legendre_table = lax.optimization_barrier(
        (above, below, others, table, legendre_table)
    )
    near = jnp.concatenate([near, *others], axis=0)
    far = partner(near, 1)
    deep = rows + 2 * DEEP
    edge_tiles = f32((deep // 2 + 1) * SUB, cols)
    whole = pltpu.VMEM((deep * SUB, cols), jnp.float32)
    first, last = call(pack_kernel, (edge_tiles,) * 2, 1.5, scratch=[whole, whole])(
        *own, above, below
    )
    left = lax.ppermute(last, "lon", [(i, (i + 1) % lon_count) for i in range(lon_count)])
    right = lax.ppermute(first, "lon", [((i + 1) % lon_count, i) for i in range(lon_count)])
    theta = ((lat_index * rows + jnp.arange(rows)).astype(jnp.float32) + 0.5) * (
        jnp.pi / total_lat
    )
    weight = jnp.broadcast_to((jnp.sin(theta) / (4.0 * total_lat))[:, None], (rows, LANES))

    steps = layers // SUB

    def worked(t, height):
        return (t, 2, height * SUB, LANES)

    flat = pltpu.VMEM((lon_count, share, rows, cols), jnp.float32)
    near_shape = pltpu.VMEM((2 * LANES, 2 * LANES), HALF)
    out = call(
        functools.partial(first_sweeps_kernel, lon_count, total_lat),
        (f32(share, rows, cols),) * lon_count
        + (f32(*worked(steps, deep)),) * 3
        + (f32(*worked(1, deep)),),
        6.6,
        scratch=[pltpu.VMEM(worked(steps, deep), jnp.float32)] * 2
        + [pltpu.VMEM(worked(1, deep), jnp.float32), flat, near_shape],
        smem=(0, 1, 2, 3),
    )(index, shear, restoring, contrast, *own, above, below, left, right)
    pieces, state = out[:lon_count], out[lon_count:]
    for iteration in range(ITERS):
        margin = SHALLOW if iteration < ITERS - 1 else 0
        parts = exchange(pieces)
        scale = 2.0 * math.pi / total_lon
        if iteration == 0:
            spectrum, turned_green = call(
                functools.partial(forward_and_turn_kernel, lon_count, scale, green.shape[0]),
                (
                    f32(owners, rows, LANES),
                    f32(LMAX // LANES, layers * layers, LANES),
                ),
                3.0,
                scratch=[pltpu.VMEM((LMAX, layers * layers), jnp.float32)],
                smem=(0,),
            )(index, weight, *table, *parts, near, far)
        else:
            spectrum = call(
                functools.partial(forward_kernel, lon_count, scale),
                f32(owners, rows, LANES),
                2.0,
                smem=(0,),
            )(index, weight, *table, *parts)
        spectrum = lax.all_to_all(spectrum, BOTH, 0, 0, tiled=True)
        square = pltpu.VMEM((width // LANES, lon_count * LANES, LANES), jnp.float32)
        coeff_shape = pltpu.VMEM((LMAX // LANES, lon_count * LANES, LANES), jnp.float32)
        synth = call(
            functools.partial(spectral_kernel, margin),
            f32(lat_count, lon_count, rows + 2 * margin, LANES),
            4.0,
            scratch=[square, coeff_shape, coeff_shape],
        )(
            *legendre_table,
            turned_green,
            spectrum.reshape(lat_count, lon_count, rows, LANES),
        )
        synth = lax.all_to_all(
            synth.reshape(owners, rows + 2 * margin, LANES), BOTH, 0, 0, tiled=True
        )
        high = rows + 2 * margin
        sent = share * high + (high if margin > 0 else 0)
        parts = call(
            functools.partial(inverse_kernel, lon_count, margin),
            (f32(sent, cols),) * lon_count,
            2.0,
            scratch=[pltpu.VMEM((lon_count, share * high, cols), jnp.float32)],
            smem=(0,),
        )(index, *table, synth)
        parts = exchange(parts)
        if iteration < ITERS - 1:
            out = call(
                functools.partial(second_sweeps_kernel, lon_count),
                (f32(share, rows, cols),) * lon_count + (f32(layers, rows, cols),),
                5.4,
                scratch=[pltpu.VMEM(worked(steps, tall), jnp.float32)] * 3
                + [
                    pltpu.VMEM((steps, tall * SUB, LANES), jnp.float32),
                    pltpu.VMEM((tall * SUB, LANES), jnp.float32),
                    flat,
                    near_shape,
                ],
                smem=(0, 1),
            )(index, contrast, own[1], *state, *parts)
            pieces, field = out[:lon_count], out[lon_count]
    potential = call(
        functools.partial(assemble_kernel, lon_count),
        f32(lon_count, share * rows, cols),
        1.0,
        scratch=[pltpu.SemaphoreType.DMA((lon_count,))],
        smem=(0,),
        hbm=(0,),
    )(index, *parts)
    return (field, potential.reshape(layers, rows, cols))


def aligned(mesh, displacement):
    lat_count, lon_count = mesh.shape["lat"], mesh.shape["lon"]
    layers, total_lat, total_lon = displacement.shape
    rows, cols = total_lat // lat_count, total_lon // lon_count
    owners = lat_count * lon_count
    return (
        ITERS == 2
        and cols == LANES
        and rows % 8 == 0
        and rows + 2 * DEEP <= SUB * SUB
        and layers % SUB == 0
        and 2 * (layers // SUB) * 2 * DEEP <= LANES
        and (layers // lon_count) % (layers // SUB) == 0
        and lat_count > 2
        and lon_count % 2 == 0
        and lat_count & (lat_count - 1) == 0
        and layers % lon_count == 0
        and LMAX % owners == 0
        and 2 * (LMAX // owners) * (layers // lon_count) == LANES
        and 2 * (LMAX // owners) == 2 * DEEP
        and LMAX == 2 * LANES
    )


def solution(mesh):
    in_specs = (
        P(None, "lat", "lon"),
        P(None, "lat", "lon"),
        P("lat", "lon"),
        P("lat", "lon"),
        P(),
        P(),
        P(),
        P("lat", None, None),
    )
    out_specs = (P(None, "lat", "lon"), P(None, "lat", "lon"))

    def step(displacement, *others):
        device = on_device if aligned(mesh, displacement) else general_device
        return jax.shard_map(
            device, mesh=mesh, in_specs=in_specs, out_specs=out_specs, check_vma=False
        )(displacement, *others)

    return step
```

```python
import functools
import math

import jax
import jax.numpy as jnp
from jax import lax
from jax.experimental import pallas as pl
from jax.experimental.pallas import tpu as pltpu
from jax.sharding import PartitionSpec as P

LMAX = 256
NMAT = 4
ITERS = 2
SWEEPS = 4
LANES = 128
DEEP = 8
SHALLOW = 4
HALF = jnp.bfloat16
VMEM_LIMIT = 16 * 1024 * 1024
BOTH = ("lat", "lon")


def extended(cells, sides, width, closed):
    for axis, dim in sides:
        count = lax.axis_size(axis)
        ends = count if closed else count - 1
        head = lax.slice_in_dim(cells, 0, width, axis=dim)
        tail = lax.slice_in_dim(cells, cells.shape[dim] - width, cells.shape[dim], axis=dim)
        cells = jnp.concatenate(
            [
                lax.ppermute(tail, axis, [(i, (i + 1) % count) for i in range(ends)]),
                cells,
                lax.ppermute(head, axis, [((i + 1) % count, i) for i in range(ends)]),
            ],
            axis=dim,
        )
    return cells


def legendre(theta):
    orders = jnp.arange(LMAX)
    order_f = orders.astype(jnp.float32)
    cosine = jnp.cos(theta)[:, None]
    sine = jnp.sin(theta)[:, None]
    safe = jnp.maximum(order_f, 1.0)
    growth = jnp.where(orders >= 2, 0.5 * jnp.log((2.0 * safe + 1.0) / (2.0 * safe)), 0.0)
    log_diag = jnp.where(orders >= 1, 0.5 * jnp.log(3.0) + jnp.cumsum(growth), 0.0)
    diagonal = jnp.exp(log_diag[None, :] + order_f[None, :] * jnp.log(sine))

    def advance(carry, degree):
        prev_one, prev_two = carry
        deg_f = degree.astype(jnp.float32)
        first = jnp.sqrt(
            (4.0 * deg_f * deg_f - 1.0) / jnp.maximum(deg_f * deg_f - order_f * order_f, 1.0)
        )
        second = jnp.sqrt(
            jnp.maximum((deg_f - 1.0) ** 2 - order_f * order_f, 0.0)
            / jnp.maximum(4.0 * (deg_f - 1.0) ** 2 - 1.0, 1.0)
        )
        general = first * (cosine * prev_one - second * prev_two)
        start_next = jnp.sqrt(2.0 * order_f + 3.0) * cosine * diagonal
        value = jnp.where(
            orders == degree,
            diagonal,
            jnp.where(
                orders == degree - 1, start_next, jnp.where(orders < degree - 1, general, 0.0)
            ),
        )
        return ((value, prev_one), value)

    zeros = jnp.zeros((theta.shape[0], LMAX), jnp.float32)
    _, table = lax.scan(advance, (zeros, zeros), jnp.arange(LMAX), unroll=8)
    return table


def fourier_tables(columns, total):
    orders = jnp.arange(LMAX)
    phase = columns[:, None] * orders[None, :] % total
    angle = 2.0 * jnp.pi / total * phase.astype(jnp.float32)
    forward = jnp.concatenate([jnp.cos(angle), jnp.sin(angle)], axis=1) * (2.0 * jnp.pi / total)
    inverse = jnp.concatenate([jnp.cos(angle), jnp.sin(angle)], axis=1).T
    return (forward, inverse)


def lookup(materials, table):
    result = jnp.zeros(materials.shape, jnp.float32)
    for material in range(NMAT):
        result = result + jnp.where(materials == material, table[material], 0.0)
    return result


def crop_block(block, margin):
    return block[:, margin : block.shape[1] - margin, margin : block.shape[2] - margin]


def margin_sweeps(field, force, stiff, restore, depth, lat_first, total_lat):
    stacked = jnp.stack([field, force, stiff, restore], axis=0)
    lat_wide = extended(stacked, (("lat", 2),), depth, False)
    wide = extended(lat_wide, (("lon", 3),), depth, True)
    current = wide[0]
    rows_wide = wide.shape[2]
    global_rows = lat_first - depth + jnp.arange(rows_wide)
    inside = ((global_rows >= 0) & (global_rows < total_lat))[None, :, None]
    for step in range(depth):
        margin = step + 1
        inner = current[:, 1:-1, 1:-1]
        beside_all = (
            current[:, 2:, 1:-1]
            + current[:, :-2, 1:-1]
            + current[:, 1:-1, 2:]
            + current[:, 1:-1, :-2]
        )
        layer_pad = jnp.pad(inner, ((1, 1), (0, 0), (0, 0)))
        beside_all = beside_all + layer_pad[2:] + layer_pad[:-2]
        force_part = crop_block(wide[1], margin)
        stiff_part = crop_block(wide[2], margin)
        restore_part = crop_block(wide[3], margin)
        valid = inside[:, margin : rows_wide - margin, :]
        denominator = jnp.where(valid, 6.0 * stiff_part + restore_part, 1.0)
        current = jnp.where(valid, (force_part + stiff_part * beside_all) / denominator, 0.0)
    return current


def general_device(displacement, materials, ice_mask, ice_height, shear, restoring, contrast, green):
    highest = lax.Precision.HIGHEST
    layers, lat_rows, lon_cols = displacement.shape
    lon_count = lax.axis_size("lon")
    lat_count = lax.axis_size("lat")
    total_lat = lat_rows * lat_count
    total_lon = lon_cols * lon_count
    layer_share = layers // lon_count
    stiff = lookup(materials, shear)
    restore = lookup(materials, restoring)
    rho_scale = lookup(materials, contrast)
    surface = (ice_mask.astype(jnp.float32) * ice_height)[None]
    load = jnp.concatenate(
        [surface, jnp.zeros((layers - 1, lat_rows, lon_cols), jnp.float32)], axis=0
    )
    lat_first = lax.axis_index("lat") * lat_rows
    theta = ((lat_first + jnp.arange(lat_rows)).astype(jnp.float32) + 0.5) * (jnp.pi / total_lat)
    table = legendre(theta)
    weights = jnp.sin(theta) / (4.0 * total_lat)
    own_columns = lax.axis_index("lon") * lon_cols + jnp.arange(lon_cols)
    layer_first = lax.axis_index("lon") * layer_share
    depth = 1
    for candidate in range(1, SWEEPS + 1):
        if SWEEPS % candidate == 0 and candidate <= min(lat_rows, lon_cols):
            depth = candidate
    forward, inverse = fourier_tables(own_columns, total_lon)
    field = displacement
    potential = jnp.zeros((layers, lat_rows, lon_cols), jnp.float32)
    for iteration in range(ITERS):
        force = load + potential
        field = margin_sweeps(field, force, stiff, restore, depth, lat_first, total_lat)
        density = rho_scale * field
        product = jnp.dot(
            density.reshape(layer_share * lax.axis_size("lon") * lat_rows, lon_cols),
            forward,
            precision=highest,
            preferred_element_type=jnp.float32,
        )
        spectrum = lax.psum_scatter(
            product.reshape(layer_share * lax.axis_size("lon"), lat_rows, 2 * LMAX),
            "lon",
            scatter_dimension=0,
            tiled=True,
        )
        weighted = spectrum.reshape(layer_share, lat_rows, 2, LMAX) * weights[None, :, None, None]
        coeffs = lax.psum_scatter(
            jnp.einsum("lam,kacm->lkcm", table, weighted, precision=highest),
            "lat",
            scatter_dimension=0,
            tiled=True,
        )
        green_part = lax.dynamic_slice_in_dim(green, layer_first, layer_share, 2)
        partial_pot = jnp.einsum("lkj,ljcm->lkcm", green_part, coeffs, precision=highest)
        pot_coeffs = lax.psum_scatter(partial_pot, "lon", scatter_dimension=1, tiled=True)
        synth = jnp.einsum(
            "lam,lkcm->kacm",
            table,
            lax.all_gather(pot_coeffs, "lat", axis=0, tiled=True),
            precision=highest,
        )
        synth = synth.reshape(layer_share, lat_rows, 2 * LMAX)
        piece = lax.all_gather(synth, "lon", axis=0, tiled=True)
        synth_product = jnp.dot(
            piece.reshape(piece.shape[0] * lat_rows, 2 * LMAX),
            inverse,
            precision=highest,
            preferred_element_type=jnp.float32,
        )
        potential = synth_product.reshape(piece.shape[0], lat_rows, lon_cols)
    return (field, potential)


def call(kernel, outs, micros, scratch=(), smem=(), far=(), hbm=()):
    def place(i, scalars, away):
        space = pltpu.SMEM if i in scalars else pltpu.HBM if i in away else pltpu.VMEM
        return pl.BlockSpec(memory_space=space)

    def run(*args):
        return pl.pallas_call(
            kernel,
            out_shape=outs,
            in_specs=[place(i, smem, far) for i in range(len(args))],
            out_specs=tuple(place(i, (), hbm) for i in range(len(outs)))
            if type(outs) is tuple
            else place(0, (), hbm),
            scratch_shapes=list(scratch),
            compiler_params=pltpu.CompilerParams(vmem_limit_bytes=VMEM_LIMIT),
            cost_estimate=pl.CostEstimate(
                flops=int(micros * 1e9), bytes_accessed=1, transcendentals=0
            ),
        )(*args)

    return run


def copy_all(sem, *pairs):
    copies = [pltpu.make_async_copy(*pair, sem.at[i]) for i, pair in enumerate(pairs)]
    for copy in copies:
        copy.start()
    for copy in copies:
        copy.wait()


def f32(*shape):
    return jax.ShapeDtypeStruct(shape, jnp.float32)


def halves(x):
    high = x.astype(HALF)
    return high, (x - high.astype(jnp.float32)).astype(HALF)


def dot(a, b, dims):
    return lax.dot_general(a, b, (dims, ((), ())), preferred_element_type=jnp.float32)


def dot3(a, b, dims):
    rows = a[0].shape[0]
    both = dot(jnp.concatenate(a, axis=0), b[0], dims)
    return both[:rows] + (both[rows:] + dot(a[0], b[1], dims))


def every(ref, start, stride, count):
    at = pl.ds(start, count, stride=stride)
    return jnp.concatenate([ref[c, at, :] for c in range(ref.shape[0])], axis=1)


def put_every(ref, start, stride, value):
    at = pl.ds(start, value.shape[0], stride=stride)
    for c in range(ref.shape[0]):
        ref[c, at, :] = value[:, c * LANES : (c + 1) * LANES]


NN = ((1,), (0,))
NT = ((1,), (1,))


def iota(shape, dim):
    return lax.broadcasted_iota(jnp.int32, shape, dim)


def fourier_kernel(total, share, high_ref, low_ref):
    shape = (16, 2 * LMAX)
    column = iota(shape, 1)
    part = share // 2
    order = column // share % 2 * (LMAX // 2) + column // (2 * share) * part + column % part
    shift = column // part % 2 * (total - total // 4)
    first = iota(shape, 0) * order + shift
    quarter, half = total // 4, total // 2

    def block(i, carry):
        phase = first + order * (i * shape[0])
        phase = phase & (total - 1) if total & (total - 1) == 0 else lax.rem(phase, total)
        near = jnp.minimum(phase, total - phase)
        beyond = near > quarter
        angle = jnp.where(beyond, half - near, near).astype(jnp.float32) * (2.0 * math.pi / total)
        square = angle * angle
        value = jnp.full(shape, 1.0 / math.factorial(14), jnp.float32)
        for n in range(12, -1, -2):
            value = 1.0 / math.factorial(n) - square * value
        high, low = halves(jnp.where(beyond, -value, value))
        at = pl.ds(pl.multiple_of(i * shape[0], shape[0]), shape[0])
        high_ref[at, :] = high
        low_ref[at, :] = low
        return carry

    lax.fori_loop(0, total // shape[0], block, 0, unroll=2)


def legendre_kernel(total_lat, share, index_ref, high_ref, low_ref, table):
    width = table.shape[0] * LANES
    part = share // 2
    shape = (share, width)

    def orders(shape):
        i = iota(shape, 0)
        return i // part * (LMAX // 2) + index_ref[0] * part + i % part

    order = orders(shape)
    order_f = order.astype(jnp.float32)
    row = iota(shape, 1)
    theta = (row.astype(jnp.float32) + 0.5) * (math.pi / total_lat)
    cosine = jnp.cos(theta)
    sine = jnp.where(row < total_lat, jnp.sin(theta), 1.0)
    terms = (share, LMAX)
    term = iota(terms, 1)
    term_f = jnp.maximum(term.astype(jnp.float32), 1.0)
    growth = 0.5 * jnp.log((2.0 * term_f + 1.0) / (2.0 * term_f))
    used = (term >= 2) & (term <= orders(terms))
    total = jnp.sum(jnp.where(used, growth, 0.0), axis=1, keepdims=True)
    log_diag = jnp.where(order >= 1, 0.5 * math.log(3.0) + total, 0.0)
    diagonal = jnp.exp(log_diag + order_f * jnp.log(sine))
    diagonal = jnp.where(row < total_lat, diagonal, 0.0)
    start_next = jnp.sqrt(2.0 * order_f + 3.0) * cosine * diagonal
    narrow = (share, LANES)
    square = orders(narrow).astype(jnp.float32) ** 2

    def wide(x):
        return jnp.concatenate([x] * (width // LANES), axis=1)

    def advance(degree, carry):
        prev_one, prev_two = carry
        deg = jnp.full(narrow, degree, jnp.int32).astype(jnp.float32)
        first = jnp.sqrt((4.0 * deg * deg - 1.0) / jnp.maximum(deg * deg - square, 1.0))
        below = (deg - 1.0) * (deg - 1.0)
        second = jnp.sqrt(jnp.maximum(below - square, 0.0) / jnp.maximum(4.0 * below - 1.0, 1.0))
        general = wide(first) * (cosine * prev_one - wide(second) * prev_two)
        value = jnp.where(
            order == degree,
            diagonal,
            jnp.where(
                order == degree - 1, start_next, jnp.where(order < degree - 1, general, 0.0)
            ),
        )
        for c in range(width // LANES):
            at = pl.ds(pl.multiple_of(degree * share, share), share)
            table[c, at, :] = value[:, c * LANES : (c + 1) * LANES]
        return (value, prev_one)

    table[:, 0:share, :] = jnp.zeros((width // LANES, share, LANES), jnp.float32)
    zeros = jnp.concatenate([table[c, 0:share, :] for c in range(width // LANES)], axis=1)
    lax.fori_loop(0, LMAX, advance, (zeros, zeros), unroll=8)
    for m in range(share):
        high, low = halves(every(table, m, share, LMAX))
        high_ref[m] = high
        low_ref[m] = low


def turn_kernel(size, index_ref, near_ref, far_ref, o_ref, ordered):
    count = 2 * near_ref.shape[0] // size
    for i in range(count):
        partner = 2 * i if 2 * i < count else 2 * i - count + 1
        block = near_ref if 2 * i < count else far_ref
        first = i % (count // 2) * size
        at = pl.ds(pl.multiple_of((index_ref[0] ^ partner) * size, size), size)
        ordered[at, :] = block[first : first + size, :]
    for c in range(o_ref.shape[0]):
        o_ref[c] = ordered[c * LANES : (c + 1) * LANES, :].T


def slab_kernel(u_ref, mat_ref, surface_ref, first_ref, last_ref):
    layers, rows, _ = u_ref.shape
    for ref, at in ((first_ref, pl.ds(0, DEEP)), (last_ref, pl.ds(rows - DEEP, DEEP))):
        for k in range(layers):
            ref[k] = u_ref[k, at, :]
            ref[layers + k] = mat_ref[k, at, :].astype(jnp.float32)
        ref[2 * layers] = surface_ref[at, :]


SUB = 8
PARTS = 1
UNROLL = True


def roll(x, shift, axis):
    shift = shift % x.shape[axis]
    return x if shift == 0 else pltpu.roll(x, shift, axis)


def pick(material, table):
    value = jnp.full(material.shape, table[NMAT - 1], jnp.float32)
    for i in range(NMAT - 1):
        value = jnp.where(material == i, table[i], value)
    return value


def tile(row):
    return pl.ds(pl.multiple_of(row * SUB, SUB), SUB)


def by_layer(ref, rows, first, t, steps, row):
    return ref[pl.ds((first + t) * rows + row, SUB, stride=steps * rows), :].astype(jnp.float32)


def for_rows(rows, own, above, below, body):
    u_ref, mat_ref, surface_ref = own
    steps = u_ref.shape[0] // rows // SUB
    layers = SUB * steps

    def margin(ref, offset):
        def one(i, carry):
            body(
                i + offset,
                lambda t: by_layer(ref, DEEP, 0, t, steps, i),
                lambda t: by_layer(ref, DEEP, layers, t, steps, i),
                ref[pl.ds(2 * layers * DEEP + i, 1), :],
            )
            return carry

        lax.fori_loop(0, DEEP, one, 0, unroll=8)

    def inner(i, carry):
        body(
            i + DEEP,
            lambda t: by_layer(u_ref, rows, 0, t, steps, i),
            lambda t: by_layer(mat_ref, rows, 0, t, steps, i),
            surface_ref[pl.ds(i, 1), :],
        )
        return carry

    margin(above, 0)
    lax.fori_loop(0, rows, inner, 0, unroll=True)
    margin(below, rows + DEEP)


def pack_kernel(
    u_ref, mat_ref, surface_ref, above_ref, below_ref, first_ref, last_ref, ends, loads
):
    rows = surface_ref.shape[0]
    steps = u_ref.shape[0] // rows // SUB
    lane = iota((SUB, LANES), 1)
    chunk = 2 * DEEP

    def body(row, u, mat, load):
        both = jnp.zeros((SUB, LANES), jnp.float32)
        fields = [u(t) for t in range(steps)] + [mat(t) for t in range(steps)]
        for i, x in enumerate(fields):
            both = jnp.where(lane // chunk == i, roll(x, i * chunk + DEEP, 1), both)
        ends[tile(row), :] = both
        loads[tile(row), :] = jnp.broadcast_to(load, (SUB, LANES))

    for_rows(rows, (u_ref, mat_ref, surface_ref), above_ref, below_ref, body)
    is_last = lane % chunk < DEEP
    half = ends.shape[0] // 2
    for j in range(0, half, SUB):
        low, high = ends[j : j + SUB, :], ends[half + j : half + j + SUB, :]
        first_ref[j : j + SUB, :] = jnp.where(is_last, roll(high, LANES - DEEP, 1), low)
        last_ref[j : j + SUB, :] = jnp.where(is_last, low, roll(high, DEEP, 1))
    sub = iota((SUB, LANES), 0)
    first = jnp.zeros((SUB, LANES), jnp.float32)
    last = first
    tall = loads.shape[0] // SUB
    for i in range(SUB):
        x = first
        for r in range(i, tall, SUB):
            x = jnp.where(sub == r // SUB, loads[r * SUB : (r + 1) * SUB, :], x)
        chosen = lane // chunk == i
        first = jnp.where(chosen, roll(x, i * chunk, 1), first)
        last = jnp.where(chosen, roll(x, i * chunk + DEEP, 1), last)
    first_ref[half:, :] = first
    last_ref[half:, :] = last


def lon_neighbours(near):
    width = near.shape[0]
    apart = iota(near.shape, 0) - iota(near.shape, 1)
    apart = jnp.where(apart < 0, apart + width, apart)
    near[...] = ((apart == 1) | (apart == width - 1)).astype(jnp.float32).astype(HALF)


def run_sweeps(src, offset, a_ref, f_ref, two, near):
    steps = a_ref.shape[0]
    rows = a_ref.shape[2] // SUB - 2 * offset
    for sweep in range(SWEEPS):
        dst = two[sweep % 2]
        shift = offset if sweep == 0 else 0
        size = (rows - 2 - 2 * sweep) // PARTS

        def block(i, carry, src=src, dst=dst, shift=shift, size=size, sweep=sweep):
            first = sweep + 1 + i * size

            def at(row):
                return pl.ds(pl.multiple_of(row * SUB, SUB), size * SUB)

            def tiles(t, c, move):
                return src[t, c, at(first + shift + move), :].reshape(size, SUB, LANES)

            sub = iota((size, SUB, LANES), 1)
            x = [[tiles(t, c, 0) for c in range(2)] for t in range(steps)]
            for t in range(steps):
                both = jnp.concatenate([x[t][c].reshape(size * SUB, LANES) for c in range(2)], axis=1)
                high, low = halves(both)
                beside = dot(high, near[...], NN) + dot(low, near[...], NN)
                for c in range(2):
                    total = beside[:, c * LANES : (c + 1) * LANES].reshape(size, SUB, LANES)
                    total = total + (tiles(t, c, -1) + tiles(t, c, 1))
                    if t > 0:
                        under = x[t - 1][c]
                    else:
                        under = jnp.where(sub == 0, 0.0, roll(x[steps - 1][c], 1, 1))
                    if t < steps - 1:
                        over = x[t + 1][c]
                    else:
                        over = jnp.where(sub == SUB - 1, 0.0, roll(x[0][c], SUB - 1, 1))
                    total = (total + (under + over)).reshape(size * SUB, LANES)
                    value = a_ref[t, c, at(first + offset), :] * total
                    if t < f_ref.shape[0]:
                        value = value + f_ref[t, c, at(first), :]
                    dst[t, c, at(first), :] = value
            return carry

        lax.fori_loop(0, PARTS, block, 0, unroll=UNROLL)
        src = dst


def put_density(mat_ref, contrast, field, index_ref, scratch, pieces):
    lon_count = len(pieces)
    share, rows, _ = pieces[0].shape
    for k in range(lon_count * share):
        material = mat_ref[k * rows : (k + 1) * rows, :]
        scratch[k // share, k % share] = pick(material, contrast) * field(k)
    for s in range(lon_count):
        pieces[s][...] = scratch[lax.rem(index_ref[1] + s, lon_count)]


def layer_of(ref, k, margin, rows):
    steps = ref.shape[0]
    return ref[k % steps, 0, pl.ds(margin * SUB + k // steps, rows, stride=SUB), :]


def first_sweeps_kernel(
    lon_count, total_lat, index_ref, shear_ref, restoring_ref, contrast_ref, u_ref, mat_ref,
    surface_ref, above_ref, below_ref, left_ref, right_ref, *rest,
):
    pieces, rest = rest[:lon_count], rest[lon_count:]
    u_out, a_out, b_out, load_out, first, middle, f_scr, d_scr, near = rest
    rows = surface_ref.shape[0]
    steps = u_out.shape[0]
    a_of, b_of = [], []
    for i in range(NMAT):
        stiff = jnp.full((SUB, LANES), shear_ref[i], jnp.float32)
        restore = jnp.full((SUB, LANES), restoring_ref[i], jnp.float32)
        b_of.append(1.0 / (6.0 * stiff + restore))
        a_of.append(stiff * b_of[i])
    lane = iota((SUB, LANES), 1)
    sub = iota((SUB, LANES), 0)

    half = rows // 2 + DEEP

    def body(row, u, mat, load):
        at = tile(row)
        upper = row >= half
        ends_at = tile(row - jnp.where(upper, half, 0))
        left, right = left_ref[ends_at, :], right_ref[ends_at, :]
        left = jnp.where(upper, roll(left, LANES - DEEP, 1), left)
        right = jnp.where(upper, roll(right, DEEP, 1), right)
        global_row = index_ref[0] * rows - DEEP + row
        inside = ((global_row >= 0) & (global_row < total_lat)).astype(jnp.float32)

        ends = jnp.where(lane % (2 * DEEP) < DEEP, left, right)

        def side(i):
            return roll(ends, LANES - (2 * i + 1) * DEEP, 1)

        load_at = pl.ds(half * SUB + row // SUB, 1)
        place = row % SUB * 2 * DEEP
        after = jnp.broadcast_to(right_ref[load_at, :], (SUB, LANES))
        after = pltpu.roll(after, (LANES - place) % LANES, 1)
        before = jnp.broadcast_to(left_ref[load_at, :], (SUB, LANES))
        before = pltpu.roll(before, (2 * LANES - DEEP - place) % LANES, 1)
        load_side = jnp.where(lane < DEEP, after, before)
        loads = (jnp.broadcast_to(load, (SUB, LANES)), load_side)
        for t in range(steps):
            fields = ((u(t), mat(t)), (side(t), side(steps + t)))
            for c in range(2):
                value, material = fields[c]
                first[t, c, at, :] = value
                a_out[t, c, at, :] = pick(material, a_of) * inside
                b = pick(material, b_of) * inside
                b_out[t, c, at, :] = b
                if t == 0:
                    surface = jnp.where(sub == 0, loads[c], 0.0)
                    load_out[0, c, at, :] = surface
                    f_scr[0, c, at, :] = b * surface

    for_rows(rows, (u_ref, mat_ref, surface_ref), above_ref, below_ref, body)
    lon_neighbours(near)
    run_sweeps(first, 0, a_out, f_scr, (middle, u_out), near)
    put_density(
        mat_ref, contrast_ref, lambda k: layer_of(u_out, k, DEEP, rows), index_ref, d_scr, pieces
    )


def second_sweeps_kernel(
    lon_count, index_ref, contrast_ref, mat_ref, u_ref, a_ref, b_ref, load_ref, *rest
):
    parts, rest = rest[:lon_count], rest[lon_count:]
    pieces, rest = rest[:lon_count], rest[lon_count:]
    field_out, middle, last, f_scr, pot, edge, d_scr, near = rest
    layers, rows, _ = field_out.shape
    steps = u_ref.shape[0]
    tall = rows + 2 * SHALLOW
    share = layers // lon_count
    spread = share // steps
    chunk = LANES // share
    lane = iota((SUB, LANES), 1)
    for s in range(lon_count):
        source = lax.rem(index_ref[1] + (lon_count - s), lon_count)
        for k in range(share):
            at = pl.ds(source * spread + k // steps, tall, stride=SUB)
            pot[k % steps, at, :] = parts[s][k * tall : (k + 1) * tall, :]
        packed = parts[s][share * tall :, :]
        for e in range(spread):
            at = pl.ds(source * spread + e, tall, stride=SUB)
            edge[at, :] = roll(packed, LANES - e * steps * chunk, 1)

    def force(row, carry):
        at, deep = tile(row), tile(row + DEEP - SHALLOW)
        ends = edge[at, :]
        for t in range(steps):
            potential = (pot[t, at, :], roll(ends, LANES - t * chunk - DEEP, 1))
            for c in range(2):
                value = potential[c]
                if t == 0:
                    value = value + load_ref[0, c, deep, :]
                f_scr[t, c, at, :] = b_ref[t, c, deep, :] * value
        return carry

    lax.fori_loop(0, tall, force, 0, unroll=True)
    lon_neighbours(near)
    run_sweeps(u_ref, DEEP - SHALLOW, a_ref, f_scr, (middle, last), near)
    for k in range(layers):
        field_out[k] = layer_of(last, k, SHALLOW, rows)
    put_density(mat_ref, contrast_ref, lambda k: field_out[k], index_ref, d_scr, pieces)


def swap_chunks(blocks, chunk):
    blocks = list(blocks)
    lane = iota(blocks[0].shape, 1)
    step = 1
    while step < len(blocks):
        upper = (lane // (chunk * step)) % 2 == 1
        for i in range(len(blocks)):
            if i & step:
                continue
            a, b = blocks[i], blocks[i + step]
            blocks[i] = jnp.where(upper, roll(b, chunk * step, 1), a)
            blocks[i + step] = jnp.where(upper, b, roll(a, LANES - chunk * step, 1))
        step *= 2
    return blocks


def forward_kernel(lon_count, scale, index_ref, weight_ref, high_ref, low_ref, *rest):
    parts, (o_ref,) = rest[:lon_count], rest[lon_count:]
    share, rows, cols = parts[0].shape
    chunk = LANES // share
    x = jnp.concatenate([part[...].reshape(share * rows, cols) for part in parts], axis=1)
    places = []
    for s in range(lon_count):
        source = lax.rem(index_ref[1] + (lon_count - s), lon_count)
        places.append(pl.ds(pl.multiple_of(source * cols, cols), cols))
    tables = [jnp.concatenate([ref[at, :] for at in places], axis=0) for ref in (high_ref, low_ref)]
    product = dot3(halves(x), tables, NN)
    weight = weight_ref[...] * scale
    for g in range(product.shape[1] // LANES):
        blocks = swap_chunks(
            [
                product[k * rows : (k + 1) * rows, g * LANES : (g + 1) * LANES] * weight
                for k in range(share)
            ],
            chunk,
        )
        for i in range(share):
            o_ref[g * share + i] = blocks[i]


def forward_and_turn_kernel(lon_count, scale, size, *refs):
    *inputs, near_ref, far_ref, o_ref, green_ref, ordered = refs
    turn_kernel(size, inputs[0], near_ref, far_ref, green_ref, ordered)
    forward_kernel(lon_count, scale, *inputs, o_ref)


def spectral_kernel(margin, high_ref, low_ref, green_ref, x_ref, o_ref, turned, coeffs, pots):
    share, degrees, width = high_ref.shape
    lat_count, lon_count, rows, _ = x_ref.shape
    total_lat = lat_count * rows
    size = 2 * share
    layers = turned.shape[1] // size
    part = share // 2
    spots = [[m // part * share + c * part + m % part for c in range(2)] for m in range(share)]
    skip = [m // part for m in range(share)]
    used = [slice(first * LANES, degrees) for first in skip]

    def put(ref, m, y):
        first = ref.shape[0] - y.shape[1] // LANES
        for i, r in enumerate(spots[m]):
            put_every(ref.at[first:], r, size, y[i * layers : (i + 1) * layers, :])

    pad = jnp.zeros((width - total_lat, LANES), jnp.float32)
    for q in range(lon_count):
        x = x_ref[:, q].reshape(total_lat, LANES)
        x = jnp.concatenate([x, pad], axis=0)
        for c in range(width // LANES):
            turned[c, q * LANES : (q + 1) * LANES, :] = x[c * LANES : (c + 1) * LANES].T
    for m in range(share):
        x = halves(jnp.concatenate([every(turned, r, size, layers) for r in spots[m]], axis=0))
        y = dot3(x, [ref[m, used[m], :] for ref in (high_ref, low_ref)], NT)
        put(coeffs, m, y)
    block = 8

    def targets(i, carry):
        for c in range(degrees // LANES):
            live = size if c > 0 else share
            sums = [jnp.zeros((live, LANES), jnp.float32) for _ in range(block)]
            for k in range(layers):
                x = coeffs[c, k * size : k * size + live, :]
                for t in range(block):
                    row = green_ref[c, pl.ds((i * block + t) * layers + k, 1), :]
                    sums[t] = sums[t] + row * x
            for t in range(block):
                pots[c, pl.ds(pl.multiple_of((i * block + t) * size, size), live), :] = sums[t]
        return carry

    lax.fori_loop(0, layers // block, targets, 0, unroll=True)
    for m in range(share):
        x = [every(pots.at[skip[m] :], r, size, layers) for r in spots[m]]
        x = halves(jnp.concatenate(x, axis=0))
        y = dot3(x, [ref[m, used[m], :] for ref in (high_ref, low_ref)], NN)
        put(turned, m, y)
    for q in range(lon_count):
        x = [turned[c, q * LANES : (q + 1) * LANES, :].T for c in range(width // LANES)]
        x = jnp.concatenate(x, axis=0)[:total_lat]
        if margin > 0:
            edge = jnp.zeros((margin, LANES), jnp.float32)
            x = jnp.concatenate([edge, x, edge], axis=0)
        for i in range(lat_count):
            o_ref[i, q] = x[i * rows : (i + 1) * rows + 2 * margin]


def inverse_kernel(lon_count, margin, index_ref, high_ref, low_ref, x_ref, *rest):
    pieces, (columns,) = rest[:lon_count], rest[lon_count:]
    owners, rows, _ = x_ref.shape
    cols = high_ref.shape[0] // lon_count
    share = columns.shape[1] // rows
    chunk = LANES // share
    groups = [
        swap_chunks([x_ref[g * share + i] for i in range(share)], chunk)
        for g in range(owners // share)
    ]
    terms = jnp.concatenate(
        [jnp.concatenate([group[k] for group in groups], axis=1) for k in range(share)], axis=0
    )
    terms = halves(terms)
    whole = dot3(terms, (high_ref[...], low_ref[...]), NT)
    for q in range(lon_count):
        columns[q] = whole[:, q * cols : (q + 1) * cols]
    lane = iota((rows, LANES), 1)
    for s in range(lon_count):
        dest = lax.rem(index_ref[1] + s, lon_count)
        pieces[s][0 : share * rows] = columns[dest]
        if margin == 0:
            continue
        after = lax.rem(dest + 1, lon_count)
        before = lax.rem(dest + lon_count - 1, lon_count)
        packed = jnp.zeros((rows, LANES), jnp.float32)
        for k in range(share):
            at = slice(k * rows, (k + 1) * rows)
            ends = jnp.where(lane < LANES - DEEP, columns[after, at, :], columns[before, at, :])
            packed = jnp.where(lane // chunk == k, roll(ends, k * chunk + DEEP, 1), packed)
        pieces[s][share * rows :] = packed


def assemble_kernel(lon_count, index_ref, *rest):
    parts, o_hbm, sem = rest[:lon_count], rest[lon_count], rest[lon_count + 1]
    sources = [lax.rem(index_ref[1] + (lon_count - s), lon_count) for s in range(lon_count)]
    copy_all(sem, *((part, o_hbm.at[source]) for part, source in zip(parts, sources)))


def exchange(pieces):
    count = len(pieces)
    got = {0: pieces[0]}
    for s in (2, 1, 3) if count == 4 else range(1, count):
        got[s] = lax.ppermute(pieces[s], "lon", [(i, (i + s) % count) for i in range(count)])
    return [got[s] for s in range(count)]


def on_device(displacement, materials, ice_mask, ice_height, shear, restoring, contrast, green):
    layers, rows, cols = displacement.shape
    lat_count, lon_count = lax.axis_size("lat"), lax.axis_size("lon")
    total_lat, total_lon = rows * lat_count, cols * lon_count
    owners = lat_count * lon_count
    share, orders = layers // lon_count, LMAX // owners
    width = -(-total_lat // LANES) * LANES
    tall = rows + 2 * SHALLOW
    lat_index = lax.axis_index("lat")
    index = jnp.stack([lat_index, lax.axis_index("lon")]).astype(jnp.int32)
    owner = (index[0] * lon_count + index[1])[None]

    surface = ice_mask.astype(jnp.float32) * ice_height
    own = (
        displacement.reshape(layers * rows, cols),
        materials.reshape(layers * rows, cols),
        surface,
    )
    first, last = call(
        slab_kernel,
        (f32(2 * layers + 1, DEEP, cols),) * 2,
        1.0,
    )(displacement, materials, surface)
    green, first, last = lax.optimization_barrier((green, first, last))
    first, last = (x.reshape(-1, cols) for x in (first, last))
    above = lax.ppermute(last, "lat", [(i, i + 1) for i in range(lat_count - 1)])
    below = lax.ppermute(first, "lat", [(i + 1, i) for i in range(lat_count - 1)])
    table = call(
        functools.partial(fourier_kernel, total_lon, orders),
        (jax.ShapeDtypeStruct((total_lon, 2 * LMAX), HALF),) * 2,
        1.2,
    )()
    def partner(x, step):
        return lax.ppermute(x, "lat", [(i, i ^ step) for i in range(lat_count)])

    near = green.reshape(green.shape[0], layers * layers)
    near, table = lax.optimization_barrier((near, table))
    others = [partner(near, i) for i in range(2, lat_count, 2)]
    half_table = (orders, LMAX, width)
    legendre_table = call(
        functools.partial(legendre_kernel, total_lat, orders),
        (jax.ShapeDtypeStruct(half_table, HALF),) * 2,
        2.9,
        scratch=[pltpu.VMEM((width // LANES, LMAX * orders, LANES), jnp.float32)],
        smem=(0,),
    )(owner)
    above, below, others, table, legendre_table = lax.optimization_barrier(
        (above, below, others, table, legendre_table)
    )
    near = jnp.concatenate([near, *others], axis=0)
    far = partner(near, 1)
    deep = rows + 2 * DEEP
    edge_tiles = f32((deep // 2 + 1) * SUB, cols)
    whole = pltpu.VMEM((deep * SUB, cols), jnp.float32)
    first, last = call(pack_kernel, (edge_tiles,) * 2, 1.5, scratch=[whole, whole])(
        *own, above, below
    )
    left = lax.ppermute(last, "lon", [(i, (i + 1) % lon_count) for i in range(lon_count)])
    right = lax.ppermute(first, "lon", [((i + 1) % lon_count, i) for i in range(lon_count)])
    theta = ((lat_index * rows + jnp.arange(rows)).astype(jnp.float32) + 0.5) * (
        jnp.pi / total_lat
    )
    weight = jnp.broadcast_to((jnp.sin(theta) / (4.0 * total_lat))[:, None], (rows, LANES))

    steps = layers // SUB

    def worked(t, height):
        return (t, 2, height * SUB, LANES)

    flat = pltpu.VMEM((lon_count, share, rows, cols), jnp.float32)
    near_shape = pltpu.VMEM((2 * LANES, 2 * LANES), HALF)
    out = call(
        functools.partial(first_sweeps_kernel, lon_count, total_lat),
        (f32(share, rows, cols),) * lon_count
        + (f32(*worked(steps, deep)),) * 3
        + (f32(*worked(1, deep)),),
        6.6,
        scratch=[pltpu.VMEM(worked(steps, deep), jnp.float32)] * 2
        + [pltpu.VMEM(worked(1, deep), jnp.float32), flat, near_shape],
        smem=(0, 1, 2, 3),
    )(index, shear, restoring, contrast, *own, above, below, left, right)
    pieces, state = out[:lon_count], out[lon_count:]
    for iteration in range(ITERS):
        margin = SHALLOW if iteration < ITERS - 1 else 0
        parts = exchange(pieces)
        scale = 2.0 * math.pi / total_lon
        if iteration == 0:
            spectrum, turned_green = call(
                functools.partial(forward_and_turn_kernel, lon_count, scale, green.shape[0]),
                (
                    f32(owners, rows, LANES),
                    f32(LMAX // LANES, layers * layers, LANES),
                ),
                3.0,
                scratch=[pltpu.VMEM((LMAX, layers * layers), jnp.float32)],
                smem=(0,),
            )(index, weight, *table, *parts, near, far)
        else:
            spectrum = call(
                functools.partial(forward_kernel, lon_count, scale),
                f32(owners, rows, LANES),
                2.0,
                smem=(0,),
            )(index, weight, *table, *parts)
        spectrum = lax.all_to_all(spectrum, BOTH, 0, 0, tiled=True)
        square = pltpu.VMEM((width // LANES, lon_count * LANES, LANES), jnp.float32)
        coeff_shape = pltpu.VMEM((LMAX // LANES, lon_count * LANES, LANES), jnp.float32)
        synth = call(
            functools.partial(spectral_kernel, margin),
            f32(lat_count, lon_count, rows + 2 * margin, LANES),
            4.0,
            scratch=[square, coeff_shape, coeff_shape],
        )(
            *legendre_table,
            turned_green,
            spectrum.reshape(lat_count, lon_count, rows, LANES),
        )
        synth = lax.all_to_all(
            synth.reshape(owners, rows + 2 * margin, LANES), BOTH, 0, 0, tiled=True
        )
        high = rows + 2 * margin
        sent = share * high + (high if margin > 0 else 0)
        parts = call(
            functools.partial(inverse_kernel, lon_count, margin),
            (f32(sent, cols),) * lon_count,
            2.0,
            scratch=[pltpu.VMEM((lon_count, share * high, cols), jnp.float32)],
            smem=(0,),
        )(index, *table, synth)
        parts = exchange(parts)
        if iteration < ITERS - 1:
            out = call(
                functools.partial(second_sweeps_kernel, lon_count),
                (f32(share, rows, cols),) * lon_count + (f32(layers, rows, cols),),
                5.4,
                scratch=[pltpu.VMEM(worked(steps, tall), jnp.float32)] * 3
                + [
                    pltpu.VMEM((steps, tall * SUB, LANES), jnp.float32),
                    pltpu.VMEM((tall * SUB, LANES), jnp.float32),
                    flat,
                    near_shape,
                ],
                smem=(0, 1),
            )(index, contrast, own[1], *state, *parts)
            pieces, field = out[:lon_count], out[lon_count]
    potential = call(
        functools.partial(assemble_kernel, lon_count),
        f32(lon_count, share * rows, cols),
        1.0,
        scratch=[pltpu.SemaphoreType.DMA((lon_count,))],
        smem=(0,),
        hbm=(0,),
    )(index, *parts)
    return (field, potential.reshape(layers, rows, cols))


def aligned(mesh, displacement):
    lat_count, lon_count = mesh.shape["lat"], mesh.shape["lon"]
    layers, total_lat, total_lon = displacement.shape
    rows, cols = total_lat // lat_count, total_lon // lon_count
    owners = lat_count * lon_count
    return (
        ITERS == 2
        and cols == LANES
        and rows % 8 == 0
        and rows + 2 * DEEP <= SUB * SUB
        and layers % SUB == 0
        and 2 * (layers // SUB) * 2 * DEEP <= LANES
        and (layers // lon_count) % (layers // SUB) == 0
        and lat_count > 2
        and lon_count % 2 == 0
        and lat_count & (lat_count - 1) == 0
        and layers % lon_count == 0
        and LMAX % owners == 0
        and 2 * (LMAX // owners) * (layers // lon_count) == LANES
        and 2 * (LMAX // owners) == 2 * DEEP
        and LMAX == 2 * LANES
    )


def solution(mesh):
    in_specs = (
        P(None, "lat", "lon"),
        P(None, "lat", "lon"),
        P("lat", "lon"),
        P("lat", "lon"),
        P(),
        P(),
        P(),
        P("lat", None, None),
    )
    out_specs = (P(None, "lat", "lon"), P(None, "lat", "lon"))

    def step(displacement, *others):
        device = on_device if aligned(mesh, displacement) else general_device
        return jax.shard_map(
            device, mesh=mesh, in_specs=in_specs, out_specs=out_specs, check_vma=False
        )(displacement, *others)

    return step
```
